32 devices in a mesh: fsdp: 8 (over z, x), rep: 4 (over y, core).
Axes of the slice: x: 2, y: 2, z: 4, core: 2. Of those that a mesh axis runs over, the one named last changes fastest.
Arguments:
- inputs: bfloat16 [32, 512, 768], P(('fsdp', 'rep')), may hold values from -6 to 6
- lengths: int32 [32], P(('fsdp', 'rep')), may hold values from 128 to 512, as said below
- cotangent: bfloat16 [32, 512, 768], P(('fsdp', 'rep')), may hold values from -6 to 6
- query_weight: bfloat16 [768, 768], P('fsdp'), may hold values from -0.02734375 to 0.02734375
- key_weight: bfloat16 [768, 768], P('fsdp'), may hold values from -0.21875 to 0.21875
- value_weight: bfloat16 [768, 768], P('fsdp'), may hold values from -0.21875 to 0.21875
- output_weight: bfloat16 [768, 768], P('fsdp'), may hold values from -6 to 6
- attention_gain: bfloat16 [768], P('fsdp'), may hold values from 0.099609375 to 1.8984375
- bias_table: bfloat16 [32, 12], P('fsdp'), may hold values from -4 to 4
- inner_weight: bfloat16 [768, 3072], P('fsdp'), may hold values from -0.21875 to 0.21875
- outer_weight: bfloat16 [3072, 768], P('fsdp'), may hold values from -0.109375 to 0.109375
- feedforward_gain: bfloat16 [768], P('fsdp'), may hold values from 0.099609375 to 1.8984375
Outputs:
- block_output: bfloat16 [32, 512, 768], P(('fsdp', 'rep'))
- input_grad: float32 [32, 512, 768], P(('fsdp', 'rep'))
- query_grad: float32 [768, 768], P('fsdp')
- key_grad: float32 [768, 768], P('fsdp')
- value_grad: float32 [768, 768], P('fsdp')
- output_grad: float32 [768, 768], P('fsdp')
- attention_gain_grad: float32 [768], P('fsdp')
- bias_table_grad: float32 [32, 12], P('fsdp')
- inner_grad: float32 [768, 3072], P('fsdp')
- outer_grad: float32 [3072, 768], P('fsdp')
- feedforward_gain_grad: float32 [768], P('fsdp')
The draws below stay inside these ranges and needn't reach their ends.
Inputs may be any that keep to these rules, and one draw needn't show every extreme that they name: `lengths`: positions below a pair's entry hold the pair, the rest of its 512 slots is padding; some pair has exactly 512 and some exactly 128.
All inputs are finite; a program needn't handle non-finite values.
Results may differ from the reference program's by a relative error of at most 0.02.
Values may be sent and summed in bfloat16 or wider, within the bound.
A program may use at most 192 MiB of HBM per device.

```python
import math
import jax
import jax.numpy as jnp
from jax import lax

D = 768
H = 12
DH = 64
FF = 3072
NB = 32
SEQ = 512
PAIRS = 32


def draw_lengths(key, part):
    key = jax.random.fold_in(key, 11)
    key_lengths, key_long, key_gap = jax.random.split(key, 3)
    lengths_drawn = jax.random.randint(key_lengths, (PAIRS,), SEQ // 4, SEQ + 1)
    longest = jax.random.randint(key_long, (), 0, PAIRS)
    gap_size = jax.random.randint(key_gap, (), 1, PAIRS)
    shortest = (longest + gap_size) % PAIRS
    position_ids = jnp.arange(PAIRS)
    lengths_drawn = jnp.where(position_ids == longest, SEQ, lengths_drawn)
    lengths_drawn = jnp.where(position_ids == shortest, SEQ // 4, lengths_drawn)
    return lengths_drawn.astype(jnp.int32)


def block_levels(own_key, extent, cuts, low, largest):
    def one(axis_at, parts):
        heights = jax.random.uniform(jax.random.fold_in(jax.random.fold_in(own_key, 6), axis_at), (parts,), jnp.float32, low / len(cuts), largest / len(cuts))
        return jnp.repeat(jnp.exp(heights), extent[axis_at] // parts).reshape((-1,) + (1,) * (len(extent) - axis_at - 1))

    level = one(*cuts[0])
    for cut in cuts[1:]:
        level = level * one(*cut)
    return level


def scatter_about(stream_key, shape, width, most, cuts=(), kind=jnp.bfloat16):
    values = jax.random.normal(stream_key, shape, jnp.float32) * width
    if len(cuts) > 0:
        values = block_levels(stream_key, shape, cuts, -0.22, 0.18) * values
    return jnp.clip(values, min=-most, max=most).astype(kind)


def setup_inputs(seed: int = 0) -> dict:
    seeds = jax.random.split(jax.random.key(seed), 13)
    inputs = scatter_about(seeds[0], (PAIRS, SEQ, D), 1.0, 6.0, ((0, 32),))
    lengths = draw_lengths(jax.random.fold_in(seeds[12], 71), 0)
    cotangent = scatter_about(seeds[2], (PAIRS, SEQ, D), 1.0, 6.0, ((0, 32),))
    query_weight = scatter_about(seeds[3], (D, D), (D * DH) ** -0.5, 0.02734375, ((0, 8),))
    key_weight = scatter_about(seeds[4], (D, D), D ** -0.5, 0.21875, ((0, 8),))
    value_weight = scatter_about(seeds[5], (D, D), D ** -0.5, 0.21875, ((0, 8),))
    output_weight = scatter_about(seeds[6], (D, D), (max(1, D // SEQ)) ** -0.5, 6.0, ((0, 8),))
    attention_gain = jnp.clip(1.0 + 0.18 * jax.random.normal(seeds[7], (D,), jnp.float32), 0.099609375, 1.8984375).astype(jnp.bfloat16)
    bias_table = scatter_about(seeds[8], (NB, H), 0.7, 4.0, ((0, 8),))
    inner_weight = scatter_about(seeds[9], (D, FF), D ** -0.5, 0.21875, ((0, 8),))
    outer_weight = scatter_about(seeds[10], (FF, D), FF ** -0.5, 0.109375, ((0, 8),))
    feedforward_gain = jnp.clip(1.0 + 0.18 * jax.random.normal(seeds[11], (D,), jnp.float32), 0.099609375, 1.8984375).astype(jnp.bfloat16)
    return {"inputs": inputs, "lengths": lengths, "cotangent": cotangent, "query_weight": query_weight, "key_weight": key_weight, "value_weight": value_weight, "output_weight": output_weight, "attention_gain": attention_gain, "bias_table": bias_table, "inner_weight": inner_weight, "outer_weight": outer_weight, "feedforward_gain": feedforward_gain}


epsilon = 1e-06
highest = lax.Precision.HIGHEST
gelu_coeff = 0.7978845608028654
masked_score = -1e+30

@jax.custom_vjp
def low(v):
    return lax.optimization_barrier(v.astype(jnp.bfloat16)).astype(jnp.float32)

@jax.custom_vjp
def low_back(v):
    return v

def low_keep(v):
    return (low(v), None)

def low_pass(kept, grad):
    return (grad,)

def back_keep(v):
    return (v, None)

def back_low(kept, grad):
    return (low(grad),)
low.defvjp(low_keep, low_pass)
low_back.defvjp(back_keep, back_low)

def bucket_of(offset):
    half_count = NB // 2
    exact_count = half_count // 2
    distance = jnp.abs(offset)
    beyond = jnp.full(offset.shape, exact_count, jnp.int32)
    for exponent in range(1, half_count - exact_count):
        beyond = beyond + (distance * distance >= exact_count * exact_count * 2 ** exponent).astype(jnp.int32)
    nearby = jnp.where(distance < exact_count, distance, beyond).astype(jnp.int32)
    return jnp.where(offset > 0, half_count, 0).astype(jnp.int32) + nearby

def rms_norm(values, gain_vector):
    inverse_rms = lax.rsqrt(lax.optimization_barrier(jnp.mean(values * values, axis=-1, keepdims=True)) + epsilon)
    return values * inverse_rms * gain_vector

def gelu(values):
    return 0.5 * values * (1.0 + jnp.tanh(gelu_coeff * (values + 0.044715 * values * values * values)))

def forward(inputs, lengths, params):
    query_weight, key_weight, value_weight, output_weight, attention_gain, bias_table, inner_weight, outer_weight, feedforward_gain = params
    group_size, seq_len, model_width = inputs.shape
    head_count = bias_table.shape[1]
    head_size = model_width // head_count
    normed = low(rms_norm(inputs, attention_gain))

    def project(weight):
        product = jnp.einsum('gld,de->gle', normed, weight, precision=highest)
        return low(low_back(product)).reshape(group_size, seq_len, head_count, head_size)
    queries = project(query_weight)
    key_rows = project(key_weight)
    value_rows = project(value_weight)
    positions = jnp.arange(seq_len, dtype=jnp.int32)
    buckets = bucket_of(positions[None, :] - positions[:, None])
    bias_rows = jnp.transpose(jnp.take(bias_table, buckets, axis=0), (2, 0, 1))
    scores = jnp.einsum('gihe,gjhe->ghij', queries, key_rows, precision=highest) + bias_rows[None]
    scores = low_back(scores)
    key_valid = positions[None, :] < lengths[:, None]
    scores = jnp.where(key_valid[:, None, None, :], scores, masked_score)
    shifted = scores - lax.optimization_barrier(jnp.max(scores, axis=-1, keepdims=True))
    exp_scores = jnp.exp(shifted)
    soft_probs = low(exp_scores / lax.optimization_barrier(jnp.sum(exp_scores, axis=-1, keepdims=True)))
    attended = jnp.einsum('ghij,gjhe->gihe', soft_probs, value_rows, precision=highest)
    attended = low(low_back(attended.reshape(group_size, seq_len, model_width)))
    branch = low_back(jnp.einsum('gld,de->gle', attended, output_weight, precision=highest))
    middle = inputs + branch
    normed_ffn = low(rms_norm(middle, feedforward_gain))
    raised = low_back(jnp.einsum('gld,df->glf', normed_ffn, inner_weight, precision=highest))
    active = low(gelu(raised))
    lowered = low_back(jnp.einsum('glf,fd->gld', active, outer_weight, precision=highest))
    return middle + lowered

def reference(inputs, lengths, cotangent, query_weight, key_weight, value_weight, output_weight, attention_gain, bias_table, inner_weight, outer_weight, feedforward_gain):
    group_size = math.gcd(PAIRS, max(1, 4096 // SEQ))
    blocks = PAIRS // group_size
    weights = (query_weight.astype(jnp.float32), key_weight.astype(jnp.float32), value_weight.astype(jnp.float32), output_weight.astype(jnp.float32), attention_gain.astype(jnp.float32), bias_table.astype(jnp.float32), inner_weight.astype(jnp.float32), outer_weight.astype(jnp.float32), feedforward_gain.astype(jnp.float32))
    positions = jnp.arange(SEQ, dtype=jnp.int32)
    row_live = (positions[None, :] < lengths[:, None]).astype(jnp.float32)
    seed_rows = cotangent.astype(jnp.float32) * row_live[:, :, None]
    grouped_inputs = inputs.astype(jnp.float32).reshape(blocks, group_size, SEQ, D)
    grouped_seeds = seed_rows.reshape(blocks, group_size, SEQ, D)
    grouped_lengths = lengths.reshape(blocks, group_size)

    def one_block(totals, block_items):
        block_inputs, block_lengths, block_seeds = block_items

        def local_pass(block_in, params):
            return forward(block_in, block_lengths, params)
        result, pullback = jax.vjp(local_pass, block_inputs, weights)
        input_part, weight_parts = pullback(block_seeds)
        totals = jax.tree.map(lambda left, right: left + right, totals, weight_parts)
        return (totals, (result, input_part))
    zero_tree = jax.tree.map(jnp.zeros_like, weights)
    totals, (outputs, input_grads) = lax.scan(one_block, zero_tree, (grouped_inputs, grouped_lengths, grouped_seeds))
    return (outputs.reshape(PAIRS, SEQ, D).astype(jnp.bfloat16), input_grads.reshape(PAIRS, SEQ, D), totals[0], totals[1], totals[2], totals[3], totals[4], totals[5], totals[6], totals[7], totals[8])
```

```python
import functools

import jax
import jax.numpy as jnp
from jax import lax
import jax.experimental.pallas as pl
import jax.experimental.pallas.tpu as pltpu
from jax.sharding import PartitionSpec as P

NB = 32


epsilon = 1e-06
highest = lax.Precision.HIGHEST
gelu_coeff = 0.7978845608028654
masked_score = -1e30


def bucket_of(offset):
    half_count = NB // 2
    exact_count = half_count // 2
    distance = jnp.abs(offset)
    beyond = jnp.full(offset.shape, exact_count, jnp.int32)
    for exponent in range(1, half_count - exact_count):
        beyond = beyond + (distance * distance >= exact_count * exact_count * 2**exponent).astype(
            jnp.int32
        )
    nearby = jnp.where(distance < exact_count, distance, beyond)
    return jnp.where(offset > 0, half_count, 0).astype(jnp.int32) + nearby


def rms_norm(values, gain_vector):
    inverse_rms = lax.rsqrt(jnp.mean(values * values, axis=-1, keepdims=True) + epsilon)
    return values * inverse_rms * gain_vector


def gelu(values):
    return (
        0.5 * values * (1.0 + jnp.tanh(gelu_coeff * (values + 0.044715 * values * values * values)))
    )


def dot(a,b): return jnp.dot(a,b,preferred_element_type=jnp.float32)
def dot_t(a,b): return lax.dot_general(a,b,(((1,),(1,)),((),())),preferred_element_type=jnp.float32)
def dot_c(a,b): return lax.dot_general(a,b,(((0,),(0,)),((),())),preferred_element_type=jnp.float32)

def fwd_kernel(T, len_ref, q_ref, k_ref, v_ref, rel_ref, o_ref, p_ref, strip):
    hp=pl.program_id(0)
    seq=q_ref.shape[0]; nb=seq//T
    lane=lax.broadcasted_iota(jnp.int32,(1,128),1)
    kcol=lax.broadcasted_iota(jnp.int32,(1,seq),1)
    mask=jnp.where(kcol<len_ref[0],0.0,-1e30)
    k=k_ref[...]; v=v_ref[...]
    for hh in range(2):
        mine=(lane>=64) if hh else (lane<64)
        rel=rel_ref[pl.ds(hh,1),:]
        W=4*T
        rolled=pltpu.roll(jnp.broadcast_to(rel,(T,W)),0,axis=1,stride=1,stride_axis=0)
        strip[:, 2*T:5*T]=rolled[:, :3*T]
        far_neg=rel[:, 0:1]; far_pos=rel[:, 3*T-1:3*T]
        strip[:, 0:2*T]=jnp.broadcast_to(far_neg,(T,2*T))
        strip[:, 5*T:7*T]=jnp.broadcast_to(far_pos,(T,2*T))
        for I in range(nb):
            q=jnp.where(mine,q_ref[I*T:(I+1)*T,:],jnp.bfloat16(0))
            s=dot_t(q,k)+(strip[:, (3-I)*T:(3-I)*T+seq]+mask)
            m=jnp.max(s,axis=-1,keepdims=True)
            e=jnp.exp(s-m)
            tot=jnp.sum(e,axis=-1,keepdims=True)
            p=(e*(1.0/tot)).astype(jnp.bfloat16)
            p_ref[hh,I*T:(I+1)*T,:]=p
            o=dot(p,v)
            if hh==0:
                o_ref[I*T:(I+1)*T,:]=o.astype(jnp.bfloat16)
            else:
                o_ref[I*T:(I+1)*T,:]=jnp.where(mine,o.astype(jnp.bfloat16),o_ref[I*T:(I+1)*T,:])

def bwd_kernel(T, q_ref, k_ref, v_ref, do_ref, p_ref, dq_ref, dk_ref, dv_ref, db_ref, ds_ref):
    seq=q_ref.shape[0]; nb=seq//T
    lane=lax.broadcasted_iota(jnp.int32,(1,128),1)
    k=k_ref[...]; v=v_ref[...]
    dks=[];dvs=[]
    for hh in range(2):
        mine=(lane>=64) if hh else (lane<64)
        acc=[None]*5
        for I in range(nb):
            sl=slice(I*T,(I+1)*T)
            do=jnp.where(mine,do_ref[sl,:],jnp.bfloat16(0))
            dp=dot_t(do,v)
            p=p_ref[hh,sl,:].astype(jnp.float32)
            t=p*dp
            delta=jnp.sum(t,axis=-1,keepdims=True)
            ds=(t-p*delta).astype(jnp.bfloat16)
            ds_ref[sl,:]=ds
            dsf=ds.astype(jnp.float32)
            for J in range(nb):
                d=min(2,max(-2,J-I))+2
                x=dsf[:,J*T:(J+1)*T]
                acc[d]=x if acc[d] is None else acc[d]+x
            dq=dot(ds,k)
            if hh==0: dq_ref[sl,:]=dq.astype(jnp.bfloat16)
            else: dq_ref[sl,:]=jnp.where(mine,dq.astype(jnp.bfloat16),dq_ref[sl,:])
        near=jnp.concatenate([acc[1],acc[2],acc[3],jnp.zeros((T,T),jnp.float32)],axis=1)
        total=shear_sum(near,4*T)
        far=jnp.concatenate([jnp.zeros((1,2*T),jnp.float32),jnp.sum(acc[4],axis=0,keepdims=True),jnp.sum(acc[0],axis=0,keepdims=True)],axis=1)
        db_ref[hh:hh+1,:]=total+far
        dk=dot_c(q_ref[...],ds_ref[...]).T; dv=dot_c(do_ref[...],p_ref[hh]).T
        dks.append(dk); dvs.append(dv)
    dk_ref[...]=jnp.where(lane<64,dks[0],dks[1]).astype(jnp.bfloat16)
    dv_ref[...]=jnp.where(lane<64,dvs[0],dvs[1]).astype(jnp.bfloat16)

def rel_hits(tile):
    slot = jnp.arange(4 * tile, dtype=jnp.int32)
    offset = jnp.where(slot < 3 * tile, slot - tile, slot - 5 * tile)
    bucket_ids = jnp.arange(NB, dtype=jnp.int32)
    return (bucket_of(offset)[None, :] == bucket_ids[:, None]).astype(jnp.bfloat16)


def rel_vec(table, tile):
    return dot_c(table, rel_hits(tile))


def shear_sum(block, width):
    rows = block.shape[0]
    while rows > 8:
        rows //= 2
        block = block[:rows] + pltpu.roll(block[rows:], width - rows, axis=1)
    total = block[0:1]
    for r in range(1, 8):
        total = total + pltpu.roll(block[r : r + 1], width - r, axis=1)
    return total


def att_fwd(q,k,v,rel,length,T=128):
    seq,D=q.shape; H=rel.shape[0]
    blk=pl.BlockSpec((seq,128),lambda h: (0,h))
    return pl.pallas_call(functools.partial(fwd_kernel,T),grid=(H//2,),
        in_specs=[pl.BlockSpec(memory_space=pltpu.SMEM),blk,blk,blk,pl.BlockSpec((None,2,4*T),lambda h:(h,0,0))],
        out_specs=[blk,pl.BlockSpec((2,seq,seq),lambda h:(h,0,0))],
        out_shape=[jax.ShapeDtypeStruct((seq,D),jnp.bfloat16),jax.ShapeDtypeStruct((H,seq,seq),jnp.bfloat16)],
        scratch_shapes=[pltpu.VMEM((T,7*T),jnp.float32)],
        compiler_params=pltpu.CompilerParams(vmem_limit_bytes=40*2**20))(length,q,k,v,rel.reshape(H//2,2,4*T))
def att_bwd(q,k,v,do,p,T=128):
    seq,D=q.shape; H=p.shape[0]
    blk=pl.BlockSpec((seq,128),lambda h: (0,h))
    o=jax.ShapeDtypeStruct((seq,D),jnp.bfloat16)
    outs=pl.pallas_call(functools.partial(bwd_kernel,T),grid=(H//2,),
        in_specs=[blk,blk,blk,blk,pl.BlockSpec((2,seq,seq),lambda h:(h,0,0))],
        out_specs=[blk,blk,blk,pl.BlockSpec((None,2,4*T),lambda h:(h,0,0))],
        out_shape=[o,o,o,jax.ShapeDtypeStruct((H//2,2,4*T),jnp.float32)],
        scratch_shapes=[pltpu.VMEM((seq,seq),jnp.bfloat16)],
        compiler_params=pltpu.CompilerParams(vmem_limit_bytes=40*2**20))(q,k,v,do,p)
    return *outs[:3],outs[3].reshape(H,4*T)

def contract_rows(left, right):
    return lax.dot_general(
        left, right, (((0,), (0,)), ((), ())), preferred_element_type=jnp.float32
    )


def contract_cols(left, right):
    return lax.dot_general(
        left, right, (((1,), (1,)), ((), ())), preferred_element_type=jnp.float32
    )


def local(
    inputs,
    lengths,
    cotangent,
    query_weight,
    key_weight,
    value_weight,
    output_weight,
    attention_gain,
    bias_table,
    inner_weight,
    outer_weight,
    feedforward_gain,
):
    pairs_here, seq_len, model_width = inputs.shape
    row_count = pairs_here * seq_len
    full_query, full_key, full_value, full_output, full_gain, full_table = (
        lax.all_gather(query_weight, "fsdp", axis=0, tiled=True),
        lax.all_gather(key_weight, "fsdp", axis=0, tiled=True),
        lax.all_gather(value_weight, "fsdp", axis=0, tiled=True),
        lax.all_gather(output_weight, "fsdp", axis=0, tiled=True),
        lax.all_gather(attention_gain, "fsdp", axis=0, tiled=True),
        lax.all_gather(bias_table, "fsdp", axis=0, tiled=True),
    )
    head_count = full_table.shape[1]
    tile = 128
    relative = rel_vec(full_table, tile)
    flat_inputs = inputs.reshape(row_count, model_width).astype(jnp.float32)
    normed = rms_norm(flat_inputs, full_gain.astype(jnp.float32)).astype(jnp.bfloat16)
    joined = jnp.concatenate((full_query, full_key, full_value), axis=1)
    projected = jnp.dot(normed, joined, preferred_element_type=jnp.float32).astype(jnp.bfloat16)
    queries = projected[:, :model_width]
    key_rows = projected[:, model_width : 2 * model_width]
    value_rows = projected[:, 2 * model_width :]
    pair_rows = [slice(n * seq_len, (n + 1) * seq_len) for n in range(pairs_here)]
    forward_parts = [
        att_fwd(queries[r], key_rows[r], value_rows[r], relative, lengths[n : n + 1], tile)
        for n, r in enumerate(pair_rows)
    ]
    attended = jnp.concatenate([part[0] for part in forward_parts], axis=0)
    middle = flat_inputs + jnp.dot(attended, full_output, preferred_element_type=jnp.float32)
    full_inner, full_outer, full_ffn_gain = (
        lax.all_gather(inner_weight, "fsdp", axis=0, tiled=True),
        lax.all_gather(outer_weight, "fsdp", axis=0, tiled=True),
        lax.all_gather(feedforward_gain, "fsdp", axis=0, tiled=True),
    )
    normed_ffn = rms_norm(middle, full_ffn_gain.astype(jnp.float32)).astype(jnp.bfloat16)
    raised = jnp.dot(normed_ffn, full_inner, preferred_element_type=jnp.float32)
    active = gelu(raised).astype(jnp.bfloat16)
    lowered = jnp.dot(active, full_outer, preferred_element_type=jnp.float32)
    block_output = (middle + lowered).astype(jnp.bfloat16).reshape(pairs_here, seq_len, model_width)
    positions = jnp.arange(seq_len, dtype=jnp.int32)
    row_live = (positions[None, :] < lengths[:, None]).astype(jnp.float32)
    seed_rows = (cotangent.astype(jnp.float32) * row_live[:, :, None]).reshape(
        row_count, model_width
    )
    full_inner, full_outer, full_ffn_gain = (
        lax.all_gather(inner_weight, "fsdp", axis=0, tiled=True),
        lax.all_gather(outer_weight, "fsdp", axis=0, tiled=True),
        lax.all_gather(feedforward_gain, "fsdp", axis=0, tiled=True),
    )
    seed_low = seed_rows.astype(jnp.bfloat16)
    grad_active = contract_cols(seed_low, full_outer)
    grad_outer = contract_rows(active, seed_low)
    grad_raised = jax.vjp(gelu, raised)[1](grad_active)[0].astype(jnp.bfloat16)
    grad_inner = contract_rows(normed_ffn, grad_raised)
    grad_normed_ffn = contract_cols(grad_raised, full_inner)
    ffn_pull = jax.vjp(rms_norm, middle, full_ffn_gain.astype(jnp.float32))[1]
    grad_middle_part, grad_ffn_gain = ffn_pull(grad_normed_ffn)
    grad_middle = seed_rows + grad_middle_part
    full_query, full_key, full_value, full_output, full_gain, full_table = (
        lax.all_gather(query_weight, "fsdp", axis=0, tiled=True),
        lax.all_gather(key_weight, "fsdp", axis=0, tiled=True),
        lax.all_gather(value_weight, "fsdp", axis=0, tiled=True),
        lax.all_gather(output_weight, "fsdp", axis=0, tiled=True),
        lax.all_gather(attention_gain, "fsdp", axis=0, tiled=True),
        lax.all_gather(bias_table, "fsdp", axis=0, tiled=True),
    )
    joined = jnp.concatenate((full_query, full_key, full_value), axis=1)
    middle_low = grad_middle.astype(jnp.bfloat16)
    grad_attended = contract_cols(middle_low, full_output).astype(jnp.bfloat16)
    grad_output = contract_rows(attended, middle_low)
    backward_parts = [
        att_bwd(
            queries[r], key_rows[r], value_rows[r], grad_attended[r], forward_parts[n][1], tile
        )
        for n, r in enumerate(pair_rows)
    ]
    grad_projected = jnp.concatenate(
        [jnp.concatenate(part[:3], axis=1) for part in backward_parts], axis=0
    )
    grad_joined = contract_rows(normed, grad_projected)
    grad_normed = contract_cols(grad_projected, joined)
    attention_pull = jax.vjp(rms_norm, flat_inputs, full_gain.astype(jnp.float32))[1]
    grad_inputs_part, grad_attention_gain = attention_pull(grad_normed)
    input_grad = (grad_middle + grad_inputs_part).reshape(pairs_here, seq_len, model_width)
    grad_relative = sum(part[3] for part in backward_parts)
    grad_table = lax.dot_general(
        rel_hits(tile).astype(jnp.float32),
        grad_relative,
        (((1,), (1,)), ((), ())),
        precision=highest,
    )
    gradients = (
        grad_joined[:, :model_width],
        grad_joined[:, model_width : 2 * model_width],
        grad_joined[:, 2 * model_width :],
        grad_output,
        grad_attention_gain,
        grad_table,
        grad_inner,
        grad_outer,
        grad_ffn_gain,
    )
    shard_inner, shard_outer, shard_ffn_gain = (
        lax.psum_scatter(
            gradients[6].astype(jnp.bfloat16), "fsdp", scatter_dimension=0, tiled=True
        ).astype(jnp.float32),
        lax.psum_scatter(
            gradients[7].astype(jnp.bfloat16), "fsdp", scatter_dimension=0, tiled=True
        ).astype(jnp.float32),
        lax.psum_scatter(
            gradients[8].astype(jnp.bfloat16), "fsdp", scatter_dimension=0, tiled=True
        ).astype(jnp.float32),
    )
    shard_query, shard_key, shard_value, shard_output, shard_attention_gain, shard_table = (
        lax.psum_scatter(
            gradients[0].astype(jnp.bfloat16), "fsdp", scatter_dimension=0, tiled=True
        ).astype(jnp.float32),
        lax.psum_scatter(
            gradients[1].astype(jnp.bfloat16), "fsdp", scatter_dimension=0, tiled=True
        ).astype(jnp.float32),
        lax.psum_scatter(
            gradients[2].astype(jnp.bfloat16), "fsdp", scatter_dimension=0, tiled=True
        ).astype(jnp.float32),
        lax.psum_scatter(
            gradients[3].astype(jnp.bfloat16), "fsdp", scatter_dimension=0, tiled=True
        ).astype(jnp.float32),
        lax.psum_scatter(
            gradients[4].astype(jnp.bfloat16), "fsdp", scatter_dimension=0, tiled=True
        ).astype(jnp.float32),
        lax.psum_scatter(
            gradients[5].astype(jnp.bfloat16), "fsdp", scatter_dimension=0, tiled=True
        ).astype(jnp.float32),
    )
    summed = (
        lax.psum(shard_query.astype(jnp.bfloat16), "rep").astype(jnp.float32),
        lax.psum(shard_key.astype(jnp.bfloat16), "rep").astype(jnp.float32),
        lax.psum(shard_value.astype(jnp.bfloat16), "rep").astype(jnp.float32),
        lax.psum(shard_output.astype(jnp.bfloat16), "rep").astype(jnp.float32),
        lax.psum(shard_attention_gain.astype(jnp.bfloat16), "rep").astype(jnp.float32),
        lax.psum(shard_table.astype(jnp.bfloat16), "rep").astype(jnp.float32),
        lax.psum(shard_inner.astype(jnp.bfloat16), "rep").astype(jnp.float32),
        lax.psum(shard_outer.astype(jnp.bfloat16), "rep").astype(jnp.float32),
        lax.psum(shard_ffn_gain.astype(jnp.bfloat16), "rep").astype(jnp.float32),
    )
    return (
        block_output,
        input_grad,
        summed[0],
        summed[1],
        summed[2],
        summed[3],
        summed[4],
        summed[5],
        summed[6],
        summed[7],
        summed[8],
    )


def solution(mesh):
    placed = (
        P(("fsdp", "rep"), None, None),
        P(("fsdp", "rep")),
        P(("fsdp", "rep"), None, None),
        P("fsdp", None),
        P("fsdp", None),
        P("fsdp", None),
        P("fsdp", None),
        P("fsdp"),
        P("fsdp", None),
        P("fsdp", None),
        P("fsdp", None),
        P("fsdp"),
    )
    return jax.shard_map(
        local,
        mesh=mesh,
        in_specs=placed,
        out_specs=(
            P(("fsdp", "rep"), None, None),
            P(("fsdp", "rep"), None, None),
            P("fsdp", None),
            P("fsdp", None),
            P("fsdp", None),
            P("fsdp", None),
            P("fsdp"),
            P("fsdp", None),
            P("fsdp", None),
            P("fsdp", None),
            P("fsdp"),
        ),
        check_vma=False,
    )
```

```python
import functools

import jax
import jax.numpy as jnp
from jax import lax
import jax.experimental.pallas as pl
import jax.experimental.pallas.tpu as pltpu
from jax.sharding import PartitionSpec as P

NB = 32


epsilon = 1e-06
highest = lax.Precision.HIGHEST
gelu_coeff = 0.7978845608028654
masked_score = -1e30


def bucket_of(offset):
    half_count = NB // 2
    exact_count = half_count // 2
    distance = jnp.abs(offset)
    beyond = jnp.full(offset.shape, exact_count, jnp.int32)
    for exponent in range(1, half_count - exact_count):
        beyond = beyond + (distance * distance >= exact_count * exact_count * 2**exponent).astype(
            jnp.int32
        )
    nearby = jnp.where(distance < exact_count, distance, beyond)
    return jnp.where(offset > 0, half_count, 0).astype(jnp.int32) + nearby


def rms_norm(values, gain_vector):
    inverse_rms = lax.rsqrt(jnp.mean(values * values, axis=-1, keepdims=True) + epsilon)
    return values * inverse_rms * gain_vector


def gelu(values):
    return (
        0.5 * values * (1.0 + jnp.tanh(gelu_coeff * (values + 0.044715 * values * values * values)))
    )


def dot(a,b): return jnp.dot(a,b,preferred_element_type=jnp.float32)
def dot_t(a,b): return lax.dot_general(a,b,(((1,),(1,)),((),())),preferred_element_type=jnp.float32)
def dot_c(a,b): return lax.dot_general(a,b,(((0,),(0,)),((),())),preferred_element_type=jnp.float32)

def fwd_kernel(T, len_ref, q_ref, k_ref, v_ref, rel_ref, o_ref, p_ref, strip):
    hp=pl.program_id(0)
    seq=q_ref.shape[0]; nb=seq//T
    lane=lax.broadcasted_iota(jnp.int32,(1,128),1)
    kcol=lax.broadcasted_iota(jnp.int32,(1,seq),1)
    mask=jnp.where(kcol<len_ref[0],0.0,-1e30)
    k=k_ref[...]; v=v_ref[...]
    for hh in range(2):
        mine=(lane>=64) if hh else (lane<64)
        rel=rel_ref[pl.ds(hh,1),:]
        W=4*T
        rolled=pltpu.roll(jnp.broadcast_to(rel,(T,W)),0,axis=1,stride=1,stride_axis=0)
        strip[:, 2*T:5*T]=rolled[:, :3*T]
        far_neg=rel[:, 0:1]; far_pos=rel[:, 3*T-1:3*T]
        strip[:, 0:2*T]=jnp.broadcast_to(far_neg,(T,2*T))
        strip[:, 5*T:7*T]=jnp.broadcast_to(far_pos,(T,2*T))
        for I in range(nb):
            q=jnp.where(mine,q_ref[I*T:(I+1)*T,:],jnp.bfloat16(0))
            s=dot_t(q,k)+(strip[:, (3-I)*T:(3-I)*T+seq]+mask)
            m=jnp.max(s,axis=-1,keepdims=True)
            e=jnp.exp(s-m)
            tot=jnp.sum(e,axis=-1,keepdims=True)
            p=(e*(1.0/tot)).astype(jnp.bfloat16)
            p_ref[hh,I*T:(I+1)*T,:]=p
            o=dot(p,v)
            if hh==0:
                o_ref[I*T:(I+1)*T,:]=o.astype(jnp.bfloat16)
            else:
                o_ref[I*T:(I+1)*T,:]=jnp.where(mine,o.astype(jnp.bfloat16),o_ref[I*T:(I+1)*T,:])

def bwd_kernel(T, q_ref, k_ref, v_ref, do_ref, p_ref, dq_ref, dk_ref, dv_ref, db_ref, ds_ref):
    seq=q_ref.shape[0]; nb=seq//T
    lane=lax.broadcasted_iota(jnp.int32,(1,128),1)
    k=k_ref[...]; v=v_ref[...]
    dks=[];dvs=[]
    for hh in range(2):
        mine=(lane>=64) if hh else (lane<64)
        acc=[None]*5
        for I in range(nb):
            sl=slice(I*T,(I+1)*T)
            do=jnp.where(mine,do_ref[sl,:],jnp.bfloat16(0))
            dp=dot_t(do,v)
            p=p_ref[hh,sl,:].astype(jnp.float32)
            t=p*dp
            delta=jnp.sum(t,axis=-1,keepdims=True)
            ds=(t-p*delta).astype(jnp.bfloat16)
            ds_ref[sl,:]=ds
            dsf=ds.astype(jnp.float32)
            for J in range(nb):
                d=min(2,max(-2,J-I))+2
                x=dsf[:,J*T:(J+1)*T]
                acc[d]=x if acc[d] is None else acc[d]+x
            dq=dot(ds,k)
            if hh==0: dq_ref[sl,:]=dq.astype(jnp.bfloat16)
            else: dq_ref[sl,:]=jnp.where(mine,dq.astype(jnp.bfloat16),dq_ref[sl,:])
        near=jnp.concatenate([acc[1],acc[2],acc[3],jnp.zeros((T,T),jnp.float32)],axis=1)
        total=shear_sum(near,4*T)
        far=jnp.concatenate([jnp.zeros((1,2*T),jnp.float32),jnp.sum(acc[4],axis=0,keepdims=True),jnp.sum(acc[0],axis=0,keepdims=True)],axis=1)
        db_ref[hh:hh+1,:]=total+far
        dk=dot_c(q_ref[...],ds_ref[...]).T; dv=dot_c(do_ref[...],p_ref[hh]).T
        dks.append(dk); dvs.append(dv)
    dk_ref[...]=jnp.where(lane<64,dks[0],dks[1]).astype(jnp.bfloat16)
    dv_ref[...]=jnp.where(lane<64,dvs[0],dvs[1]).astype(jnp.bfloat16)

def rel_hits(tile):
    slot = jnp.arange(4 * tile, dtype=jnp.int32)
    offset = jnp.where(slot < 3 * tile, slot - tile, slot - 5 * tile)
    bucket_ids = jnp.arange(NB, dtype=jnp.int32)
    return (bucket_of(offset)[None, :] == bucket_ids[:, None]).astype(jnp.bfloat16)


def rel_vec(table, tile):
    return dot_c(table, rel_hits(tile))


def shear_sum(block, width):
    rows = block.shape[0]
    while rows > 8:
        rows //= 2
        block = block[:rows] + pltpu.roll(block[rows:], width - rows, axis=1)
    total = block[0:1]
    for r in range(1, 8):
        total = total + pltpu.roll(block[r : r + 1], width - r, axis=1)
    return total


def att_fwd(q,k,v,rel,length,T=128):
    seq,D=q.shape; H=rel.shape[0]
    blk=pl.BlockSpec((seq,128),lambda h: (0,h))
    return pl.pallas_call(functools.partial(fwd_kernel,T),grid=(H//2,),
        in_specs=[pl.BlockSpec(memory_space=pltpu.SMEM),blk,blk,blk,pl.BlockSpec((None,2,4*T),lambda h:(h,0,0))],
        out_specs=[blk,pl.BlockSpec((2,seq,seq),lambda h:(h,0,0))],
        out_shape=[jax.ShapeDtypeStruct((seq,D),jnp.bfloat16),jax.ShapeDtypeStruct((H,seq,seq),jnp.bfloat16)],
        scratch_shapes=[pltpu.VMEM((T,7*T),jnp.float32)],
        compiler_params=pltpu.CompilerParams(vmem_limit_bytes=40*2**20))(length,q,k,v,rel.reshape(H//2,2,4*T))
def att_bwd(q,k,v,do,p,T=128):
    seq,D=q.shape; H=p.shape[0]
    blk=pl.BlockSpec((seq,128),lambda h: (0,h))
    o=jax.ShapeDtypeStruct((seq,D),jnp.bfloat16)
    outs=pl.pallas_call(functools.partial(bwd_kernel,T),grid=(H//2,),
        in_specs=[blk,blk,blk,blk,pl.BlockSpec((2,seq,seq),lambda h:(h,0,0))],
        out_specs=[blk,blk,blk,pl.BlockSpec((None,2,4*T),lambda h:(h,0,0))],
        out_shape=[o,o,o,jax.ShapeDtypeStruct((H//2,2,4*T),jnp.float32)],
        scratch_shapes=[pltpu.VMEM((seq,seq),jnp.bfloat16)],
        compiler_params=pltpu.CompilerParams(vmem_limit_bytes=40*2**20))(q,k,v,do,p)
    return *outs[:3],outs[3].reshape(H,4*T)

def contract_rows(left, right):
    return lax.dot_general(
        left, right, (((0,), (0,)), ((), ())), preferred_element_type=jnp.float32
    )


def contract_cols(left, right):
    return lax.dot_general(
        left, right, (((1,), (1,)), ((), ())), preferred_element_type=jnp.float32
    )


MESH = pl.DeviceIdType.MESH


def coords():
    shard = lax.axis_index("fsdp")
    copy = lax.axis_index("rep")
    return shard // 2, shard % 2, copy // 2, copy % 2


def greet():
    barrier = pltpu.get_barrier_semaphore()
    shard = lax.axis_index("fsdp")
    copy = lax.axis_index("rep")
    for k in range(1, 8):
        peer = (lax.rem(shard + k, 8), copy)
        pl.semaphore_signal(barrier, inc=1, device_id=peer, device_id_type=MESH)
    for k in range(1, 4):
        peer = (shard, lax.rem(copy + k, 4))
        pl.semaphore_signal(barrier, inc=1, device_id=peer, device_id_type=MESH)
    pl.semaphore_wait(barrier, 10)


def schedule(stages, count):
    last = max(lag for _, lag in stages)

    def step(t, carry):
        for stage, lag in stages:
            g = t - lag
            pl.when((g >= 0) & (g < count))(functools.partial(stage, g))
        return carry

    lax.fori_loop(0, count + last, step, 0)


class Links:
    def __init__(self, rows, send_sems, recv_sems):
        self.send_sems, self.recv_sems = send_sems, recv_sems
        self.z, self.x, self.y, self.c = coords()
        half = rows // 2
        part = half // 3
        at = lambda start, size: pl.ds(pl.multiple_of(start, part), size)
        first = half * self.c
        other = half * (1 - self.c)
        self.half, self.other_half = at(first, half), at(other, half)
        self.plane = at(first + part * self.y, 2 * part)
        self.shared = at(first + part, part)
        self.own_third = at(first + 2 * part * self.y, part)
        self.other_third = at(first + 2 * part * (1 - self.y), part)
        self.shared_in = at(part * self.y, part)
        self.third_in = at(part * (1 - self.y), part)

    def copy(self, src, dst, g, slot, device):
        return pltpu.make_async_remote_copy(
            src_ref=src,
            dst_ref=dst,
            send_sem=self.send_sems.at[g, slot],
            recv_sem=self.recv_sems.at[g, slot],
            device_id=device,
            device_id_type=MESH,
        )

    def to_x(self):
        return (self.z * 2 + 1 - self.x, self.y * 2 + self.c)

    def to_y(self):
        return (self.z * 2 + self.x, (1 - self.y) * 2 + self.c)

    def to_core(self):
        return (self.z * 2 + self.x, self.y * 2 + 1 - self.c)

    def to_z(self, k):
        return (lax.rem(self.z + k, 4) * 2 + self.x, self.y * 2 + self.c)

    def z_before(self, k):
        return lax.rem(self.z + 4 - k, 4)


class Gather(Links):
    slots = 15

    def __init__(self, own, full, send_sems, recv_sems):
        super().__init__(own.shape[1], send_sems, recv_sems)
        self.own, self.full = own, full

    def block(self, g, k, rows):
        return self.full.at[self.z_before(k), self.x, g, rows]

    def column(self, g, rows):
        return self.full.at[:, 1 - self.x, g, rows]

    def z_copy(self, g, k):
        return self.copy(
            self.own.at[g, self.plane],
            self.full.at[self.z, self.x, g, self.plane],
            g,
            k - 1,
            self.to_z(k),
        )

    def x_copy(self, g, k):
        there = self.block(g, k, self.plane)
        here = self.own.at[g, self.plane] if k == 0 else there
        return self.copy(here, there, g, 3 + k, self.to_x())

    def y_copy(self, g, k):
        rows = self.own_third
        part = self.block(g, k, rows) if k < 4 else self.column(g, rows)
        return self.copy(part, part, g, 6 + k, self.to_y())

    def core_copy(self, g, k):
        part = self.block(g, k, self.half) if k < 4 else self.column(g, self.half)
        return self.copy(part, part, g, 10 + k, self.to_core())

    def arrived(self, part, g, slot, device):
        self.copy(part, part, g, slot, device).wait_recv()

    def start(self, g):
        self.x_copy(g, 0).start()
        for k in (1, 2, 3):
            self.z_copy(g, k).start()

    def after_z(self, g):
        for k in (1, 2, 3):
            self.arrived(self.block(g, k, self.plane), g, k - 1, self.to_z(k))
            self.x_copy(g, k).start()
            self.y_copy(g, k).start()

    def after_x(self, g):
        for k in range(4):
            part = self.full.at[self.z_before(k), 1 - self.x, g, self.plane]
            self.arrived(part, g, 3 + k, self.to_x())
        self.y_copy(g, 4).start()

    def after_y(self, g):
        for k in (1, 2, 3):
            self.arrived(self.block(g, k, self.other_third), g, 6 + k, self.to_y())
            self.core_copy(g, k).start()
        self.arrived(self.column(g, self.other_third), g, 10, self.to_y())
        self.core_copy(g, 4).start()

    def after_core(self, g):
        for k in (1, 2, 3):
            self.arrived(self.block(g, k, self.other_half), g, 10 + k, self.to_core())
        self.arrived(self.column(g, self.other_half), g, 14, self.to_core())

    def drain(self, g):
        self.x_copy(g, 0).wait_send()
        for k in (1, 2, 3):
            self.z_copy(g, k).wait_send()
            self.x_copy(g, k).wait_send()
            self.y_copy(g, k).wait_send()
            self.core_copy(g, k).wait_send()
        self.y_copy(g, 4).wait_send()
        self.core_copy(g, 4).wait_send()


class Scatter(Links):
    slots = 8

    def __init__(self, full, own, from_core, from_y, from_x, from_z, send_sems, recv_sems):
        super().__init__(own.shape[1], send_sems, recv_sems)
        self.full, self.own = full, own
        self.from_core, self.from_y, self.from_x, self.from_z = from_core, from_y, from_x, from_z

    def core_copy(self, g):
        part = self.full.at[:, :, g, self.other_half]
        return self.copy(part, self.from_core.at[g], g, 0, self.to_core())

    def y_copy(self, g):
        part = self.full.at[:, :, g, self.other_third]
        return self.copy(part, self.from_y.at[g], g, 1, self.to_y())

    def x_copy(self, g):
        part = self.full.at[:, 1 - self.x, g, self.plane]
        return self.copy(part, self.from_x.at[g], g, 2, self.to_x())

    def z_copy(self, g, k):
        part = self.full.at[lax.rem(self.z + k, 4), self.x, g, self.plane]
        return self.copy(part, self.from_z.at[g, k - 1], g, 2 + k, self.to_z(k))

    def back_y_copy(self, g):
        part = self.own.at[g, self.plane]
        return self.copy(part, self.from_z.at[g, 3], g, 6, self.to_y())

    def back_core_copy(self, g):
        part = self.own.at[g, self.half]
        return self.copy(part, part, g, 7, self.to_core())

    def start(self, g):
        self.core_copy(g).start()

    def after_core(self, g):
        self.core_copy(g).wait_recv()
        for a in range(4):
            for b in range(2):
                self.full[a, b, g, self.half] += self.from_core[g, a, b]
        self.y_copy(g).start()

    def after_y(self, g):
        self.y_copy(g).wait_recv()
        for a in range(4):
            for b in range(2):
                self.full[a, b, g, self.own_third] += self.from_y[g, a, b]
        self.x_copy(g).start()

    def after_x(self, g):
        self.x_copy(g).wait_recv()
        for a in range(4):
            self.full[a, self.x, g, self.plane] += self.from_x[g, a]
        for k in (1, 2, 3):
            self.z_copy(g, k).start()

    def after_z(self, g):
        total = self.full[self.z, self.x, g, self.plane].astype(jnp.float32)
        for k in (1, 2, 3):
            self.z_copy(g, k).wait_recv()
            total = total + self.from_z[g, k - 1].astype(jnp.float32)
        self.own[g, self.plane] = total.astype(jnp.bfloat16)
        self.back_y_copy(g).start()

    def after_back_y(self, g):
        self.back_y_copy(g).wait_recv()
        self.back_y_copy(g).wait_send()
        got = self.from_z.at[g, 3]
        self.own[g, self.shared] += got[self.shared_in]
        self.own[g, self.other_third] = got[self.third_in]
        self.back_core_copy(g).start()

    def after_back_core(self, g):
        part = self.own.at[g, self.other_half]
        self.copy(part, part, g, 7, self.to_core()).wait_recv()

    def drain(self, g):
        self.core_copy(g).wait_send()
        self.y_copy(g).wait_send()
        self.x_copy(g).wait_send()
        for k in (1, 2, 3):
            self.z_copy(g, k).wait_send()
        self.back_core_copy(g).wait_send()


def small_gather(small, all_small, send_sems, recv_sems):
    shard = lax.axis_index("fsdp")
    copy = lax.axis_index("rep")
    return [
        pltpu.make_async_remote_copy(
            src_ref=small,
            dst_ref=all_small.at[shard],
            send_sem=send_sems.at[k - 1],
            recv_sem=recv_sems.at[k - 1],
            device_id=(lax.rem(shard + k, 8), copy),
            device_id_type=MESH,
        )
        for k in range(1, 8)
    ]


def gather_kernel(lags, own, small, full, all_small, sends, recvs, small_sends, small_recvs, sem):
    shard = lax.axis_index("fsdp")
    greet()
    smalls = small_gather(small, all_small, small_sends, small_recvs)
    for copy in smalls:
        copy.start()
    moves = Gather(own, full, sends, recvs)
    keep = pltpu.make_async_copy(own, full.at[moves.z, moves.x], sem.at[0])
    keep_small = pltpu.make_async_copy(small, all_small.at[shard], sem.at[1])
    keep.start()
    keep_small.start()
    units = own.shape[0]
    stages = (moves.after_y, moves.after_x, moves.after_z, moves.start, moves.after_core)
    schedule(list(zip(stages, lags)), units)

    def drain(g, carry):
        moves.drain(g)
        return carry

    lax.fori_loop(0, units, drain, 0)
    for copy in smalls:
        copy.wait()
    keep.wait()
    keep_small.wait()


def gather_call(own, small):
    units = own.shape[0]
    anywhere = pl.BlockSpec(memory_space=pl.ANY)
    sems = pltpu.SemaphoreType.DMA
    return pl.pallas_call(
        functools.partial(gather_kernel, (6, 4, 2, 0, 7)),
        out_shape=(
            jax.ShapeDtypeStruct((4, 2) + own.shape, own.dtype),
            jax.ShapeDtypeStruct((8,) + small.shape, small.dtype),
        ),
        in_specs=[anywhere, anywhere],
        out_specs=[anywhere, anywhere],
        scratch_shapes=[
            sems((units, Gather.slots)),
            sems((units, Gather.slots)),
            sems((7,)),
            sems((7,)),
            sems((2,)),
        ],
        compiler_params=pltpu.CompilerParams(collective_id=0, has_side_effects=True),
    )(own, small)


def scatter_kernel(
    lags, full_in, small, own_out, small_out, full, own, from_core, from_y, from_x, from_z,
    small_in, small_rep, sends, recvs, load_sems, store_sems, small_sends, small_recvs, rep_sends,
    rep_recvs,
):
    units = own.shape[0]
    shard = lax.axis_index("fsdp")
    copy_id = lax.axis_index("rep")

    def load(g):
        return pltpu.make_async_copy(full_in.at[:, :, g], full.at[:, :, g], load_sems.at[g])

    def store(g):
        return pltpu.make_async_copy(own.at[g], own_out.at[g], store_sems.at[g])

    def begin(g, carry):
        load(g).start()
        return carry

    lax.fori_loop(0, units, begin, 0)
    greet()
    smalls = [
        pltpu.make_async_remote_copy(
            src_ref=small.at[lax.rem(shard + k, 8)],
            dst_ref=small_in.at[k - 1],
            send_sem=small_sends.at[k - 1],
            recv_sem=small_recvs.at[k - 1],
            device_id=(lax.rem(shard + k, 8), copy_id),
            device_id_type=MESH,
        )
        for k in range(1, 8)
    ]
    for copy in smalls:
        copy.start()
    moves = Scatter(full, own, from_core, from_y, from_x, from_z, sends, recvs)

    def first(g):
        load(g).wait()
        moves.start(g)

    def last(g):
        moves.after_back_core(g)
        store(g).start()

    stages = (
        last, moves.after_back_y, moves.after_z, moves.after_x, moves.after_y, moves.after_core,
        first,
    )
    schedule(list(zip(stages, lags)), units)
    total = small[shard]
    for k, copy in enumerate(smalls):
        copy.wait_recv()
        total = total + small_in[k]
    small_rep[copy_id] = total
    reps = [
        pltpu.make_async_remote_copy(
            src_ref=small_rep.at[copy_id],
            dst_ref=small_rep.at[copy_id],
            send_sem=rep_sends.at[k - 1],
            recv_sem=rep_recvs.at[k - 1],
            device_id=(shard, lax.rem(copy_id + k, 4)),
            device_id_type=MESH,
        )
        for k in range(1, 4)
    ]
    for copy in reps:
        copy.start()
    for k in range(1, 4):
        there = small_rep.at[lax.rem(copy_id + 4 - k, 4)]
        pltpu.make_async_remote_copy(
            src_ref=there,
            dst_ref=there,
            send_sem=rep_sends.at[k - 1],
            recv_sem=rep_recvs.at[k - 1],
            device_id=(shard, lax.rem(copy_id + k, 4)),
            device_id_type=MESH,
        ).wait_recv()
    small_out[...] = (small_rep[0] + small_rep[1]) + (small_rep[2] + small_rep[3])

    def drain(g, carry):
        moves.drain(g)
        store(g).wait()
        return carry

    lax.fori_loop(0, units, drain, 0)
    for copy in smalls + reps:
        copy.wait_send()


def scatter_call(full, small):
    units, rows, width = full.shape[2:]
    half = rows // 2
    part = half // 3
    anywhere = pl.BlockSpec(memory_space=pl.ANY)
    within = pl.BlockSpec(memory_space=pltpu.VMEM)
    sems = pltpu.SemaphoreType.DMA
    kind = full.dtype
    return pl.pallas_call(
        functools.partial(scatter_kernel, (9, 8, 7, 5, 3, 1, 0)),
        out_shape=(
            jax.ShapeDtypeStruct((units, rows, width), kind),
            jax.ShapeDtypeStruct(small.shape[1:], small.dtype),
        ),
        in_specs=[anywhere, within],
        out_specs=[anywhere, within],
        scratch_shapes=[
            pltpu.VMEM(full.shape, kind),
            pltpu.VMEM((units, rows, width), kind),
            pltpu.VMEM((units, 4, 2, half, width), kind),
            pltpu.VMEM((units, 4, 2, part, width), kind),
            pltpu.VMEM((units, 4, 2 * part, width), kind),
            pltpu.VMEM((units, 4, 2 * part, width), kind),
            pltpu.VMEM((7,) + small.shape[1:], small.dtype),
            pltpu.VMEM((4,) + small.shape[1:], small.dtype),
            sems((units, Scatter.slots)),
            sems((units, Scatter.slots)),
            sems((units,)),
            sems((units,)),
            sems((7,)),
            sems((7,)),
            sems((3,)),
            sems((3,)),
        ],
        compiler_params=pltpu.CompilerParams(
            collective_id=1, has_side_effects=True, vmem_limit_bytes=60 * 2**20
        ),
    )(full, small)


def pack_small(gain_a, gain_f, table, kind, rows):
    def put(part, rows_here):
        part = part.reshape(part.shape[:-1] + (rows_here, -1)) if rows_here == 1 else part
        lead = [(0, 0)] * (part.ndim - 1)
        return jnp.pad(part, lead + [(0, 128 - part.shape[-1])])

    block = jnp.concatenate(
        (put(gain_a, 1), put(gain_f, 1), put(table, table.shape[-2])), axis=-2
    ).astype(kind)
    lead = [(0, 0)] * (block.ndim - 2)
    return jnp.pad(block, lead + [(0, rows - block.shape[-2]), (0, 0)])


def compute(inputs, lengths, cotangent, weights):
    (
        full_query, full_key, full_value, full_output, full_gain, full_table, full_inner,
        full_outer, full_ffn_gain,
    ) = weights
    pairs_here, seq_len, model_width = inputs.shape
    row_count = pairs_here * seq_len
    head_count = full_table.shape[1]
    tile = 128
    relative = rel_vec(full_table, tile)
    flat_inputs = inputs.reshape(row_count, model_width).astype(jnp.float32)
    normed = rms_norm(flat_inputs, full_gain.astype(jnp.float32)).astype(jnp.bfloat16)
    joined = jnp.concatenate((full_query, full_key, full_value), axis=1)
    projected = jnp.dot(normed, joined, preferred_element_type=jnp.float32).astype(jnp.bfloat16)
    queries = projected[:, :model_width]
    key_rows = projected[:, model_width : 2 * model_width]
    value_rows = projected[:, 2 * model_width :]
    pair_rows = [slice(n * seq_len, (n + 1) * seq_len) for n in range(pairs_here)]
    forward_parts = [
        att_fwd(queries[r], key_rows[r], value_rows[r], relative, lengths[n : n + 1], tile)
        for n, r in enumerate(pair_rows)
    ]
    attended = jnp.concatenate([part[0] for part in forward_parts], axis=0)
    middle = flat_inputs + jnp.dot(attended, full_output, preferred_element_type=jnp.float32)
    normed_ffn = rms_norm(middle, full_ffn_gain.astype(jnp.float32)).astype(jnp.bfloat16)
    raised = jnp.dot(normed_ffn, full_inner, preferred_element_type=jnp.float32)
    active = gelu(raised).astype(jnp.bfloat16)
    lowered = jnp.dot(active, full_outer, preferred_element_type=jnp.float32)
    block_output = (middle + lowered).astype(jnp.bfloat16).reshape(pairs_here, seq_len, model_width)
    positions = jnp.arange(seq_len, dtype=jnp.int32)
    row_live = (positions[None, :] < lengths[:, None]).astype(jnp.float32)
    seed_rows = (cotangent.astype(jnp.float32) * row_live[:, :, None]).reshape(
        row_count, model_width
    )
    seed_low = seed_rows.astype(jnp.bfloat16)
    grad_active = contract_cols(seed_low, full_outer)
    grad_outer = contract_rows(active, seed_low)
    grad_raised = jax.vjp(gelu, raised)[1](grad_active)[0].astype(jnp.bfloat16)
    grad_inner = contract_rows(normed_ffn, grad_raised)
    grad_normed_ffn = contract_cols(grad_raised, full_inner)
    ffn_pull = jax.vjp(rms_norm, middle, full_ffn_gain.astype(jnp.float32))[1]
    grad_middle_part, grad_ffn_gain = ffn_pull(grad_normed_ffn)
    grad_middle = seed_rows + grad_middle_part
    joined = jnp.concatenate((full_query, full_key, full_value), axis=1)
    middle_low = grad_middle.astype(jnp.bfloat16)
    grad_attended = contract_cols(middle_low, full_output).astype(jnp.bfloat16)
    grad_output = contract_rows(attended, middle_low)
    backward_parts = [
        att_bwd(
            queries[r], key_rows[r], value_rows[r], grad_attended[r], forward_parts[n][1], tile
        )
        for n, r in enumerate(pair_rows)
    ]
    grad_projected = jnp.concatenate(
        [jnp.concatenate(part[:3], axis=1) for part in backward_parts], axis=0
    )
    grad_joined = contract_rows(normed, grad_projected)
    grad_normed = contract_cols(grad_projected, joined)
    attention_pull = jax.vjp(rms_norm, flat_inputs, full_gain.astype(jnp.float32))[1]
    grad_inputs_part, grad_attention_gain = attention_pull(grad_normed)
    input_grad = (grad_middle + grad_inputs_part).reshape(pairs_here, seq_len, model_width)
    grad_relative = sum(part[3] for part in backward_parts)
    grad_table = lax.dot_general(
        rel_hits(tile).astype(jnp.float32),
        grad_relative,
        (((1,), (1,)), ((), ())),
        precision=highest,
    )
    return block_output, input_grad, (
        grad_joined[:, :model_width],
        grad_joined[:, model_width : 2 * model_width],
        grad_joined[:, 2 * model_width :],
        grad_output,
        grad_attention_gain,
        grad_table,
        grad_inner,
        grad_outer,
        grad_ffn_gain,
    )


def gather_all(query_weight, key_weight, value_weight, output_weight, attention_gain, bias_table,
               inner_weight, outer_weight, feedforward_gain):
    return tuple(
        lax.all_gather(part, "fsdp", axis=0, tiled=True)
        for part in (
            query_weight, key_weight, value_weight, output_weight, attention_gain, bias_table,
            inner_weight, outer_weight, feedforward_gain,
        )
    )


def sum_all(gradients):
    def one(part):
        part = lax.psum_scatter(
            part.astype(jnp.bfloat16), "fsdp", scatter_dimension=0, tiled=True
        )
        return lax.psum(part, "rep").astype(jnp.float32)

    return tuple(one(part) for part in gradients)


def gather_linked(query_weight, key_weight, value_weight, output_weight, attention_gain,
                  bias_table, inner_weight, outer_weight, feedforward_gain):
    rows, width = query_weight.shape
    chunks = inner_weight.shape[1] // width
    inner_units = jnp.transpose(inner_weight.reshape(rows, chunks, width), (1, 0, 2))
    outer_units = outer_weight.reshape(chunks, rows, width)
    own = jnp.concatenate(
        (
            jnp.stack((query_weight, key_weight, value_weight, output_weight)),
            inner_units,
            outer_units,
        )
    )
    small = pack_small(attention_gain, feedforward_gain, bias_table, jnp.bfloat16, 16)
    full, all_small = gather_call(own, small)
    square = [full[:, :, u].reshape(8 * rows, width) for u in range(4)]
    inner = jnp.concatenate(
        [full[:, :, 4 + u].reshape(8 * rows, width) for u in range(chunks)], axis=1
    )
    outer = full[:, :, 4 + chunks :].reshape(8 * chunks * rows, width)
    table_rows, heads = bias_table.shape
    return (
        *square,
        all_small[:, 0, :rows].reshape(-1),
        all_small[:, 2 : 2 + table_rows, :heads].reshape(8 * table_rows, heads),
        inner,
        outer,
        all_small[:, 1, :rows].reshape(-1),
    )


def sum_linked(gradients):
    query, key, value, output, gain, table, inner, outer, ffn_gain = gradients
    width = query.shape[1]
    rows = query.shape[0] // 8
    chunks = inner.shape[1] // width
    inner_units = jnp.transpose(inner.reshape(4, 2, rows, chunks, width), (0, 1, 3, 2, 4))
    full = jnp.concatenate(
        [part.reshape(4, 2, 1, rows, width).astype(jnp.bfloat16) for part in (query, key, value, output)]
        + [
            inner_units.astype(jnp.bfloat16),
            outer.reshape(4, 2, chunks, rows, width).astype(jnp.bfloat16),
        ],
        axis=2,
    )
    table_rows = table.shape[0] // 8
    heads = table.shape[1]
    small = pack_small(
        gain.reshape(8, rows), ffn_gain.reshape(8, rows), table.reshape(8, table_rows, heads),
        jnp.float32, 8,
    )
    own, own_small = scatter_call(full, small)
    own = own.astype(jnp.float32)
    return (
        own[0],
        own[1],
        own[2],
        own[3],
        own_small[0, :rows],
        own_small[2 : 2 + table_rows, :heads],
        jnp.transpose(own[4 : 4 + chunks], (1, 0, 2)).reshape(rows, chunks * width),
        own[4 + chunks :].reshape(chunks * rows, width),
        own_small[1, :rows],
    )


def local(linked, inputs, lengths, cotangent, query_weight, key_weight, value_weight,
          output_weight, attention_gain, bias_table, inner_weight, outer_weight,
          feedforward_gain):
    gather, reduce = (gather_linked, sum_linked) if linked else (gather_all, sum_all)
    weights = gather(
        query_weight, key_weight, value_weight, output_weight, attention_gain, bias_table,
        inner_weight, outer_weight, feedforward_gain,
    )
    block_output, input_grad, gradients = compute(inputs, lengths, cotangent, weights)
    return (block_output, input_grad) + reduce(gradients)


def can_link(mesh):
    return mesh.shape["fsdp"] == 8 and mesh.shape["rep"] == 4


def solution(mesh):
    placed = (
        P(("fsdp", "rep"), None, None),
        P(("fsdp", "rep")),
        P(("fsdp", "rep"), None, None),
        P("fsdp", None),
        P("fsdp", None),
        P("fsdp", None),
        P("fsdp", None),
        P("fsdp"),
        P("fsdp", None),
        P("fsdp", None),
        P("fsdp", None),
        P("fsdp"),
    )
    return jax.shard_map(
        functools.partial(local, can_link(mesh)),
        mesh=mesh,
        in_specs=placed,
        out_specs=(
            P(("fsdp", "rep"), None, None),
            P(("fsdp", "rep"), None, None),
            P("fsdp", None),
            P("fsdp", None),
            P("fsdp", None),
            P("fsdp", None),
            P("fsdp"),
            P("fsdp", None),
            P("fsdp", None),
            P("fsdp", None),
            P("fsdp"),
        ),
        check_vma=False,
    )
```

```python
import functools

import jax
import jax.numpy as jnp
from jax import lax
import jax.experimental.pallas as pl
import jax.experimental.pallas.tpu as pltpu
from jax.sharding import PartitionSpec as P

NB = 32


epsilon = 1e-06
highest = lax.Precision.HIGHEST
gelu_coeff = 0.7978845608028654
masked_score = -1e30


def bucket_of(offset):
    half_count = NB // 2
    exact_count = half_count // 2
    distance = jnp.abs(offset)
    beyond = jnp.full(offset.shape, exact_count, jnp.int32)
    for exponent in range(1, half_count - exact_count):
        beyond = beyond + (distance * distance >= exact_count * exact_count * 2**exponent).astype(
            jnp.int32
        )
    nearby = jnp.where(distance < exact_count, distance, beyond)
    return jnp.where(offset > 0, half_count, 0).astype(jnp.int32) + nearby


def rms_norm(values, gain_vector):
    inverse_rms = lax.rsqrt(jnp.mean(values * values, axis=-1, keepdims=True) + epsilon)
    return values * inverse_rms * gain_vector


def gelu(values):
    return (
        0.5 * values * (1.0 + jnp.tanh(gelu_coeff * (values + 0.044715 * values * values * values)))
    )


def dot(a,b): return jnp.dot(a,b,preferred_element_type=jnp.float32)
def dot_t(a,b): return lax.dot_general(a,b,(((1,),(1,)),((),())),preferred_element_type=jnp.float32)
def dot_c(a,b): return lax.dot_general(a,b,(((0,),(0,)),((),())),preferred_element_type=jnp.float32)

def fwd_kernel(T, len_ref, q_ref, k_ref, v_ref, rel_ref, o_ref, p_ref, strip):
    hp=pl.program_id(0)
    seq=q_ref.shape[0]; nb=seq//T
    lane=lax.broadcasted_iota(jnp.int32,(1,128),1)
    kcol=lax.broadcasted_iota(jnp.int32,(1,seq),1)
    mask=jnp.where(kcol<len_ref[0],0.0,-1e30)
    k=k_ref[...]; v=v_ref[...]
    for hh in range(2):
        mine=(lane>=64) if hh else (lane<64)
        rel=rel_ref[pl.ds(hh,1),:]
        W=4*T
        rolled=pltpu.roll(jnp.broadcast_to(rel,(T,W)),0,axis=1,stride=1,stride_axis=0)
        strip[:, 2*T:5*T]=rolled[:, :3*T]
        far_neg=rel[:, 0:1]; far_pos=rel[:, 3*T-1:3*T]
        strip[:, 0:2*T]=jnp.broadcast_to(far_neg,(T,2*T))
        strip[:, 5*T:7*T]=jnp.broadcast_to(far_pos,(T,2*T))
        for I in range(nb):
            q=jnp.where(mine,q_ref[I*T:(I+1)*T,:],jnp.bfloat16(0))
            s=dot_t(q,k)+(strip[:, (3-I)*T:(3-I)*T+seq]+mask)
            m=jnp.max(s,axis=-1,keepdims=True)
            e=jnp.exp(s-m)
            tot=jnp.sum(e,axis=-1,keepdims=True)
            p=(e*(1.0/tot)).astype(jnp.bfloat16)
            p_ref[hh,I*T:(I+1)*T,:]=p
            o=dot(p,v)
            if hh==0:
                o_ref[I*T:(I+1)*T,:]=o.astype(jnp.bfloat16)
            else:
                o_ref[I*T:(I+1)*T,:]=jnp.where(mine,o.astype(jnp.bfloat16),o_ref[I*T:(I+1)*T,:])

def bwd_kernel(T, q_ref, k_ref, v_ref, do_ref, p_ref, dq_ref, dk_ref, dv_ref, db_ref, ds_ref):
    seq=q_ref.shape[0]; nb=seq//T
    lane=lax.broadcasted_iota(jnp.int32,(1,128),1)
    k=k_ref[...]; v=v_ref[...]
    dks=[];dvs=[]
    for hh in range(2):
        mine=(lane>=64) if hh else (lane<64)
        acc=[None]*5
        for I in range(nb):
            sl=slice(I*T,(I+1)*T)
            do=jnp.where(mine,do_ref[sl,:],jnp.bfloat16(0))
            dp=dot_t(do,v)
            p=p_ref[hh,sl,:].astype(jnp.float32)
            t=p*dp
            delta=jnp.sum(t,axis=-1,keepdims=True)
            ds=(t-p*delta).astype(jnp.bfloat16)
            ds_ref[sl,:]=ds
            dsf=ds.astype(jnp.float32)
            for J in range(nb):
                d=min(2,max(-2,J-I))+2
                x=dsf[:,J*T:(J+1)*T]
                acc[d]=x if acc[d] is None else acc[d]+x
            dq=dot(ds,k)
            if hh==0: dq_ref[sl,:]=dq.astype(jnp.bfloat16)
            else: dq_ref[sl,:]=jnp.where(mine,dq.astype(jnp.bfloat16),dq_ref[sl,:])
        near=jnp.concatenate([acc[1],acc[2],acc[3],jnp.zeros((T,T),jnp.float32)],axis=1)
        total=shear_sum(near,4*T)
        far=jnp.concatenate([jnp.zeros((1,2*T),jnp.float32),jnp.sum(acc[4],axis=0,keepdims=True),jnp.sum(acc[0],axis=0,keepdims=True)],axis=1)
        db_ref[hh:hh+1,:]=total+far
        dk=dot_c(q_ref[...],ds_ref[...]).T; dv=dot_c(do_ref[...],p_ref[hh]).T
        dks.append(dk); dvs.append(dv)
    dk_ref[...]=jnp.where(lane<64,dks[0],dks[1]).astype(jnp.bfloat16)
    dv_ref[...]=jnp.where(lane<64,dvs[0],dvs[1]).astype(jnp.bfloat16)

def rel_hits(tile):
    slot = jnp.arange(4 * tile, dtype=jnp.int32)
    offset = jnp.where(slot < 3 * tile, slot - tile, slot - 5 * tile)
    bucket_ids = jnp.arange(NB, dtype=jnp.int32)
    return (bucket_of(offset)[None, :] == bucket_ids[:, None]).astype(jnp.bfloat16)


def rel_vec(table, tile):
    return dot_c(table, rel_hits(tile))


def shear_sum(block, width):
    rows = block.shape[0]
    while rows > 8:
        rows //= 2
        block = block[:rows] + pltpu.roll(block[rows:], width - rows, axis=1)
    total = block[0:1]
    for r in range(1, 8):
        total = total + pltpu.roll(block[r : r + 1], width - r, axis=1)
    return total


def att_fwd(q,k,v,rel,length,T=128):
    seq,D=q.shape; H=rel.shape[0]
    blk=pl.BlockSpec((seq,128),lambda h: (0,h))
    return pl.pallas_call(functools.partial(fwd_kernel,T),grid=(H//2,),
        in_specs=[pl.BlockSpec(memory_space=pltpu.SMEM),blk,blk,blk,pl.BlockSpec((None,2,4*T),lambda h:(h,0,0))],
        out_specs=[blk,pl.BlockSpec((2,seq,seq),lambda h:(h,0,0))],
        out_shape=[jax.ShapeDtypeStruct((seq,D),jnp.bfloat16),jax.ShapeDtypeStruct((H,seq,seq),jnp.bfloat16)],
        scratch_shapes=[pltpu.VMEM((T,7*T),jnp.float32)],
        compiler_params=pltpu.CompilerParams(vmem_limit_bytes=40*2**20))(length,q,k,v,rel.reshape(H//2,2,4*T))
def att_bwd(q,k,v,do,p,T=128):
    seq,D=q.shape; H=p.shape[0]
    blk=pl.BlockSpec((seq,128),lambda h: (0,h))
    o=jax.ShapeDtypeStruct((seq,D),jnp.bfloat16)
    outs=pl.pallas_call(functools.partial(bwd_kernel,T),grid=(H//2,),
        in_specs=[blk,blk,blk,blk,pl.BlockSpec((2,seq,seq),lambda h:(h,0,0))],
        out_specs=[blk,blk,blk,pl.BlockSpec((None,2,4*T),lambda h:(h,0,0))],
        out_shape=[o,o,o,jax.ShapeDtypeStruct((H//2,2,4*T),jnp.float32)],
        scratch_shapes=[pltpu.VMEM((seq,seq),jnp.bfloat16)],
        compiler_params=pltpu.CompilerParams(vmem_limit_bytes=40*2**20))(q,k,v,do,p)
    return *outs[:3],outs[3].reshape(H,4*T)

def contract_rows(left, right):
    return lax.dot_general(
        left, right, (((0,), (0,)), ((), ())), preferred_element_type=jnp.float32
    )


def contract_cols(left, right):
    return lax.dot_general(
        left, right, (((1,), (1,)), ((), ())), preferred_element_type=jnp.float32
    )


MESH = pl.DeviceIdType.MESH


def coords():
    shard = lax.axis_index("fsdp")
    copy = lax.axis_index("rep")
    return shard // 2, shard % 2, copy // 2, copy % 2


def greet():
    barrier = pltpu.get_barrier_semaphore()
    shard = lax.axis_index("fsdp")
    copy = lax.axis_index("rep")
    for k in range(1, 8):
        peer = (lax.rem(shard + k, 8), copy)
        pl.semaphore_signal(barrier, inc=1, device_id=peer, device_id_type=MESH)
    for k in range(1, 4):
        peer = (shard, lax.rem(copy + k, 4))
        pl.semaphore_signal(barrier, inc=1, device_id=peer, device_id_type=MESH)
    pl.semaphore_wait(barrier, 10)


def schedule(stages, count):
    last = max(lag for _, lag in stages)

    def step(t, carry):
        for stage, lag in stages:
            g = t - lag
            pl.when((g >= 0) & (g < count))(functools.partial(stage, g))
        return carry

    lax.fori_loop(0, count + last, step, 0)


class Links:
    def __init__(self, rows, send_sems, recv_sems):
        self.send_sems, self.recv_sems = send_sems, recv_sems
        self.z, self.x, self.y, self.c = coords()
        half = rows // 2
        part = half // 3
        at = lambda start, size: pl.ds(pl.multiple_of(start, part), size)
        first = half * self.c
        other = half * (1 - self.c)
        self.half, self.other_half = at(first, half), at(other, half)
        self.plane = at(first + part * self.y, 2 * part)
        self.shared = at(first + part, part)
        self.own_third = at(first + 2 * part * self.y, part)
        self.other_third = at(first + 2 * part * (1 - self.y), part)
        self.shared_in = at(part * self.y, part)
        self.third_in = at(part * (1 - self.y), part)

    def copy(self, src, dst, g, slot, device):
        return pltpu.make_async_remote_copy(
            src_ref=src,
            dst_ref=dst,
            send_sem=self.send_sems.at[g, slot],
            recv_sem=self.recv_sems.at[g, slot],
            device_id=device,
            device_id_type=MESH,
        )

    def to_x(self):
        return (self.z * 2 + 1 - self.x, self.y * 2 + self.c)

    def to_y(self):
        return (self.z * 2 + self.x, (1 - self.y) * 2 + self.c)

    def to_core(self):
        return (self.z * 2 + self.x, self.y * 2 + 1 - self.c)

    def to_z(self, k):
        return (lax.rem(self.z + k, 4) * 2 + self.x, self.y * 2 + self.c)

    def z_before(self, k):
        return lax.rem(self.z + 4 - k, 4)


class Gather(Links):
    slots = 15

    def __init__(self, own, full, send_sems, recv_sems):
        super().__init__(own.shape[1], send_sems, recv_sems)
        self.own, self.full = own, full

    def block(self, g, k, rows):
        return self.full.at[self.z_before(k), self.x, g, rows]

    def column(self, g, rows):
        return self.full.at[:, 1 - self.x, g, rows]

    def z_copy(self, g, k):
        return self.copy(
            self.own.at[g, self.plane],
            self.full.at[self.z, self.x, g, self.plane],
            g,
            k - 1,
            self.to_z(k),
        )

    def x_copy(self, g, k):
        there = self.block(g, k, self.plane)
        here = self.own.at[g, self.plane] if k == 0 else there
        return self.copy(here, there, g, 3 + k, self.to_x())

    def y_copy(self, g, k):
        rows = self.own_third
        part = self.block(g, k, rows) if k < 4 else self.column(g, rows)
        return self.copy(part, part, g, 6 + k, self.to_y())

    def core_copy(self, g, k):
        part = self.block(g, k, self.half) if k < 4 else self.column(g, self.half)
        return self.copy(part, part, g, 10 + k, self.to_core())

    def arrived(self, part, g, slot, device):
        self.copy(part, part, g, slot, device).wait_recv()

    def start(self, g):
        self.x_copy(g, 0).start()
        for k in (1, 2, 3):
            self.z_copy(g, k).start()

    def after_z(self, g):
        for k in (1, 2, 3):
            self.arrived(self.block(g, k, self.plane), g, k - 1, self.to_z(k))
            self.x_copy(g, k).start()
            self.y_copy(g, k).start()

    def after_x(self, g):
        for k in range(4):
            part = self.full.at[self.z_before(k), 1 - self.x, g, self.plane]
            self.arrived(part, g, 3 + k, self.to_x())
        self.y_copy(g, 4).start()

    def after_y(self, g):
        for k in (1, 2, 3):
            self.arrived(self.block(g, k, self.other_third), g, 6 + k, self.to_y())
            self.core_copy(g, k).start()
        self.arrived(self.column(g, self.other_third), g, 10, self.to_y())
        self.core_copy(g, 4).start()

    def after_core(self, g):
        for k in (1, 2, 3):
            self.arrived(self.block(g, k, self.other_half), g, 10 + k, self.to_core())
        self.arrived(self.column(g, self.other_half), g, 14, self.to_core())

    def drain(self, g):
        self.x_copy(g, 0).wait_send()
        for k in (1, 2, 3):
            self.z_copy(g, k).wait_send()
            self.x_copy(g, k).wait_send()
            self.y_copy(g, k).wait_send()
            self.core_copy(g, k).wait_send()
        self.y_copy(g, 4).wait_send()
        self.core_copy(g, 4).wait_send()


class Scatter(Links):
    slots = 8

    def __init__(self, slot, full, own, from_core, from_y, from_x, from_z, send_sems, recv_sems):
        super().__init__(own.shape[1], send_sems, recv_sems)
        self.slot, self.full, self.own = slot, full, own
        self.from_core, self.from_y, self.from_x, self.from_z = from_core, from_y, from_x, from_z

    def core_copy(self, g):
        part = self.full.at[:, :, self.slot(g), self.other_half]
        return self.copy(part, self.from_core.at[g], g, 0, self.to_core())

    def y_copy(self, g):
        part = self.full.at[:, :, self.slot(g), self.other_third]
        return self.copy(part, self.from_y.at[g], g, 1, self.to_y())

    def x_copy(self, g):
        part = self.full.at[:, 1 - self.x, self.slot(g), self.plane]
        return self.copy(part, self.from_x.at[g], g, 2, self.to_x())

    def z_copy(self, g, k):
        part = self.full.at[lax.rem(self.z + k, 4), self.x, self.slot(g), self.plane]
        return self.copy(part, self.from_z.at[g, k - 1], g, 2 + k, self.to_z(k))

    def back_y_copy(self, g):
        part = self.own.at[g, self.plane]
        return self.copy(part, self.from_z.at[g, 3], g, 6, self.to_y())

    def back_core_copy(self, g):
        part = self.own.at[g, self.half]
        return self.copy(part, part, g, 7, self.to_core())

    def start(self, g):
        self.core_copy(g).start()

    def after_core(self, g):
        self.core_copy(g).wait_recv()
        for a in range(4):
            for b in range(2):
                self.full[a, b, self.slot(g), self.half] += self.from_core[g, a, b]
        self.y_copy(g).start()

    def after_y(self, g):
        self.y_copy(g).wait_recv()
        for a in range(4):
            for b in range(2):
                self.full[a, b, self.slot(g), self.own_third] += self.from_y[g, a, b]
        self.x_copy(g).start()

    def after_x(self, g):
        self.x_copy(g).wait_recv()
        for a in range(4):
            self.full[a, self.x, self.slot(g), self.plane] += self.from_x[g, a]
        for k in (1, 2, 3):
            self.z_copy(g, k).start()

    def after_z(self, g):
        total = self.full[self.z, self.x, self.slot(g), self.plane].astype(jnp.float32)
        for k in (1, 2, 3):
            self.z_copy(g, k).wait_recv()
            total = total + self.from_z[g, k - 1].astype(jnp.float32)
        self.own[g, self.plane] = total.astype(jnp.bfloat16)
        self.back_y_copy(g).start()

    def after_back_y(self, g):
        self.back_y_copy(g).wait_recv()
        self.back_y_copy(g).wait_send()
        got = self.from_z.at[g, 3]
        self.own[g, self.shared] += got[self.shared_in]
        self.own[g, self.other_third] = got[self.third_in]
        self.back_core_copy(g).start()

    def after_back_core(self, g):
        part = self.own.at[g, self.other_half]
        self.copy(part, part, g, 7, self.to_core()).wait_recv()

    def drain(self, g):
        self.core_copy(g).wait_send()
        self.y_copy(g).wait_send()
        self.x_copy(g).wait_send()
        for k in (1, 2, 3):
            self.z_copy(g, k).wait_send()
        self.back_core_copy(g).wait_send()


def compute(inputs, lengths, cotangent, weights):
    (
        full_query, full_key, full_value, full_output, full_gain, full_table, full_inner,
        full_outer, full_ffn_gain,
    ) = weights
    pairs_here, seq_len, model_width = inputs.shape
    row_count = pairs_here * seq_len
    head_count = full_table.shape[1]
    tile = 128
    relative = rel_vec(full_table, tile)
    flat_inputs = inputs.reshape(row_count, model_width).astype(jnp.float32)
    normed = rms_norm(flat_inputs, full_gain.astype(jnp.float32)).astype(jnp.bfloat16)
    joined = jnp.concatenate((full_query, full_key, full_value), axis=1)
    projected = jnp.dot(normed, joined, preferred_element_type=jnp.float32).astype(jnp.bfloat16)
    queries = projected[:, :model_width]
    key_rows = projected[:, model_width : 2 * model_width]
    value_rows = projected[:, 2 * model_width :]
    pair_rows = [slice(n * seq_len, (n + 1) * seq_len) for n in range(pairs_here)]
    forward_parts = [
        att_fwd(queries[r], key_rows[r], value_rows[r], relative, lengths[n : n + 1], tile)
        for n, r in enumerate(pair_rows)
    ]
    attended = jnp.concatenate([part[0] for part in forward_parts], axis=0)
    middle = flat_inputs + jnp.dot(attended, full_output, preferred_element_type=jnp.float32)
    normed_ffn = rms_norm(middle, full_ffn_gain.astype(jnp.float32)).astype(jnp.bfloat16)
    raised = jnp.dot(normed_ffn, full_inner, preferred_element_type=jnp.float32)
    active = gelu(raised).astype(jnp.bfloat16)
    lowered = jnp.dot(active, full_outer, preferred_element_type=jnp.float32)
    block_output = (middle + lowered).astype(jnp.bfloat16).reshape(pairs_here, seq_len, model_width)
    positions = jnp.arange(seq_len, dtype=jnp.int32)
    row_live = (positions[None, :] < lengths[:, None]).astype(jnp.float32)
    seed_rows = (cotangent.astype(jnp.float32) * row_live[:, :, None]).reshape(
        row_count, model_width
    )
    seed_low = seed_rows.astype(jnp.bfloat16)
    grad_active = contract_cols(seed_low, full_outer)
    grad_outer = contract_rows(active, seed_low)
    grad_raised = jax.vjp(gelu, raised)[1](grad_active)[0].astype(jnp.bfloat16)
    grad_inner = contract_rows(normed_ffn, grad_raised)
    grad_normed_ffn = contract_cols(grad_raised, full_inner)
    ffn_pull = jax.vjp(rms_norm, middle, full_ffn_gain.astype(jnp.float32))[1]
    grad_middle_part, grad_ffn_gain = ffn_pull(grad_normed_ffn)
    grad_middle = seed_rows + grad_middle_part
    joined = jnp.concatenate((full_query, full_key, full_value), axis=1)
    middle_low = grad_middle.astype(jnp.bfloat16)
    grad_attended = contract_cols(middle_low, full_output).astype(jnp.bfloat16)
    grad_output = contract_rows(attended, middle_low)
    backward_parts = [
        att_bwd(
            queries[r], key_rows[r], value_rows[r], grad_attended[r], forward_parts[n][1], tile
        )
        for n, r in enumerate(pair_rows)
    ]
    grad_projected = jnp.concatenate(
        [jnp.concatenate(part[:3], axis=1) for part in backward_parts], axis=0
    )
    grad_joined = contract_rows(normed, grad_projected)
    grad_normed = contract_cols(grad_projected, joined)
    attention_pull = jax.vjp(rms_norm, flat_inputs, full_gain.astype(jnp.float32))[1]
    grad_inputs_part, grad_attention_gain = attention_pull(grad_normed)
    input_grad = (grad_middle + grad_inputs_part).reshape(pairs_here, seq_len, model_width)
    grad_relative = sum(part[3] for part in backward_parts)
    grad_table = lax.dot_general(
        rel_hits(tile).astype(jnp.float32),
        grad_relative,
        (((1,), (1,)), ((), ())),
        precision=highest,
    )
    return block_output, input_grad, (
        grad_joined[:, :model_width],
        grad_joined[:, model_width : 2 * model_width],
        grad_joined[:, 2 * model_width :],
        grad_output,
        grad_attention_gain,
        grad_table,
        grad_inner,
        grad_outer,
        grad_ffn_gain,
    )


def gather_all(query_weight, key_weight, value_weight, output_weight, attention_gain, bias_table,
               inner_weight, outer_weight, feedforward_gain):
    return tuple(
        lax.all_gather(part, "fsdp", axis=0, tiled=True)
        for part in (
            query_weight, key_weight, value_weight, output_weight, attention_gain, bias_table,
            inner_weight, outer_weight, feedforward_gain,
        )
    )


def sum_all(gradients):
    def one(part):
        part = lax.psum_scatter(
            part.astype(jnp.bfloat16), "fsdp", scatter_dimension=0, tiled=True
        )
        return lax.psum(part, "rep").astype(jnp.float32)

    return tuple(one(part) for part in gradients)


def gelu_parts(z):
    square = z * z
    t = jnp.tanh(gelu_coeff * z * (1.0 + 0.044715 * square))
    half = 0.5 * (1.0 + t)
    slope = half + (0.5 * gelu_coeff) * z * (1.0 - t * t) * (1.0 + (3 * 0.044715) * square)
    return z * half, slope


def lanes(start, size):
    return pl.ds(pl.multiple_of(start, 128), size)


def rows_at(start, size):
    return pl.ds(pl.multiple_of(start, size), size)


def loop(count, body):
    def step(n, carry):
        body(n)
        return carry

    lax.fori_loop(0, count, step, 0)


def norm_back(grad, gain, values):
    inverse = lax.rsqrt(jnp.mean(values * values, axis=-1, keepdims=True) + epsilon)
    scaled = grad * gain
    centre = jnp.mean(scaled * values, axis=-1, keepdims=True)
    back = inverse * scaled - values * (inverse * inverse * inverse * centre)
    return back, jnp.sum(grad * values * inverse, axis=0, keepdims=True)


class Layer:
    def __init__(self, **refs):
        self.__dict__.update(refs)
        self.seq, self.width = self.x.shape
        self.tile = 128
        self.row_block = 128
        self.shard_rows = self.bank.shape[3]

    def unit(self, u, column=None, size=None):
        if column is None:
            block = self.bank[:, :, u]
        else:
            block = self.bank[:, :, u, :, lanes(column, size)]
        return block.reshape(-1, block.shape[-1])

    def row_chunks(self, body):
        size = self.row_block
        loop(self.seq // size, lambda n: body(rows_at(n * size, size)))

    def small_arrays(self):
        flat = self.all_small[...].reshape(-1, 128)
        tile = self.tile
        slot = lax.broadcasted_iota(jnp.int32, (flat.shape[0], 4 * tile), 1)
        offset = jnp.where(slot < 3 * tile, slot - tile, slot - 5 * tile)
        row = lax.broadcasted_iota(jnp.int32, (flat.shape[0], 4 * tile), 0)
        per = NB // 8
        inside = row % 16 - 2
        wanted = jnp.where((inside >= 0) & (inside < per), (row // 16) * per + inside, -1)
        hits = (bucket_of(offset) == wanted).astype(jnp.bfloat16)
        self.rel[...] = dot_c(flat, hits)[: self.rel.shape[0]]
        for index, ref in ((0, self.gain_a), (1, self.gain_f)):
            total = jnp.zeros((1, self.width), jnp.float32)
            for shard in range(8):
                part = self.all_small[shard].astype(jnp.float32)[index : index + 1]
                wide = jnp.concatenate(
                    [part, jnp.zeros((1, self.width - 128), jnp.float32)], axis=1
                )
                total = total + (
                    pltpu.roll(wide, shard * self.shard_rows, axis=1) if shard else wide
                )
            ref[...] = total

    def norm_in(self):
        gain = self.gain_a[...]

        def body(r):
            self.normed[r] = rms_norm(self.x[r].astype(jnp.float32), gain).astype(jnp.bfloat16)

        self.row_chunks(body)

    def mask_seed(self):
        def body(r):
            index = lax.broadcasted_iota(jnp.int32, (self.row_block, 1), 0) + r.start
            live = index < self.length[0]
            self.seed[r] = jnp.where(live, self.cot[r], jnp.bfloat16(0))

        self.row_chunks(body)

    def project(self, u):
        def body(n):
            self.qkv[u, :, lanes(n * 256, 256)] = dot(
                self.normed[...], self.unit(u, n * 256, 256)
            ).astype(jnp.bfloat16)

        loop(self.width // 256, body)

    def strip_for(self, head):
        tile = self.tile
        rel = self.rel[pl.ds(head, 1), :]
        rolled = pltpu.roll(
            jnp.broadcast_to(rel, (tile, 4 * tile)), 0, axis=1, stride=1, stride_axis=0
        )
        self.strip[:, 2 * tile : 5 * tile] = rolled[:, : 3 * tile]
        self.strip[:, : 2 * tile] = jnp.broadcast_to(rel[:, :1], (tile, 2 * tile))
        self.strip[:, 5 * tile :] = jnp.broadcast_to(
            rel[:, 3 * tile - 1 : 3 * tile], (tile, 2 * tile)
        )

    def probs_store(self, pair, slot):
        return pltpu.make_async_copy(
            self.probs.at[slot], self.probs_far.at[pair], self.probs_sems.at[slot]
        )

    def probs_load(self, pair, slot):
        return pltpu.make_async_copy(
            self.probs_far.at[pair], self.probs.at[slot], self.probs_sems.at[slot]
        )

    def attend(self, pair):
        tile, seq = self.tile, self.seq
        slot = lax.rem(pair, 2)
        pl.when(pair >= 2)(lambda: self.probs_store(pair, slot).wait())
        lane = lax.broadcasted_iota(jnp.int32, (1, 128), 1)
        key_at = lax.broadcasted_iota(jnp.int32, (1, seq), 1)
        mask = jnp.where(key_at < self.length[0], 0.0, masked_score)
        cols = lanes(pair * 128, 128)
        k = self.qkv[1, :, cols]
        v = self.qkv[2, :, cols]
        for head in range(2):
            mine = (lane >= 64) if head else (lane < 64)
            self.strip_for(pair * 2 + head)
            for block in range(seq // tile):
                r = slice(block * tile, (block + 1) * tile)
                q = jnp.where(mine, self.qkv[0, r, cols], jnp.bfloat16(0))
                first = (seq // tile - 1 - block) * tile
                scores = dot_t(q, k) + (self.strip[:, first : first + seq] + mask)
                peak = jnp.max(scores, axis=-1, keepdims=True)
                raised = jnp.exp(scores - peak)
                total = jnp.sum(raised, axis=-1, keepdims=True)
                probs = (raised * (1.0 / total)).astype(jnp.bfloat16)
                self.probs[slot, head, r, :] = probs
                out = dot(probs, v).astype(jnp.bfloat16)
                if head:
                    out = jnp.where(mine, out, self.attended[r, cols])
                self.attended[r, cols] = out
        self.probs_store(pair, slot).start()

    def middle_rows(self):
        def body(n):
            c = lanes(n * 256, 256)
            self.middle[:, c] = self.x[:, c].astype(jnp.float32) + dot(
                self.attended[...], self.unit(3, n * 256, 256)
            )

        loop(self.width // 256, body)
        gain = self.gain_f[...]

        def norm(r):
            self.normed_ffn[r] = rms_norm(self.middle[r], gain).astype(jnp.bfloat16)

        self.row_chunks(norm)

    def raise_unit(self, i):
        def body(n):
            raised = dot(self.normed_ffn[...], self.unit(4 + i, n * 256, 256))
            active, slope = gelu_parts(raised)
            c = lanes(i * self.width + n * 256, 256)
            self.active[:, c] = active.astype(jnp.bfloat16)
            self.slope[:, c] = slope.astype(jnp.bfloat16)

        loop(self.width // 256, body)

    def outer_grad(self, shard):
        size = 4 * self.shard_rows
        block = dot_c(self.active[:, lanes(shard * size, size)], self.seed[...])
        self.bank[shard // 2, shard % 2, 12:16] = block.astype(jnp.bfloat16).reshape(
            4, self.shard_rows, self.width
        )

    def lower(self):
        def body(n):
            outer = self.bank[:, :, 8:12, :, lanes(n * 256, 256)].reshape(-1, 256)
            c = lanes(n * 256, 256)
            self.block_out[:, c] = (self.middle[:, c] + dot(self.active[...], outer)).astype(
                jnp.bfloat16
            )

        loop(self.width // 256, body)

    def raised_grad(self, shard):
        size = 4 * self.shard_rows
        outer = self.bank[shard // 2, shard % 2, 8:12].reshape(size, self.width)
        c = lanes(shard * size, size)
        grad = dot_t(self.seed[...], outer) * self.slope[:, c].astype(jnp.float32)
        self.slope[:, c] = grad.astype(jnp.bfloat16)

    def inner_grad(self, i):
        def body(n):
            c = lanes(i * self.width + n * 256, 256)
            block = dot_c(self.normed_ffn[...], self.slope[:, c]).astype(jnp.bfloat16)
            self.bank[:, :, 16 + i, :, lanes(n * 256, 256)] = block.reshape(
                4, 2, self.shard_rows, 256
            )

        loop(self.width // 256, body)

    def middle_grad(self):
        for part in range(2):
            total = None
            for i in range(4):
                inner = self.bank[2 * part : 2 * part + 2, :, 4 + i]
                inner = inner.reshape(-1, self.width)
                term = dot_t(self.slope[:, i * self.width : (i + 1) * self.width], inner)
                total = term if total is None else total + term
            size = self.width // 2
            self.grad_mid[:, part * size : (part + 1) * size] = total
        gain = self.gain_f[...]
        self.gain_f_grad[...] = jnp.zeros_like(self.gain_f_grad)

        def body(r):
            back, terms = norm_back(self.grad_mid[r], gain, self.middle[r])
            total = self.seed[r].astype(jnp.float32) + back
            self.gain_f_grad[...] += terms
            self.grad_mid[r] = total
            self.mid_low[r] = total.astype(jnp.bfloat16)

        self.row_chunks(body)

    def square_grad(self, left, right, slot):
        def body(n):
            block = dot_c(left[...], right(lanes(n * 256, 256))).astype(jnp.bfloat16)
            self.bank[:, :, slot, :, lanes(n * 256, 256)] = block.reshape(
                4, 2, self.shard_rows, 256
            )

        loop(self.width // 256, body)

    def attended_grad(self):
        size = self.width // 2
        for part in range(2):
            weight = self.bank[2 * part : 2 * part + 2, :, 3].reshape(size, self.width)
            self.grad_att[:, part * size : (part + 1) * size] = dot_t(
                self.mid_low[...], weight
            ).astype(jnp.bfloat16)

    def attend_back(self, pair):
        tile, seq = self.tile, self.seq
        slot = lax.rem(pair, 2)
        self.probs_load(pair, slot).wait()
        lane = lax.broadcasted_iota(jnp.int32, (1, 128), 1)
        cols = lanes(pair * 128, 128)
        k = self.qkv[1, :, cols]
        v = self.qkv[2, :, cols]
        blocks = seq // tile
        grads = []
        for head in range(2):
            mine = (lane >= 64) if head else (lane < 64)
            sums = [None] * 5
            for block in range(blocks):
                r = slice(block * tile, (block + 1) * tile)
                grad_out = jnp.where(mine, self.grad_att[r, cols], jnp.bfloat16(0))
                probs = self.probs[slot, head, r, :].astype(jnp.float32)
                weighted = probs * dot_t(grad_out, v)
                centre = jnp.sum(weighted, axis=-1, keepdims=True)
                low = (weighted - probs * centre).astype(jnp.bfloat16)
                self.grad_scores[r, :] = low
                wide = low.astype(jnp.float32)
                for other in range(blocks):
                    apart = min(2, max(-2, other - block)) + 2
                    part = wide[:, other * tile : (other + 1) * tile]
                    sums[apart] = part if sums[apart] is None else sums[apart] + part
                out = dot(low, k).astype(jnp.bfloat16)
                if head:
                    out = jnp.where(mine, out, self.grad_q[r, :])
                self.grad_q[r, :] = out
            zero = jnp.zeros((tile, tile), jnp.float32)
            near = shear_sum(jnp.concatenate([sums[1], sums[2], sums[3], zero], axis=1), 4 * tile)
            far = jnp.concatenate(
                [
                    jnp.zeros((1, 2 * tile), jnp.float32),
                    jnp.sum(sums[4], axis=0, keepdims=True),
                    jnp.sum(sums[0], axis=0, keepdims=True),
                ],
                axis=1,
            )
            self.rel_grad[pl.ds(pair * 2 + head, 1), :] = near + far
            grads.append(
                (
                    dot_c(self.qkv[0, :, cols], self.grad_scores[...]).T,
                    dot_c(self.grad_att[:, cols], self.probs[slot, head]).T,
                )
            )
        first = lane < 64
        self.qkv[0, :, cols] = self.grad_q[...]
        self.qkv[1, :, cols] = jnp.where(first, grads[0][0], grads[1][0]).astype(jnp.bfloat16)
        self.qkv[2, :, cols] = jnp.where(first, grads[0][1], grads[1][1]).astype(jnp.bfloat16)
        pl.when(pair + 2 < self.probs_far.shape[0])(
            lambda: self.probs_load(pair + 2, slot).start()
        )

    def input_grad(self):
        size = self.width // 2
        for part in range(2):
            total = None
            for u in range(3):
                weight = self.bank[2 * part : 2 * part + 2, :, u].reshape(size, self.width)
                term = dot_t(self.qkv[u], weight)
                total = term if total is None else total + term
            self.middle[:, part * size : (part + 1) * size] = total
        gain = self.gain_a[...]
        self.gain_a_grad[...] = jnp.zeros_like(self.gain_a_grad)

        def body(r):
            back, terms = norm_back(self.middle[r], gain, self.x[r].astype(jnp.float32))
            self.gain_a_grad[...] += terms
            self.grad_mid[r] += back

        self.row_chunks(body)

    def small_grads(self):
        tile = self.tile
        shape = (64, 4 * tile)
        slot = lax.broadcasted_iota(jnp.int32, shape, 1)
        offset = jnp.where(slot < 3 * tile, slot - tile, slot - 5 * tile)
        row = lax.broadcasted_iota(jnp.int32, shape, 0)
        per = NB // 8
        inside = row % 8 - 2
        wanted = jnp.where((inside >= 0) & (inside < per), (row // 8) * per + inside, -1)
        hits = (bucket_of(offset) == wanted).astype(jnp.float32)
        table = lax.dot_general(
            hits,
            self.rel_grad[...],
            (((1,), (1,)), ((), ())),
            precision=highest,
            preferred_element_type=jnp.float32,
        )
        rows = lax.broadcasted_iota(jnp.int32, (8, 128), 0)
        lane = lax.broadcasted_iota(jnp.int32, (8, 128), 1)
        for shard in range(8):
            block = table[8 * shard : 8 * shard + 8]
            for index, ref in ((0, self.gain_a_grad), (1, self.gain_f_grad)):
                wide = ref[...]
                if shard:
                    wide = pltpu.roll(wide, self.width - shard * self.shard_rows, axis=1)
                here = (rows == index) & (lane < self.shard_rows)
                block = jnp.where(here, jnp.broadcast_to(wide[:, :128], (8, 128)), block)
            self.small_out[shard] = block


def order_slot(n):
    return jnp.where(n < 8, n + 12, jnp.where(n == 8, 7, n - 5))


def fused_kernel(
    length, x, cot, small, own, block_far, grad_far, own_far, small_result, probs_far,
    bank, own_sum, from_core, from_y, from_x, from_z, all_small, small_out, small_in, small_rep,
    probs, normed, qkv, attended, middle, normed_ffn, active, slope, seed, grad_mid, mid_low,
    grad_att, block_out, rel, rel_grad, gain_a, gain_f, gain_a_grad, gain_f_grad, strip,
    grad_scores, grad_q,
    sends, recvs, sum_sends, sum_recvs, small_sends, small_recvs, back_sends, back_recvs,
    rep_sends, rep_recvs, probs_sems, misc_sems, store_sems,
):
    shard = lax.axis_index("fsdp")
    copy_id = lax.axis_index("rep")
    layer = Layer(
        length=length, x=x, cot=cot, bank=bank, all_small=all_small, small_out=small_out,
        probs=probs, probs_far=probs_far, probs_sems=probs_sems, normed=normed, qkv=qkv,
        attended=attended, middle=middle, normed_ffn=normed_ffn, active=active, slope=slope,
        seed=seed, grad_mid=grad_mid, mid_low=mid_low, grad_att=grad_att, block_out=block_out,
        rel=rel, rel_grad=rel_grad, gain_a=gain_a, gain_f=gain_f, gain_a_grad=gain_a_grad,
        gain_f_grad=gain_f_grad, strip=strip, grad_scores=grad_scores, grad_q=grad_q,
    )
    units = own.shape[0]
    gather = Gather(own, bank, sends, recvs)
    scatter = Scatter(
        order_slot, bank, own_sum, from_core, from_y, from_x, from_z, sum_sends, sum_recvs
    )
    pairs = probs_far.shape[0]

    def remote(src, dst, send, recv, device):
        return pltpu.make_async_remote_copy(
            src_ref=src, dst_ref=dst, send_sem=send, recv_sem=recv, device_id=device,
            device_id_type=MESH,
        )

    def peer(k):
        return (lax.rem(shard + k, 8), copy_id)

    def rep_peer(k):
        return (shard, lax.rem(copy_id + k, 4))

    greet()
    small_copies = [
        remote(small, all_small.at[shard], small_sends.at[k - 1], small_recvs.at[k - 1], peer(k))
        for k in range(1, 8)
    ]
    for copy in small_copies:
        copy.start()
    keep = pltpu.make_async_copy(
        own, bank.at[gather.z, gather.x, 0:units], misc_sems.at[0]
    )
    keep_small = pltpu.make_async_copy(small, all_small.at[shard], misc_sems.at[1])
    keep.start()
    keep_small.start()

    stages = (
        (gather.after_y, 6), (gather.after_x, 4), (gather.after_z, 2), (gather.start, 0),
        (gather.after_core, 7),
    )
    schedule(stages, units)
    keep.wait()
    keep_small.wait()
    for copy in small_copies:
        copy.wait()
    loop(units, gather.drain)

    layer.small_arrays()
    layer.mask_seed()
    layer.norm_in()
    loop(3, layer.project)
    loop(pairs, layer.attend)
    for pair in (pairs - 2, pairs - 1):
        layer.probs_store(pair, pair % 2).wait()
    layer.middle_rows()
    loop(4, layer.raise_unit)
    loop(8, layer.outer_grad)
    layer.lower()
    block_store = pltpu.make_async_copy(block_out, block_far, misc_sems.at[2])
    block_store.start()
    loop(8, layer.raised_grad)
    loop(4, layer.inner_grad)
    for pair in (0, 1):
        layer.probs_load(pair, pair).start()
    layer.middle_grad()
    layer.square_grad(attended, lambda c: mid_low[:, c], 7)
    layer.attended_grad()
    rel_grad[...] = jnp.zeros_like(rel_grad)
    loop(pairs, layer.attend_back)
    for u in range(3):
        layer.square_grad(normed, lambda c, u=u: qkv[u, :, c], 4 + u)
    layer.input_grad()
    grad_store = pltpu.make_async_copy(grad_mid, grad_far, misc_sems.at[3])
    grad_store.start()
    layer.small_grads()

    back_copies = [
        remote(
            small_out.at[lax.rem(shard + k, 8)], small_in.at[k - 1], back_sends.at[k - 1],
            back_recvs.at[k - 1], peer(k),
        )
        for k in range(1, 8)
    ]
    for copy in back_copies:
        copy.start()

    def store(n):
        return pltpu.make_async_copy(own_sum.at[n], own_far.at[n], store_sems.at[n])

    def last(n):
        scatter.after_back_core(n)
        store(n).start()

    stages = (
        (last, 9), (scatter.after_back_y, 8), (scatter.after_z, 7), (scatter.after_x, 5),
        (scatter.after_y, 3), (scatter.after_core, 1), (scatter.start, 0),
    )
    schedule(stages, units)

    total = small_out[shard]
    for k, copy in enumerate(back_copies):
        copy.wait_recv()
        total = total + small_in[k]
    small_rep[copy_id] = total
    rep_copies = [
        remote(
            small_rep.at[copy_id], small_rep.at[copy_id], rep_sends.at[k - 1],
            rep_recvs.at[k - 1], rep_peer(k),
        )
        for k in range(1, 4)
    ]
    for copy in rep_copies:
        copy.start()
    for k in range(1, 4):
        there = small_rep.at[lax.rem(copy_id + 4 - k, 4)]
        remote(there, there, rep_sends.at[k - 1], rep_recvs.at[k - 1], rep_peer(k)).wait_recv()
    small_result[...] = (small_rep[0] + small_rep[1]) + (small_rep[2] + small_rep[3])

    def drain(n):
        scatter.drain(n)
        store(n).wait()

    loop(units, drain)
    for copy in back_copies + rep_copies:
        copy.wait_send()
    block_store.wait()
    grad_store.wait()


def fused_call(length, x, cot, small, own, heads):
    units, rows, width = own.shape
    seq = x.shape[0]
    half = rows // 2
    part = half // 3
    hidden = 4 * width
    low, wide = jnp.bfloat16, jnp.float32
    anywhere = pl.BlockSpec(memory_space=pl.ANY)
    within = pl.BlockSpec(memory_space=pltpu.VMEM)
    sems = pltpu.SemaphoreType.DMA
    vm = pltpu.VMEM
    head_rows = -(-heads // 8) * 8
    return pl.pallas_call(
        fused_kernel,
        out_shape=(
            jax.ShapeDtypeStruct((seq, width), low),
            jax.ShapeDtypeStruct((seq, width), wide),
            jax.ShapeDtypeStruct((units, rows, width), low),
            jax.ShapeDtypeStruct((8, 128), wide),
            jax.ShapeDtypeStruct((heads // 2, 2, seq, seq), low),
        ),
        in_specs=[pl.BlockSpec(memory_space=pltpu.SMEM), within, within, within, anywhere],
        out_specs=[anywhere, anywhere, anywhere, within, anywhere],
        scratch_shapes=[
            vm((4, 2, units + 8, rows, width), low),
            vm((units, rows, width), low),
            vm((units, 4, 2, half, width), low),
            vm((units, 4, 2, part, width), low),
            vm((units, 4, 2 * part, width), low),
            vm((units, 4, 2 * part, width), low),
            vm((8, 16, 128), low),
            vm((8, 8, 128), wide),
            vm((7, 8, 128), wide),
            vm((4, 8, 128), wide),
            vm((2, 2, seq, seq), low),
            vm((seq, width), low),
            vm((3, seq, width), low),
            vm((seq, width), low),
            vm((seq, width), wide),
            vm((seq, width), low),
            vm((seq, hidden), low),
            vm((seq, hidden), low),
            vm((seq, width), low),
            vm((seq, width), wide),
            vm((seq, width), low),
            vm((seq, width), low),
            vm((seq, width), low),
            vm((head_rows, 512), wide),
            vm((128, 512), wide),
            vm((1, width), wide),
            vm((1, width), wide),
            vm((1, width), wide),
            vm((1, width), wide),
            vm((128, 128 * 7), wide),
            vm((seq, seq), low),
            vm((seq, 128), low),
            sems((units, Gather.slots)),
            sems((units, Gather.slots)),
            sems((units, Scatter.slots)),
            sems((units, Scatter.slots)),
            sems((7,)),
            sems((7,)),
            sems((7,)),
            sems((7,)),
            sems((3,)),
            sems((3,)),
            sems((2,)),
            sems((4,)),
            sems((units,)),
        ],
        compiler_params=pltpu.CompilerParams(
            collective_id=0, has_side_effects=True, vmem_limit_bytes=63 * 2**20
        ),
    )(length, x, cot, small, own)


def pack_small(gain_a, gain_f, table):
    parts = (gain_a.reshape(1, -1), gain_f.reshape(1, -1), table)
    block = jnp.concatenate(
        [jnp.pad(part, ((0, 0), (0, 128 - part.shape[1]))) for part in parts]
    )
    return jnp.pad(block, ((0, 16 - block.shape[0]), (0, 0)))


def local_linked(
    inputs, lengths, cotangent, query_weight, key_weight, value_weight, output_weight,
    attention_gain, bias_table, inner_weight, outer_weight, feedforward_gain,
):
    rows, width = query_weight.shape
    chunks = inner_weight.shape[1] // width
    own = jnp.concatenate(
        (
            jnp.stack((query_weight, key_weight, value_weight, output_weight)),
            jnp.transpose(inner_weight.reshape(rows, chunks, width), (1, 0, 2)),
            outer_weight.reshape(chunks, rows, width),
        )
    )
    small = pack_small(attention_gain, feedforward_gain, bias_table)
    table_rows, heads = bias_table.shape
    block_output, input_grad, sums, small_sum, _ = fused_call(
        lengths, inputs[0], cotangent[0], small, own, heads
    )
    sums = sums.astype(jnp.float32)
    return (
        block_output[None],
        input_grad[None],
        sums[9],
        sums[10],
        sums[11],
        sums[8],
        small_sum[0, :rows],
        small_sum[2 : 2 + table_rows, :heads],
        jnp.transpose(sums[4:8], (1, 0, 2)).reshape(rows, chunks * width),
        sums[:4].reshape(chunks * rows, width),
        small_sum[1, :rows],
    )


def local(inputs, lengths, cotangent, *shards):
    block_output, input_grad, gradients = compute(inputs, lengths, cotangent, gather_all(*shards))
    return (block_output, input_grad) + sum_all(gradients)


def can_link(mesh):
    return mesh.shape["fsdp"] == 8 and mesh.shape["rep"] == 4


def solution(mesh):
    placed = (
        P(("fsdp", "rep"), None, None),
        P(("fsdp", "rep")),
        P(("fsdp", "rep"), None, None),
        P("fsdp", None),
        P("fsdp", None),
        P("fsdp", None),
        P("fsdp", None),
        P("fsdp"),
        P("fsdp", None),
        P("fsdp", None),
        P("fsdp", None),
        P("fsdp"),
    )
    return jax.shard_map(
        local_linked if can_link(mesh) else local,
        mesh=mesh,
        in_specs=placed,
        out_specs=(
            P(("fsdp", "rep"), None, None),
            P(("fsdp", "rep"), None, None),
            P("fsdp", None),
            P("fsdp", None),
            P("fsdp", None),
            P("fsdp", None),
            P("fsdp"),
            P("fsdp", None),
            P("fsdp", None),
            P("fsdp", None),
            P("fsdp"),
        ),
        check_vma=False,
    )
```

```python
import functools

import jax
import jax.numpy as jnp
from jax import lax
import jax.experimental.pallas as pl
import jax.experimental.pallas.tpu as pltpu
from jax.sharding import PartitionSpec as P

NB = 32


epsilon = 1e-06
highest = lax.Precision.HIGHEST
gelu_coeff = 0.7978845608028654
masked_score = -1e30


def bucket_of(offset):
    half_count = NB // 2
    exact_count = half_count // 2
    distance = jnp.abs(offset)
    beyond = jnp.full(offset.shape, exact_count, jnp.int32)
    for exponent in range(1, half_count - exact_count):
        beyond = beyond + (distance * distance >= exact_count * exact_count * 2**exponent).astype(
            jnp.int32
        )
    nearby = jnp.where(distance < exact_count, distance, beyond)
    return jnp.where(offset > 0, half_count, 0).astype(jnp.int32) + nearby


def rms_norm(values, gain_vector):
    inverse_rms = lax.rsqrt(jnp.mean(values * values, axis=-1, keepdims=True) + epsilon)
    return values * inverse_rms * gain_vector


def gelu(values):
    return (
        0.5 * values * (1.0 + jnp.tanh(gelu_coeff * (values + 0.044715 * values * values * values)))
    )


def dot(a,b): return jnp.dot(a,b,preferred_element_type=jnp.float32)
def dot_t(a,b): return lax.dot_general(a,b,(((1,),(1,)),((),())),preferred_element_type=jnp.float32)
def dot_c(a,b): return lax.dot_general(a,b,(((0,),(0,)),((),())),preferred_element_type=jnp.float32)

def fwd_kernel(T, len_ref, q_ref, k_ref, v_ref, rel_ref, o_ref, p_ref, strip):
    hp=pl.program_id(0)
    seq=q_ref.shape[0]; nb=seq//T
    lane=lax.broadcasted_iota(jnp.int32,(1,128),1)
    kcol=lax.broadcasted_iota(jnp.int32,(1,seq),1)
    mask=jnp.where(kcol<len_ref[0],0.0,-1e30)
    k=k_ref[...]; v=v_ref[...]
    for hh in range(2):
        mine=(lane>=64) if hh else (lane<64)
        rel=rel_ref[pl.ds(hh,1),:]
        W=4*T
        rolled=pltpu.roll(jnp.broadcast_to(rel,(T,W)),0,axis=1,stride=1,stride_axis=0)
        strip[:, 2*T:5*T]=rolled[:, :3*T]
        far_neg=rel[:, 0:1]; far_pos=rel[:, 3*T-1:3*T]
        strip[:, 0:2*T]=jnp.broadcast_to(far_neg,(T,2*T))
        strip[:, 5*T:7*T]=jnp.broadcast_to(far_pos,(T,2*T))
        for I in range(nb):
            q=jnp.where(mine,q_ref[I*T:(I+1)*T,:],jnp.bfloat16(0))
            s=dot_t(q,k)+(strip[:, (3-I)*T:(3-I)*T+seq]+mask)
            m=jnp.max(s,axis=-1,keepdims=True)
            e=jnp.exp(s-m)
            tot=jnp.sum(e,axis=-1,keepdims=True)
            p=(e*(1.0/tot)).astype(jnp.bfloat16)
            p_ref[hh,I*T:(I+1)*T,:]=p
            o=dot(p,v)
            if hh==0:
                o_ref[I*T:(I+1)*T,:]=o.astype(jnp.bfloat16)
            else:
                o_ref[I*T:(I+1)*T,:]=jnp.where(mine,o.astype(jnp.bfloat16),o_ref[I*T:(I+1)*T,:])

def bwd_kernel(T, q_ref, k_ref, v_ref, do_ref, p_ref, dq_ref, dk_ref, dv_ref, db_ref, ds_ref):
    seq=q_ref.shape[0]; nb=seq//T
    lane=lax.broadcasted_iota(jnp.int32,(1,128),1)
    k=k_ref[...]; v=v_ref[...]
    dks=[];dvs=[]
    for hh in range(2):
        mine=(lane>=64) if hh else (lane<64)
        acc=[None]*5
        for I in range(nb):
            sl=slice(I*T,(I+1)*T)
            do=jnp.where(mine,do_ref[sl,:],jnp.bfloat16(0))
            dp=dot_t(do,v)
            p=p_ref[hh,sl,:].astype(jnp.float32)
            t=p*dp
            delta=jnp.sum(t,axis=-1,keepdims=True)
            ds=(t-p*delta).astype(jnp.bfloat16)
            ds_ref[sl,:]=ds
            dsf=ds.astype(jnp.float32)
            for J in range(nb):
                d=min(2,max(-2,J-I))+2
                x=dsf[:,J*T:(J+1)*T]
                acc[d]=x if acc[d] is None else acc[d]+x
            dq=dot(ds,k)
            if hh==0: dq_ref[sl,:]=dq.astype(jnp.bfloat16)
            else: dq_ref[sl,:]=jnp.where(mine,dq.astype(jnp.bfloat16),dq_ref[sl,:])
        near=jnp.concatenate([acc[1],acc[2],acc[3],jnp.zeros((T,T),jnp.float32)],axis=1)
        total=shear_sum(near,4*T)
        far=jnp.concatenate([jnp.zeros((1,2*T),jnp.float32),jnp.sum(acc[4],axis=0,keepdims=True),jnp.sum(acc[0],axis=0,keepdims=True)],axis=1)
        db_ref[hh:hh+1,:]=total+far
        dk=dot_c(q_ref[...],ds_ref[...]).T; dv=dot_c(do_ref[...],p_ref[hh]).T
        dks.append(dk); dvs.append(dv)
    dk_ref[...]=jnp.where(lane<64,dks[0],dks[1]).astype(jnp.bfloat16)
    dv_ref[...]=jnp.where(lane<64,dvs[0],dvs[1]).astype(jnp.bfloat16)

def rel_hits(tile):
    slot = jnp.arange(4 * tile, dtype=jnp.int32)
    offset = jnp.where(slot < 3 * tile, slot - tile, slot - 5 * tile)
    bucket_ids = jnp.arange(NB, dtype=jnp.int32)
    return (bucket_of(offset)[None, :] == bucket_ids[:, None]).astype(jnp.bfloat16)


def rel_vec(table, tile):
    return dot_c(table, rel_hits(tile))


def shear_sum(block, width):
    rows = block.shape[0]
    while rows > 8:
        rows //= 2
        block = block[:rows] + pltpu.roll(block[rows:], width - rows, axis=1)
    total = block[0:1]
    for r in range(1, 8):
        total = total + pltpu.roll(block[r : r + 1], width - r, axis=1)
    return total


def att_fwd(q,k,v,rel,length,T=128):
    seq,D=q.shape; H=rel.shape[0]
    blk=pl.BlockSpec((seq,128),lambda h: (0,h))
    return pl.pallas_call(functools.partial(fwd_kernel,T),grid=(H//2,),
        in_specs=[pl.BlockSpec(memory_space=pltpu.SMEM),blk,blk,blk,pl.BlockSpec((None,2,4*T),lambda h:(h,0,0))],
        out_specs=[blk,pl.BlockSpec((2,seq,seq),lambda h:(h,0,0))],
        out_shape=[jax.ShapeDtypeStruct((seq,D),jnp.bfloat16),jax.ShapeDtypeStruct((H,seq,seq),jnp.bfloat16)],
        scratch_shapes=[pltpu.VMEM((T,7*T),jnp.float32)],
        compiler_params=pltpu.CompilerParams(vmem_limit_bytes=40*2**20))(length,q,k,v,rel.reshape(H//2,2,4*T))
def att_bwd(q,k,v,do,p,T=128):
    seq,D=q.shape; H=p.shape[0]
    blk=pl.BlockSpec((seq,128),lambda h: (0,h))
    o=jax.ShapeDtypeStruct((seq,D),jnp.bfloat16)
    outs=pl.pallas_call(functools.partial(bwd_kernel,T),grid=(H//2,),
        in_specs=[blk,blk,blk,blk,pl.BlockSpec((2,seq,seq),lambda h:(h,0,0))],
        out_specs=[blk,blk,blk,pl.BlockSpec((None,2,4*T),lambda h:(h,0,0))],
        out_shape=[o,o,o,jax.ShapeDtypeStruct((H//2,2,4*T),jnp.float32)],
        scratch_shapes=[pltpu.VMEM((seq,seq),jnp.bfloat16)],
        compiler_params=pltpu.CompilerParams(vmem_limit_bytes=40*2**20))(q,k,v,do,p)
    return *outs[:3],outs[3].reshape(H,4*T)

def contract_rows(left, right):
    return lax.dot_general(
        left, right, (((0,), (0,)), ((), ())), preferred_element_type=jnp.float32
    )


def contract_cols(left, right):
    return lax.dot_general(
        left, right, (((1,), (1,)), ((), ())), preferred_element_type=jnp.float32
    )


MESH = pl.DeviceIdType.MESH


def coords():
    shard = lax.axis_index("fsdp")
    copy = lax.axis_index("rep")
    return shard // 2, shard % 2, copy // 2, copy % 2


def greet():
    barrier = pltpu.get_barrier_semaphore()
    shard = lax.axis_index("fsdp")
    copy = lax.axis_index("rep")
    for k in range(1, 8):
        peer = (lax.rem(shard + k, 8), copy)
        pl.semaphore_signal(barrier, inc=1, device_id=peer, device_id_type=MESH)
    for k in range(1, 4):
        peer = (shard, lax.rem(copy + k, 4))
        pl.semaphore_signal(barrier, inc=1, device_id=peer, device_id_type=MESH)
    pl.semaphore_wait(barrier, 10)


def stepper(stages, count):
    def step(t):
        for stage, lag in stages:
            g = t - lag
            if isinstance(g, int):
                if 0 <= g < count:
                    stage(g)
            else:
                pl.when((g >= 0) & (g < count))(functools.partial(stage, g))

    return step


class Links:
    def __init__(self, rows, send_sems, recv_sems):
        self.send_sems, self.recv_sems = send_sems, recv_sems
        self.z, self.x, self.y, self.c = coords()
        half = rows // 2
        part = half // 3
        at = lambda start, size: pl.ds(pl.multiple_of(start, part), size)
        first = half * self.c
        other = half * (1 - self.c)
        self.half, self.other_half = at(first, half), at(other, half)
        self.plane = at(first + part * self.y, 2 * part)
        self.shared = at(first + part, part)
        self.own_third = at(first + 2 * part * self.y, part)
        self.other_third = at(first + 2 * part * (1 - self.y), part)
        self.shared_in = at(part * self.y, part)
        self.third_in = at(part * (1 - self.y), part)

    def copy(self, src, dst, g, slot, device):
        return pltpu.make_async_remote_copy(
            src_ref=src,
            dst_ref=dst,
            send_sem=self.send_sems.at[g, slot],
            recv_sem=self.recv_sems.at[g, slot],
            device_id=device,
            device_id_type=MESH,
        )

    def to_x(self):
        return (self.z * 2 + 1 - self.x, self.y * 2 + self.c)

    def to_y(self):
        return (self.z * 2 + self.x, (1 - self.y) * 2 + self.c)

    def to_core(self):
        return (self.z * 2 + self.x, self.y * 2 + 1 - self.c)

    def to_z(self, k):
        return (lax.rem(self.z + k, 4) * 2 + self.x, self.y * 2 + self.c)

    def z_before(self, k):
        return lax.rem(self.z + 4 - k, 4)


class Gather(Links):
    slots = 15

    def __init__(self, full, send_sems, recv_sems):
        super().__init__(full.shape[3], send_sems, recv_sems)
        self.full = full

    def block(self, g, k, rows):
        return self.full.at[self.z_before(k), self.x, g, rows]

    def column(self, g, rows):
        return self.full.at[:, 1 - self.x, g, rows]

    def z_copy(self, g, k):
        part = self.block(g, 0, self.plane)
        return self.copy(part, part, g, k - 1, self.to_z(k))

    def x_copy(self, g, k):
        part = self.block(g, k, self.plane)
        return self.copy(part, part, g, 3 + k, self.to_x())

    def y_copy(self, g, k):
        rows = self.own_third
        part = self.block(g, k, rows) if k < 4 else self.column(g, rows)
        return self.copy(part, part, g, 6 + k, self.to_y())

    def core_copy(self, g, k):
        part = self.block(g, k, self.half) if k < 4 else self.column(g, self.half)
        return self.copy(part, part, g, 10 + k, self.to_core())

    def arrived(self, part, g, slot, device):
        self.copy(part, part, g, slot, device).wait_recv()

    def start(self, g):
        self.x_copy(g, 0).start()
        for k in (1, 2, 3):
            self.z_copy(g, k).start()

    def after_z(self, g):
        for k in (1, 2, 3):
            self.arrived(self.block(g, k, self.plane), g, k - 1, self.to_z(k))
            self.x_copy(g, k).start()
            self.y_copy(g, k).start()

    def after_x(self, g):
        for k in range(4):
            part = self.full.at[self.z_before(k), 1 - self.x, g, self.plane]
            self.arrived(part, g, 3 + k, self.to_x())
        self.y_copy(g, 4).start()

    def after_y(self, g):
        for k in (1, 2, 3):
            self.arrived(self.block(g, k, self.other_third), g, 6 + k, self.to_y())
            self.core_copy(g, k).start()
        self.arrived(self.column(g, self.other_third), g, 10, self.to_y())
        self.core_copy(g, 4).start()

    def after_core(self, g):
        for k in (1, 2, 3):
            self.arrived(self.block(g, k, self.other_half), g, 10 + k, self.to_core())
        self.arrived(self.column(g, self.other_half), g, 14, self.to_core())

    def drain(self, g):
        self.x_copy(g, 0).wait_send()
        for k in (1, 2, 3):
            self.z_copy(g, k).wait_send()
            self.x_copy(g, k).wait_send()
            self.y_copy(g, k).wait_send()
            self.core_copy(g, k).wait_send()
        self.y_copy(g, 4).wait_send()
        self.core_copy(g, 4).wait_send()


class Scatter(Links):
    slots = 8

    def __init__(self, slot, full, own, from_core, from_y, from_x, from_z, send_sems, recv_sems):
        super().__init__(own.shape[1], send_sems, recv_sems)
        self.slot, self.full, self.own = slot, full, own
        self.from_core, self.from_y, self.from_x, self.from_z = from_core, from_y, from_x, from_z

    def core_copy(self, g):
        part = self.full.at[:, :, self.slot(g), self.other_half]
        return self.copy(part, self.from_core.at[g], g, 0, self.to_core())

    def y_copy(self, g):
        part = self.full.at[:, :, self.slot(g), self.other_third]
        return self.copy(part, self.from_y.at[g], g, 1, self.to_y())

    def x_copy(self, g):
        part = self.full.at[:, 1 - self.x, self.slot(g), self.plane]
        return self.copy(part, self.from_x.at[g], g, 2, self.to_x())

    def z_copy(self, g, k):
        part = self.full.at[lax.rem(self.z + k, 4), self.x, self.slot(g), self.plane]
        return self.copy(part, self.from_z.at[g, k - 1], g, 2 + k, self.to_z(k))

    def back_y_copy(self, g):
        part = self.own.at[g, self.plane]
        return self.copy(part, self.from_z.at[g, 3], g, 6, self.to_y())

    def back_core_copy(self, g):
        part = self.own.at[g, self.half]
        return self.copy(part, part, g, 7, self.to_core())

    def start(self, g):
        self.core_copy(g).start()

    def after_core(self, g):
        self.core_copy(g).wait_recv()
        for a in range(4):
            for b in range(2):
                self.full[a, b, self.slot(g), self.half] += self.from_core[g, a, b]
        self.y_copy(g).start()

    def after_y(self, g):
        self.y_copy(g).wait_recv()
        for a in range(4):
            for b in range(2):
                self.full[a, b, self.slot(g), self.own_third] += self.from_y[g, a, b]
        self.x_copy(g).start()

    def after_x(self, g):
        self.x_copy(g).wait_recv()
        for a in range(4):
            self.full[a, self.x, self.slot(g), self.plane] += self.from_x[g, a]
        for k in (1, 2, 3):
            self.z_copy(g, k).start()

    def after_z(self, g):
        total = self.full[self.z, self.x, self.slot(g), self.plane].astype(jnp.float32)
        for k in (1, 2, 3):
            self.z_copy(g, k).wait_recv()
            total = total + self.from_z[g, k - 1].astype(jnp.float32)
        self.own[g, self.plane] = total.astype(jnp.bfloat16)
        self.back_y_copy(g).start()

    def after_back_y(self, g):
        self.back_y_copy(g).wait_recv()
        self.back_y_copy(g).wait_send()
        got = self.from_z.at[g, 3]
        self.own[g, self.shared] += got[self.shared_in]
        self.own[g, self.other_third] = got[self.third_in]
        self.back_core_copy(g).start()

    def after_back_core(self, g):
        part = self.own.at[g, self.other_half]
        self.copy(part, part, g, 7, self.to_core()).wait_recv()

    def drain(self, g):
        self.core_copy(g).wait_send()
        self.y_copy(g).wait_send()
        self.x_copy(g).wait_send()
        for k in (1, 2, 3):
            self.z_copy(g, k).wait_send()
        self.back_core_copy(g).wait_send()


def compute(inputs, lengths, cotangent, weights):
    (
        full_query, full_key, full_value, full_output, full_gain, full_table, full_inner,
        full_outer, full_ffn_gain,
    ) = weights
    pairs_here, seq_len, model_width = inputs.shape
    row_count = pairs_here * seq_len
    head_count = full_table.shape[1]
    tile = 128
    relative = rel_vec(full_table, tile)
    flat_inputs = inputs.reshape(row_count, model_width).astype(jnp.float32)
    normed = rms_norm(flat_inputs, full_gain.astype(jnp.float32)).astype(jnp.bfloat16)
    joined = jnp.concatenate((full_query, full_key, full_value), axis=1)
    projected = jnp.dot(normed, joined, preferred_element_type=jnp.float32).astype(jnp.bfloat16)
    queries = projected[:, :model_width]
    key_rows = projected[:, model_width : 2 * model_width]
    value_rows = projected[:, 2 * model_width :]
    pair_rows = [slice(n * seq_len, (n + 1) * seq_len) for n in range(pairs_here)]
    forward_parts = [
        att_fwd(queries[r], key_rows[r], value_rows[r], relative, lengths[n : n + 1], tile)
        for n, r in enumerate(pair_rows)
    ]
    attended = jnp.concatenate([part[0] for part in forward_parts], axis=0)
    middle = flat_inputs + jnp.dot(attended, full_output, preferred_element_type=jnp.float32)
    normed_ffn = rms_norm(middle, full_ffn_gain.astype(jnp.float32)).astype(jnp.bfloat16)
    raised = jnp.dot(normed_ffn, full_inner, preferred_element_type=jnp.float32)
    active = gelu(raised).astype(jnp.bfloat16)
    lowered = jnp.dot(active, full_outer, preferred_element_type=jnp.float32)
    block_output = (middle + lowered).astype(jnp.bfloat16).reshape(pairs_here, seq_len, model_width)
    positions = jnp.arange(seq_len, dtype=jnp.int32)
    row_live = (positions[None, :] < lengths[:, None]).astype(jnp.float32)
    seed_rows = (cotangent.astype(jnp.float32) * row_live[:, :, None]).reshape(
        row_count, model_width
    )
    seed_low = seed_rows.astype(jnp.bfloat16)
    grad_active = contract_cols(seed_low, full_outer)
    grad_outer = contract_rows(active, seed_low)
    grad_raised = jax.vjp(gelu, raised)[1](grad_active)[0].astype(jnp.bfloat16)
    grad_inner = contract_rows(normed_ffn, grad_raised)
    grad_normed_ffn = contract_cols(grad_raised, full_inner)
    ffn_pull = jax.vjp(rms_norm, middle, full_ffn_gain.astype(jnp.float32))[1]
    grad_middle_part, grad_ffn_gain = ffn_pull(grad_normed_ffn)
    grad_middle = seed_rows + grad_middle_part
    joined = jnp.concatenate((full_query, full_key, full_value), axis=1)
    middle_low = grad_middle.astype(jnp.bfloat16)
    grad_attended = contract_cols(middle_low, full_output).astype(jnp.bfloat16)
    grad_output = contract_rows(attended, middle_low)
    backward_parts = [
        att_bwd(
            queries[r], key_rows[r], value_rows[r], grad_attended[r], forward_parts[n][1], tile
        )
        for n, r in enumerate(pair_rows)
    ]
    grad_projected = jnp.concatenate(
        [jnp.concatenate(part[:3], axis=1) for part in backward_parts], axis=0
    )
    grad_joined = contract_rows(normed, grad_projected)
    grad_normed = contract_cols(grad_projected, joined)
    attention_pull = jax.vjp(rms_norm, flat_inputs, full_gain.astype(jnp.float32))[1]
    grad_inputs_part, grad_attention_gain = attention_pull(grad_normed)
    input_grad = (grad_middle + grad_inputs_part).reshape(pairs_here, seq_len, model_width)
    grad_relative = sum(part[3] for part in backward_parts)
    grad_table = lax.dot_general(
        rel_hits(tile).astype(jnp.float32),
        grad_relative,
        (((1,), (1,)), ((), ())),
        precision=highest,
    )
    return block_output, input_grad, (
        grad_joined[:, :model_width],
        grad_joined[:, model_width : 2 * model_width],
        grad_joined[:, 2 * model_width :],
        grad_output,
        grad_attention_gain,
        grad_table,
        grad_inner,
        grad_outer,
        grad_ffn_gain,
    )


def gather_all(query_weight, key_weight, value_weight, output_weight, attention_gain, bias_table,
               inner_weight, outer_weight, feedforward_gain):
    return tuple(
        lax.all_gather(part, "fsdp", axis=0, tiled=True)
        for part in (
            query_weight, key_weight, value_weight, output_weight, attention_gain, bias_table,
            inner_weight, outer_weight, feedforward_gain,
        )
    )


def sum_all(gradients):
    def one(part):
        part = lax.psum_scatter(
            part.astype(jnp.bfloat16), "fsdp", scatter_dimension=0, tiled=True
        )
        return lax.psum(part, "rep").astype(jnp.float32)

    return tuple(one(part) for part in gradients)


def gelu_parts(z):
    square = z * z
    t = jnp.tanh(gelu_coeff * z * (1.0 + 0.044715 * square))
    half = 0.5 * (1.0 + t)
    slope = half + (0.5 * gelu_coeff) * z * (1.0 - t * t) * (1.0 + (3 * 0.044715) * square)
    return z * half, slope


def lanes(start, size):
    return pl.ds(pl.multiple_of(start, 128), size)


def rows_at(start, size):
    return pl.ds(pl.multiple_of(start, size), size)


def loop(count, body):
    def step(n, carry):
        body(n)
        return carry

    lax.fori_loop(0, count, step, 0)


def norm_back(grad, gain, values):
    inverse = lax.rsqrt(jnp.mean(values * values, axis=-1, keepdims=True) + epsilon)
    scaled = grad * gain
    centre = jnp.mean(scaled * values, axis=-1, keepdims=True)
    back = inverse * scaled - values * (inverse * inverse * inverse * centre)
    return back, jnp.sum(grad * values * inverse, axis=0, keepdims=True)


class Layer:
    def __init__(self, **refs):
        self.__dict__.update(refs)
        self.seq, self.width = self.x.shape
        self.tile = 128
        self.row_block = 128
        self.shard_rows = self.bank.shape[3]

    def unit(self, u, column=None, size=None):
        if column is None:
            block = self.bank[:, :, u]
        else:
            block = self.bank[:, :, u, :, lanes(column, size)]
        return block.reshape(-1, block.shape[-1])

    def row_chunks(self, body):
        size = self.row_block
        loop(self.seq // size, lambda n: body(rows_at(n * size, size)))

    def small_arrays(self):
        flat = self.all_small[...].reshape(-1, 128)
        tile = self.tile
        slot = lax.broadcasted_iota(jnp.int32, (flat.shape[0], 4 * tile), 1)
        offset = jnp.where(slot < 3 * tile, slot - tile, slot - 5 * tile)
        row = lax.broadcasted_iota(jnp.int32, (flat.shape[0], 4 * tile), 0)
        per = NB // 8
        inside = row % 16 - 2
        wanted = jnp.where((inside >= 0) & (inside < per), (row // 16) * per + inside, -1)
        hits = (bucket_of(offset) == wanted).astype(jnp.bfloat16)
        self.rel[...] = dot_c(flat, hits)[: self.rel.shape[0]]
        for index, ref in ((0, self.gain_a), (1, self.gain_f)):
            total = jnp.zeros((1, self.width), jnp.float32)
            for shard in range(8):
                part = self.all_small[shard].astype(jnp.float32)[index : index + 1]
                wide = jnp.concatenate(
                    [part, jnp.zeros((1, self.width - 128), jnp.float32)], axis=1
                )
                total = total + (
                    pltpu.roll(wide, shard * self.shard_rows, axis=1) if shard else wide
                )
            ref[...] = total

    def norm_in(self):
        gain = self.gain_a[...]

        def body(r):
            self.normed[r] = rms_norm(self.x[r].astype(jnp.float32), gain).astype(jnp.bfloat16)

        self.row_chunks(body)

    def mask_seed(self):
        def body(r):
            index = lax.broadcasted_iota(jnp.int32, (self.row_block, 1), 0) + r.start
            live = index < self.length[0]
            self.seed[r] = jnp.where(live, self.cot[r], jnp.bfloat16(0))

        self.row_chunks(body)

    def project(self, u):
        def body(n):
            self.qkv[u, :, lanes(n * 256, 256)] = dot(
                self.normed[...], self.unit(u, n * 256, 256)
            ).astype(jnp.bfloat16)

        loop(self.width // 256, body)

    def strip_for(self, head):
        tile = self.tile
        rel = self.rel[pl.ds(head, 1), :]
        rolled = pltpu.roll(
            jnp.broadcast_to(rel, (tile, 4 * tile)), 0, axis=1, stride=1, stride_axis=0
        )
        self.strip[:, 2 * tile : 5 * tile] = rolled[:, : 3 * tile]
        self.strip[:, : 2 * tile] = jnp.broadcast_to(rel[:, :1], (tile, 2 * tile))
        self.strip[:, 5 * tile :] = jnp.broadcast_to(
            rel[:, 3 * tile - 1 : 3 * tile], (tile, 2 * tile)
        )

    def probs_store(self, pair, slot):
        return pltpu.make_async_copy(
            self.probs.at[slot], self.probs_far.at[pair], self.probs_sems.at[slot]
        )

    def probs_load(self, pair, slot):
        return pltpu.make_async_copy(
            self.probs_far.at[pair], self.probs.at[slot], self.probs_sems.at[slot]
        )

    def attend(self, pair):
        tile, seq = self.tile, self.seq
        slot = lax.rem(pair, 2)
        pl.when(pair >= 2)(lambda: self.probs_store(pair, slot).wait())
        lane = lax.broadcasted_iota(jnp.int32, (1, 128), 1)
        key_at = lax.broadcasted_iota(jnp.int32, (1, seq), 1)
        mask = jnp.where(key_at < self.length[0], 0.0, masked_score)
        cols = lanes(pair * 128, 128)
        k = self.qkv[1, :, cols]
        v = self.qkv[2, :, cols]
        for head in range(2):
            mine = (lane >= 64) if head else (lane < 64)
            self.strip_for(pair * 2 + head)
            for block in range(seq // tile):
                r = slice(block * tile, (block + 1) * tile)
                q = jnp.where(mine, self.qkv[0, r, cols], jnp.bfloat16(0))
                first = (seq // tile - 1 - block) * tile
                scores = dot_t(q, k) + (self.strip[:, first : first + seq] + mask)
                peak = jnp.max(scores, axis=-1, keepdims=True)
                raised = jnp.exp(scores - peak)
                total = jnp.sum(raised, axis=-1, keepdims=True)
                probs = (raised * (1.0 / total)).astype(jnp.bfloat16)
                self.probs[slot, head, r, :] = probs
                out = dot(probs, v).astype(jnp.bfloat16)
                if head:
                    out = jnp.where(mine, out, self.attended[r, cols])
                self.attended[r, cols] = out
        self.probs_store(pair, slot).start()

    def middle_rows(self):
        def body(n):
            c = lanes(n * 256, 256)
            self.middle[:, c] = self.x[:, c].astype(jnp.float32) + dot(
                self.attended[...], self.unit(3, n * 256, 256)
            )

        loop(self.width // 256, body)
        gain = self.gain_f[...]

        def norm(r):
            self.normed_ffn[r] = rms_norm(self.middle[r], gain).astype(jnp.bfloat16)

        self.row_chunks(norm)

    def raise_unit(self, i):
        def body(n):
            raised = dot(self.normed_ffn[...], self.unit(4 + i, n * 256, 256))
            active, slope = gelu_parts(raised)
            c = lanes(i * self.width + n * 256, 256)
            self.active[:, c] = active.astype(jnp.bfloat16)
            self.slope[:, c] = slope.astype(jnp.bfloat16)

        loop(self.width // 256, body)

    def outer_grad(self, shard):
        size = 4 * self.shard_rows
        block = dot_c(self.active[:, lanes(shard * size, size)], self.seed[...])
        self.bank[shard // 2, shard % 2, 12:16] = block.astype(jnp.bfloat16).reshape(
            4, self.shard_rows, self.width
        )

    def lower(self):
        def body(n):
            outer = self.bank[:, :, 8:12, :, lanes(n * 256, 256)].reshape(-1, 256)
            c = lanes(n * 256, 256)
            self.block_out[:, c] = (self.middle[:, c] + dot(self.active[...], outer)).astype(
                jnp.bfloat16
            )

        loop(self.width // 256, body)

    def raised_grad(self, shard):
        size = 4 * self.shard_rows
        outer = self.bank[shard // 2, shard % 2, 8:12].reshape(size, self.width)
        c = lanes(shard * size, size)
        grad = dot_t(self.seed[...], outer) * self.slope[:, c].astype(jnp.float32)
        self.slope[:, c] = grad.astype(jnp.bfloat16)

    def inner_grad(self, i):
        def body(n):
            c = lanes(i * self.width + n * 256, 256)
            block = dot_c(self.normed_ffn[...], self.slope[:, c]).astype(jnp.bfloat16)
            self.bank[:, :, 16 + i, :, lanes(n * 256, 256)] = block.reshape(
                4, 2, self.shard_rows, 256
            )

        loop(self.width // 256, body)

    def middle_grad(self):
        for part in range(2):
            total = None
            for i in range(4):
                inner = self.bank[2 * part : 2 * part + 2, :, 4 + i]
                inner = inner.reshape(-1, self.width)
                term = dot_t(self.slope[:, i * self.width : (i + 1) * self.width], inner)
                total = term if total is None else total + term
            size = self.width // 2
            self.grad_mid[:, part * size : (part + 1) * size] = total
        gain = self.gain_f[...]
        self.gain_f_grad[...] = jnp.zeros_like(self.gain_f_grad)

        def body(r):
            back, terms = norm_back(self.grad_mid[r], gain, self.middle[r])
            total = self.seed[r].astype(jnp.float32) + back
            self.gain_f_grad[...] += terms
            self.grad_mid[r] = total
            self.mid_low[r] = total.astype(jnp.bfloat16)

        self.row_chunks(body)

    def square_grad(self, left, right, slot):
        def body(n):
            block = dot_c(left[...], right(lanes(n * 256, 256))).astype(jnp.bfloat16)
            self.bank[:, :, slot, :, lanes(n * 256, 256)] = block.reshape(
                4, 2, self.shard_rows, 256
            )

        loop(self.width // 256, body)

    def attended_grad(self):
        size = self.width // 2
        for part in range(2):
            weight = self.bank[2 * part : 2 * part + 2, :, 3].reshape(size, self.width)
            self.grad_att[:, part * size : (part + 1) * size] = dot_t(
                self.mid_low[...], weight
            ).astype(jnp.bfloat16)

    def attend_back(self, pair):
        tile, seq = self.tile, self.seq
        slot = lax.rem(pair, 2)
        self.probs_load(pair, slot).wait()
        lane = lax.broadcasted_iota(jnp.int32, (1, 128), 1)
        cols = lanes(pair * 128, 128)
        k = self.qkv[1, :, cols]
        v = self.qkv[2, :, cols]
        blocks = seq // tile
        grads = []
        for head in range(2):
            mine = (lane >= 64) if head else (lane < 64)
            sums = [None] * 5
            for block in range(blocks):
                r = slice(block * tile, (block + 1) * tile)
                grad_out = jnp.where(mine, self.grad_att[r, cols], jnp.bfloat16(0))
                probs = self.probs[slot, head, r, :].astype(jnp.float32)
                weighted = probs * dot_t(grad_out, v)
                centre = jnp.sum(weighted, axis=-1, keepdims=True)
                low = (weighted - probs * centre).astype(jnp.bfloat16)
                self.grad_scores[r, :] = low
                wide = low.astype(jnp.float32)
                for other in range(blocks):
                    apart = min(2, max(-2, other - block)) + 2
                    part = wide[:, other * tile : (other + 1) * tile]
                    sums[apart] = part if sums[apart] is None else sums[apart] + part
                out = dot(low, k).astype(jnp.bfloat16)
                if head:
                    out = jnp.where(mine, out, self.grad_q[r, :])
                self.grad_q[r, :] = out
            zero = jnp.zeros((tile, tile), jnp.float32)
            near = shear_sum(jnp.concatenate([sums[1], sums[2], sums[3], zero], axis=1), 4 * tile)
            far = jnp.concatenate(
                [
                    jnp.zeros((1, 2 * tile), jnp.float32),
                    jnp.sum(sums[4], axis=0, keepdims=True),
                    jnp.sum(sums[0], axis=0, keepdims=True),
                ],
                axis=1,
            )
            self.rel_grad[pl.ds(pair * 2 + head, 1), :] = near + far
            grads.append(
                (
                    dot_c(self.qkv[0, :, cols], self.grad_scores[...]).T,
                    dot_c(self.grad_att[:, cols], self.probs[slot, head]).T,
                )
            )
        first = lane < 64
        self.qkv[0, :, cols] = self.grad_q[...]
        self.qkv[1, :, cols] = jnp.where(first, grads[0][0], grads[1][0]).astype(jnp.bfloat16)
        self.qkv[2, :, cols] = jnp.where(first, grads[0][1], grads[1][1]).astype(jnp.bfloat16)
        pl.when(pair + 2 < self.probs_far.shape[0])(
            lambda: self.probs_load(pair + 2, slot).start()
        )

    def input_grad(self):
        size = self.width // 2
        for part in range(2):
            total = None
            for u in range(3):
                weight = self.bank[2 * part : 2 * part + 2, :, u].reshape(size, self.width)
                term = dot_t(self.qkv[u], weight)
                total = term if total is None else total + term
            self.middle[:, part * size : (part + 1) * size] = total
        gain = self.gain_a[...]
        self.gain_a_grad[...] = jnp.zeros_like(self.gain_a_grad)

        def body(r):
            back, terms = norm_back(self.middle[r], gain, self.x[r].astype(jnp.float32))
            self.gain_a_grad[...] += terms
            self.grad_mid[r] += back

        self.row_chunks(body)

    def small_grads(self):
        tile = self.tile
        shape = (64, 4 * tile)
        slot = lax.broadcasted_iota(jnp.int32, shape, 1)
        offset = jnp.where(slot < 3 * tile, slot - tile, slot - 5 * tile)
        row = lax.broadcasted_iota(jnp.int32, shape, 0)
        per = NB // 8
        inside = row % 8 - 2
        wanted = jnp.where((inside >= 0) & (inside < per), (row // 8) * per + inside, -1)
        hits = (bucket_of(offset) == wanted).astype(jnp.float32)
        table = lax.dot_general(
            hits,
            self.rel_grad[...],
            (((1,), (1,)), ((), ())),
            precision=highest,
            preferred_element_type=jnp.float32,
        )
        rows = lax.broadcasted_iota(jnp.int32, (8, 128), 0)
        lane = lax.broadcasted_iota(jnp.int32, (8, 128), 1)
        for shard in range(8):
            block = table[8 * shard : 8 * shard + 8]
            for index, ref in ((0, self.gain_a_grad), (1, self.gain_f_grad)):
                wide = ref[...]
                if shard:
                    wide = pltpu.roll(wide, self.width - shard * self.shard_rows, axis=1)
                here = (rows == index) & (lane < self.shard_rows)
                block = jnp.where(here, jnp.broadcast_to(wide[:, :128], (8, 128)), block)
            self.small_out[shard] = block


def order_slot(n):
    return jnp.where(n < 8, n + 12, jnp.where(n == 8, 7, n - 5))


def fused_kernel(
    length, x, cot, gain_a_own, gain_f_own, table_own, query_own, key_own, value_own, output_own,
    inner_own, outer_own,
    block_far, grad_far, own_far, small_result, probs_far,
    bank, own_sum, from_core, from_y, from_x, from_z, small_wide, small, all_small, small_out,
    small_in, small_rep, probs, normed, qkv, attended, middle, normed_ffn, active, slope, seed,
    grad_mid, mid_low, grad_att, block_out, rel, rel_grad, gain_a, gain_f, gain_a_grad,
    gain_f_grad, strip, grad_scores, grad_q,
    sends, recvs, sum_sends, sum_recvs, small_sends, small_recvs, back_sends, back_recvs,
    rep_sends, rep_recvs, probs_sems, misc_sems, store_sems, keep_sems,
):
    shard = lax.axis_index("fsdp")
    copy_id = lax.axis_index("rep")
    layer = Layer(
        length=length, x=x, cot=cot, bank=bank, all_small=all_small, small_out=small_out,
        probs=probs, probs_far=probs_far, probs_sems=probs_sems, normed=normed, qkv=qkv,
        attended=attended, middle=middle, normed_ffn=normed_ffn, active=active, slope=slope,
        seed=seed, grad_mid=grad_mid, mid_low=mid_low, grad_att=grad_att, block_out=block_out,
        rel=rel, rel_grad=rel_grad, gain_a=gain_a, gain_f=gain_f, gain_a_grad=gain_a_grad,
        gain_f_grad=gain_f_grad, strip=strip, grad_scores=grad_scores, grad_q=grad_q,
    )
    rows, width = query_own.shape
    chunks = inner_own.shape[1] // width
    units = 4 + 2 * chunks
    gather = Gather(bank, sends, recvs)
    scatter = Scatter(
        order_slot, bank, own_sum, from_core, from_y, from_x, from_z, sum_sends, sum_recvs
    )
    pairs = probs_far.shape[0]

    def remote(src, dst, send, recv, device):
        return pltpu.make_async_remote_copy(
            src_ref=src, dst_ref=dst, send_sem=send, recv_sem=recv, device_id=device,
            device_id_type=MESH,
        )

    def peer(k):
        return (lax.rem(shard + k, 8), copy_id)

    def rep_peer(k):
        return (shard, lax.rem(copy_id + k, 4))

    parts = [query_own, key_own, value_own, output_own]
    parts += [inner_own.at[:, pl.ds(i * width, width)] for i in range(chunks)]
    parts += [outer_own.at[pl.ds(i * rows, rows)] for i in range(chunks)]
    keeps = [
        pltpu.make_async_copy(part, bank.at[gather.z, gather.x, u], keep_sems.at[u])
        for u, part in enumerate(parts)
    ]
    for copy in keeps:
        copy.start()
    small_wide[...] = jnp.zeros_like(small_wide)
    small_wide[0:1, :rows] = gain_a_own[...].astype(jnp.float32)
    small_wide[1:2, :rows] = gain_f_own[...].astype(jnp.float32)
    per, heads = table_own.shape
    small_wide[2 : 2 + per, :heads] = table_own[...].astype(jnp.float32)
    small[...] = small_wide[...].astype(jnp.bfloat16)
    all_small[shard] = small[...]
    for copy in keeps:
        copy.wait()
    greet()
    small_copies = [
        remote(small, all_small.at[shard], small_sends.at[k - 1], small_recvs.at[k - 1], peer(k))
        for k in range(1, 8)
    ]
    for copy in small_copies:
        copy.start()
    gather_step = stepper(
        (
            (gather.after_y, 6), (gather.after_x, 4), (gather.after_z, 2), (gather.start, 0),
            (gather.after_core, 7),
        ),
        units,
    )
    loop(2, gather_step)
    layer.mask_seed()
    for copy in small_copies:
        copy.wait()
    layer.small_arrays()
    layer.norm_in()

    def early(n):
        gather_step(n + 2)

    loop(5, early)

    def projects(u):
        gather_step(u + 7)
        layer.project(u)

    loop(3, projects)

    def attends(pair):
        gather_step(pair + 10)
        layer.attend(pair)

    loop(pairs, attends)
    layer.middle_rows()

    def raises(i):
        gather_step(i + 16)
        layer.raise_unit(i)

    loop(4, raises)
    for pair in (pairs - 2, pairs - 1):
        layer.probs_store(pair, pair % 2).wait()
    for pair in (0, 1):
        layer.probs_load(pair, pair).start()
    loop(8, layer.outer_grad)

    def store(n):
        return pltpu.make_async_copy(own_sum.at[n], own_far.at[n], store_sems.at[n])

    def last(n):
        scatter.after_back_core(n)
        store(n).start()

    sum_step = stepper(
        (
            (last, 9), (scatter.after_back_y, 8), (scatter.after_z, 7), (scatter.after_x, 5),
            (scatter.after_y, 3), (scatter.after_core, 1), (scatter.start, 0),
        ),
        units,
    )
    sum_step(0)
    layer.lower()
    block_store = pltpu.make_async_copy(block_out, block_far, misc_sems.at[0])
    block_store.start()
    sum_step(1)
    loop(8, layer.raised_grad)
    sum_step(2)

    def inners(i):
        layer.inner_grad(2 * i)
        layer.inner_grad(2 * i + 1)
        sum_step(i + 3)
        gather.drain(4 + 2 * i)
        gather.drain(5 + 2 * i)

    loop(2, inners)
    layer.middle_grad()
    layer.square_grad(attended, lambda c: mid_low[:, c], 7)
    layer.attended_grad()
    rel_grad[...] = jnp.zeros_like(rel_grad)

    def attend_backs(n):
        sum_step(n + 5)
        layer.attend_back(2 * n)
        layer.attend_back(2 * n + 1)

    loop(pairs // 2, attend_backs)
    sum_step(8)

    def square_grads(u):
        layer.square_grad(normed, lambda c: qkv[u, :, c], 4 + u)
        sum_step(u + 9)

    loop(3, square_grads)
    layer.input_grad()
    grad_store = pltpu.make_async_copy(grad_mid, grad_far, misc_sems.at[1])
    grad_store.start()
    layer.small_grads()
    back_copies = [
        remote(
            small_out.at[lax.rem(shard + k, 8)], small_in.at[k - 1], back_sends.at[k - 1],
            back_recvs.at[k - 1], peer(k),
        )
        for k in range(1, 8)
    ]
    for copy in back_copies:
        copy.start()
    loop(4, gather.drain)
    loop(units - 8, lambda n: gather.drain(n + 8))

    def late(n):
        sum_step(n + 12)

    loop(5, late)
    total = small_out[shard]
    for k, copy in enumerate(back_copies):
        copy.wait_recv()
        total = total + small_in[k]
    small_rep[copy_id] = total
    rep_copies = [
        remote(
            small_rep.at[copy_id], small_rep.at[copy_id], rep_sends.at[k - 1],
            rep_recvs.at[k - 1], rep_peer(k),
        )
        for k in range(1, 4)
    ]
    for copy in rep_copies:
        copy.start()

    def later(n):
        sum_step(n + 17)

    loop(4, later)
    for k in range(1, 4):
        there = small_rep.at[lax.rem(copy_id + 4 - k, 4)]
        remote(there, there, rep_sends.at[k - 1], rep_recvs.at[k - 1], rep_peer(k)).wait_recv()
    small_result[...] = (small_rep[0] + small_rep[1]) + (small_rep[2] + small_rep[3])

    def drain(n):
        scatter.drain(n)
        store(n).wait()

    loop(units, drain)
    for copy in back_copies + rep_copies:
        copy.wait_send()
    block_store.wait()
    grad_store.wait()


def fused_call(length, x, cot, gain_a, gain_f, table, square, inner, outer):
    rows, width = square[0].shape
    units = 4 + 2 * (inner.shape[1] // width)
    heads = table.shape[1]
    seq = x.shape[0]
    half = rows // 2
    part = half // 3
    hidden = inner.shape[1]
    low, wide = jnp.bfloat16, jnp.float32
    anywhere = pl.BlockSpec(memory_space=pl.ANY)
    within = pl.BlockSpec(memory_space=pltpu.VMEM)
    sems = pltpu.SemaphoreType.DMA
    vm = pltpu.VMEM
    head_rows = -(-heads // 8) * 8
    return pl.pallas_call(
        fused_kernel,
        out_shape=(
            jax.ShapeDtypeStruct((seq, width), low),
            jax.ShapeDtypeStruct((seq, width), wide),
            jax.ShapeDtypeStruct((units, rows, width), low),
            jax.ShapeDtypeStruct((8, 128), wide),
            jax.ShapeDtypeStruct((heads // 2, 2, seq, seq), low),
        ),
        in_specs=[pl.BlockSpec(memory_space=pltpu.SMEM)] + [within] * 5 + [anywhere] * 6,
        out_specs=[anywhere, anywhere, anywhere, within, anywhere],
        scratch_shapes=[
            vm((4, 2, units + 8, rows, width), low),
            vm((units, rows, width), low),
            vm((units, 4, 2, half, width), low),
            vm((units, 4, 2, part, width), low),
            vm((units, 4, 2 * part, width), low),
            vm((units, 4, 2 * part, width), low),
            vm((16, 128), wide),
            vm((16, 128), low),
            vm((8, 16, 128), low),
            vm((8, 8, 128), wide),
            vm((7, 8, 128), wide),
            vm((4, 8, 128), wide),
            vm((2, 2, seq, seq), low),
            vm((seq, width), low),
            vm((3, seq, width), low),
            vm((seq, width), low),
            vm((seq, width), wide),
            vm((seq, width), low),
            vm((seq, hidden), low),
            vm((seq, hidden), low),
            vm((seq, width), low),
            vm((seq, width), wide),
            vm((seq, width), low),
            vm((seq, width), low),
            vm((seq, width), low),
            vm((head_rows, 512), wide),
            vm((128, 512), wide),
            vm((1, width), wide),
            vm((1, width), wide),
            vm((1, width), wide),
            vm((1, width), wide),
            vm((128, 128 * 7), wide),
            vm((seq, seq), low),
            vm((seq, 128), low),
            sems((units, Gather.slots)),
            sems((units, Gather.slots)),
            sems((units, Scatter.slots)),
            sems((units, Scatter.slots)),
            sems((7,)),
            sems((7,)),
            sems((7,)),
            sems((7,)),
            sems((3,)),
            sems((3,)),
            sems((2,)),
            sems((2,)),
            sems((units,)),
            sems((units,)),
        ],
        compiler_params=pltpu.CompilerParams(
            collective_id=0, has_side_effects=True, vmem_limit_bytes=63 * 2**20
        ),
    )(length, x, cot, gain_a, gain_f, table, *square, inner, outer)


def finish_kernel(
    block_in, grad_in, sums, small, block_out, grad_out, query, key, value, output, gain_a, table,
    inner, outer, gain_f, sems,
):
    copies = [
        pltpu.make_async_copy(block_in, block_out, sems.at[0]),
        pltpu.make_async_copy(grad_in, grad_out, sems.at[1]),
    ]
    for copy in copies:
        copy.start()
    rows, width = query.shape
    chunks = inner.shape[1] // width
    for i in range(chunks):
        outer[i * rows : (i + 1) * rows, :] = sums[i].astype(jnp.float32)
        inner[:, i * width : (i + 1) * width] = sums[chunks + i].astype(jnp.float32)
    for n, ref in enumerate((output, query, key, value)):
        ref[...] = sums[2 * chunks + n].astype(jnp.float32)
    gain_a[...] = small[0:1, :rows]
    gain_f[...] = small[1:2, :rows]
    table[...] = small[2 : 2 + table.shape[0], : table.shape[1]]
    for copy in copies:
        copy.wait()


def finish_call(block, grad, sums, small, table_shape, inner_shape, outer_shape):
    rows, width = sums.shape[1:]
    wide = jnp.float32
    anywhere = pl.BlockSpec(memory_space=pl.ANY)
    within = pl.BlockSpec(memory_space=pltpu.VMEM)
    shapes = [(rows, width)] * 4 + [(1, rows), table_shape, inner_shape, outer_shape, (1, rows)]
    return pl.pallas_call(
        finish_kernel,
        out_shape=[
            jax.ShapeDtypeStruct(block.shape, block.dtype),
            jax.ShapeDtypeStruct(grad.shape, grad.dtype),
        ]
        + [jax.ShapeDtypeStruct(shape, wide) for shape in shapes],
        in_specs=[anywhere, anywhere, within, within],
        out_specs=[anywhere, anywhere] + [within] * len(shapes),
        scratch_shapes=[pltpu.SemaphoreType.DMA((2,))],
        compiler_params=pltpu.CompilerParams(vmem_limit_bytes=32 * 2**20),
    )(block, grad, sums, small)


def local_linked(
    inputs, lengths, cotangent, query_weight, key_weight, value_weight, output_weight,
    attention_gain, bias_table, inner_weight, outer_weight, feedforward_gain,
):
    rows = query_weight.shape[0]
    square = (query_weight, key_weight, value_weight, output_weight)
    block, grad, sums, small, _ = fused_call(
        lengths, inputs[0], cotangent[0], attention_gain.reshape(1, rows),
        feedforward_gain.reshape(1, rows), bias_table, square, inner_weight, outer_weight,
    )
    block, grad, query, key, value, output, gain_a, table, inner, outer, gain_f = finish_call(
        block, grad, sums, small, bias_table.shape, inner_weight.shape, outer_weight.shape
    )
    return (
        block[None], grad[None], query, key, value, output, gain_a.reshape(rows), table, inner,
        outer, gain_f.reshape(rows),
    )


def local(inputs, lengths, cotangent, *shards):
    block_output, input_grad, gradients = compute(inputs, lengths, cotangent, gather_all(*shards))
    return (block_output, input_grad) + sum_all(gradients)


def can_link(mesh):
    return mesh.shape["fsdp"] == 8 and mesh.shape["rep"] == 4


def solution(mesh):
    placed = (
        P(("fsdp", "rep"), None, None),
        P(("fsdp", "rep")),
        P(("fsdp", "rep"), None, None),
        P("fsdp", None),
        P("fsdp", None),
        P("fsdp", None),
        P("fsdp", None),
        P("fsdp"),
        P("fsdp", None),
        P("fsdp", None),
        P("fsdp", None),
        P("fsdp"),
    )
    return jax.shard_map(
        local_linked if can_link(mesh) else local,
        mesh=mesh,
        in_specs=placed,
        out_specs=(
            P(("fsdp", "rep"), None, None),
            P(("fsdp", "rep"), None, None),
            P("fsdp", None),
            P("fsdp", None),
            P("fsdp", None),
            P("fsdp", None),
            P("fsdp"),
            P("fsdp", None),
            P("fsdp", None),
            P("fsdp", None),
            P("fsdp"),
        ),
        check_vma=False,
    )
```

```python
import functools

import jax
import jax.numpy as jnp
from jax import lax
import jax.experimental.pallas as pl
import jax.experimental.pallas.tpu as pltpu
from jax.sharding import PartitionSpec as P

NB = 32


epsilon = 1e-06
highest = lax.Precision.HIGHEST
gelu_coeff = 0.7978845608028654
masked_score = -1e30


def bucket_of(offset):
    half_count = NB // 2
    exact_count = half_count // 2
    distance = jnp.abs(offset)
    beyond = jnp.full(offset.shape, exact_count, jnp.int32)
    for exponent in range(1, half_count - exact_count):
        beyond = beyond + (distance * distance >= exact_count * exact_count * 2**exponent).astype(
            jnp.int32
        )
    nearby = jnp.where(distance < exact_count, distance, beyond)
    return jnp.where(offset > 0, half_count, 0).astype(jnp.int32) + nearby


def rms_norm(values, gain_vector):
    inverse_rms = lax.rsqrt(jnp.mean(values * values, axis=-1, keepdims=True) + epsilon)
    return values * inverse_rms * gain_vector


def gelu(values):
    return (
        0.5 * values * (1.0 + jnp.tanh(gelu_coeff * (values + 0.044715 * values * values * values)))
    )


def dot(a,b): return jnp.dot(a,b,preferred_element_type=jnp.float32)
def dot_t(a,b): return lax.dot_general(a,b,(((1,),(1,)),((),())),preferred_element_type=jnp.float32)
def dot_c(a,b): return lax.dot_general(a,b,(((0,),(0,)),((),())),preferred_element_type=jnp.float32)

def fwd_kernel(T, len_ref, q_ref, k_ref, v_ref, rel_ref, o_ref, p_ref, strip):
    hp=pl.program_id(0)
    seq=q_ref.shape[0]; nb=seq//T
    lane=lax.broadcasted_iota(jnp.int32,(1,128),1)
    kcol=lax.broadcasted_iota(jnp.int32,(1,seq),1)
    mask=jnp.where(kcol<len_ref[0],0.0,-1e30)
    k=k_ref[...]; v=v_ref[...]
    for hh in range(2):
        mine=(lane>=64) if hh else (lane<64)
        rel=rel_ref[pl.ds(hh,1),:]
        W=4*T
        rolled=pltpu.roll(jnp.broadcast_to(rel,(T,W)),0,axis=1,stride=1,stride_axis=0)
        strip[:, 2*T:5*T]=rolled[:, :3*T]
        far_neg=rel[:, 0:1]; far_pos=rel[:, 3*T-1:3*T]
        strip[:, 0:2*T]=jnp.broadcast_to(far_neg,(T,2*T))
        strip[:, 5*T:7*T]=jnp.broadcast_to(far_pos,(T,2*T))
        for I in range(nb):
            q=jnp.where(mine,q_ref[I*T:(I+1)*T,:],jnp.bfloat16(0))
            s=dot_t(q,k)+(strip[:, (3-I)*T:(3-I)*T+seq]+mask)
            m=jnp.max(s,axis=-1,keepdims=True)
            e=jnp.exp(s-m)
            tot=jnp.sum(e,axis=-1,keepdims=True)
            p=(e*(1.0/tot)).astype(jnp.bfloat16)
            p_ref[hh,I*T:(I+1)*T,:]=p
            o=dot(p,v)
            if hh==0:
                o_ref[I*T:(I+1)*T,:]=o.astype(jnp.bfloat16)
            else:
                o_ref[I*T:(I+1)*T,:]=jnp.where(mine,o.astype(jnp.bfloat16),o_ref[I*T:(I+1)*T,:])

def bwd_kernel(T, q_ref, k_ref, v_ref, do_ref, p_ref, dq_ref, dk_ref, dv_ref, db_ref, ds_ref):
    seq=q_ref.shape[0]; nb=seq//T
    lane=lax.broadcasted_iota(jnp.int32,(1,128),1)
    k=k_ref[...]; v=v_ref[...]
    dks=[];dvs=[]
    for hh in range(2):
        mine=(lane>=64) if hh else (lane<64)
        acc=[None]*5
        for I in range(nb):
            sl=slice(I*T,(I+1)*T)
            do=jnp.where(mine,do_ref[sl,:],jnp.bfloat16(0))
            dp=dot_t(do,v)
            p=p_ref[hh,sl,:].astype(jnp.float32)
            t=p*dp
            delta=jnp.sum(t,axis=-1,keepdims=True)
            ds=(t-p*delta).astype(jnp.bfloat16)
            ds_ref[sl,:]=ds
            dsf=ds.astype(jnp.float32)
            for J in range(nb):
                d=min(2,max(-2,J-I))+2
                x=dsf[:,J*T:(J+1)*T]
                acc[d]=x if acc[d] is None else acc[d]+x
            dq=dot(ds,k)
            if hh==0: dq_ref[sl,:]=dq.astype(jnp.bfloat16)
            else: dq_ref[sl,:]=jnp.where(mine,dq.astype(jnp.bfloat16),dq_ref[sl,:])
        near=jnp.concatenate([acc[1],acc[2],acc[3],jnp.zeros((T,T),jnp.float32)],axis=1)
        total=shear_sum(near,4*T)
        far=jnp.concatenate([jnp.zeros((1,2*T),jnp.float32),jnp.sum(acc[4],axis=0,keepdims=True),jnp.sum(acc[0],axis=0,keepdims=True)],axis=1)
        db_ref[hh:hh+1,:]=total+far
        dk=dot_c(q_ref[...],ds_ref[...]).T; dv=dot_c(do_ref[...],p_ref[hh]).T
        dks.append(dk); dvs.append(dv)
    dk_ref[...]=jnp.where(lane<64,dks[0],dks[1]).astype(jnp.bfloat16)
    dv_ref[...]=jnp.where(lane<64,dvs[0],dvs[1]).astype(jnp.bfloat16)

def rel_hits(tile):
    slot = jnp.arange(4 * tile, dtype=jnp.int32)
    offset = jnp.where(slot < 3 * tile, slot - tile, slot - 5 * tile)
    bucket_ids = jnp.arange(NB, dtype=jnp.int32)
    return (bucket_of(offset)[None, :] == bucket_ids[:, None]).astype(jnp.bfloat16)


def rel_vec(table, tile):
    return dot_c(table, rel_hits(tile))


def shear_sum(block, width):
    rows = block.shape[0]
    while rows > 8:
        rows //= 2
        block = block[:rows] + pltpu.roll(block[rows:], width - rows, axis=1)
    total = block[0:1]
    for r in range(1, 8):
        total = total + pltpu.roll(block[r : r + 1], width - r, axis=1)
    return total


def att_fwd(q,k,v,rel,length,T=128):
    seq,D=q.shape; H=rel.shape[0]
    blk=pl.BlockSpec((seq,128),lambda h: (0,h))
    return pl.pallas_call(functools.partial(fwd_kernel,T),grid=(H//2,),
        in_specs=[pl.BlockSpec(memory_space=pltpu.SMEM),blk,blk,blk,pl.BlockSpec((None,2,4*T),lambda h:(h,0,0))],
        out_specs=[blk,pl.BlockSpec((2,seq,seq),lambda h:(h,0,0))],
        out_shape=[jax.ShapeDtypeStruct((seq,D),jnp.bfloat16),jax.ShapeDtypeStruct((H,seq,seq),jnp.bfloat16)],
        scratch_shapes=[pltpu.VMEM((T,7*T),jnp.float32)],
        compiler_params=pltpu.CompilerParams(vmem_limit_bytes=40*2**20))(length,q,k,v,rel.reshape(H//2,2,4*T))
def att_bwd(q,k,v,do,p,T=128):
    seq,D=q.shape; H=p.shape[0]
    blk=pl.BlockSpec((seq,128),lambda h: (0,h))
    o=jax.ShapeDtypeStruct((seq,D),jnp.bfloat16)
    outs=pl.pallas_call(functools.partial(bwd_kernel,T),grid=(H//2,),
        in_specs=[blk,blk,blk,blk,pl.BlockSpec((2,seq,seq),lambda h:(h,0,0))],
        out_specs=[blk,blk,blk,pl.BlockSpec((None,2,4*T),lambda h:(h,0,0))],
        out_shape=[o,o,o,jax.ShapeDtypeStruct((H//2,2,4*T),jnp.float32)],
        scratch_shapes=[pltpu.VMEM((seq,seq),jnp.bfloat16)],
        compiler_params=pltpu.CompilerParams(vmem_limit_bytes=40*2**20))(q,k,v,do,p)
    return *outs[:3],outs[3].reshape(H,4*T)

def contract_rows(left, right):
    return lax.dot_general(
        left, right, (((0,), (0,)), ((), ())), preferred_element_type=jnp.float32
    )


def contract_cols(left, right):
    return lax.dot_general(
        left, right, (((1,), (1,)), ((), ())), preferred_element_type=jnp.float32
    )


MESH = pl.DeviceIdType.MESH


def coords():
    shard = lax.axis_index("fsdp")
    copy = lax.axis_index("rep")
    return shard // 2, shard % 2, copy // 2, copy % 2


def greet():
    barrier = pltpu.get_barrier_semaphore()
    shard = lax.axis_index("fsdp")
    copy = lax.axis_index("rep")
    for k in range(1, 8):
        peer = (lax.rem(shard + k, 8), copy)
        pl.semaphore_signal(barrier, inc=1, device_id=peer, device_id_type=MESH)
    for k in range(1, 4):
        peer = (shard, lax.rem(copy + k, 4))
        pl.semaphore_signal(barrier, inc=1, device_id=peer, device_id_type=MESH)
    pl.semaphore_wait(barrier, 10)


def stepper(stages, count):
    def step(t):
        for stage, lag in stages:
            g = t - lag
            if isinstance(g, int):
                if 0 <= g < count:
                    stage(g)
            else:
                pl.when((g >= 0) & (g < count))(functools.partial(stage, g))

    return step


class Links:
    def __init__(self, rows, send_sems, recv_sems):
        self.send_sems, self.recv_sems = send_sems, recv_sems
        self.z, self.x, self.y, self.c = coords()
        half = rows // 2
        part = half // 3
        at = lambda start, size: pl.ds(pl.multiple_of(start, part), size)
        first = half * self.c
        other = half * (1 - self.c)
        self.half, self.other_half = at(first, half), at(other, half)
        self.plane = at(first + part * self.y, 2 * part)
        self.shared = at(first + part, part)
        self.own_third = at(first + 2 * part * self.y, part)
        self.other_third = at(first + 2 * part * (1 - self.y), part)
        self.shared_in = at(part * self.y, part)
        self.third_in = at(part * (1 - self.y), part)

    def copy(self, src, dst, g, slot, device):
        return pltpu.make_async_remote_copy(
            src_ref=src,
            dst_ref=dst,
            send_sem=self.send_sems.at[g, slot],
            recv_sem=self.recv_sems.at[g, slot],
            device_id=device,
            device_id_type=MESH,
        )

    def to_x(self):
        return (self.z * 2 + 1 - self.x, self.y * 2 + self.c)

    def to_y(self):
        return (self.z * 2 + self.x, (1 - self.y) * 2 + self.c)

    def to_core(self):
        return (self.z * 2 + self.x, self.y * 2 + 1 - self.c)

    def to_z(self, k):
        return (lax.rem(self.z + k, 4) * 2 + self.x, self.y * 2 + self.c)

    def z_before(self, k):
        return lax.rem(self.z + 4 - k, 4)


class Gather(Links):
    slots = 20

    def __init__(self, full, send_sems, recv_sems):
        super().__init__(full.shape[3], send_sems, recv_sems)
        self.full = full
        self.beside = self.z + 1 - 2 * lax.rem(self.z, 2)
        self.second = lax.rem(self.z + 2, 4)
        self.across = 3 - self.z
        self.at_end = (self.z == 0) | (self.z == 3)

    def block(self, g, a, rows):
        return self.full.at[a, self.x, g, rows]

    def column(self, g, rows):
        return self.full.at[:, 1 - self.x, g, rows]

    def move(self, part, g, send_slot, recv_slot, device):
        return pltpu.make_async_remote_copy(
            src_ref=part,
            dst_ref=part,
            send_sem=self.send_sems.at[g, send_slot],
            recv_sem=self.recv_sems.at[g, recv_slot],
            device_id=device,
            device_id_type=MESH,
        )

    def at_z(self, a):
        return (a * 2 + self.x, self.y * 2 + self.c)

    def z_copy(self, g, to):
        return self.move(self.block(g, self.z, self.plane), g, to, self.z, self.at_z(to))

    def pass_copy(self, g):
        return self.move(
            self.block(g, self.second, self.plane), g, self.z, self.second, self.at_z(self.beside)
        )

    def x_copy(self, g, a):
        return self.move(self.block(g, a, self.plane), g, 4 + a, 4 + a, self.to_x())

    def y_copy(self, g, a):
        return self.move(self.block(g, a, self.own_third), g, 8 + a, 8 + a, self.to_y())

    def y_column_copy(self, g):
        return self.move(self.column(g, self.own_third), g, 12, 12, self.to_y())

    def core_copy(self, g, a):
        return self.move(self.block(g, a, self.half), g, 13 + a, 13 + a, self.to_core())

    def core_column_copy(self, g):
        return self.move(self.column(g, self.half), g, 17, 17, self.to_core())

    def arrived(self, part, g, slot):
        self.move(part, g, slot, slot, self.to_x()).wait_recv()

    def others(self):
        return (self.beside, self.second, self.across)

    def start(self, g):
        self.z_copy(g, self.second).start()
        self.z_copy(g, self.beside).start()
        pl.when(~self.at_end)(lambda: self.z_copy(g, self.across).start())
        self.x_copy(g, self.z).start()

    def spread(self, g, a):
        self.arrived(self.block(g, a, self.plane), g, a)
        self.x_copy(g, a).start()
        self.y_copy(g, a).start()

    def after_z(self, g):
        self.arrived(self.block(g, self.second, self.plane), g, self.second)
        pl.when(~self.at_end)(lambda: self.pass_copy(g).start())
        self.x_copy(g, self.second).start()
        self.y_copy(g, self.second).start()
        self.spread(g, self.beside)
        pl.when(~self.at_end)(lambda: self.spread(g, self.across))

    def after_pass(self, g):
        pl.when(self.at_end)(lambda: self.spread(g, self.across))

    def after_x(self, g):
        for a in range(4):
            self.arrived(self.full.at[a, 1 - self.x, g, self.plane], g, 4 + a)
        self.y_column_copy(g).start()

    def after_y(self, g):
        for a in self.others():
            self.arrived(self.block(g, a, self.other_third), g, 8 + a)
            self.core_copy(g, a).start()
        self.arrived(self.column(g, self.other_third), g, 12)
        self.core_column_copy(g).start()

    def after_core(self, g):
        for a in self.others():
            self.arrived(self.block(g, a, self.other_half), g, 13 + a)
        self.arrived(self.column(g, self.other_half), g, 17)

    def drain(self, g):
        self.z_copy(g, self.second).wait_send()
        self.z_copy(g, self.beside).wait_send()
        pl.when(~self.at_end)(lambda: self.z_copy(g, self.across).wait_send())
        pl.when(~self.at_end)(lambda: self.pass_copy(g).wait_send())
        for a in range(4):
            self.x_copy(g, a).wait_send()
        for a in self.others():
            self.y_copy(g, a).wait_send()
            self.core_copy(g, a).wait_send()
        self.y_column_copy(g).wait_send()
        self.core_column_copy(g).wait_send()


class Scatter(Links):
    slots = 8

    def __init__(self, slot, full, own, from_core, from_y, from_x, from_z, send_sems, recv_sems):
        super().__init__(own.shape[1], send_sems, recv_sems)
        self.slot, self.full, self.own = slot, full, own
        self.from_core, self.from_y, self.from_x, self.from_z = from_core, from_y, from_x, from_z

    def core_copy(self, g):
        part = self.full.at[:, :, self.slot(g), self.other_half]
        ring = lax.rem(g, self.from_core.shape[0])
        return self.copy(part, self.from_core.at[ring], g, 0, self.to_core())

    def y_copy(self, g):
        part = self.full.at[:, :, self.slot(g), self.other_third]
        return self.copy(part, self.from_y.at[g], g, 1, self.to_y())

    def x_copy(self, g):
        part = self.full.at[:, 1 - self.x, self.slot(g), self.plane]
        return self.copy(part, self.from_x.at[g], g, 2, self.to_x())

    def z_copy(self, g, k):
        part = self.full.at[lax.rem(self.z + k, 4), self.x, self.slot(g), self.plane]
        return self.copy(part, self.from_z.at[g, k - 1], g, 2 + k, self.to_z(k))

    def back_y_copy(self, g):
        part = self.own.at[g, self.plane]
        return self.copy(part, self.from_z.at[g, 3], g, 6, self.to_y())

    def back_core_copy(self, g):
        part = self.own.at[g, self.half]
        return self.copy(part, part, g, 7, self.to_core())

    def start(self, g):
        self.core_copy(g).start()

    def after_core(self, g):
        self.core_copy(g).wait_recv()
        ring = lax.rem(g, self.from_core.shape[0])
        for a in range(4):
            for b in range(2):
                self.full[a, b, self.slot(g), self.half] += self.from_core[ring, a, b]
        self.y_copy(g).start()

    def after_y(self, g):
        self.y_copy(g).wait_recv()
        for a in range(4):
            for b in range(2):
                self.full[a, b, self.slot(g), self.own_third] += self.from_y[g, a, b]
        self.x_copy(g).start()

    def after_x(self, g):
        self.x_copy(g).wait_recv()
        for a in range(4):
            self.full[a, self.x, self.slot(g), self.plane] += self.from_x[g, a]
        for k in (1, 2, 3):
            self.z_copy(g, k).start()

    def after_z(self, g):
        total = self.full[self.z, self.x, self.slot(g), self.plane].astype(jnp.float32)
        for k in (1, 2, 3):
            self.z_copy(g, k).wait_recv()
            total = total + self.from_z[g, k - 1].astype(jnp.float32)
        self.own[g, self.plane] = total.astype(jnp.bfloat16)
        self.back_y_copy(g).start()

    def after_back_y(self, g):
        self.back_y_copy(g).wait_recv()
        self.back_y_copy(g).wait_send()
        got = self.from_z.at[g, 3]
        self.own[g, self.shared] += got[self.shared_in]
        self.own[g, self.other_third] = got[self.third_in]
        self.back_core_copy(g).start()

    def after_back_core(self, g):
        part = self.own.at[g, self.other_half]
        self.copy(part, part, g, 7, self.to_core()).wait_recv()

    def drain(self, g):
        self.core_copy(g).wait_send()
        self.y_copy(g).wait_send()
        self.x_copy(g).wait_send()
        for k in (1, 2, 3):
            self.z_copy(g, k).wait_send()
        self.back_core_copy(g).wait_send()


def compute(inputs, lengths, cotangent, weights):
    (
        full_query, full_key, full_value, full_output, full_gain, full_table, full_inner,
        full_outer, full_ffn_gain,
    ) = weights
    pairs_here, seq_len, model_width = inputs.shape
    row_count = pairs_here * seq_len
    head_count = full_table.shape[1]
    tile = 128
    relative = rel_vec(full_table, tile)
    flat_inputs = inputs.reshape(row_count, model_width).astype(jnp.float32)
    normed = rms_norm(flat_inputs, full_gain.astype(jnp.float32)).astype(jnp.bfloat16)
    joined = jnp.concatenate((full_query, full_key, full_value), axis=1)
    projected = jnp.dot(normed, joined, preferred_element_type=jnp.float32).astype(jnp.bfloat16)
    queries = projected[:, :model_width]
    key_rows = projected[:, model_width : 2 * model_width]
    value_rows = projected[:, 2 * model_width :]
    pair_rows = [slice(n * seq_len, (n + 1) * seq_len) for n in range(pairs_here)]
    forward_parts = [
        att_fwd(queries[r], key_rows[r], value_rows[r], relative, lengths[n : n + 1], tile)
        for n, r in enumerate(pair_rows)
    ]
    attended = jnp.concatenate([part[0] for part in forward_parts], axis=0)
    middle = flat_inputs + jnp.dot(attended, full_output, preferred_element_type=jnp.float32)
    normed_ffn = rms_norm(middle, full_ffn_gain.astype(jnp.float32)).astype(jnp.bfloat16)
    raised = jnp.dot(normed_ffn, full_inner, preferred_element_type=jnp.float32)
    active = gelu(raised).astype(jnp.bfloat16)
    lowered = jnp.dot(active, full_outer, preferred_element_type=jnp.float32)
    block_output = (middle + lowered).astype(jnp.bfloat16).reshape(pairs_here, seq_len, model_width)
    positions = jnp.arange(seq_len, dtype=jnp.int32)
    row_live = (positions[None, :] < lengths[:, None]).astype(jnp.float32)
    seed_rows = (cotangent.astype(jnp.float32) * row_live[:, :, None]).reshape(
        row_count, model_width
    )
    seed_low = seed_rows.astype(jnp.bfloat16)
    grad_active = contract_cols(seed_low, full_outer)
    grad_outer = contract_rows(active, seed_low)
    grad_raised = jax.vjp(gelu, raised)[1](grad_active)[0].astype(jnp.bfloat16)
    grad_inner = contract_rows(normed_ffn, grad_raised)
    grad_normed_ffn = contract_cols(grad_raised, full_inner)
    ffn_pull = jax.vjp(rms_norm, middle, full_ffn_gain.astype(jnp.float32))[1]
    grad_middle_part, grad_ffn_gain = ffn_pull(grad_normed_ffn)
    grad_middle = seed_rows + grad_middle_part
    joined = jnp.concatenate((full_query, full_key, full_value), axis=1)
    middle_low = grad_middle.astype(jnp.bfloat16)
    grad_attended = contract_cols(middle_low, full_output).astype(jnp.bfloat16)
    grad_output = contract_rows(attended, middle_low)
    backward_parts = [
        att_bwd(
            queries[r], key_rows[r], value_rows[r], grad_attended[r], forward_parts[n][1], tile
        )
        for n, r in enumerate(pair_rows)
    ]
    grad_projected = jnp.concatenate(
        [jnp.concatenate(part[:3], axis=1) for part in backward_parts], axis=0
    )
    grad_joined = contract_rows(normed, grad_projected)
    grad_normed = contract_cols(grad_projected, joined)
    attention_pull = jax.vjp(rms_norm, flat_inputs, full_gain.astype(jnp.float32))[1]
    grad_inputs_part, grad_attention_gain = attention_pull(grad_normed)
    input_grad = (grad_middle + grad_inputs_part).reshape(pairs_here, seq_len, model_width)
    grad_relative = sum(part[3] for part in backward_parts)
    grad_table = lax.dot_general(
        rel_hits(tile).astype(jnp.float32),
        grad_relative,
        (((1,), (1,)), ((), ())),
        precision=highest,
    )
    return block_output, input_grad, (
        grad_joined[:, :model_width],
        grad_joined[:, model_width : 2 * model_width],
        grad_joined[:, 2 * model_width :],
        grad_output,
        grad_attention_gain,
        grad_table,
        grad_inner,
        grad_outer,
        grad_ffn_gain,
    )


def gather_all(query_weight, key_weight, value_weight, output_weight, attention_gain, bias_table,
               inner_weight, outer_weight, feedforward_gain):
    return tuple(
        lax.all_gather(part, "fsdp", axis=0, tiled=True)
        for part in (
            query_weight, key_weight, value_weight, output_weight, attention_gain, bias_table,
            inner_weight, outer_weight, feedforward_gain,
        )
    )


def sum_all(gradients):
    def one(part):
        part = lax.psum_scatter(
            part.astype(jnp.bfloat16), "fsdp", scatter_dimension=0, tiled=True
        )
        return lax.psum(part, "rep").astype(jnp.float32)

    return tuple(one(part) for part in gradients)


def gelu_parts(z):
    square = z * z
    t = jnp.tanh(gelu_coeff * z * (1.0 + 0.044715 * square))
    half = 0.5 * (1.0 + t)
    slope = half + (0.5 * gelu_coeff) * z * (1.0 - t * t) * (1.0 + (3 * 0.044715) * square)
    return z * half, slope


def lanes(start, size):
    return pl.ds(pl.multiple_of(start, 128), size)


def rows_at(start, size):
    return pl.ds(pl.multiple_of(start, size), size)


def loop(count, body):
    def step(n, carry):
        body(n)
        return carry

    lax.fori_loop(0, count, step, 0)


def norm_back(grad, gain, values):
    inverse = lax.rsqrt(jnp.mean(values * values, axis=-1, keepdims=True) + epsilon)
    scaled = grad * gain
    centre = jnp.mean(scaled * values, axis=-1, keepdims=True)
    back = inverse * scaled - values * (inverse * inverse * inverse * centre)
    return back, jnp.sum(grad * values * inverse, axis=0, keepdims=True)


class Layer:
    def __init__(self, **refs):
        self.__dict__.update(refs)
        self.seq, self.width = self.x.shape
        self.tile = 128
        self.row_block = 128
        self.shard_rows = self.bank.shape[3]

    def unit(self, u, column=None, size=None):
        if column is None:
            block = self.bank[:, :, u]
        else:
            block = self.bank[:, :, u, :, lanes(column, size)]
        return block.reshape(-1, block.shape[-1])

    def row_chunks(self, body):
        size = self.row_block
        loop(self.seq // size, lambda n: body(rows_at(n * size, size)))

    def small_arrays(self):
        flat = self.all_small[...].reshape(-1, 128)
        tile = self.tile
        slot = lax.broadcasted_iota(jnp.int32, (flat.shape[0], 4 * tile), 1)
        offset = jnp.where(slot < 3 * tile, slot - tile, slot - 5 * tile)
        row = lax.broadcasted_iota(jnp.int32, (flat.shape[0], 4 * tile), 0)
        per = NB // 8
        inside = row % 16 - 2
        wanted = jnp.where((inside >= 0) & (inside < per), (row // 16) * per + inside, -1)
        hits = (bucket_of(offset) == wanted).astype(jnp.bfloat16)
        self.rel[...] = dot_c(flat, hits)[: self.rel.shape[0]]
        for index, ref in ((0, self.gain_a), (1, self.gain_f)):
            total = jnp.zeros((1, self.width), jnp.float32)
            for shard in range(8):
                part = self.all_small[shard].astype(jnp.float32)[index : index + 1]
                wide = jnp.concatenate(
                    [part, jnp.zeros((1, self.width - 128), jnp.float32)], axis=1
                )
                total = total + (
                    pltpu.roll(wide, shard * self.shard_rows, axis=1) if shard else wide
                )
            ref[...] = total

    def norm_in(self):
        gain = self.gain_a[...]

        def body(r):
            self.normed[r] = rms_norm(self.x[r].astype(jnp.float32), gain).astype(jnp.bfloat16)

        self.row_chunks(body)

    def mask_seed(self):
        def body(r):
            index = lax.broadcasted_iota(jnp.int32, (self.row_block, 1), 0) + r.start
            live = index < self.length[0]
            self.seed[r] = jnp.where(live, self.seed[r], jnp.bfloat16(0))

        self.row_chunks(body)

    def project(self, u):
        def body(n):
            self.qkv[u, :, lanes(n * 256, 256)] = dot(
                self.normed[...], self.unit(u, n * 256, 256)
            ).astype(jnp.bfloat16)

        loop(self.width // 256, body)

    def strip_for(self, head, strip):
        tile = self.tile
        rel = self.rel[pl.ds(head, 1), :]
        rolled = pltpu.roll(
            jnp.broadcast_to(rel, (tile, 4 * tile)), 0, axis=1, stride=1, stride_axis=0
        )
        strip[:, 2 * tile : 5 * tile] = rolled[:, : 3 * tile]
        strip[:, : 2 * tile] = jnp.broadcast_to(rel[:, :1], (tile, 2 * tile))
        strip[:, 5 * tile :] = jnp.broadcast_to(rel[:, 3 * tile - 1 : 3 * tile], (tile, 2 * tile))

    def pair_lanes(self, pair):
        third = self.width // 3
        first = lax.rem(pair, 2) * 128
        return pair // 2, [lanes(first + n * third, 128) for n in range(3)]

    def probs_store(self, pair, slot):
        return pltpu.make_async_copy(
            self.probs.at[slot], self.probs_far.at[pair], self.probs_sems.at[slot]
        )

    def probs_load(self, pair, slot):
        return pltpu.make_async_copy(
            self.probs_far.at[pair], self.probs.at[slot], self.probs_sems.at[slot]
        )

    def attend(self, pair):
        tile, seq = self.tile, self.seq
        slot = lax.rem(pair, 2)
        pl.when(pair >= 2)(lambda: self.probs_store(pair, slot).wait())
        lane = lax.broadcasted_iota(jnp.int32, (1, 128), 1)
        own = (lane < 64, lane >= 64)
        key_at = lax.broadcasted_iota(jnp.int32, (1, seq), 1)
        mask = jnp.where(key_at < self.length[0], 0.0, masked_score)
        unit, (q_at, k_at, v_at) = self.pair_lanes(pair)
        q = self.qkv[unit, :, q_at]
        k = self.qkv[unit, :, k_at]
        v = self.qkv[unit, :, v_at]
        for head in range(2):
            self.strip_for(pair * 2 + head, self.strip.at[head])
            self.scores[head] = dot_t(jnp.where(own[head], q, jnp.bfloat16(0)), k)

        def soften(head):
            for block in range(seq // tile):
                r = slice(block * tile, (block + 1) * tile)
                first = (seq // tile - 1 - block) * tile
                bias = self.strip[head, :, first : first + seq]
                scores = self.scores[head, r, :] + (bias + mask)
                peak = jnp.max(scores, axis=-1, keepdims=True)
                raised = jnp.exp(scores - peak)
                total = jnp.sum(raised, axis=-1, keepdims=True)
                self.probs[slot, head, r, :] = (raised * (1.0 / total)).astype(jnp.bfloat16)
            return dot(self.probs[slot, head], v)

        outs = [soften(head) for head in range(2)]
        self.attended[:, lanes(pair * 128, 128)] = jnp.where(own[0], *outs).astype(jnp.bfloat16)
        self.probs_store(pair, slot).start()

    def middle_rows(self):
        def body(n):
            c = lanes(n * 256, 256)
            self.middle[:, c] = self.x[:, c].astype(jnp.float32) + dot(
                self.attended[...], self.unit(3, n * 256, 256)
            )

        loop(self.width // 256, body)
        gain = self.gain_f[...]

        def norm(r):
            self.normed_ffn[r] = rms_norm(self.middle[r], gain).astype(jnp.bfloat16)

        self.row_chunks(norm)

    def raise_unit(self, i):
        def body(n):
            raised = dot(self.normed_ffn[...], self.unit(4 + i, n * 256, 256))
            active, slope = gelu_parts(raised)
            c = lanes(i * self.width + n * 256, 256)
            self.active[:, c] = active.astype(jnp.bfloat16)
            self.slope[:, c] = slope.astype(jnp.bfloat16)

        loop(self.width // 256, body)

    def outer_grad(self, shard):
        size = 4 * self.shard_rows
        block = dot_c(self.active[:, lanes(shard * size, size)], self.seed[...])
        self.bank[shard // 2, shard % 2, 12:16] = block.astype(jnp.bfloat16).reshape(
            4, self.shard_rows, self.width
        )

    def lower(self):
        def body(n):
            outer = self.bank[:, :, 8:12, :, lanes(n * 256, 256)].reshape(-1, 256)
            c = lanes(n * 256, 256)
            self.mid_low[:, c] = (self.middle[:, c] + dot(self.active[...], outer)).astype(
                jnp.bfloat16
            )

        loop(self.width // 256, body)

    def raised_grad(self, shard):
        size = 4 * self.shard_rows
        outer = self.bank[shard // 2, shard % 2, 8:12].reshape(size, self.width)
        c = lanes(shard * size, size)
        grad = dot_t(self.seed[...], outer) * self.slope[:, c].astype(jnp.float32)
        self.slope[:, c] = grad.astype(jnp.bfloat16)

    def inner_grad(self, i):
        def body(n):
            c = lanes(i * self.width + n * 256, 256)
            block = dot_c(self.normed_ffn[...], self.slope[:, c]).astype(jnp.bfloat16)
            self.bank[:, :, 16 + i, :, lanes(n * 256, 256)] = block.reshape(
                4, 2, self.shard_rows, 256
            )

        loop(self.width // 256, body)

    def middle_grad(self):
        for part in range(2):
            total = None
            for i in range(4):
                inner = self.bank[2 * part : 2 * part + 2, :, 4 + i]
                inner = inner.reshape(-1, self.width)
                term = dot_t(self.slope[:, i * self.width : (i + 1) * self.width], inner)
                total = term if total is None else total + term
            size = self.width // 2
            self.grad_mid[:, part * size : (part + 1) * size] = total
        gain = self.gain_f[...]
        self.gain_f_grad[...] = jnp.zeros_like(self.gain_f_grad)

        def body(r):
            back, terms = norm_back(self.grad_mid[r], gain, self.middle[r])
            total = self.seed[r].astype(jnp.float32) + back
            self.gain_f_grad[...] += terms
            self.grad_mid[r] = total
            self.mid_low[r] = total.astype(jnp.bfloat16)

        self.row_chunks(body)

    def square_grad(self, left, right, slot):
        def body(n):
            block = dot_c(left[...], right(lanes(n * 256, 256))).astype(jnp.bfloat16)
            self.bank[:, :, slot, :, lanes(n * 256, 256)] = block.reshape(
                4, 2, self.shard_rows, 256
            )

        loop(self.width // 256, body)

    def attended_grad(self):
        size = self.width // 2
        for part in range(2):
            weight = self.bank[2 * part : 2 * part + 2, :, 3].reshape(size, self.width)
            self.attended[:, part * size : (part + 1) * size] = dot_t(
                self.mid_low[...], weight
            ).astype(jnp.bfloat16)

    def attend_back(self, pair):
        tile, seq = self.tile, self.seq
        slot = lax.rem(pair, 2)
        self.probs_load(pair, slot).wait()
        lane = lax.broadcasted_iota(jnp.int32, (1, 128), 1)
        own = (lane < 64, lane >= 64)
        unit, (q_at, k_at, v_at) = self.pair_lanes(pair)
        q = self.qkv[unit, :, q_at]
        k = self.qkv[unit, :, k_at]
        v = self.qkv[unit, :, v_at]
        grad_out = self.attended[:, lanes(pair * 128, 128)]
        blocks = seq // tile
        for head in range(2):
            self.scores[head] = dot_t(jnp.where(own[head], grad_out, jnp.bfloat16(0)), v)

        def back(head):
            sums = [None] * 5
            for block in range(blocks):
                r = slice(block * tile, (block + 1) * tile)
                probs = self.probs[slot, head, r, :].astype(jnp.float32)
                weighted = probs * self.scores[head, r, :]
                centre = jnp.sum(weighted, axis=-1, keepdims=True)
                grad = weighted - probs * centre
                self.grad_scores[head, r, :] = grad.astype(jnp.bfloat16)
                for other in range(blocks):
                    apart = min(2, max(-2, other - block)) + 2
                    part = grad[:, other * tile : (other + 1) * tile]
                    sums[apart] = part if sums[apart] is None else sums[apart] + part
            zero = jnp.zeros((tile, tile), jnp.float32)
            near = shear_sum(jnp.concatenate([sums[1], sums[2], sums[3], zero], axis=1), 4 * tile)
            far = jnp.concatenate(
                [
                    jnp.zeros((1, 2 * tile), jnp.float32),
                    jnp.sum(sums[4], axis=0, keepdims=True),
                    jnp.sum(sums[0], axis=0, keepdims=True),
                ],
                axis=1,
            )
            self.rel_grad[pl.ds(pair * 2 + head, 1), :] = near + far
            return (
                dot(self.grad_scores[head], k),
                dot_c(q, self.grad_scores[head]).T,
                dot_c(grad_out, self.probs[slot, head]).T,
            )

        for at, first, second in zip((q_at, k_at, v_at), back(0), back(1)):
            self.qkv[unit, :, at] = jnp.where(own[0], first, second).astype(jnp.bfloat16)
        pl.when(pair + 2 < self.probs_far.shape[0])(
            lambda: self.probs_load(pair + 2, slot).start()
        )

    def input_grad(self):
        size = self.width // 2
        for part in range(2):
            total = None
            for u in range(3):
                weight = self.bank[2 * part : 2 * part + 2, :, u].reshape(size, self.width)
                term = dot_t(self.qkv[u], weight)
                total = term if total is None else total + term
            self.middle[:, part * size : (part + 1) * size] = total
        gain = self.gain_a[...]
        self.gain_a_grad[...] = jnp.zeros_like(self.gain_a_grad)

        def body(r):
            back, terms = norm_back(self.middle[r], gain, self.x[r].astype(jnp.float32))
            self.gain_a_grad[...] += terms
            self.grad_mid[r] += back

        self.row_chunks(body)

    def small_grads(self):
        tile = self.tile
        shape = (64, 4 * tile)
        slot = lax.broadcasted_iota(jnp.int32, shape, 1)
        offset = jnp.where(slot < 3 * tile, slot - tile, slot - 5 * tile)
        row = lax.broadcasted_iota(jnp.int32, shape, 0)
        per = NB // 8
        inside = row % 8 - 2
        wanted = jnp.where((inside >= 0) & (inside < per), (row // 8) * per + inside, -1)
        hits = (bucket_of(offset) == wanted).astype(jnp.float32)
        table = lax.dot_general(
            hits,
            self.rel_grad[...],
            (((1,), (1,)), ((), ())),
            precision=highest,
            preferred_element_type=jnp.float32,
        )
        rows = lax.broadcasted_iota(jnp.int32, (8, 128), 0)
        lane = lax.broadcasted_iota(jnp.int32, (8, 128), 1)
        for shard in range(8):
            block = table[8 * shard : 8 * shard + 8]
            for index, ref in ((0, self.gain_a_grad), (1, self.gain_f_grad)):
                wide = ref[...]
                if shard:
                    wide = pltpu.roll(wide, self.width - shard * self.shard_rows, axis=1)
                here = (rows == index) & (lane < self.shard_rows)
                block = jnp.where(here, jnp.broadcast_to(wide[:, :128], (8, 128)), block)
            self.small_out[shard] = block


def order_slot(n):
    return jnp.where(n < 8, n + 12, jnp.where(n == 8, 7, n - 5))


def fused_kernel(
    length, x, cot, gain_a_own, gain_f_own, table_own, query_own, key_own, value_own, output_own,
    inner_own, outer_own,
    block_far, grad_far, own_far, small_result, probs_far,
    bank, own_sum, from_core, from_y, from_x, from_z, small_wide, small, all_small, small_out,
    small_in, small_rep, probs, normed, qkv, attended, middle, normed_ffn, active, slope, seed,
    grad_mid, mid_low, scores, rel, rel_grad, gain_a, gain_f, gain_a_grad,
    gain_f_grad, strip, grad_scores,
    sends, recvs, sum_sends, sum_recvs, small_sends, small_recvs, back_sends, back_recvs,
    rep_sends, rep_recvs, probs_sems, misc_sems, store_sems, keep_sems,
):
    shard = lax.axis_index("fsdp")
    copy_id = lax.axis_index("rep")
    layer = Layer(
        length=length, x=x, bank=bank, all_small=all_small, small_out=small_out,
        probs=probs, probs_far=probs_far, probs_sems=probs_sems, normed=normed, qkv=qkv,
        attended=attended, middle=middle, normed_ffn=normed_ffn, active=active, slope=slope,
        seed=seed, grad_mid=grad_mid, mid_low=mid_low, scores=scores,
        rel=rel, rel_grad=rel_grad, gain_a=gain_a, gain_f=gain_f, gain_a_grad=gain_a_grad,
        gain_f_grad=gain_f_grad, strip=strip, grad_scores=grad_scores,
    )
    rows, width = query_own.shape
    chunks = inner_own.shape[1] // width
    units = 4 + 2 * chunks
    gather = Gather(bank, sends, recvs)
    scatter = Scatter(
        order_slot, bank, own_sum, from_core, from_y, from_x, from_z, sum_sends, sum_recvs
    )
    pairs = probs_far.shape[0]

    def remote(src, dst, send, recv, device):
        return pltpu.make_async_remote_copy(
            src_ref=src, dst_ref=dst, send_sem=send, recv_sem=recv, device_id=device,
            device_id_type=MESH,
        )

    def peer(k):
        return (lax.rem(shard + k, 8), copy_id)

    def rep_peer(k):
        return (shard, lax.rem(copy_id + k, 4))

    parts = [output_own]
    parts += [inner_own.at[:, pl.ds(i * width, width)] for i in range(chunks)]
    parts += [outer_own.at[pl.ds(i * rows, rows)] for i in range(chunks)]
    third = width // 3
    homes = [
        (part.at[:, pl.ds(u * third, third)], bank.at[gather.z, gather.x, u, :, pl.ds(n * third, third)])
        for u in range(3)
        for n, part in enumerate((query_own, key_own, value_own))
    ]
    homes += [(part, bank.at[gather.z, gather.x, 3 + u]) for u, part in enumerate(parts)]
    keeps = [
        pltpu.make_async_copy(part, home, keep_sems.at[u]) for u, (part, home) in enumerate(homes)
    ]
    keeps.append(pltpu.make_async_copy(cot, seed, misc_sems.at[0]))
    for copy in keeps:
        copy.start()
    small_wide[...] = jnp.zeros_like(small_wide)
    small_wide[0:1, :rows] = gain_a_own[...].astype(jnp.float32)
    small_wide[1:2, :rows] = gain_f_own[...].astype(jnp.float32)
    per, heads = table_own.shape
    small_wide[2 : 2 + per, :heads] = table_own[...].astype(jnp.float32)
    small[...] = small_wide[...].astype(jnp.bfloat16)
    all_small[shard] = small[...]
    for copy in keeps:
        copy.wait()
    greet()
    small_copies = [
        remote(small, all_small.at[shard], small_sends.at[k - 1], small_recvs.at[k - 1], peer(k))
        for k in range(1, 8)
    ]
    for copy in small_copies:
        copy.start()
    gather_step = stepper(
        (
            (gather.after_y, 7), (gather.after_x, 5), (gather.after_pass, 3), (gather.after_z, 2),
            (gather.start, 0), (gather.after_core, 8),
        ),
        units,
    )
    loop(2, gather_step)
    layer.mask_seed()
    for copy in small_copies:
        copy.wait()
    layer.small_arrays()
    layer.norm_in()
    loop(6, lambda n: gather_step(n + 2))

    def heads(u):
        gather_step(u + 8)
        layer.project(u)
        layer.attend(2 * u)
        layer.attend(2 * u + 1)

    loop(3, heads)
    gather_step(11)
    layer.middle_rows()

    def raises(i):
        gather_step(i + 12)
        layer.raise_unit(i)

    loop(4, raises)
    for pair in (pairs - 2, pairs - 1):
        layer.probs_store(pair, pair % 2).wait()
    for pair in (0, 1):
        layer.probs_load(pair, pair).start()

    def outers(i):
        gather_step(i + 16)
        layer.outer_grad(4 * i)
        layer.outer_grad(4 * i + 1)
        layer.outer_grad(4 * i + 2)
        layer.outer_grad(4 * i + 3)

    loop(2, outers)

    def store(n):
        return pltpu.make_async_copy(own_sum.at[n], own_far.at[n], store_sems.at[n])

    def last(n):
        scatter.after_back_core(n)
        store(n).start()

    sum_step = stepper(
        (
            (last, 9), (scatter.after_back_y, 8), (scatter.after_z, 7), (scatter.after_x, 5),
            (scatter.after_y, 3), (scatter.after_core, 1), (scatter.start, 0),
        ),
        units,
    )
    sum_step(0)
    gather_step(18)
    sum_step(1)
    gather_step(19)
    layer.lower()
    block_store = pltpu.make_async_copy(mid_low, block_far, misc_sems.at[0])
    block_store.start()
    loop(8, layer.raised_grad)
    sum_step(2)

    def inners(i):
        layer.inner_grad(2 * i)
        layer.inner_grad(2 * i + 1)
        sum_step(i + 3)
        gather.drain(4 + 2 * i)
        gather.drain(5 + 2 * i)

    loop(2, inners)
    block_store.wait()
    layer.middle_grad()
    layer.square_grad(attended, lambda c: mid_low[:, c], 7)
    layer.attended_grad()
    rel_grad[...] = jnp.zeros_like(rel_grad)

    def heads_back(u):
        sum_step(u + 5)
        layer.attend_back(2 * u)
        layer.attend_back(2 * u + 1)
        layer.square_grad(normed, lambda c: qkv[u, :, c], 4 + u)

    loop(3, heads_back)
    loop(4, lambda n: sum_step(n + 8))
    layer.input_grad()
    grad_store = pltpu.make_async_copy(grad_mid, grad_far, misc_sems.at[1])
    grad_store.start()
    layer.small_grads()
    back_copies = [
        remote(
            small_out.at[lax.rem(shard + k, 8)], small_in.at[k - 1], back_sends.at[k - 1],
            back_recvs.at[k - 1], peer(k),
        )
        for k in range(1, 8)
    ]
    for copy in back_copies:
        copy.start()
    loop(4, gather.drain)
    loop(units - 8, lambda n: gather.drain(n + 8))

    def late(n):
        sum_step(n + 12)

    loop(5, late)
    total = small_out[shard]
    for k, copy in enumerate(back_copies):
        copy.wait_recv()
        total = total + small_in[k]
    small_rep[copy_id] = total
    rep_copies = [
        remote(
            small_rep.at[copy_id], small_rep.at[copy_id], rep_sends.at[k - 1],
            rep_recvs.at[k - 1], rep_peer(k),
        )
        for k in range(1, 4)
    ]
    for copy in rep_copies:
        copy.start()

    def later(n):
        sum_step(n + 17)

    loop(4, later)
    for k in range(1, 4):
        there = small_rep.at[lax.rem(copy_id + 4 - k, 4)]
        remote(there, there, rep_sends.at[k - 1], rep_recvs.at[k - 1], rep_peer(k)).wait_recv()
    small_result[...] = (small_rep[0] + small_rep[1]) + (small_rep[2] + small_rep[3])

    def drain(n):
        scatter.drain(n)
        store(n).wait()

    loop(units, drain)
    for copy in back_copies + rep_copies:
        copy.wait_send()
    grad_store.wait()


def fused_call(length, x, cot, gain_a, gain_f, table, square, inner, outer):
    rows, width = square[0].shape
    units = 4 + 2 * (inner.shape[1] // width)
    heads = table.shape[1]
    seq = x.shape[0]
    half = rows // 2
    part = half // 3
    hidden = inner.shape[1]
    low, wide = jnp.bfloat16, jnp.float32
    anywhere = pl.BlockSpec(memory_space=pl.ANY)
    within = pl.BlockSpec(memory_space=pltpu.VMEM)
    sems = pltpu.SemaphoreType.DMA
    vm = pltpu.VMEM
    head_rows = -(-heads // 8) * 8
    return pl.pallas_call(
        fused_kernel,
        out_shape=(
            jax.ShapeDtypeStruct((seq, width), low),
            jax.ShapeDtypeStruct((seq, width), wide),
            jax.ShapeDtypeStruct((units, rows, width), low),
            jax.ShapeDtypeStruct((8, 128), wide),
            jax.ShapeDtypeStruct((heads // 2, 2, seq, seq), low),
        ),
        in_specs=[pl.BlockSpec(memory_space=pltpu.SMEM), within, anywhere]
        + [within] * 3
        + [anywhere] * 6,
        out_specs=[anywhere, anywhere, anywhere, within, anywhere],
        scratch_shapes=[
            vm((4, 2, units + 8, rows, width), low),
            vm((units, rows, width), low),
            vm((4, 4, 2, half, width), low),
            vm((units, 4, 2, part, width), low),
            vm((units, 4, 2 * part, width), low),
            vm((units, 4, 2 * part, width), low),
            vm((16, 128), wide),
            vm((16, 128), low),
            vm((8, 16, 128), low),
            vm((8, 8, 128), wide),
            vm((7, 8, 128), wide),
            vm((4, 8, 128), wide),
            vm((2, 2, seq, seq), low),
            vm((seq, width), low),
            vm((3, seq, width), low),
            vm((seq, width), low),
            vm((seq, width), wide),
            vm((seq, width), low),
            vm((seq, hidden), low),
            vm((seq, hidden), low),
            vm((seq, width), low),
            vm((seq, width), wide),
            vm((seq, width), low),
            vm((2, seq, seq), wide),
            vm((head_rows, 512), wide),
            vm((128, 512), wide),
            vm((1, width), wide),
            vm((1, width), wide),
            vm((1, width), wide),
            vm((1, width), wide),
            vm((2, 128, 128 * 7), wide),
            vm((2, seq, seq), low),
            sems((units, Gather.slots)),
            sems((units, Gather.slots)),
            sems((units, Scatter.slots)),
            sems((units, Scatter.slots)),
            sems((7,)),
            sems((7,)),
            sems((7,)),
            sems((7,)),
            sems((3,)),
            sems((3,)),
            sems((2,)),
            sems((2,)),
            sems((units,)),
            sems((units + 6,)),
        ],
        compiler_params=pltpu.CompilerParams(
            collective_id=0, has_side_effects=True, vmem_limit_bytes=63 * 2**20
        ),
    )(length, x, cot, gain_a, gain_f, table, *square, inner, outer)


def finish_kernel(
    block_in, grad_in, sums_far, small, block_out, grad_out, query, key, value, output, gain_a,
    table, inner, outer, gain_f, sums, sems, sum_sems,
):
    units, rows, width = sums.shape
    loads = [pltpu.make_async_copy(sums_far.at[n], sums.at[n], sum_sems.at[n]) for n in range(units)]
    copies = [
        pltpu.make_async_copy(block_in, block_out, sems.at[0]),
        pltpu.make_async_copy(grad_in, grad_out, sems.at[1]),
    ]
    for copy in loads + copies:
        copy.start()
    gain_a[...] = small[0:1, :rows]
    gain_f[...] = small[1:2, :rows]
    table[...] = small[2 : 2 + table.shape[0], : table.shape[1]]
    chunks = inner.shape[1] // width
    third = width // 3
    for i in range(chunks):
        loads[i].wait()
        outer[i * rows : (i + 1) * rows, :] = sums[i].astype(jnp.float32)
    for i in range(chunks):
        loads[chunks + i].wait()
        inner[:, i * width : (i + 1) * width] = sums[chunks + i].astype(jnp.float32)
    loads[2 * chunks].wait()
    output[...] = sums[2 * chunks].astype(jnp.float32)
    for u in range(3):
        loads[2 * chunks + 1 + u].wait()
        for n, ref in enumerate((query, key, value)):
            ref[:, u * third : (u + 1) * third] = sums[
                2 * chunks + 1 + u, :, n * third : (n + 1) * third
            ].astype(jnp.float32)
    for copy in copies:
        copy.wait()


def finish_call(block, grad, sums, small, table_shape, inner_shape, outer_shape):
    units, rows, width = sums.shape
    wide = jnp.float32
    anywhere = pl.BlockSpec(memory_space=pl.ANY)
    within = pl.BlockSpec(memory_space=pltpu.VMEM)
    shapes = [(rows, width)] * 4 + [(1, rows), table_shape, inner_shape, outer_shape, (1, rows)]
    return pl.pallas_call(
        finish_kernel,
        out_shape=[
            jax.ShapeDtypeStruct(block.shape, block.dtype),
            jax.ShapeDtypeStruct(grad.shape, grad.dtype),
        ]
        + [jax.ShapeDtypeStruct(shape, wide) for shape in shapes],
        in_specs=[anywhere, anywhere, anywhere, within],
        out_specs=[within] * (2 + len(shapes)),
        scratch_shapes=[
            pltpu.VMEM(sums.shape, sums.dtype),
            pltpu.SemaphoreType.DMA((2,)),
            pltpu.SemaphoreType.DMA((units,)),
        ],
        compiler_params=pltpu.CompilerParams(vmem_limit_bytes=63 * 2**20),
    )(block, grad, sums, small)


def local_linked(
    inputs, lengths, cotangent, query_weight, key_weight, value_weight, output_weight,
    attention_gain, bias_table, inner_weight, outer_weight, feedforward_gain,
):
    rows = query_weight.shape[0]
    square = (query_weight, key_weight, value_weight, output_weight)
    block, grad, sums, small, _ = fused_call(
        lengths, inputs[0], cotangent[0], attention_gain.reshape(1, rows),
        feedforward_gain.reshape(1, rows), bias_table, square, inner_weight, outer_weight,
    )
    block, grad, query, key, value, output, gain_a, table, inner, outer, gain_f = finish_call(
        block, grad, sums, small, bias_table.shape, inner_weight.shape, outer_weight.shape
    )
    return (
        block[None], grad[None], query, key, value, output, gain_a.reshape(rows), table, inner,
        outer, gain_f.reshape(rows),
    )


def local(inputs, lengths, cotangent, *shards):
    block_output, input_grad, gradients = compute(inputs, lengths, cotangent, gather_all(*shards))
    return (block_output, input_grad) + sum_all(gradients)


def can_link(mesh):
    return mesh.shape["fsdp"] == 8 and mesh.shape["rep"] == 4


def solution(mesh):
    placed = (
        P(("fsdp", "rep"), None, None),
        P(("fsdp", "rep")),
        P(("fsdp", "rep"), None, None),
        P("fsdp", None),
        P("fsdp", None),
        P("fsdp", None),
        P("fsdp", None),
        P("fsdp"),
        P("fsdp", None),
        P("fsdp", None),
        P("fsdp", None),
        P("fsdp"),
    )
    return jax.shard_map(
        local_linked if can_link(mesh) else local,
        mesh=mesh,
        in_specs=placed,
        out_specs=(
            P(("fsdp", "rep"), None, None),
            P(("fsdp", "rep"), None, None),
            P("fsdp", None),
            P("fsdp", None),
            P("fsdp", None),
            P("fsdp", None),
            P("fsdp"),
            P("fsdp", None),
            P("fsdp", None),
            P("fsdp", None),
            P("fsdp"),
        ),
        check_vma=False,
    )
```

```python
import functools

import jax
import jax.numpy as jnp
from jax import lax
import jax.experimental.pallas as pl
import jax.experimental.pallas.tpu as pltpu
from jax.sharding import PartitionSpec as P

NB = 32


epsilon = 1e-06
highest = lax.Precision.HIGHEST
gelu_coeff = 0.7978845608028654
masked_score = -1e30


def bucket_of(offset):
    half_count = NB // 2
    exact_count = half_count // 2
    distance = jnp.abs(offset)
    beyond = jnp.full(offset.shape, exact_count, jnp.int32)
    for exponent in range(1, half_count - exact_count):
        beyond = beyond + (distance * distance >= exact_count * exact_count * 2**exponent).astype(
            jnp.int32
        )
    nearby = jnp.where(distance < exact_count, distance, beyond)
    return jnp.where(offset > 0, half_count, 0).astype(jnp.int32) + nearby


def rms_norm(values, gain_vector):
    inverse_rms = lax.rsqrt(jnp.mean(values * values, axis=-1, keepdims=True) + epsilon)
    return values * inverse_rms * gain_vector


def gelu(values):
    return (
        0.5 * values * (1.0 + jnp.tanh(gelu_coeff * (values + 0.044715 * values * values * values)))
    )


def dot(a,b): return jnp.dot(a,b,preferred_element_type=jnp.float32)
def dot_t(a,b): return lax.dot_general(a,b,(((1,),(1,)),((),())),preferred_element_type=jnp.float32)
def dot_c(a,b): return lax.dot_general(a,b,(((0,),(0,)),((),())),preferred_element_type=jnp.float32)

def fwd_kernel(T, len_ref, q_ref, k_ref, v_ref, rel_ref, o_ref, p_ref, strip):
    hp=pl.program_id(0)
    seq=q_ref.shape[0]; nb=seq//T
    lane=lax.broadcasted_iota(jnp.int32,(1,128),1)
    kcol=lax.broadcasted_iota(jnp.int32,(1,seq),1)
    mask=jnp.where(kcol<len_ref[0],0.0,-1e30)
    k=k_ref[...]; v=v_ref[...]
    for hh in range(2):
        mine=(lane>=64) if hh else (lane<64)
        rel=rel_ref[pl.ds(hh,1),:]
        W=4*T
        rolled=pltpu.roll(jnp.broadcast_to(rel,(T,W)),0,axis=1,stride=1,stride_axis=0)
        strip[:, 2*T:5*T]=rolled[:, :3*T]
        far_neg=rel[:, 0:1]; far_pos=rel[:, 3*T-1:3*T]
        strip[:, 0:2*T]=jnp.broadcast_to(far_neg,(T,2*T))
        strip[:, 5*T:7*T]=jnp.broadcast_to(far_pos,(T,2*T))
        for I in range(nb):
            q=jnp.where(mine,q_ref[I*T:(I+1)*T,:],jnp.bfloat16(0))
            s=dot_t(q,k)+(strip[:, (3-I)*T:(3-I)*T+seq]+mask)
            m=jnp.max(s,axis=-1,keepdims=True)
            e=jnp.exp(s-m)
            tot=jnp.sum(e,axis=-1,keepdims=True)
            p=(e*(1.0/tot)).astype(jnp.bfloat16)
            p_ref[hh,I*T:(I+1)*T,:]=p
            o=dot(p,v)
            if hh==0:
                o_ref[I*T:(I+1)*T,:]=o.astype(jnp.bfloat16)
            else:
                o_ref[I*T:(I+1)*T,:]=jnp.where(mine,o.astype(jnp.bfloat16),o_ref[I*T:(I+1)*T,:])

def bwd_kernel(T, q_ref, k_ref, v_ref, do_ref, p_ref, dq_ref, dk_ref, dv_ref, db_ref, ds_ref):
    seq=q_ref.shape[0]; nb=seq//T
    lane=lax.broadcasted_iota(jnp.int32,(1,128),1)
    k=k_ref[...]; v=v_ref[...]
    dks=[];dvs=[]
    for hh in range(2):
        mine=(lane>=64) if hh else (lane<64)
        acc=[None]*5
        for I in range(nb):
            sl=slice(I*T,(I+1)*T)
            do=jnp.where(mine,do_ref[sl,:],jnp.bfloat16(0))
            dp=dot_t(do,v)
            p=p_ref[hh,sl,:].astype(jnp.float32)
            t=p*dp
            delta=jnp.sum(t,axis=-1,keepdims=True)
            ds=(t-p*delta).astype(jnp.bfloat16)
            ds_ref[sl,:]=ds
            dsf=ds.astype(jnp.float32)
            for J in range(nb):
                d=min(2,max(-2,J-I))+2
                x=dsf[:,J*T:(J+1)*T]
                acc[d]=x if acc[d] is None else acc[d]+x
            dq=dot(ds,k)
            if hh==0: dq_ref[sl,:]=dq.astype(jnp.bfloat16)
            else: dq_ref[sl,:]=jnp.where(mine,dq.astype(jnp.bfloat16),dq_ref[sl,:])
        near=jnp.concatenate([acc[1],acc[2],acc[3],jnp.zeros((T,T),jnp.float32)],axis=1)
        total=shear_sum(near,4*T)
        far=jnp.concatenate([jnp.zeros((1,2*T),jnp.float32),jnp.sum(acc[4],axis=0,keepdims=True),jnp.sum(acc[0],axis=0,keepdims=True)],axis=1)
        db_ref[hh:hh+1,:]=total+far
        dk=dot_c(q_ref[...],ds_ref[...]).T; dv=dot_c(do_ref[...],p_ref[hh]).T
        dks.append(dk); dvs.append(dv)
    dk_ref[...]=jnp.where(lane<64,dks[0],dks[1]).astype(jnp.bfloat16)
    dv_ref[...]=jnp.where(lane<64,dvs[0],dvs[1]).astype(jnp.bfloat16)

def rel_hits(tile):
    slot = jnp.arange(4 * tile, dtype=jnp.int32)
    offset = jnp.where(slot < 3 * tile, slot - tile, slot - 5 * tile)
    bucket_ids = jnp.arange(NB, dtype=jnp.int32)
    return (bucket_of(offset)[None, :] == bucket_ids[:, None]).astype(jnp.bfloat16)


def rel_vec(table, tile):
    return dot_c(table, rel_hits(tile))


def shear_sum(block, width):
    rows = block.shape[0]
    while rows > 8:
        rows //= 2
        block = block[:rows] + pltpu.roll(block[rows:], width - rows, axis=1)
    total = block[0:1]
    for r in range(1, 8):
        total = total + pltpu.roll(block[r : r + 1], width - r, axis=1)
    return total


def att_fwd(q,k,v,rel,length,T=128):
    seq,D=q.shape; H=rel.shape[0]
    blk=pl.BlockSpec((seq,128),lambda h: (0,h))
    return pl.pallas_call(functools.partial(fwd_kernel,T),grid=(H//2,),
        in_specs=[pl.BlockSpec(memory_space=pltpu.SMEM),blk,blk,blk,pl.BlockSpec((None,2,4*T),lambda h:(h,0,0))],
        out_specs=[blk,pl.BlockSpec((2,seq,seq),lambda h:(h,0,0))],
        out_shape=[jax.ShapeDtypeStruct((seq,D),jnp.bfloat16),jax.ShapeDtypeStruct((H,seq,seq),jnp.bfloat16)],
        scratch_shapes=[pltpu.VMEM((T,7*T),jnp.float32)],
        compiler_params=pltpu.CompilerParams(vmem_limit_bytes=40*2**20))(length,q,k,v,rel.reshape(H//2,2,4*T))
def att_bwd(q,k,v,do,p,T=128):
    seq,D=q.shape; H=p.shape[0]
    blk=pl.BlockSpec((seq,128),lambda h: (0,h))
    o=jax.ShapeDtypeStruct((seq,D),jnp.bfloat16)
    outs=pl.pallas_call(functools.partial(bwd_kernel,T),grid=(H//2,),
        in_specs=[blk,blk,blk,blk,pl.BlockSpec((2,seq,seq),lambda h:(h,0,0))],
        out_specs=[blk,blk,blk,pl.BlockSpec((None,2,4*T),lambda h:(h,0,0))],
        out_shape=[o,o,o,jax.ShapeDtypeStruct((H//2,2,4*T),jnp.float32)],
        scratch_shapes=[pltpu.VMEM((seq,seq),jnp.bfloat16)],
        compiler_params=pltpu.CompilerParams(vmem_limit_bytes=40*2**20))(q,k,v,do,p)
    return *outs[:3],outs[3].reshape(H,4*T)

def contract_rows(left, right):
    return lax.dot_general(
        left, right, (((0,), (0,)), ((), ())), preferred_element_type=jnp.float32
    )


def contract_cols(left, right):
    return lax.dot_general(
        left, right, (((1,), (1,)), ((), ())), preferred_element_type=jnp.float32
    )


MESH = pl.DeviceIdType.MESH


def coords():
    shard = lax.axis_index("fsdp")
    copy = lax.axis_index("rep")
    return shard // 2, shard % 2, copy // 2, copy % 2


def greet(peers, at_end):
    barrier = pltpu.get_barrier_semaphore()
    for peer in peers[:-1]:
        pl.semaphore_signal(barrier, inc=1, device_id=peer, device_id_type=MESH)

    def last():
        pl.semaphore_signal(barrier, inc=1, device_id=peers[-1], device_id_type=MESH)

    pl.when(~at_end)(last)


def all_greeted(peers, at_end):
    barrier = pltpu.get_barrier_semaphore()
    pl.semaphore_wait(barrier, jnp.where(at_end, len(peers) - 1, len(peers)))


class Links:
    def __init__(self, rows, send_sems, recv_sems):
        self.send_sems, self.recv_sems = send_sems, recv_sems
        self.z, self.x, self.y, self.c = coords()
        half = rows // 2
        part = half // 3
        at = lambda start, size: pl.ds(pl.multiple_of(start, part), size)
        first = half * self.c
        other = half * (1 - self.c)
        self.half, self.other_half = at(first, half), at(other, half)
        self.plane = at(first + part * self.y, 2 * part)
        self.shared = at(first + part, part)
        self.own_third = at(first + 2 * part * self.y, part)
        self.other_third = at(first + 2 * part * (1 - self.y), part)
        self.shared_in = at(part * self.y, part)
        self.third_in = at(part * (1 - self.y), part)

    def copy(self, src, dst, g, send, slot, device):
        return pltpu.make_async_remote_copy(
            src_ref=src,
            dst_ref=dst,
            send_sem=self.send_sems.at[send],
            recv_sem=self.recv_sems.at[g, slot],
            device_id=device,
            device_id_type=MESH,
        )

    def to_x(self):
        return (self.z * 2 + 1 - self.x, self.y * 2 + self.c)

    def to_y(self):
        return (self.z * 2 + self.x, (1 - self.y) * 2 + self.c)

    def to_core(self):
        return (self.z * 2 + self.x, self.y * 2 + 1 - self.c)

    def to_z(self, k):
        return (lax.rem(self.z + k, 4) * 2 + self.x, self.y * 2 + self.c)

    def z_before(self, k):
        return lax.rem(self.z + 4 - k, 4)


class Gather(Links):
    slots = 6

    def __init__(self, full, send_sems, recv_sems):
        super().__init__(full.shape[3], send_sems, recv_sems)
        self.full = full
        self.beside = self.z + 1 - 2 * lax.rem(self.z, 2)
        self.second = lax.rem(self.z + 2, 4)
        self.across = 3 - self.z
        self.at_end = (self.z == 0) | (self.z == 3)
        self.early = range(4, 8)

    def peers(self):
        near = [self.to_x(), self.to_y(), self.to_core()]
        return near + [self.at_z(a) for a in (self.second, self.beside, self.across)]

    def block(self, g, a, rows):
        return self.full.at[a, self.x, g, rows]

    def column(self, g, rows):
        return self.full.at[:, 1 - self.x, g, rows]

    def move(self, part, g, slot, device):
        return pltpu.make_async_remote_copy(
            src_ref=part,
            dst_ref=part,
            send_sem=self.send_sems.at[0 if g in self.early else 1],
            recv_sem=self.recv_sems.at[g, slot],
            device_id=device,
            device_id_type=MESH,
        )

    def at_z(self, a):
        return (a * 2 + self.x, self.y * 2 + self.c)

    def z_copy(self, g, to, slot):
        return self.move(self.block(g, self.z, self.plane), g, slot, self.at_z(to))

    def x_copy(self, g, a):
        return self.move(self.block(g, a, self.plane), g, 3, self.to_x())

    def y_copy(self, g, a):
        return self.move(self.block(g, a, self.own_third), g, 4, self.to_y())

    def core_copy(self, g, a):
        return self.move(self.block(g, a, self.half), g, 5, self.to_core())

    def arrived(self, part, g, slot):
        pltpu.make_async_copy(part, part, self.recv_sems.at[g, slot]).wait()

    def others(self):
        return (self.beside, self.second, self.across)

    def send_z(self, g):
        self.z_copy(g, self.second, 0).start()
        self.z_copy(g, self.beside, 1).start()
        pl.when(~self.at_end)(lambda: self.z_copy(g, self.across, 2).start())

    def send_x(self, g):
        self.x_copy(g, self.z).start()

    def spread(self, g, a, slot):
        self.arrived(self.block(g, a, self.plane), g, slot)
        if slot == 0:
            part = self.block(g, a, self.plane)
            pl.when(~self.at_end)(lambda: self.move(part, g, 2, self.at_z(self.beside)).start())
        self.x_copy(g, a).start()
        self.y_copy(g, a).start()

    def after_second(self, g):
        self.spread(g, self.second, 0)

    def after_beside(self, g):
        self.spread(g, self.beside, 1)

    def after_across(self, g):
        self.spread(g, self.across, 2)

    def after_x(self, g):
        self.arrived(self.column(g, self.plane), g, 3)
        self.move(self.column(g, self.own_third), g, 4, self.to_y()).start()

    def after_y(self, g):
        third = self.own_third.size
        self.arrived(self.full.at[0, 0, 0:7, 0:third], g, 4)
        for a in self.others():
            self.core_copy(g, a).start()
        self.move(self.column(g, self.half), g, 5, self.to_core()).start()

    def after_core(self, g):
        self.arrived(self.full.at[0, 0, 0:7, 0 : self.half.size], g, 5)

    def drain(self, n):
        count = len(self.early)
        units = self.full.shape[2] - 8
        rows = self.full.shape[3] * (count if n == 0 else units - count) // units

        def wait(blocks):
            part = self.full.at[:, :, 0:blocks, 0:rows]
            pltpu.make_async_copy(part, part, self.send_sems.at[n]).wait()

        pl.when(self.at_end)(lambda: wait(10))
        pl.when(~self.at_end)(lambda: wait(11))


class SmallGather(Gather):
    def move(self, part, g, slot, device):
        return pltpu.make_async_remote_copy(
            src_ref=part,
            dst_ref=part,
            send_sem=self.send_sems.at[0],
            recv_sem=self.recv_sems.at[slot],
            device_id=device,
            device_id_type=MESH,
        )

    def __init__(self, links, full, send_sems, recv_sems):
        self.__dict__.update(links.__dict__)
        self.full, self.send_sems, self.recv_sems = full, send_sems, recv_sems

    def block(self, g, a, rows):
        return self.full.at[a * 2 + self.x]

    def y_copy(self, g, a):
        return self

    def start(self):
        pass

    def arrived(self, part, g, slot):
        pltpu.make_async_copy(part, part, self.recv_sems.at[slot]).wait()

    def after_x(self, g):
        self.arrived(self.full.at[0:4], g, 3)

    def drain(self, n):
        def wait(blocks):
            part = self.full.at[0:blocks]
            pltpu.make_async_copy(part, part, self.send_sems.at[0]).wait()

        pl.when(self.at_end)(lambda: wait(6))
        pl.when(~self.at_end)(lambda: wait(8))


class Scatter(Links):
    slots = 6

    def __init__(self, slot, full, own, from_core, from_y, from_x, from_z, send_sems, recv_sems):
        super().__init__(own.shape[1], send_sems, recv_sems)
        self.slot, self.full, self.own = slot, full, own
        self.from_core, self.from_y, self.from_x, self.from_z = from_core, from_y, from_x, from_z

    def core_copy(self, g):
        part = self.full.at[:, :, self.slot(g), self.other_half]
        ring = g % self.from_core.shape[0]
        return self.copy(part, self.from_core.at[ring], g, 0, 0, self.to_core())

    def y_copy(self, g):
        part = self.full.at[:, :, self.slot(g), self.other_third]
        return self.copy(part, self.from_y.at[g], g, 1, 1, self.to_y())

    def x_copy(self, g):
        part = self.full.at[:, 1 - self.x, self.slot(g), self.plane]
        return self.copy(part, self.from_x.at[g], g, 1, 2, self.to_x())

    def z_copy(self, g, k):
        part = self.full.at[lax.rem(self.z + k, 4), self.x, self.slot(g), self.plane]
        return self.copy(part, self.from_z.at[g, k - 1], g, 2, 3, self.to_z(k))

    def back_y_copy(self, g):
        part = self.own.at[g, self.plane]
        return self.copy(part, self.from_z.at[g, 3], g, 4 + g, 4, self.to_y())

    def back_core_copy(self, g):
        part = self.own.at[g, self.half]
        return self.copy(part, part, g, 3, 5, self.to_core())

    def start(self, g):
        self.core_copy(g).start()

    def after_core(self, g):
        self.core_copy(g).wait_recv()
        ring = g % self.from_core.shape[0]
        for a in range(4):
            for b in range(2):
                self.full[a, b, self.slot(g), self.half] += self.from_core[ring, a, b]
        self.y_copy(g).start()

    def after_y(self, g):
        self.y_copy(g).wait_recv()
        for a in range(4):
            for b in range(2):
                self.full[a, b, self.slot(g), self.own_third] += self.from_y[g, a, b]
        self.x_copy(g).start()

    def after_x(self, g):
        self.x_copy(g).wait_recv()
        for a in range(4):
            self.full[a, self.x, self.slot(g), self.plane] += self.from_x[g, a]
        for k in (1, 2, 3):
            self.z_copy(g, k).start()

    def after_z(self, g):
        total = self.full[self.z, self.x, self.slot(g), self.plane].astype(jnp.float32)
        part = self.from_z.at[g, 0:3]
        pltpu.make_async_copy(part, part, self.recv_sems.at[g, 3]).wait()
        for k in (1, 2, 3):
            total = total + self.from_z[g, k - 1].astype(jnp.float32)
        self.own[g, self.plane] = total.astype(jnp.bfloat16)
        self.back_y_copy(g).start()

    def after_back_y(self, g):
        self.back_y_copy(g).wait_recv()
        self.back_y_copy(g).wait_send()
        got = self.from_z.at[g, 3]
        self.own[g, self.shared] += got[self.shared_in]
        self.own[g, self.other_third] = got[self.third_in]
        self.back_core_copy(g).start()

    def after_back_core(self, g):
        part = self.own.at[g, self.other_half]
        self.copy(part, part, g, 3, 5, self.to_core()).wait_recv()

    def drain(self):
        units, rows = self.own.shape[:2]
        half = rows // 2
        for n, part in (
            (0, self.full.at[:, :, 0 : units // 2]),
            (1, self.full.at[:, :, 0 : units // 3]),
            (2, self.full.at[:, :, 0 : units // 4, 0:half]),
            (3, self.own.at[0 : units // 2]),
        ):
            pltpu.make_async_copy(part, part, self.send_sems.at[n]).wait()


def compute(inputs, lengths, cotangent, weights):
    (
        full_query, full_key, full_value, full_output, full_gain, full_table, full_inner,
        full_outer, full_ffn_gain,
    ) = weights
    pairs_here, seq_len, model_width = inputs.shape
    row_count = pairs_here * seq_len
    head_count = full_table.shape[1]
    tile = 128
    relative = rel_vec(full_table, tile)
    flat_inputs = inputs.reshape(row_count, model_width).astype(jnp.float32)
    normed = rms_norm(flat_inputs, full_gain.astype(jnp.float32)).astype(jnp.bfloat16)
    joined = jnp.concatenate((full_query, full_key, full_value), axis=1)
    projected = jnp.dot(normed, joined, preferred_element_type=jnp.float32).astype(jnp.bfloat16)
    queries = projected[:, :model_width]
    key_rows = projected[:, model_width : 2 * model_width]
    value_rows = projected[:, 2 * model_width :]
    pair_rows = [slice(n * seq_len, (n + 1) * seq_len) for n in range(pairs_here)]
    forward_parts = [
        att_fwd(queries[r], key_rows[r], value_rows[r], relative, lengths[n : n + 1], tile)
        for n, r in enumerate(pair_rows)
    ]
    attended = jnp.concatenate([part[0] for part in forward_parts], axis=0)
    middle = flat_inputs + jnp.dot(attended, full_output, preferred_element_type=jnp.float32)
    normed_ffn = rms_norm(middle, full_ffn_gain.astype(jnp.float32)).astype(jnp.bfloat16)
    raised = jnp.dot(normed_ffn, full_inner, preferred_element_type=jnp.float32)
    active = gelu(raised).astype(jnp.bfloat16)
    lowered = jnp.dot(active, full_outer, preferred_element_type=jnp.float32)
    block_output = (middle + lowered).astype(jnp.bfloat16).reshape(pairs_here, seq_len, model_width)
    positions = jnp.arange(seq_len, dtype=jnp.int32)
    row_live = (positions[None, :] < lengths[:, None]).astype(jnp.float32)
    seed_rows = (cotangent.astype(jnp.float32) * row_live[:, :, None]).reshape(
        row_count, model_width
    )
    seed_low = seed_rows.astype(jnp.bfloat16)
    grad_active = contract_cols(seed_low, full_outer)
    grad_outer = contract_rows(active, seed_low)
    grad_raised = jax.vjp(gelu, raised)[1](grad_active)[0].astype(jnp.bfloat16)
    grad_inner = contract_rows(normed_ffn, grad_raised)
    grad_normed_ffn = contract_cols(grad_raised, full_inner)
    ffn_pull = jax.vjp(rms_norm, middle, full_ffn_gain.astype(jnp.float32))[1]
    grad_middle_part, grad_ffn_gain = ffn_pull(grad_normed_ffn)
    grad_middle = seed_rows + grad_middle_part
    joined = jnp.concatenate((full_query, full_key, full_value), axis=1)
    middle_low = grad_middle.astype(jnp.bfloat16)
    grad_attended = contract_cols(middle_low, full_output).astype(jnp.bfloat16)
    grad_output = contract_rows(attended, middle_low)
    backward_parts = [
        att_bwd(
            queries[r], key_rows[r], value_rows[r], grad_attended[r], forward_parts[n][1], tile
        )
        for n, r in enumerate(pair_rows)
    ]
    grad_projected = jnp.concatenate(
        [jnp.concatenate(part[:3], axis=1) for part in backward_parts], axis=0
    )
    grad_joined = contract_rows(normed, grad_projected)
    grad_normed = contract_cols(grad_projected, joined)
    attention_pull = jax.vjp(rms_norm, flat_inputs, full_gain.astype(jnp.float32))[1]
    grad_inputs_part, grad_attention_gain = attention_pull(grad_normed)
    input_grad = (grad_middle + grad_inputs_part).reshape(pairs_here, seq_len, model_width)
    grad_relative = sum(part[3] for part in backward_parts)
    grad_table = lax.dot_general(
        rel_hits(tile).astype(jnp.float32),
        grad_relative,
        (((1,), (1,)), ((), ())),
        precision=highest,
    )
    return block_output, input_grad, (
        grad_joined[:, :model_width],
        grad_joined[:, model_width : 2 * model_width],
        grad_joined[:, 2 * model_width :],
        grad_output,
        grad_attention_gain,
        grad_table,
        grad_inner,
        grad_outer,
        grad_ffn_gain,
    )


def gather_all(query_weight, key_weight, value_weight, output_weight, attention_gain, bias_table,
               inner_weight, outer_weight, feedforward_gain):
    return tuple(
        lax.all_gather(part, "fsdp", axis=0, tiled=True)
        for part in (
            query_weight, key_weight, value_weight, output_weight, attention_gain, bias_table,
            inner_weight, outer_weight, feedforward_gain,
        )
    )


def sum_all(gradients):
    def one(part):
        part = lax.psum_scatter(
            part.astype(jnp.bfloat16), "fsdp", scatter_dimension=0, tiled=True
        )
        return lax.psum(part, "rep").astype(jnp.float32)

    return tuple(one(part) for part in gradients)


def gelu_parts(z):
    square = z * z
    t = jnp.tanh(gelu_coeff * z * (1.0 + 0.044715 * square))
    half = 0.5 * (1.0 + t)
    slope = half + (0.5 * gelu_coeff) * z * (1.0 - t * t) * (1.0 + (3 * 0.044715) * square)
    return z * half, slope


def lanes(start, size):
    return pl.ds(start if isinstance(start, int) else pl.multiple_of(start, 128), size)


def rows_at(start, size):
    return pl.ds(pl.multiple_of(start, size), size)


def loop(count, body):
    def step(n, carry):
        body(n)
        return carry

    lax.fori_loop(0, count, step, 0)


def norm_back(grad, gain, values):
    inverse = lax.rsqrt(jnp.mean(values * values, axis=-1, keepdims=True) + epsilon)
    scaled = grad * gain
    centre = jnp.mean(scaled * values, axis=-1, keepdims=True)
    back = inverse * scaled - values * (inverse * inverse * inverse * centre)
    return back, jnp.sum(grad * values * inverse, axis=0, keepdims=True)


class Layer:
    def __init__(self, **refs):
        self.__dict__.update(refs)
        self.seq, self.width = self.x.shape
        self.tile = 128
        self.row_block = 128
        self.shard_rows = self.bank.shape[3]

    def unit(self, u, column=None, size=None):
        if column is None:
            block = self.bank[:, :, u]
        else:
            block = self.bank[:, :, u, :, lanes(column, size)]
        return block.reshape(-1, block.shape[-1])

    def row_chunks(self, body):
        size = self.row_block
        loop(self.seq // size, lambda n: body(rows_at(n * size, size)))

    def small_arrays(self):
        flat = self.all_small[...].reshape(-1, 128)
        tile = self.tile
        slot = lax.broadcasted_iota(jnp.int32, (flat.shape[0], 4 * tile), 1)
        offset = jnp.where(slot < 3 * tile, slot - tile, slot - 5 * tile)
        row = lax.broadcasted_iota(jnp.int32, (flat.shape[0], 4 * tile), 0)
        per = NB // 8
        inside = row % 16 - 2
        wanted = jnp.where((inside >= 0) & (inside < per), (row // 16) * per + inside, -1)
        hits = (bucket_of(offset) == wanted).astype(jnp.bfloat16)
        self.rel[...] = dot_c(flat, hits)[: self.rel.shape[0]]
        for index, ref in ((0, self.gain_a), (1, self.gain_f)):
            total = jnp.zeros((1, self.width), jnp.float32)
            for shard in range(8):
                part = self.all_small[shard].astype(jnp.float32)[index : index + 1]
                wide = jnp.concatenate(
                    [part, jnp.zeros((1, self.width - 128), jnp.float32)], axis=1
                )
                total = total + (
                    pltpu.roll(wide, shard * self.shard_rows, axis=1) if shard else wide
                )
            ref[...] = total

    def norm_in(self):
        gain = self.gain_a[...]

        def body(r):
            self.normed[r] = rms_norm(self.x[r].astype(jnp.float32), gain).astype(jnp.bfloat16)

        self.row_chunks(body)

    def mask_seed(self):
        def body(r):
            index = lax.broadcasted_iota(jnp.int32, (self.row_block, 1), 0) + r.start
            live = index < self.length[0]
            self.seed[r] = jnp.where(live, self.seed[r], jnp.bfloat16(0))

        self.row_chunks(body)

    def project(self, u):
        def body(n):
            self.qkv[u, :, lanes(n * 256, 256)] = dot(
                self.normed[...], self.unit(u, n * 256, 256)
            ).astype(jnp.bfloat16)

        loop(self.width // 256, body)

    def strip_for(self, head, strip):
        tile = self.tile
        rel = self.rel[pl.ds(head, 1), :]
        rolled = pltpu.roll(
            jnp.broadcast_to(rel, (tile, 4 * tile)), 0, axis=1, stride=1, stride_axis=0
        )
        strip[:, 2 * tile : 5 * tile] = rolled[:, : 3 * tile]
        strip[:, : 2 * tile] = jnp.broadcast_to(rel[:, :1], (tile, 2 * tile))
        strip[:, 5 * tile :] = jnp.broadcast_to(rel[:, 3 * tile - 1 : 3 * tile], (tile, 2 * tile))

    def pair_lanes(self, pair):
        third = self.width // 3
        first = (pair % 2) * 128
        return pair // 2, [lanes(first + n * third, 128) for n in range(3)]

    def probs_store(self, pair, slot):
        return pltpu.make_async_copy(
            self.probs.at[slot], self.probs_far.at[pair], self.probs_sems.at[slot]
        )

    def probs_load(self, pair, slot):
        return pltpu.make_async_copy(
            self.probs_far.at[pair], self.probs.at[slot], self.probs_sems.at[slot]
        )

    def attend(self, pair):
        tile, seq = self.tile, self.seq
        slot = pair % 2
        if pair >= 2:
            self.probs_store(pair, slot).wait()
        lane = lax.broadcasted_iota(jnp.int32, (1, 128), 1)
        own = (lane < 64, lane >= 64)
        key_at = lax.broadcasted_iota(jnp.int32, (1, seq), 1)
        mask = jnp.where(key_at < self.length[0], 0.0, masked_score)
        unit, (q_at, k_at, v_at) = self.pair_lanes(pair)
        q = self.qkv[unit, :, q_at]
        k = self.qkv[unit, :, k_at]
        v = self.qkv[unit, :, v_at]
        for head in range(2):
            self.strip_for(pair * 2 + head, self.strip.at[head])
            self.scores[head] = dot_t(jnp.where(own[head], q, jnp.bfloat16(0)), k)

        def soften(head):
            for block in range(seq // tile):
                r = slice(block * tile, (block + 1) * tile)
                first = (seq // tile - 1 - block) * tile
                bias = self.strip[head, :, first : first + seq]
                scores = self.scores[head, r, :] + (bias + mask)
                peak = jnp.max(scores, axis=-1, keepdims=True)
                raised = jnp.exp(scores - peak)
                total = jnp.sum(raised, axis=-1, keepdims=True)
                self.probs[slot, head, r, :] = (raised * (1.0 / total)).astype(jnp.bfloat16)
            return dot(self.probs[slot, head], v)

        outs = [soften(head) for head in range(2)]
        self.attended[:, lanes(pair * 128, 128)] = jnp.where(own[0], *outs).astype(jnp.bfloat16)
        self.probs_store(pair, slot).start()

    def middle_rows(self):
        def body(n):
            c = lanes(n * 256, 256)
            self.middle[:, c] = self.x[:, c].astype(jnp.float32) + dot(
                self.attended[...], self.unit(3, n * 256, 256)
            )

        loop(self.width // 256, body)
        gain = self.gain_f[...]

        def norm(r):
            self.normed_ffn[r] = rms_norm(self.middle[r], gain).astype(jnp.bfloat16)

        self.row_chunks(norm)

    def raise_unit(self, i):
        def body(n):
            raised = dot(self.normed_ffn[...], self.unit(4 + i, n * 256, 256))
            active, slope = gelu_parts(raised)
            c = lanes(i * self.width + n * 256, 256)
            self.active[:, c] = active.astype(jnp.bfloat16)
            self.slope[:, c] = slope.astype(jnp.bfloat16)

        loop(self.width // 256, body)

    def outer_grad(self, shard):
        size = 4 * self.shard_rows
        block = dot_c(self.active[:, lanes(shard * size, size)], self.seed[...])
        self.bank[shard // 2, shard % 2, 12:16] = block.astype(jnp.bfloat16).reshape(
            4, self.shard_rows, self.width
        )

    def lower(self, n):
        outer = self.bank[:, :, 8:12, :, lanes(n * 256, 256)].reshape(-1, 256)
        c = lanes(n * 256, 256)
        self.mid_low[:, c] = (self.middle[:, c] + dot(self.active[...], outer)).astype(
            jnp.bfloat16
        )

    def raised_grad(self, shard):
        size = 4 * self.shard_rows
        outer = self.bank[shard // 2, shard % 2, 8:12].reshape(size, self.width)
        c = lanes(shard * size, size)
        grad = dot_t(self.seed[...], outer) * self.slope[:, c].astype(jnp.float32)
        self.slope[:, c] = grad.astype(jnp.bfloat16)

    def inner_grad(self, i):
        def body(n):
            c = lanes(i * self.width + n * 256, 256)
            block = dot_c(self.normed_ffn[...], self.slope[:, c]).astype(jnp.bfloat16)
            self.bank[:, :, 16 + i, :, lanes(n * 256, 256)] = block.reshape(
                4, 2, self.shard_rows, 256
            )

        loop(self.width // 256, body)

    def middle_grad(self, part):
        total = None
        for i in range(4):
            inner = self.bank[2 * part : 2 * part + 2, :, 4 + i].reshape(-1, self.width)
            term = dot_t(self.slope[:, i * self.width : (i + 1) * self.width], inner)
            total = term if total is None else total + term
        size = self.width // 2
        self.grad_mid[:, part * size : (part + 1) * size] = total

    def middle_norm(self):
        gain = self.gain_f[...]
        self.gain_f_grad[...] = jnp.zeros_like(self.gain_f_grad)

        def body(r):
            back, terms = norm_back(self.grad_mid[r], gain, self.middle[r])
            total = self.seed[r].astype(jnp.float32) + back
            self.gain_f_grad[...] += terms
            self.grad_mid[r] = total
            self.mid_low[r] = total.astype(jnp.bfloat16)

        self.row_chunks(body)

    def square_grad(self, left, right, slot):
        def body(n):
            block = dot_c(left[...], right(lanes(n * 256, 256))).astype(jnp.bfloat16)
            self.bank[:, :, slot, :, lanes(n * 256, 256)] = block.reshape(
                4, 2, self.shard_rows, 256
            )

        loop(self.width // 256, body)

    def attended_grad(self):
        size = self.width // 2
        for part in range(2):
            weight = self.bank[2 * part : 2 * part + 2, :, 3].reshape(size, self.width)
            self.attended[:, part * size : (part + 1) * size] = dot_t(
                self.mid_low[...], weight
            ).astype(jnp.bfloat16)

    def attend_back(self, pair):
        tile, seq = self.tile, self.seq
        slot = pair % 2
        self.probs_load(pair, slot).wait()
        lane = lax.broadcasted_iota(jnp.int32, (1, 128), 1)
        own = (lane < 64, lane >= 64)
        unit, (q_at, k_at, v_at) = self.pair_lanes(pair)
        q = self.qkv[unit, :, q_at]
        k = self.qkv[unit, :, k_at]
        v = self.qkv[unit, :, v_at]
        grad_out = self.attended[:, lanes(pair * 128, 128)]
        blocks = seq // tile
        for head in range(2):
            self.scores[head] = dot_t(jnp.where(own[head], grad_out, jnp.bfloat16(0)), v)

        def back(head):
            sums = [None] * 5
            for block in range(blocks):
                r = slice(block * tile, (block + 1) * tile)
                probs = self.probs[slot, head, r, :].astype(jnp.float32)
                weighted = probs * self.scores[head, r, :]
                centre = jnp.sum(weighted, axis=-1, keepdims=True)
                grad = weighted - probs * centre
                self.grad_scores[head, r, :] = grad.astype(jnp.bfloat16)
                for other in range(blocks):
                    apart = min(2, max(-2, other - block)) + 2
                    part = grad[:, other * tile : (other + 1) * tile]
                    sums[apart] = part if sums[apart] is None else sums[apart] + part
            zero = jnp.zeros((tile, tile), jnp.float32)
            near = shear_sum(jnp.concatenate([sums[1], sums[2], sums[3], zero], axis=1), 4 * tile)
            far = jnp.concatenate(
                [
                    jnp.zeros((1, 2 * tile), jnp.float32),
                    jnp.sum(sums[4], axis=0, keepdims=True),
                    jnp.sum(sums[0], axis=0, keepdims=True),
                ],
                axis=1,
            )
            self.rel_grad[pl.ds(pair * 2 + head, 1), :] = near + far
            return (
                dot(self.grad_scores[head], k),
                dot_c(q, self.grad_scores[head]).T,
                dot_c(grad_out, self.probs[slot, head]).T,
            )

        for at, first, second in zip((q_at, k_at, v_at), back(0), back(1)):
            self.qkv[unit, :, at] = jnp.where(own[0], first, second).astype(jnp.bfloat16)
        if pair + 2 < self.probs_far.shape[0]:
            self.probs_load(pair + 2, slot).start()

    def normed_grad(self, part):
        size = self.width // 2
        total = None
        for u in range(3):
            weight = self.bank[2 * part : 2 * part + 2, :, u].reshape(size, self.width)
            term = dot_t(self.qkv[u], weight)
            total = term if total is None else total + term
        self.middle[:, part * size : (part + 1) * size] = total

    def input_grad(self):
        gain = self.gain_a[...]
        self.gain_a_grad[...] = jnp.zeros_like(self.gain_a_grad)

        def body(r):
            back, terms = norm_back(self.middle[r], gain, self.x[r].astype(jnp.float32))
            self.gain_a_grad[...] += terms
            self.grad_mid[r] += back

        self.row_chunks(body)

    def small_grads(self):
        tile = self.tile
        shape = (64, 4 * tile)
        slot = lax.broadcasted_iota(jnp.int32, shape, 1)
        offset = jnp.where(slot < 3 * tile, slot - tile, slot - 5 * tile)
        row = lax.broadcasted_iota(jnp.int32, shape, 0)
        per = NB // 8
        inside = row % 8 - 2
        wanted = jnp.where((inside >= 0) & (inside < per), (row // 8) * per + inside, -1)
        hits = (bucket_of(offset) == wanted).astype(jnp.float32)
        table = lax.dot_general(
            hits,
            self.rel_grad[...],
            (((1,), (1,)), ((), ())),
            precision=highest,
            preferred_element_type=jnp.float32,
        )
        rows = lax.broadcasted_iota(jnp.int32, (8, 128), 0)
        lane = lax.broadcasted_iota(jnp.int32, (8, 128), 1)
        for shard in range(8):
            block = table[8 * shard : 8 * shard + 8]
            for index, ref in ((0, self.gain_a_grad), (1, self.gain_f_grad)):
                wide = ref[...]
                if shard:
                    wide = pltpu.roll(wide, self.width - shard * self.shard_rows, axis=1)
                here = (rows == index) & (lane < self.shard_rows)
                block = jnp.where(here, jnp.broadcast_to(wide[:, :128], (8, 128)), block)
            self.small_out[shard] = block


(
    SEND_Z, SEND_X, GOT_SECOND, GOT_BESIDE, GOT_ACROSS, GOT_X, GOT_Y, GOT_CORE, DRAIN, SMALL_Z,
    SMALL_X, SMALL_SECOND, SMALL_BESIDE, SMALL_ACROSS, SUM_SEND, SUM_CORE, SUM_Y, SUM_X, SUM_Z,
    SUM_BACK, SUM_DONE, NORM, PROJECT, ATTEND, MIDDLE, RAISE, OUTER_GRAD, LOWER, RAISED_GRAD,
    INNER_GRAD, MIDDLE_GRAD, MIDDLE_NORM, OUTPUT_GRAD, ATTENDED_GRAD, ATTEND_BACK, SQUARE_GRAD,
    NORMED_GRAD, INPUT_GRAD, SMALL, SMALL_SUM, SMALL_DONE,
) = range(41)

ORDER = (
    (SMALL_Z, 0), (SMALL_X, 0), (SEND_X, 0), (SEND_Z, 1), (SEND_X, 1), (SEND_X, 5), (SEND_X, 2),
    (SEND_X, 4), (SEND_Z, 0), (GOT_SECOND, 1), (SEND_X, 9), (GOT_BESIDE, 1), (SMALL_SECOND, 0),
    (SMALL_BESIDE, 0), (SMALL_ACROSS, 0), (GOT_ACROSS, 1), (SEND_Z, 2), (GOT_SECOND, 0),
    (GOT_BESIDE, 0), (SEND_X, 3), (SEND_Z, 4), (GOT_X, 1), (GOT_ACROSS, 0), (SEND_Z, 3),
    (GOT_SECOND, 2), (GOT_SECOND, 4), (GOT_BESIDE, 2), (GOT_X, 0), (GOT_Y, 1), (SEND_Z, 5),
    (GOT_ACROSS, 2), (GOT_BESIDE, 4), (SEND_X, 7), (NORM, 0), (GOT_SECOND, 3), (SEND_Z, 6),
    (GOT_X, 2), (GOT_CORE, 1), (GOT_ACROSS, 4), (GOT_SECOND, 5), (GOT_BESIDE, 5), (GOT_Y, 0),
    (SEND_Z, 7), (PROJECT, 1), (GOT_CORE, 0), (PROJECT, 0), (GOT_X, 4), (GOT_ACROSS, 5),
    (GOT_Y, 2), (GOT_BESIDE, 6), (GOT_ACROSS, 3), (SEND_X, 6), (SEND_Z, 8), (ATTEND, 0),
    (GOT_BESIDE, 3), (GOT_SECOND, 6), (GOT_X, 5), (SEND_Z, 11), (ATTEND, 1), (ATTEND, 2),
    (GOT_SECOND, 7), (GOT_CORE, 2), (GOT_ACROSS, 6), (GOT_SECOND, 8), (GOT_Y, 4), (PROJECT, 2),
    (GOT_X, 3), (GOT_BESIDE, 8), (GOT_Y, 5), (GOT_ACROSS, 7), (SEND_Z, 10), (GOT_ACROSS, 8),
    (ATTEND, 3), (GOT_X, 6), (GOT_BESIDE, 7), (ATTEND, 4), (GOT_SECOND, 11), (GOT_Y, 3),
    (GOT_BESIDE, 11), (GOT_CORE, 4), (ATTEND, 5), (GOT_SECOND, 10), (SEND_X, 8), (SEND_X, 11),
    (GOT_CORE, 3), (GOT_ACROSS, 11), (SEND_Z, 9), (MIDDLE, 0), (GOT_BESIDE, 10), (GOT_Y, 6),
    (GOT_X, 7), (RAISE, 0), (GOT_ACROSS, 10), (GOT_SECOND, 9), (OUTER_GRAD, 1), (GOT_X, 8),
    (SEND_X, 10), (GOT_CORE, 6), (GOT_CORE, 5), (RAISE, 1), (GOT_Y, 7), (GOT_ACROSS, 9),
    (GOT_X, 11), (OUTER_GRAD, 0), (RAISE, 2), (GOT_BESIDE, 9), (OUTER_GRAD, 4), (GOT_X, 10),
    (GOT_Y, 8), (DRAIN, 0), (OUTER_GRAD, 5), (GOT_CORE, 7), (OUTER_GRAD, 2), (GOT_Y, 11),
    (GOT_CORE, 8), (GOT_X, 9), (RAISE, 3), (OUTER_GRAD, 6), (GOT_Y, 10), (GOT_CORE, 11),
    (OUTER_GRAD, 7), (GOT_Y, 9), (OUTER_GRAD, 3), (SUM_SEND, 0), (GOT_CORE, 10), (SUM_SEND, 1),
    (GOT_CORE, 9), (LOWER, 0), (SUM_CORE, 0), (RAISED_GRAD, 7), (RAISED_GRAD, 4),
    (RAISED_GRAD, 3), (SUM_SEND, 2), (RAISED_GRAD, 2), (RAISED_GRAD, 0), (SUM_CORE, 1),
    (RAISED_GRAD, 1), (INNER_GRAD, 0), (SUM_Y, 0), (SUM_CORE, 2), (RAISED_GRAD, 6), (SUM_SEND, 3),
    (LOWER, 1), (RAISED_GRAD, 5), (MIDDLE_GRAD, 0), (SUM_Y, 1), (SUM_CORE, 3), (MIDDLE_GRAD, 1),
    (SUM_SEND, 4), (SUM_X, 0), (INNER_GRAD, 1), (SUM_Y, 2), (SUM_CORE, 4), (SUM_SEND, 5),
    (LOWER, 2), (SUM_X, 1), (MIDDLE_NORM, 0), (SUM_CORE, 5), (SUM_Y, 3), (INNER_GRAD, 2),
    (SUM_SEND, 6), (SUM_X, 2), (INNER_GRAD, 3), (SUM_SEND, 7), (SUM_CORE, 6), (SUM_Y, 4),
    (OUTPUT_GRAD, 0), (ATTENDED_GRAD, 0), (SUM_CORE, 7), (SUM_X, 3), (ATTEND_BACK, 0), (SUM_Y, 5),
    (SUM_SEND, 8), (ATTEND_BACK, 1), (SUM_X, 4), (SQUARE_GRAD, 0), (SUM_CORE, 8), (SUM_SEND, 9),
    (SUM_Y, 6), (ATTEND_BACK, 2), (SUM_X, 5), (SUM_CORE, 9), (ATTEND_BACK, 3), (SUM_Y, 7),
    (SQUARE_GRAD, 1), (SUM_X, 6), (ATTEND_BACK, 4), (SUM_SEND, 10), (SUM_Y, 8), (ATTEND_BACK, 5),
    (SUM_X, 7), (SUM_CORE, 10), (SQUARE_GRAD, 2), (SUM_Y, 9), (SUM_SEND, 11), (NORMED_GRAD, 0),
    (SUM_X, 8), (SUM_CORE, 11), (SUM_Z, 3), (SUM_Z, 5), (SUM_Z, 0), (SUM_Y, 10), (SUM_Z, 6),
    (NORMED_GRAD, 1), (SUM_X, 9), (INPUT_GRAD, 0), (SUM_Y, 11), (SUM_Z, 2), (SMALL, 0),
    (SUM_X, 10), (SUM_Z, 1), (SUM_Z, 9), (SUM_X, 11), (SUM_BACK, 5), (SUM_BACK, 6), (SUM_BACK, 3),
    (SUM_Z, 4), (SUM_Z, 10), (SUM_DONE, 6), (SUM_BACK, 1), (SUM_Z, 7), (SMALL_SUM, 0), (SUM_Z, 8),
    (SUM_Z, 11), (SUM_BACK, 10), (SMALL_DONE, 0), (SUM_DONE, 10), (SUM_BACK, 7), (SUM_BACK, 0),
    (SUM_DONE, 5), (SUM_DONE, 3), (SUM_BACK, 4), (SUM_DONE, 1), (SUM_BACK, 2), (SUM_BACK, 9),
    (SUM_BACK, 8), (SUM_BACK, 11), (SUM_DONE, 7), (SUM_DONE, 2), (SUM_DONE, 8), (SUM_DONE, 4),
    (SUM_DONE, 0), (SUM_DONE, 9), (SUM_DONE, 11),
)


def order_slot(n):
    return n + 12 if n < 8 else (7 if n == 8 else n - 5)


def fused_kernel(
    length, x, cot, gain_a_own, gain_f_own, table_own, query_own, key_own, value_own, output_own,
    inner_own, outer_own,
    block_far, grad_far, own_far, small_result, probs_far,
    bank, own_sum, from_core, from_y, from_x, from_z, small_wide, all_small, small_out,
    small_in, small_rep, probs, normed, qkv, attended, middle, normed_ffn, active, slope, seed,
    grad_mid, mid_low, scores, rel, rel_grad, gain_a, gain_f, gain_a_grad,
    gain_f_grad, strip, grad_scores,
    sends, recvs, sum_sends, sum_recvs, small_sends, small_recvs, back_sems, probs_sems,
    misc_sems, keep_sems,
):
    shard = lax.axis_index("fsdp")
    copy_id = lax.axis_index("rep")
    layer = Layer(
        length=length, x=x, bank=bank, all_small=all_small, small_out=small_out,
        probs=probs, probs_far=probs_far, probs_sems=probs_sems, normed=normed, qkv=qkv,
        attended=attended, middle=middle, normed_ffn=normed_ffn, active=active, slope=slope,
        seed=seed, grad_mid=grad_mid, mid_low=mid_low, scores=scores,
        rel=rel, rel_grad=rel_grad, gain_a=gain_a, gain_f=gain_f, gain_a_grad=gain_a_grad,
        gain_f_grad=gain_f_grad, strip=strip, grad_scores=grad_scores,
    )
    rows, width = query_own.shape
    chunks = inner_own.shape[1] // width
    units = 4 + 2 * chunks
    gather = Gather(bank, sends, recvs)
    scatter = Scatter(
        order_slot, bank, own_sum, from_core, from_y, from_x, from_z, sum_sends, sum_recvs
    )
    pairs = probs_far.shape[0]

    def remote(src, dst, send, recv, device):
        return pltpu.make_async_remote_copy(
            src_ref=src, dst_ref=dst, send_sem=send, recv_sem=recv, device_id=device,
            device_id_type=MESH,
        )

    def peer(k):
        return (lax.rem(shard + k, 8), copy_id)

    def rep_peer(k):
        return (shard, lax.rem(copy_id + k, 4))

    parts = [output_own]
    parts += [inner_own.at[:, pl.ds(i * width, width)] for i in range(chunks)]
    parts += [outer_own.at[pl.ds(i * rows, rows)] for i in range(chunks)]
    third = width // 3
    homes = [
        (part.at[:, pl.ds(u * third, third)], bank.at[gather.z, gather.x, u, :, pl.ds(n * third, third)])
        for u in range(3)
        for n, part in enumerate((query_own, key_own, value_own))
    ]
    homes += [(part, bank.at[gather.z, gather.x, 3 + u]) for u, part in enumerate(parts)]
    keeps = [
        pltpu.make_async_copy(part, home, keep_sems.at[0]) for part, home in homes
    ]
    keep_seed = pltpu.make_async_copy(cot, seed, keep_sems.at[1])
    keeps.append(keep_seed)
    peers = gather.peers()
    greet(peers, gather.at_end)
    for copy in keeps:
        copy.start()
    small_wide[...] = jnp.zeros_like(small_wide)
    small_wide[0:1, :rows] = gain_a_own[...].astype(jnp.float32)
    small_wide[1:2, :rows] = gain_f_own[...].astype(jnp.float32)
    per, heads = table_own.shape
    small_wide[2 : 2 + per, :heads] = table_own[...].astype(jnp.float32)
    all_small[shard] = small_wide[...].astype(jnp.bfloat16)
    smalls = SmallGather(gather, all_small, small_sends, small_recvs)
    mine = bank.at[gather.z, gather.x, 0:units]
    pltpu.make_async_copy(mine, mine, keep_sems.at[0]).wait()
    all_greeted(peers, gather.at_end)

    def store(n):
        return pltpu.make_async_copy(own_sum.at[n], own_far.at[n], misc_sems.at[2])

    def sum_done(n):
        scatter.after_back_core(n)
        store(n).start()

    block_store = pltpu.make_async_copy(mid_low, block_far, misc_sems.at[0])
    grad_store = pltpu.make_async_copy(grad_mid, grad_far, misc_sems.at[1])
    back_copies = [
        remote(
            small_out.at[lax.rem(shard + k, 8)], small_in.at[k - 1], back_sems.at[0],
            back_sems.at[1], peer(k),
        )
        for k in range(1, 8)
    ]
    rep_copies = [
        remote(
            small_rep.at[copy_id], small_rep.at[copy_id], back_sems.at[2], back_sems.at[3],
            rep_peer(k),
        )
        for k in range(1, 4)
    ]

    def wait_for(part, sem):
        pltpu.make_async_copy(part, part, sem).wait()

    def norm(_):
        keep_seed.wait()
        layer.mask_seed()
        smalls.after_x(0)
        layer.small_arrays()
        layer.norm_in()

    def middle_rows(_):
        layer.middle_rows()
        for pair in (pairs - 2, pairs - 1):
            layer.probs_store(pair, pair % 2).wait()
        for pair in (0, 1):
            layer.probs_load(pair, pair).start()

    def lower(n):
        layer.lower(n)
        if n == width // 256 - 1:
            block_store.start()

    def middle_norm(_):
        block_store.wait()
        layer.middle_norm()
        rel_grad[...] = jnp.zeros_like(rel_grad)

    def input_grad(_):
        layer.input_grad()
        grad_store.start()

    def small_sums(_):
        layer.small_grads()
        for copy in back_copies:
            copy.start()

    def small_sum(_):
        wait_for(small_in, back_sems.at[1])
        total = small_out[shard]
        for k in range(7):
            total = total + small_in[k]
        small_rep[copy_id] = total
        for copy in rep_copies:
            copy.start()

    def small_done(_):
        wait_for(small_rep.at[0:3], back_sems.at[3])
        small_result[...] = (small_rep[0] + small_rep[1]) + (small_rep[2] + small_rep[3])

    work = {
        SEND_Z: gather.send_z,
        SEND_X: gather.send_x,
        GOT_SECOND: gather.after_second,
        GOT_BESIDE: gather.after_beside,
        GOT_ACROSS: gather.after_across,
        GOT_X: gather.after_x,
        GOT_Y: gather.after_y,
        GOT_CORE: gather.after_core,
        DRAIN: gather.drain,
        SMALL_Z: smalls.send_z,
        SMALL_X: smalls.send_x,
        SMALL_SECOND: smalls.after_second,
        SMALL_BESIDE: smalls.after_beside,
        SMALL_ACROSS: smalls.after_across,
        SUM_SEND: scatter.start,
        SUM_CORE: scatter.after_core,
        SUM_Y: scatter.after_y,
        SUM_X: scatter.after_x,
        SUM_Z: scatter.after_z,
        SUM_BACK: scatter.after_back_y,
        SUM_DONE: sum_done,
        NORM: norm,
        PROJECT: layer.project,
        ATTEND: layer.attend,
        MIDDLE: middle_rows,
        RAISE: layer.raise_unit,
        OUTER_GRAD: layer.outer_grad,
        LOWER: lower,
        RAISED_GRAD: layer.raised_grad,
        INNER_GRAD: layer.inner_grad,
        MIDDLE_GRAD: layer.middle_grad,
        MIDDLE_NORM: middle_norm,
        OUTPUT_GRAD: lambda _: layer.square_grad(attended, lambda c: mid_low[:, c], 7),
        ATTENDED_GRAD: lambda _: layer.attended_grad(),
        ATTEND_BACK: layer.attend_back,
        SQUARE_GRAD: lambda u: layer.square_grad(normed, lambda c: qkv[u, :, c], 4 + u),
        NORMED_GRAD: layer.normed_grad,
        INPUT_GRAD: input_grad,
        SMALL: small_sums,
        SMALL_SUM: small_sum,
        SMALL_DONE: small_done,
    }
    for name, n in ORDER:
        work[name](n)
    gather.drain(1)
    smalls.drain(0)
    scatter.drain()
    wait_for(small_in, back_sems.at[0])
    wait_for(small_rep.at[0:3], back_sems.at[2])
    wait_for(own_sum, misc_sems.at[2])
    grad_store.wait()


def fused_call(length, x, cot, gain_a, gain_f, table, square, inner, outer):
    rows, width = square[0].shape
    units = 4 + 2 * (inner.shape[1] // width)
    heads = table.shape[1]
    seq = x.shape[0]
    half = rows // 2
    part = half // 3
    hidden = inner.shape[1]
    low, wide = jnp.bfloat16, jnp.float32
    anywhere = pl.BlockSpec(memory_space=pl.ANY)
    within = pl.BlockSpec(memory_space=pltpu.VMEM)
    sems = pltpu.SemaphoreType.DMA
    vm = pltpu.VMEM
    head_rows = -(-heads // 8) * 8
    return pl.pallas_call(
        fused_kernel,
        out_shape=(
            jax.ShapeDtypeStruct((seq, width), low),
            jax.ShapeDtypeStruct((seq, width), wide),
            jax.ShapeDtypeStruct((units, rows, width), low),
            jax.ShapeDtypeStruct((8, 128), wide),
            jax.ShapeDtypeStruct((heads // 2, 2, seq, seq), low),
        ),
        in_specs=[pl.BlockSpec(memory_space=pltpu.SMEM), within, anywhere]
        + [within] * 3
        + [anywhere] * 6,
        out_specs=[anywhere, anywhere, anywhere, within, anywhere],
        scratch_shapes=[
            vm((4, 2, units + 8, rows, width), low),
            vm((units, rows, width), low),
            vm((6, 4, 2, half, width), low),
            vm((units, 4, 2, part, width), low),
            vm((units, 4, 2 * part, width), low),
            vm((units, 4, 2 * part, width), low),
            vm((16, 128), wide),
            vm((8, 16, 128), low),
            vm((8, 8, 128), wide),
            vm((7, 8, 128), wide),
            vm((4, 8, 128), wide),
            vm((2, 2, seq, seq), low),
            vm((seq, width), low),
            vm((3, seq, width), low),
            vm((seq, width), low),
            vm((seq, width), wide),
            vm((seq, width), low),
            vm((seq, hidden), low),
            vm((seq, hidden), low),
            vm((seq, width), low),
            vm((seq, width), wide),
            vm((seq, width), low),
            vm((2, seq, seq), wide),
            vm((head_rows, 512), wide),
            vm((128, 512), wide),
            vm((1, width), wide),
            vm((1, width), wide),
            vm((1, width), wide),
            vm((1, width), wide),
            vm((2, 128, 128 * 7), wide),
            vm((2, seq, seq), low),
            sems((2,)),
            sems((units, Gather.slots)),
            sems((4 + units,)),
            sems((units, Scatter.slots)),
            sems((1,)),
            sems((4,)),
            sems((4,)),
            sems((2,)),
            sems((3,)),
            sems((2,)),
        ],
        compiler_params=pltpu.CompilerParams(
            collective_id=0, has_side_effects=True, vmem_limit_bytes=63 * 2**20
        ),
    )(length, x, cot, gain_a, gain_f, table, *square, inner, outer)


def finish_kernel(
    block_in, grad_in, sums_far, small, block_out, grad_out, query_out, key_out, value_out,
    output_out, gain_a, table, inner_out, outer_out, gain_f, block, grad, query, key, value, output,
    inner, outer, sums, in_sems, out_sems,
):
    units, rows, width = sums.shape
    chunks = inner.shape[1] // width
    third = width // 3
    straight = ((block_in, block, block_out), (grad_in, grad, grad_out))
    loads = [pltpu.make_async_copy(sums_far.at[n], sums.at[n], in_sems.at[n]) for n in range(units)]
    loads += [
        pltpu.make_async_copy(far, near, in_sems.at[units + n])
        for n, (far, near, _) in enumerate(straight)
    ]
    for copy in loads:
        copy.start()
    stores = []

    def store(near, far):
        stores.append(pltpu.make_async_copy(near, far, out_sems.at[len(stores)]))
        stores[-1].start()

    gain_a[...] = small[0:1, :rows]
    gain_f[...] = small[1:2, :rows]
    table[...] = small[2 : 2 + table.shape[0], : table.shape[1]]
    for i in range(chunks):
        part = pl.ds(i * rows, rows)
        loads[i].wait()
        outer[part, :] = sums[i].astype(jnp.float32)
        store(outer.at[part], outer_out.at[part])
    for i in range(chunks):
        part = pl.ds(i * width, width)
        loads[chunks + i].wait()
        inner[:, part] = sums[chunks + i].astype(jnp.float32)
        store(inner.at[:, part], inner_out.at[:, part])
    loads[2 * chunks].wait()
    output[...] = sums[2 * chunks].astype(jnp.float32)
    store(output, output_out)
    for u in range(3):
        loads[2 * chunks + 1 + u].wait()
        for n, ref in enumerate((query, key, value)):
            ref[:, u * third : (u + 1) * third] = sums[
                2 * chunks + 1 + u, :, n * third : (n + 1) * third
            ].astype(jnp.float32)
    for near, far in ((query, query_out), (key, key_out), (value, value_out)):
        store(near, far)
    for n, (_, near, far) in enumerate(straight):
        loads[units + n].wait()
        store(near, far)
    for copy in stores:
        copy.wait()


def finish_call(block, grad, sums, small, table_shape, inner_shape, outer_shape):
    units, rows, width = sums.shape
    wide = jnp.float32
    anywhere = pl.BlockSpec(memory_space=pl.ANY)
    within = pl.BlockSpec(memory_space=pltpu.VMEM)
    shapes = [(rows, width)] * 4 + [(1, rows), table_shape, inner_shape, outer_shape, (1, rows)]
    places = [anywhere] * 4 + [within] * 2 + [anywhere] * 2 + [within]
    staged = [shape for shape, place in zip(shapes, places) if place is anywhere]
    return pl.pallas_call(
        finish_kernel,
        out_shape=[
            jax.ShapeDtypeStruct(block.shape, block.dtype),
            jax.ShapeDtypeStruct(grad.shape, grad.dtype),
        ]
        + [jax.ShapeDtypeStruct(shape, wide) for shape in shapes],
        in_specs=[anywhere, anywhere, anywhere, within],
        out_specs=[anywhere, anywhere] + places,
        scratch_shapes=[
            pltpu.VMEM(block.shape, block.dtype),
            pltpu.VMEM(grad.shape, grad.dtype),
            *[pltpu.VMEM(shape, wide) for shape in staged],
            pltpu.VMEM(sums.shape, sums.dtype),
            pltpu.SemaphoreType.DMA((units + 2,)),
            pltpu.SemaphoreType.DMA((units + 2,)),
        ],
        compiler_params=pltpu.CompilerParams(vmem_limit_bytes=63 * 2**20),
    )(block, grad, sums, small)


def local_linked(
    inputs, lengths, cotangent, query_weight, key_weight, value_weight, output_weight,
    attention_gain, bias_table, inner_weight, outer_weight, feedforward_gain,
):
    rows = query_weight.shape[0]
    square = (query_weight, key_weight, value_weight, output_weight)
    block, grad, sums, small, _ = fused_call(
        lengths, inputs[0], cotangent[0], attention_gain.reshape(1, rows),
        feedforward_gain.reshape(1, rows), bias_table, square, inner_weight, outer_weight,
    )
    block, grad, query, key, value, output, gain_a, table, inner, outer, gain_f = finish_call(
        block, grad, sums, small, bias_table.shape, inner_weight.shape, outer_weight.shape
    )
    return (
        block[None], grad[None], query, key, value, output, gain_a.reshape(rows), table, inner,
        outer, gain_f.reshape(rows),
    )


def local(inputs, lengths, cotangent, *shards):
    block_output, input_grad, gradients = compute(inputs, lengths, cotangent, gather_all(*shards))
    return (block_output, input_grad) + sum_all(gradients)


def can_link(mesh):
    return mesh.shape["fsdp"] == 8 and mesh.shape["rep"] == 4


def solution(mesh):
    placed = (
        P(("fsdp", "rep"), None, None),
        P(("fsdp", "rep")),
        P(("fsdp", "rep"), None, None),
        P("fsdp", None),
        P("fsdp", None),
        P("fsdp", None),
        P("fsdp", None),
        P("fsdp"),
        P("fsdp", None),
        P("fsdp", None),
        P("fsdp", None),
        P("fsdp"),
    )
    return jax.shard_map(
        local_linked if can_link(mesh) else local,
        mesh=mesh,
        in_specs=placed,
        out_specs=(
            P(("fsdp", "rep"), None, None),
            P(("fsdp", "rep"), None, None),
            P("fsdp", None),
            P("fsdp", None),
            P("fsdp", None),
            P("fsdp", None),
            P("fsdp"),
            P("fsdp", None),
            P("fsdp", None),
            P("fsdp", None),
            P("fsdp"),
        ),
        check_vma=False,
    )
```

```python
import functools

import jax
import jax.numpy as jnp
from jax import lax
import jax.experimental.pallas as pl
import jax.experimental.pallas.tpu as pltpu
from jax.sharding import PartitionSpec as P

NB = 32


epsilon = 1e-06
highest = lax.Precision.HIGHEST
gelu_coeff = 0.7978845608028654
masked_score = -1e30


def bucket_of(offset):
    half_count = NB // 2
    exact_count = half_count // 2
    distance = jnp.abs(offset)
    beyond = jnp.full(offset.shape, exact_count, jnp.int32)
    for exponent in range(1, half_count - exact_count):
        beyond = beyond + (distance * distance >= exact_count * exact_count * 2**exponent).astype(
            jnp.int32
        )
    nearby = jnp.where(distance < exact_count, distance, beyond)
    return jnp.where(offset > 0, half_count, 0).astype(jnp.int32) + nearby


def rms_norm(values, gain_vector):
    inverse_rms = lax.rsqrt(jnp.mean(values * values, axis=-1, keepdims=True) + epsilon)
    return values * inverse_rms * gain_vector


def gelu(values):
    return (
        0.5 * values * (1.0 + jnp.tanh(gelu_coeff * (values + 0.044715 * values * values * values)))
    )


def dot(a,b): return jnp.dot(a,b,preferred_element_type=jnp.float32)
def dot_t(a,b): return lax.dot_general(a,b,(((1,),(1,)),((),())),preferred_element_type=jnp.float32)
def dot_c(a,b): return lax.dot_general(a,b,(((0,),(0,)),((),())),preferred_element_type=jnp.float32)

def fwd_kernel(T, len_ref, q_ref, k_ref, v_ref, rel_ref, o_ref, p_ref, strip):
    hp=pl.program_id(0)
    seq=q_ref.shape[0]; nb=seq//T
    lane=lax.broadcasted_iota(jnp.int32,(1,128),1)
    kcol=lax.broadcasted_iota(jnp.int32,(1,seq),1)
    mask=jnp.where(kcol<len_ref[0],0.0,-1e30)
    k=k_ref[...]; v=v_ref[...]
    for hh in range(2):
        mine=(lane>=64) if hh else (lane<64)
        rel=rel_ref[pl.ds(hh,1),:]
        W=4*T
        rolled=pltpu.roll(jnp.broadcast_to(rel,(T,W)),0,axis=1,stride=1,stride_axis=0)
        strip[:, 2*T:5*T]=rolled[:, :3*T]
        far_neg=rel[:, 0:1]; far_pos=rel[:, 3*T-1:3*T]
        strip[:, 0:2*T]=jnp.broadcast_to(far_neg,(T,2*T))
        strip[:, 5*T:7*T]=jnp.broadcast_to(far_pos,(T,2*T))
        for I in range(nb):
            q=jnp.where(mine,q_ref[I*T:(I+1)*T,:],jnp.bfloat16(0))
            s=dot_t(q,k)+(strip[:, (3-I)*T:(3-I)*T+seq]+mask)
            m=jnp.max(s,axis=-1,keepdims=True)
            e=jnp.exp(s-m)
            tot=jnp.sum(e,axis=-1,keepdims=True)
            p=(e*(1.0/tot)).astype(jnp.bfloat16)
            p_ref[hh,I*T:(I+1)*T,:]=p
            o=dot(p,v)
            if hh==0:
                o_ref[I*T:(I+1)*T,:]=o.astype(jnp.bfloat16)
            else:
                o_ref[I*T:(I+1)*T,:]=jnp.where(mine,o.astype(jnp.bfloat16),o_ref[I*T:(I+1)*T,:])

def bwd_kernel(T, q_ref, k_ref, v_ref, do_ref, p_ref, dq_ref, dk_ref, dv_ref, db_ref, ds_ref):
    seq=q_ref.shape[0]; nb=seq//T
    lane=lax.broadcasted_iota(jnp.int32,(1,128),1)
    k=k_ref[...]; v=v_ref[...]
    dks=[];dvs=[]
    for hh in range(2):
        mine=(lane>=64) if hh else (lane<64)
        acc=[None]*5
        for I in range(nb):
            sl=slice(I*T,(I+1)*T)
            do=jnp.where(mine,do_ref[sl,:],jnp.bfloat16(0))
            dp=dot_t(do,v)
            p=p_ref[hh,sl,:].astype(jnp.float32)
            t=p*dp
            delta=jnp.sum(t,axis=-1,keepdims=True)
            ds=(t-p*delta).astype(jnp.bfloat16)
            ds_ref[sl,:]=ds
            dsf=ds.astype(jnp.float32)
            for J in range(nb):
                d=min(2,max(-2,J-I))+2
                x=dsf[:,J*T:(J+1)*T]
                acc[d]=x if acc[d] is None else acc[d]+x
            dq=dot(ds,k)
            if hh==0: dq_ref[sl,:]=dq.astype(jnp.bfloat16)
            else: dq_ref[sl,:]=jnp.where(mine,dq.astype(jnp.bfloat16),dq_ref[sl,:])
        near=jnp.concatenate([acc[1],acc[2],acc[3],jnp.zeros((T,T),jnp.float32)],axis=1)
        total=shear_sum(near,4*T)
        far=jnp.concatenate([jnp.zeros((1,2*T),jnp.float32),jnp.sum(acc[4],axis=0,keepdims=True),jnp.sum(acc[0],axis=0,keepdims=True)],axis=1)
        db_ref[hh:hh+1,:]=total+far
        dk=dot_c(q_ref[...],ds_ref[...]).T; dv=dot_c(do_ref[...],p_ref[hh]).T
        dks.append(dk); dvs.append(dv)
    dk_ref[...]=jnp.where(lane<64,dks[0],dks[1]).astype(jnp.bfloat16)
    dv_ref[...]=jnp.where(lane<64,dvs[0],dvs[1]).astype(jnp.bfloat16)

def rel_hits(tile):
    slot = jnp.arange(4 * tile, dtype=jnp.int32)
    offset = jnp.where(slot < 3 * tile, slot - tile, slot - 5 * tile)
    bucket_ids = jnp.arange(NB, dtype=jnp.int32)
    return (bucket_of(offset)[None, :] == bucket_ids[:, None]).astype(jnp.bfloat16)


def rel_vec(table, tile):
    return dot_c(table, rel_hits(tile))


def shear_sum(block, width):
    rows = block.shape[0]
    while rows > 8:
        rows //= 2
        block = block[:rows] + pltpu.roll(block[rows:], width - rows, axis=1)
    total = block[0:1]
    for r in range(1, 8):
        total = total + pltpu.roll(block[r : r + 1], width - r, axis=1)
    return total


def att_fwd(q,k,v,rel,length,T=128):
    seq,D=q.shape; H=rel.shape[0]
    blk=pl.BlockSpec((seq,128),lambda h: (0,h))
    return pl.pallas_call(functools.partial(fwd_kernel,T),grid=(H//2,),
        in_specs=[pl.BlockSpec(memory_space=pltpu.SMEM),blk,blk,blk,pl.BlockSpec((None,2,4*T),lambda h:(h,0,0))],
        out_specs=[blk,pl.BlockSpec((2,seq,seq),lambda h:(h,0,0))],
        out_shape=[jax.ShapeDtypeStruct((seq,D),jnp.bfloat16),jax.ShapeDtypeStruct((H,seq,seq),jnp.bfloat16)],
        scratch_shapes=[pltpu.VMEM((T,7*T),jnp.float32)],
        compiler_params=pltpu.CompilerParams(vmem_limit_bytes=40*2**20))(length,q,k,v,rel.reshape(H//2,2,4*T))
def att_bwd(q,k,v,do,p,T=128):
    seq,D=q.shape; H=p.shape[0]
    blk=pl.BlockSpec((seq,128),lambda h: (0,h))
    o=jax.ShapeDtypeStruct((seq,D),jnp.bfloat16)
    outs=pl.pallas_call(functools.partial(bwd_kernel,T),grid=(H//2,),
        in_specs=[blk,blk,blk,blk,pl.BlockSpec((2,seq,seq),lambda h:(h,0,0))],
        out_specs=[blk,blk,blk,pl.BlockSpec((None,2,4*T),lambda h:(h,0,0))],
        out_shape=[o,o,o,jax.ShapeDtypeStruct((H//2,2,4*T),jnp.float32)],
        scratch_shapes=[pltpu.VMEM((seq,seq),jnp.bfloat16)],
        compiler_params=pltpu.CompilerParams(vmem_limit_bytes=40*2**20))(q,k,v,do,p)
    return *outs[:3],outs[3].reshape(H,4*T)

def contract_rows(left, right):
    return lax.dot_general(
        left, right, (((0,), (0,)), ((), ())), preferred_element_type=jnp.float32
    )


def contract_cols(left, right):
    return lax.dot_general(
        left, right, (((1,), (1,)), ((), ())), preferred_element_type=jnp.float32
    )


MESH = pl.DeviceIdType.MESH


def coords():
    shard = lax.axis_index("fsdp")
    copy = lax.axis_index("rep")
    return shard // 2, shard % 2, copy // 2, copy % 2


def greet(peers, at_end):
    barrier = pltpu.get_barrier_semaphore()
    for peer in peers[:-1]:
        pl.semaphore_signal(barrier, inc=1, device_id=peer, device_id_type=MESH)

    def last():
        pl.semaphore_signal(barrier, inc=1, device_id=peers[-1], device_id_type=MESH)

    pl.when(~at_end)(last)


def all_greeted(peers, at_end):
    barrier = pltpu.get_barrier_semaphore()
    pl.semaphore_wait(barrier, jnp.where(at_end, len(peers) - 1, len(peers)))


class Links:
    def __init__(self, rows, send_sems, recv_sems):
        self.send_sems, self.recv_sems = send_sems, recv_sems
        self.z, self.x, self.y, self.c = coords()
        half = rows // 2
        part = half // 3
        at = lambda start, size: pl.ds(pl.multiple_of(start, part), size)
        first = half * self.c
        other = half * (1 - self.c)
        self.half, self.other_half = at(first, half), at(other, half)
        self.plane = at(first + part * self.y, 2 * part)
        self.shared = at(first + part, part)
        self.own_third = at(first + 2 * part * self.y, part)
        self.other_third = at(first + 2 * part * (1 - self.y), part)
        self.shared_in = at(part * self.y, part)
        self.third_in = at(part * (1 - self.y), part)

    def copy(self, src, dst, g, send, slot, device):
        return pltpu.make_async_remote_copy(
            src_ref=src,
            dst_ref=dst,
            send_sem=self.send_sems.at[send],
            recv_sem=self.recv_sems.at[g, slot],
            device_id=device,
            device_id_type=MESH,
        )

    def to_x(self):
        return (self.z * 2 + 1 - self.x, self.y * 2 + self.c)

    def to_y(self):
        return (self.z * 2 + self.x, (1 - self.y) * 2 + self.c)

    def to_core(self):
        return (self.z * 2 + self.x, self.y * 2 + 1 - self.c)

    def to_z(self, k):
        return (lax.rem(self.z + k, 4) * 2 + self.x, self.y * 2 + self.c)

    def z_before(self, k):
        return lax.rem(self.z + 4 - k, 4)


class Gather(Links):
    slots = 6

    def __init__(self, full, send_sems, recv_sems):
        super().__init__(full.shape[3], send_sems, recv_sems)
        self.full = full
        self.beside = self.z + 1 - 2 * lax.rem(self.z, 2)
        self.second = lax.rem(self.z + 2, 4)
        self.across = 3 - self.z
        self.at_end = (self.z == 0) | (self.z == 3)
        self.early = range(4, 8)

    def peers(self):
        near = [self.to_x(), self.to_y(), self.to_core()]
        return near + [self.at_z(a) for a in (self.second, self.beside, self.across)]

    def block(self, g, a, rows):
        return self.full.at[a, self.x, g, rows]

    def column(self, g, rows):
        return self.full.at[:, 1 - self.x, g, rows]

    def move(self, part, g, slot, device):
        return pltpu.make_async_remote_copy(
            src_ref=part,
            dst_ref=part,
            send_sem=self.send_sems.at[0 if g in self.early else 1],
            recv_sem=self.recv_sems.at[g, slot],
            device_id=device,
            device_id_type=MESH,
        )

    def at_z(self, a):
        return (a * 2 + self.x, self.y * 2 + self.c)

    def z_copy(self, g, to, slot):
        return self.move(self.block(g, self.z, self.plane), g, slot, self.at_z(to))

    def x_copy(self, g, a):
        return self.move(self.block(g, a, self.plane), g, 3, self.to_x())

    def y_copy(self, g, a):
        return self.move(self.block(g, a, self.own_third), g, 4, self.to_y())

    def core_copy(self, g, a):
        return self.move(self.block(g, a, self.half), g, 5, self.to_core())

    def arrived(self, part, g, slot):
        pltpu.make_async_copy(part, part, self.recv_sems.at[g, slot]).wait()

    def others(self):
        return (self.beside, self.second, self.across)

    def send_z(self, g):
        self.z_copy(g, self.second, 0).start()
        self.z_copy(g, self.beside, 1).start()
        pl.when(~self.at_end)(lambda: self.z_copy(g, self.across, 2).start())

    def send_x(self, g):
        self.x_copy(g, self.z).start()

    def spread(self, g, a, slot):
        self.arrived(self.block(g, a, self.plane), g, slot)
        if slot == 0:
            part = self.block(g, a, self.plane)
            pl.when(~self.at_end)(lambda: self.move(part, g, 2, self.at_z(self.beside)).start())
        self.x_copy(g, a).start()
        self.y_copy(g, a).start()

    def after_second(self, g):
        self.spread(g, self.second, 0)

    def after_beside(self, g):
        self.spread(g, self.beside, 1)

    def after_across(self, g):
        self.spread(g, self.across, 2)

    def after_x(self, g):
        self.arrived(self.column(g, self.plane), g, 3)
        self.move(self.column(g, self.own_third), g, 4, self.to_y()).start()

    def after_y(self, g):
        third = self.own_third.size
        self.arrived(self.full.at[0, 0, 0:7, 0:third], g, 4)
        for a in self.others():
            self.core_copy(g, a).start()
        self.move(self.column(g, self.half), g, 5, self.to_core()).start()

    def after_core(self, g):
        self.arrived(self.full.at[0, 0, 0:7, 0 : self.half.size], g, 5)

    def drain(self, n):
        count = len(self.early)
        units = self.full.shape[2] - 8
        rows = self.full.shape[3] * (count if n == 0 else units - count) // units

        def wait(blocks):
            part = self.full.at[:, :, 0:blocks, 0:rows]
            pltpu.make_async_copy(part, part, self.send_sems.at[n]).wait()

        pl.when(self.at_end)(lambda: wait(10))
        pl.when(~self.at_end)(lambda: wait(11))


class SmallGather(Gather):
    def move(self, part, g, slot, device):
        return pltpu.make_async_remote_copy(
            src_ref=part,
            dst_ref=part,
            send_sem=self.send_sems.at[0],
            recv_sem=self.recv_sems.at[slot],
            device_id=device,
            device_id_type=MESH,
        )

    def __init__(self, links, full, send_sems, recv_sems):
        self.__dict__.update(links.__dict__)
        self.full, self.send_sems, self.recv_sems = full, send_sems, recv_sems

    def block(self, g, a, rows):
        return self.full.at[a * 2 + self.x]

    def y_copy(self, g, a):
        return self

    def start(self):
        pass

    def arrived(self, part, g, slot):
        pltpu.make_async_copy(part, part, self.recv_sems.at[slot]).wait()

    def after_x(self, g):
        self.arrived(self.full.at[0:4], g, 3)

    def drain(self, n):
        def wait(blocks):
            part = self.full.at[0:blocks]
            pltpu.make_async_copy(part, part, self.send_sems.at[0]).wait()

        pl.when(self.at_end)(lambda: wait(6))
        pl.when(~self.at_end)(lambda: wait(8))


class Scatter(Links):
    slots = 6

    def __init__(self, slot, full, own, from_core, from_y, from_x, from_z, send_sems, recv_sems):
        super().__init__(own.shape[1], send_sems, recv_sems)
        self.slot, self.full, self.own = slot, full, own
        self.from_core, self.from_y, self.from_x, self.from_z = from_core, from_y, from_x, from_z

    def core_copy(self, g):
        part = self.full.at[:, :, self.slot(g), self.other_half]
        ring = g % self.from_core.shape[0]
        return self.copy(part, self.from_core.at[ring], g, 0, 0, self.to_core())

    def y_copy(self, g):
        part = self.full.at[:, :, self.slot(g), self.other_third]
        return self.copy(part, self.from_y.at[g], g, 1, 1, self.to_y())

    def x_copy(self, g):
        part = self.full.at[:, 1 - self.x, self.slot(g), self.plane]
        return self.copy(part, self.from_x.at[g], g, 1, 2, self.to_x())

    def z_copy(self, g, k):
        part = self.full.at[lax.rem(self.z + k, 4), self.x, self.slot(g), self.plane]
        return self.copy(part, self.from_z.at[g, k - 1], g, 2, 3, self.to_z(k))

    def back_y_copy(self, g):
        part = self.own.at[g, self.plane]
        return self.copy(part, self.from_z.at[g, 3], g, 4 + g, 4, self.to_y())

    def back_core_copy(self, g):
        part = self.own.at[g, self.half]
        return self.copy(part, part, g, 3, 5, self.to_core())

    def start(self, g):
        self.core_copy(g).start()

    def after_core(self, g):
        self.core_copy(g).wait_recv()
        ring = g % self.from_core.shape[0]
        for a in range(4):
            for b in range(2):
                self.full[a, b, self.slot(g), self.half] += self.from_core[ring, a, b]
        self.y_copy(g).start()

    def after_y(self, g):
        self.y_copy(g).wait_recv()
        for a in range(4):
            for b in range(2):
                self.full[a, b, self.slot(g), self.own_third] += self.from_y[g, a, b]
        self.x_copy(g).start()

    def after_x(self, g):
        self.x_copy(g).wait_recv()
        for a in range(4):
            self.full[a, self.x, self.slot(g), self.plane] += self.from_x[g, a]
        for k in (1, 2, 3):
            self.z_copy(g, k).start()

    def after_z(self, g):
        total = self.full[self.z, self.x, self.slot(g), self.plane].astype(jnp.float32)
        part = self.from_z.at[g, 0:3]
        pltpu.make_async_copy(part, part, self.recv_sems.at[g, 3]).wait()
        for k in (1, 2, 3):
            total = total + self.from_z[g, k - 1].astype(jnp.float32)
        self.own[g, self.plane] = total.astype(jnp.bfloat16)
        self.back_y_copy(g).start()

    def after_back_y(self, g):
        self.back_y_copy(g).wait_recv()
        self.back_y_copy(g).wait_send()
        got = self.from_z.at[g, 3]
        self.own[g, self.shared] += got[self.shared_in]
        self.own[g, self.other_third] = got[self.third_in]
        self.back_core_copy(g).start()

    def after_back_core(self, g):
        part = self.own.at[g, self.other_half]
        self.copy(part, part, g, 3, 5, self.to_core()).wait_recv()

    def drain(self):
        units, rows = self.own.shape[:2]
        half = rows // 2
        for n, part in (
            (0, self.full.at[:, :, 0 : units // 2]),
            (1, self.full.at[:, :, 0 : units // 3]),
            (2, self.full.at[:, :, 0 : units // 4, 0:half]),
            (3, self.own.at[0 : units // 2]),
        ):
            pltpu.make_async_copy(part, part, self.send_sems.at[n]).wait()


def compute(inputs, lengths, cotangent, weights):
    (
        full_query, full_key, full_value, full_output, full_gain, full_table, full_inner,
        full_outer, full_ffn_gain,
    ) = weights
    pairs_here, seq_len, model_width = inputs.shape
    row_count = pairs_here * seq_len
    head_count = full_table.shape[1]
    tile = 128
    relative = rel_vec(full_table, tile)
    flat_inputs = inputs.reshape(row_count, model_width).astype(jnp.float32)
    normed = rms_norm(flat_inputs, full_gain.astype(jnp.float32)).astype(jnp.bfloat16)
    joined = jnp.concatenate((full_query, full_key, full_value), axis=1)
    projected = jnp.dot(normed, joined, preferred_element_type=jnp.float32).astype(jnp.bfloat16)
    queries = projected[:, :model_width]
    key_rows = projected[:, model_width : 2 * model_width]
    value_rows = projected[:, 2 * model_width :]
    pair_rows = [slice(n * seq_len, (n + 1) * seq_len) for n in range(pairs_here)]
    forward_parts = [
        att_fwd(queries[r], key_rows[r], value_rows[r], relative, lengths[n : n + 1], tile)
        for n, r in enumerate(pair_rows)
    ]
    attended = jnp.concatenate([part[0] for part in forward_parts], axis=0)
    middle = flat_inputs + jnp.dot(attended, full_output, preferred_element_type=jnp.float32)
    normed_ffn = rms_norm(middle, full_ffn_gain.astype(jnp.float32)).astype(jnp.bfloat16)
    raised = jnp.dot(normed_ffn, full_inner, preferred_element_type=jnp.float32)
    active = gelu(raised).astype(jnp.bfloat16)
    lowered = jnp.dot(active, full_outer, preferred_element_type=jnp.float32)
    block_output = (middle + lowered).astype(jnp.bfloat16).reshape(pairs_here, seq_len, model_width)
    positions = jnp.arange(seq_len, dtype=jnp.int32)
    row_live = (positions[None, :] < lengths[:, None]).astype(jnp.float32)
    seed_rows = (cotangent.astype(jnp.float32) * row_live[:, :, None]).reshape(
        row_count, model_width
    )
    seed_low = seed_rows.astype(jnp.bfloat16)
    grad_active = contract_cols(seed_low, full_outer)
    grad_outer = contract_rows(active, seed_low)
    grad_raised = jax.vjp(gelu, raised)[1](grad_active)[0].astype(jnp.bfloat16)
    grad_inner = contract_rows(normed_ffn, grad_raised)
    grad_normed_ffn = contract_cols(grad_raised, full_inner)
    ffn_pull = jax.vjp(rms_norm, middle, full_ffn_gain.astype(jnp.float32))[1]
    grad_middle_part, grad_ffn_gain = ffn_pull(grad_normed_ffn)
    grad_middle = seed_rows + grad_middle_part
    joined = jnp.concatenate((full_query, full_key, full_value), axis=1)
    middle_low = grad_middle.astype(jnp.bfloat16)
    grad_attended = contract_cols(middle_low, full_output).astype(jnp.bfloat16)
    grad_output = contract_rows(attended, middle_low)
    backward_parts = [
        att_bwd(
            queries[r], key_rows[r], value_rows[r], grad_attended[r], forward_parts[n][1], tile
        )
        for n, r in enumerate(pair_rows)
    ]
    grad_projected = jnp.concatenate(
        [jnp.concatenate(part[:3], axis=1) for part in backward_parts], axis=0
    )
    grad_joined = contract_rows(normed, grad_projected)
    grad_normed = contract_cols(grad_projected, joined)
    attention_pull = jax.vjp(rms_norm, flat_inputs, full_gain.astype(jnp.float32))[1]
    grad_inputs_part, grad_attention_gain = attention_pull(grad_normed)
    input_grad = (grad_middle + grad_inputs_part).reshape(pairs_here, seq_len, model_width)
    grad_relative = sum(part[3] for part in backward_parts)
    grad_table = lax.dot_general(
        rel_hits(tile).astype(jnp.float32),
        grad_relative,
        (((1,), (1,)), ((), ())),
        precision=highest,
    )
    return block_output, input_grad, (
        grad_joined[:, :model_width],
        grad_joined[:, model_width : 2 * model_width],
        grad_joined[:, 2 * model_width :],
        grad_output,
        grad_attention_gain,
        grad_table,
        grad_inner,
        grad_outer,
        grad_ffn_gain,
    )


def gather_all(query_weight, key_weight, value_weight, output_weight, attention_gain, bias_table,
               inner_weight, outer_weight, feedforward_gain):
    return tuple(
        lax.all_gather(part, "fsdp", axis=0, tiled=True)
        for part in (
            query_weight, key_weight, value_weight, output_weight, attention_gain, bias_table,
            inner_weight, outer_weight, feedforward_gain,
        )
    )


def sum_all(gradients):
    def one(part):
        part = lax.psum_scatter(
            part.astype(jnp.bfloat16), "fsdp", scatter_dimension=0, tiled=True
        )
        return lax.psum(part, "rep").astype(jnp.float32)

    return tuple(one(part) for part in gradients)


def gelu_parts(z):
    square = z * z
    t = jnp.tanh(gelu_coeff * z * (1.0 + 0.044715 * square))
    half = 0.5 * (1.0 + t)
    slope = half + (0.5 * gelu_coeff) * z * (1.0 - t * t) * (1.0 + (3 * 0.044715) * square)
    return z * half, slope


def lanes(start, size):
    return pl.ds(start if isinstance(start, int) else pl.multiple_of(start, 128), size)


def rows_at(start, size):
    return pl.ds(pl.multiple_of(start, size), size)


def loop(count, body):
    def step(n, carry):
        body(n)
        return carry

    lax.fori_loop(0, count, step, 0)


def norm_back(grad, gain, values):
    inverse = lax.rsqrt(jnp.mean(values * values, axis=-1, keepdims=True) + epsilon)
    scaled = grad * gain
    centre = jnp.mean(scaled * values, axis=-1, keepdims=True)
    back = inverse * scaled - values * (inverse * inverse * inverse * centre)
    return back, jnp.sum(grad * values * inverse, axis=0, keepdims=True)


class Layer:
    def __init__(self, **refs):
        self.__dict__.update(refs)
        self.seq, self.width = self.x.shape
        self.tile = 128
        self.row_block = 128
        self.shard_rows = self.bank.shape[3]

    def unit(self, u, column=None, size=None):
        if column is None:
            block = self.bank[:, :, u]
        else:
            block = self.bank[:, :, u, :, lanes(column, size)]
        return block.reshape(-1, block.shape[-1])

    def row_chunks(self, body):
        size = self.row_block
        loop(self.seq // size, lambda n: body(rows_at(n * size, size)))

    def small_arrays(self):
        flat = self.all_small[...].reshape(-1, 128)
        tile = self.tile
        slot = lax.broadcasted_iota(jnp.int32, (flat.shape[0], 4 * tile), 1)
        offset = jnp.where(slot < 3 * tile, slot - tile, slot - 5 * tile)
        row = lax.broadcasted_iota(jnp.int32, (flat.shape[0], 4 * tile), 0)
        per = NB // 8
        inside = row % 16 - 2
        wanted = jnp.where((inside >= 0) & (inside < per), (row // 16) * per + inside, -1)
        hits = (bucket_of(offset) == wanted).astype(jnp.bfloat16)
        self.rel[...] = dot_c(flat, hits)[: self.rel.shape[0]]
        for index, ref in ((0, self.gain_a), (1, self.gain_f)):
            total = jnp.zeros((1, self.width), jnp.float32)
            for shard in range(8):
                part = self.all_small[shard].astype(jnp.float32)[index : index + 1]
                wide = jnp.concatenate(
                    [part, jnp.zeros((1, self.width - 128), jnp.float32)], axis=1
                )
                total = total + (
                    pltpu.roll(wide, shard * self.shard_rows, axis=1) if shard else wide
                )
            ref[...] = total

    def norm_in(self):
        gain = self.gain_a[...]

        def body(r):
            self.normed[r] = rms_norm(self.x[r].astype(jnp.float32), gain).astype(jnp.bfloat16)

        self.row_chunks(body)

    def mask_seed(self):
        def body(r):
            index = lax.broadcasted_iota(jnp.int32, (self.row_block, 1), 0) + r.start
            live = index < self.length[0]
            self.seed[r] = jnp.where(live, self.seed[r], jnp.bfloat16(0))

        self.row_chunks(body)

    def project(self, u):
        def body(n):
            self.qkv[u, :, lanes(n * 256, 256)] = dot(
                self.normed[...], self.unit(u, n * 256, 256)
            ).astype(jnp.bfloat16)

        loop(self.width // 256, body)

    def strip_for(self, head, strip):
        tile = self.tile
        rel = self.rel[pl.ds(head, 1), :]
        rolled = pltpu.roll(
            jnp.broadcast_to(rel, (tile, 4 * tile)), 0, axis=1, stride=1, stride_axis=0
        )
        strip[:, 2 * tile : 5 * tile] = rolled[:, : 3 * tile]
        strip[:, : 2 * tile] = jnp.broadcast_to(rel[:, :1], (tile, 2 * tile))
        strip[:, 5 * tile :] = jnp.broadcast_to(rel[:, 3 * tile - 1 : 3 * tile], (tile, 2 * tile))

    def pair_lanes(self, slot):
        third = self.width // 3
        return [lanes(slot * 128 + n * third, 128) for n in range(3)]

    def probs_store(self, pair, slot):
        return pltpu.make_async_copy(
            self.probs.at[slot], self.probs_far.at[pair], self.probs_sems.at[slot]
        )

    def probs_load(self, pair, slot):
        return pltpu.make_async_copy(
            self.probs_far.at[pair], self.probs.at[slot], self.probs_sems.at[slot]
        )

    def attend(self, unit, slot):
        tile, seq = self.tile, self.seq
        pair = 2 * unit + slot
        if unit > 0:
            self.probs_store(pair, slot).wait()
        lane = lax.broadcasted_iota(jnp.int32, (1, 128), 1)
        own = (lane < 64, lane >= 64)
        key_at = lax.broadcasted_iota(jnp.int32, (1, seq), 1)
        mask = jnp.where(key_at < self.length[0], 0.0, masked_score)
        q_at, k_at, v_at = self.pair_lanes(slot)
        q = self.qkv[unit, :, q_at]
        k = self.qkv[unit, :, k_at]
        v = self.qkv[unit, :, v_at]
        for head in range(2):
            self.strip_for(pair * 2 + head, self.strip.at[head])
            self.scores[head] = dot_t(jnp.where(own[head], q, jnp.bfloat16(0)), k)

        def soften(head):
            for block in range(seq // tile):
                r = slice(block * tile, (block + 1) * tile)
                first = (seq // tile - 1 - block) * tile
                bias = self.strip[head, :, first : first + seq]
                scores = self.scores[head, r, :] + (bias + mask)
                peak = jnp.max(scores, axis=-1, keepdims=True)
                raised = jnp.exp(scores - peak)
                total = jnp.sum(raised, axis=-1, keepdims=True)
                self.probs[slot, head, r, :] = (raised * (1.0 / total)).astype(jnp.bfloat16)
            return dot(self.probs[slot, head], v)

        outs = [soften(head) for head in range(2)]
        self.attended[:, lanes(pair * 128, 128)] = jnp.where(own[0], *outs).astype(jnp.bfloat16)
        self.probs_store(pair, slot).start()

    def middle_rows(self):
        def body(n):
            c = lanes(n * 256, 256)
            self.middle[:, c] = self.x[:, c].astype(jnp.float32) + dot(
                self.attended[...], self.unit(3, n * 256, 256)
            )

        loop(self.width // 256, body)
        gain = self.gain_f[...]

        def norm(r):
            self.normed_ffn[r] = rms_norm(self.middle[r], gain).astype(jnp.bfloat16)

        self.row_chunks(norm)

    def raise_unit(self, i):
        def body(n):
            raised = dot(self.normed_ffn[...], self.unit(4 + i, n * 256, 256))
            active, slope = gelu_parts(raised)
            c = lanes(i * self.width + n * 256, 256)
            self.active[:, c] = active.astype(jnp.bfloat16)
            self.slope[:, c] = slope.astype(jnp.bfloat16)

        loop(self.width // 256, body)

    def outer_grad(self, shard):
        size = 4 * self.shard_rows
        block = dot_c(self.active[:, lanes(shard * size, size)], self.seed[...])
        self.bank[shard // 2, shard % 2, 12:16] = block.astype(jnp.bfloat16).reshape(
            4, self.shard_rows, self.width
        )

    def lower(self, n):
        outer = self.bank[:, :, 8:12, :, lanes(n * 256, 256)].reshape(-1, 256)
        c = lanes(n * 256, 256)
        self.mid_low[:, c] = (self.middle[:, c] + dot(self.active[...], outer)).astype(
            jnp.bfloat16
        )

    def raised_grad(self, shard):
        size = 4 * self.shard_rows
        outer = self.bank[shard // 2, shard % 2, 8:12].reshape(size, self.width)
        c = lanes(shard * size, size)
        grad = dot_t(self.seed[...], outer) * self.slope[:, c].astype(jnp.float32)
        self.slope[:, c] = grad.astype(jnp.bfloat16)

    def inner_grad(self, i):
        def body(n):
            c = lanes(i * self.width + n * 256, 256)
            block = dot_c(self.normed_ffn[...], self.slope[:, c]).astype(jnp.bfloat16)
            self.bank[:, :, 16 + i, :, lanes(n * 256, 256)] = block.reshape(
                4, 2, self.shard_rows, 256
            )

        loop(self.width // 256, body)

    def middle_grad(self, part):
        total = None
        for i in range(4):
            inner = self.bank[2 * part : 2 * part + 2, :, 4 + i].reshape(-1, self.width)
            term = dot_t(self.slope[:, i * self.width : (i + 1) * self.width], inner)
            total = term if total is None else total + term
        size = self.width // 2
        self.grad_mid[:, part * size : (part + 1) * size] = total

    def middle_norm(self):
        gain = self.gain_f[...]
        self.gain_f_grad[...] = jnp.zeros_like(self.gain_f_grad)

        def body(r):
            back, terms = norm_back(self.grad_mid[r], gain, self.middle[r])
            total = self.seed[r].astype(jnp.float32) + back
            self.gain_f_grad[...] += terms
            self.grad_mid[r] = total
            self.mid_low[r] = total.astype(jnp.bfloat16)

        self.row_chunks(body)

    def square_grad(self, left, right, slot):
        def body(n):
            block = dot_c(left[...], right(lanes(n * 256, 256))).astype(jnp.bfloat16)
            self.bank[:, :, slot, :, lanes(n * 256, 256)] = block.reshape(
                4, 2, self.shard_rows, 256
            )

        loop(self.width // 256, body)

    def attended_grad(self):
        size = self.width // 2
        for part in range(2):
            weight = self.bank[2 * part : 2 * part + 2, :, 3].reshape(size, self.width)
            self.attended[:, part * size : (part + 1) * size] = dot_t(
                self.mid_low[...], weight
            ).astype(jnp.bfloat16)

    def attend_back(self, unit, slot):
        tile, seq = self.tile, self.seq
        pair = 2 * unit + slot
        self.probs_load(pair, slot).wait()
        lane = lax.broadcasted_iota(jnp.int32, (1, 128), 1)
        own = (lane < 64, lane >= 64)
        q_at, k_at, v_at = self.pair_lanes(slot)
        q = self.qkv[unit, :, q_at]
        k = self.qkv[unit, :, k_at]
        v = self.qkv[unit, :, v_at]
        grad_out = self.attended[:, lanes(pair * 128, 128)]
        blocks = seq // tile
        for head in range(2):
            self.scores[head] = dot_t(jnp.where(own[head], grad_out, jnp.bfloat16(0)), v)

        def back(head):
            sums = [None] * 5
            for block in range(blocks):
                r = slice(block * tile, (block + 1) * tile)
                probs = self.probs[slot, head, r, :].astype(jnp.float32)
                weighted = probs * self.scores[head, r, :]
                centre = jnp.sum(weighted, axis=-1, keepdims=True)
                grad = weighted - probs * centre
                self.grad_scores[head, r, :] = grad.astype(jnp.bfloat16)
                for other in range(blocks):
                    apart = min(2, max(-2, other - block)) + 2
                    part = grad[:, other * tile : (other + 1) * tile]
                    sums[apart] = part if sums[apart] is None else sums[apart] + part
            zero = jnp.zeros((tile, tile), jnp.float32)
            near = shear_sum(jnp.concatenate([sums[1], sums[2], sums[3], zero], axis=1), 4 * tile)
            far = jnp.concatenate(
                [
                    jnp.zeros((1, 2 * tile), jnp.float32),
                    jnp.sum(sums[4], axis=0, keepdims=True),
                    jnp.sum(sums[0], axis=0, keepdims=True),
                ],
                axis=1,
            )
            self.rel_grad[pl.ds(pair * 2 + head, 1), :] = near + far
            return (
                dot(self.grad_scores[head], k),
                dot_c(q, self.grad_scores[head]).T,
                dot_c(grad_out, self.probs[slot, head]).T,
            )

        for at, first, second in zip((q_at, k_at, v_at), back(0), back(1)):
            self.qkv[unit, :, at] = jnp.where(own[0], first, second).astype(jnp.bfloat16)
        if 2 * unit + 2 < self.probs_far.shape[0]:
            self.probs_load(pair + 2, slot).start()

    def normed_grad(self, part):
        size = self.width // 2
        total = None
        for u in range(3):
            weight = self.bank[2 * part : 2 * part + 2, :, u].reshape(size, self.width)
            term = dot_t(self.qkv[u], weight)
            total = term if total is None else total + term
        self.middle[:, part * size : (part + 1) * size] = total

    def input_grad(self):
        gain = self.gain_a[...]
        self.gain_a_grad[...] = jnp.zeros_like(self.gain_a_grad)

        def body(r):
            back, terms = norm_back(self.middle[r], gain, self.x[r].astype(jnp.float32))
            self.gain_a_grad[...] += terms
            self.grad_mid[r] += back

        self.row_chunks(body)

    def small_grads(self):
        tile = self.tile
        shape = (64, 4 * tile)
        slot = lax.broadcasted_iota(jnp.int32, shape, 1)
        offset = jnp.where(slot < 3 * tile, slot - tile, slot - 5 * tile)
        row = lax.broadcasted_iota(jnp.int32, shape, 0)
        per = NB // 8
        inside = row % 8 - 2
        wanted = jnp.where((inside >= 0) & (inside < per), (row // 8) * per + inside, -1)
        hits = (bucket_of(offset) == wanted).astype(jnp.float32)
        table = lax.dot_general(
            hits,
            self.rel_grad[...],
            (((1,), (1,)), ((), ())),
            precision=highest,
            preferred_element_type=jnp.float32,
        )
        rows = lax.broadcasted_iota(jnp.int32, (8, 128), 0)
        lane = lax.broadcasted_iota(jnp.int32, (8, 128), 1)
        for shard in range(8):
            block = table[8 * shard : 8 * shard + 8]
            for index, ref in ((0, self.gain_a_grad), (1, self.gain_f_grad)):
                wide = ref[...]
                if shard:
                    wide = pltpu.roll(wide, self.width - shard * self.shard_rows, axis=1)
                here = (rows == index) & (lane < self.shard_rows)
                block = jnp.where(here, jnp.broadcast_to(wide[:, :128], (8, 128)), block)
            self.small_out[shard] = block


(
    SEND_Z, SEND_X, GOT_SECOND, GOT_BESIDE, GOT_ACROSS, GOT_X, GOT_Y, GOT_CORE, DRAIN, SMALL_Z,
    SMALL_X, SMALL_SECOND, SMALL_BESIDE, SMALL_ACROSS, SUM_SEND, SUM_CORE, SUM_Y, SUM_X, SUM_Z,
    SUM_BACK, SUM_DONE, NORM, PROJECT, ATTEND, MIDDLE, RAISE, OUTER_GRAD, LOWER, RAISED_GRAD,
    INNER_GRAD, MIDDLE_GRAD, MIDDLE_NORM, OUTPUT_GRAD, ATTENDED_GRAD, ATTEND_BACK, SQUARE_GRAD,
    NORMED_GRAD, INPUT_GRAD, SMALL, SMALL_SUM, SMALL_DONE,
) = range(41)

ORDER = (
    (SMALL_Z, 0), (SMALL_X, 0), (SEND_X, 4), (SEND_Z, 1), (SEND_X, 7), (SEND_X, 1), (SEND_X, 2),
    (SEND_X, 0), (SEND_Z, 0), (GOT_SECOND, 1), (GOT_SECOND, 0), (SMALL_SECOND, 0),
    (SMALL_BESIDE, 0), (SMALL_ACROSS, 0), (SEND_X, 6), (SEND_Z, 2), (GOT_BESIDE, 1), (NORM, 0),
    (GOT_ACROSS, 1), (SEND_Z, 3), (GOT_ACROSS, 0), (GOT_BESIDE, 0), (GOT_BESIDE, 2),
    (GOT_SECOND, 2), (GOT_X, 1), (SEND_Z, 5), (GOT_X, 0), (SEND_X, 3), (GOT_ACROSS, 2),
    (GOT_SECOND, 3), (SEND_Z, 4), (GOT_SECOND, 5), (GOT_ACROSS, 3), (GOT_BESIDE, 5), (GOT_Y, 1),
    (GOT_Y, 0), (GOT_X, 2), (GOT_BESIDE, 3), (SEND_Z, 6), (SEND_Z, 11), (SEND_X, 5),
    (GOT_CORE, 1), (PROJECT, 1), (GOT_CORE, 0), (GOT_SECOND, 4), (PROJECT, 0), (SEND_Z, 7),
    (GOT_ACROSS, 5), (GOT_Y, 2), (SEND_X, 11), (GOT_X, 3), (GOT_BESIDE, 4), (ATTEND, 0),
    (GOT_SECOND, 6), (SEND_Z, 9), (GOT_ACROSS, 4), (GOT_X, 5), (GOT_BESIDE, 6), (GOT_CORE, 2),
    (PROJECT, 2), (GOT_BESIDE, 11), (GOT_SECOND, 11), (ATTEND, 1), (GOT_ACROSS, 6), (GOT_X, 4),
    (GOT_Y, 3), (GOT_SECOND, 7), (SEND_Z, 10), (ATTEND, 2), (GOT_Y, 5), (SEND_Z, 8),
    (GOT_ACROSS, 7), (GOT_BESIDE, 7), (GOT_SECOND, 9), (GOT_CORE, 3), (GOT_X, 6), (SEND_X, 9),
    (GOT_Y, 4), (MIDDLE, 0), (GOT_BESIDE, 9), (GOT_ACROSS, 11), (GOT_CORE, 5), (GOT_CORE, 4),
    (RAISE, 0), (GOT_ACROSS, 9), (GOT_X, 7), (GOT_SECOND, 8), (GOT_Y, 6), (RAISE, 1),
    (GOT_ACROSS, 8), (GOT_BESIDE, 8), (GOT_BESIDE, 10), (SEND_X, 8), (GOT_CORE, 6), (RAISE, 2),
    (GOT_X, 11), (GOT_Y, 7), (GOT_SECOND, 10), (OUTER_GRAD, 0), (GOT_X, 9), (GOT_CORE, 7),
    (GOT_ACROSS, 10), (RAISE, 3), (SEND_X, 10), (GOT_X, 8), (GOT_Y, 11), (OUTER_GRAD, 1),
    (GOT_X, 10), (SUM_SEND, 0), (SUM_SEND, 1), (GOT_Y, 9), (SUM_CORE, 0), (GOT_Y, 8),
    (SUM_CORE, 1), (DRAIN, 0), (GOT_Y, 10), (GOT_CORE, 9), (GOT_CORE, 11), (SUM_SEND, 2),
    (GOT_CORE, 8), (SUM_SEND, 3), (GOT_CORE, 10), (RAISED_GRAD, 0), (SUM_Y, 0), (SUM_CORE, 2),
    (INNER_GRAD, 0), (SUM_CORE, 3), (SUM_SEND, 4), (LOWER, 0), (SUM_Y, 1), (RAISED_GRAD, 1),
    (SUM_SEND, 5), (SUM_CORE, 4), (LOWER, 1), (SUM_X, 0), (SUM_Y, 2), (MIDDLE_GRAD, 0),
    (SUM_X, 1), (INNER_GRAD, 1), (SUM_SEND, 6), (SUM_CORE, 5), (SUM_Y, 3), (MIDDLE_GRAD, 1),
    (SUM_CORE, 6), (LOWER, 2), (SUM_X, 2), (SUM_SEND, 7), (MIDDLE_NORM, 0), (SUM_Y, 4),
    (OUTPUT_GRAD, 0), (ATTENDED_GRAD, 0), (SUM_X, 3), (SUM_SEND, 8), (SUM_CORE, 7),
    (ATTEND_BACK, 0), (SUM_X, 4), (SUM_Y, 5), (SUM_CORE, 8), (ATTEND_BACK, 1), (SUM_Y, 7),
    (SUM_Z, 4), (SUM_X, 5), (SQUARE_GRAD, 0), (SUM_SEND, 9), (SQUARE_GRAD, 1), (SUM_Y, 8),
    (SUM_Z, 0), (SUM_SEND, 10), (SUM_Y, 6), (SUM_Z, 1), (SUM_CORE, 9), (SUM_X, 7),
    (ATTEND_BACK, 2), (SUM_X, 8), (SUM_CORE, 10), (SQUARE_GRAD, 2), (SUM_Y, 9), (SUM_SEND, 11),
    (SUM_X, 6), (SUM_CORE, 11), (SUM_Z, 3), (SUM_Z, 2), (SUM_BACK, 4), (NORMED_GRAD, 0),
    (SUM_Y, 10), (NORMED_GRAD, 1), (SUM_X, 9), (INPUT_GRAD, 0), (SUM_BACK, 1), (SUM_Y, 11),
    (SUM_Z, 5), (SUM_Z, 7), (SUM_Z, 8), (SUM_X, 10), (SUM_BACK, 2), (SUM_BACK, 5), (SUM_DONE, 2),
    (SUM_Z, 6), (SUM_X, 11), (SUM_BACK, 6), (SMALL, 0), (SUM_BACK, 7), (SUM_BACK, 3), (SUM_Z, 10),
    (SUM_Z, 9), (SMALL_SUM, 0), (SUM_BACK, 0), (SUM_Z, 11), (SUM_DONE, 5), (SUM_DONE, 3),
    (SUM_DONE, 1), (SUM_BACK, 10), (SUM_BACK, 8), (SUM_DONE, 0), (SMALL_DONE, 0), (SUM_DONE, 8),
    (SUM_DONE, 6), (SUM_BACK, 9), (SUM_BACK, 11), (SUM_DONE, 9), (SUM_DONE, 10), (SUM_DONE, 7),
    (SUM_DONE, 4), (SUM_DONE, 11),
)


def order_slot(n):
    return n + 12 if n < 8 else (7 if n == 8 else n - 5)


def fused_kernel(
    length, x, cot, gain_a_own, gain_f_own, table_own, query_own, key_own, value_own, output_own,
    inner_own, outer_own,
    block_far, grad_far, own_far, small_result, probs_far,
    bank, own_sum, from_core, from_y, from_x, from_z, small_wide, all_small, small_out,
    small_in, small_rep, probs, normed, qkv, attended, middle, normed_ffn, active, slope, seed,
    grad_mid, mid_low, scores, rel, rel_grad, gain_a, gain_f, gain_a_grad,
    gain_f_grad, strip, grad_scores,
    sends, recvs, sum_sends, sum_recvs, small_sends, small_recvs, back_sems, probs_sems,
    misc_sems, keep_sems,
):
    shard = lax.axis_index("fsdp")
    copy_id = lax.axis_index("rep")
    layer = Layer(
        length=length, x=x, bank=bank, all_small=all_small, small_out=small_out,
        probs=probs, probs_far=probs_far, probs_sems=probs_sems, normed=normed, qkv=qkv,
        attended=attended, middle=middle, normed_ffn=normed_ffn, active=active, slope=slope,
        seed=seed, grad_mid=grad_mid, mid_low=mid_low, scores=scores,
        rel=rel, rel_grad=rel_grad, gain_a=gain_a, gain_f=gain_f, gain_a_grad=gain_a_grad,
        gain_f_grad=gain_f_grad, strip=strip, grad_scores=grad_scores,
    )
    rows, width = query_own.shape
    chunks = inner_own.shape[1] // width
    units = 4 + 2 * chunks
    gather = Gather(bank, sends, recvs)
    scatter = Scatter(
        order_slot, bank, own_sum, from_core, from_y, from_x, from_z, sum_sends, sum_recvs
    )
    pairs = probs_far.shape[0]

    def remote(src, dst, send, recv, device):
        return pltpu.make_async_remote_copy(
            src_ref=src, dst_ref=dst, send_sem=send, recv_sem=recv, device_id=device,
            device_id_type=MESH,
        )

    def peer(k):
        return (lax.rem(shard + k, 8), copy_id)

    def rep_peer(k):
        return (shard, lax.rem(copy_id + k, 4))

    parts = [output_own]
    parts += [inner_own.at[:, pl.ds(i * width, width)] for i in range(chunks)]
    parts += [outer_own.at[pl.ds(i * rows, rows)] for i in range(chunks)]
    third = width // 3
    homes = [
        (part.at[:, pl.ds(u * third, third)], bank.at[gather.z, gather.x, u, :, pl.ds(n * third, third)])
        for u in range(3)
        for n, part in enumerate((query_own, key_own, value_own))
    ]
    homes += [(part, bank.at[gather.z, gather.x, 3 + u]) for u, part in enumerate(parts)]
    keeps = [
        pltpu.make_async_copy(part, home, keep_sems.at[0]) for part, home in homes
    ]
    keep_seed = pltpu.make_async_copy(cot, seed, keep_sems.at[1])
    keeps.append(keep_seed)
    peers = gather.peers()
    greet(peers, gather.at_end)
    for copy in keeps:
        copy.start()
    small_wide[...] = jnp.zeros_like(small_wide)
    small_wide[0:1, :rows] = gain_a_own[...].astype(jnp.float32)
    small_wide[1:2, :rows] = gain_f_own[...].astype(jnp.float32)
    per, heads = table_own.shape
    small_wide[2 : 2 + per, :heads] = table_own[...].astype(jnp.float32)
    all_small[shard] = small_wide[...].astype(jnp.bfloat16)
    smalls = SmallGather(gather, all_small, small_sends, small_recvs)
    mine = bank.at[gather.z, gather.x, 0:units]
    pltpu.make_async_copy(mine, mine, keep_sems.at[0]).wait()
    all_greeted(peers, gather.at_end)

    def store(n):
        return pltpu.make_async_copy(own_sum.at[n], own_far.at[n], misc_sems.at[2])

    def sum_done(n):
        scatter.after_back_core(n)
        store(n).start()

    block_store = pltpu.make_async_copy(mid_low, block_far, misc_sems.at[0])
    grad_store = pltpu.make_async_copy(grad_mid, grad_far, misc_sems.at[1])
    back_copies = [
        remote(
            small_out.at[lax.rem(shard + k, 8)], small_in.at[k - 1], back_sems.at[0],
            back_sems.at[1], peer(k),
        )
        for k in range(1, 8)
    ]
    rep_copies = [
        remote(
            small_rep.at[copy_id], small_rep.at[copy_id], back_sems.at[2], back_sems.at[3],
            rep_peer(k),
        )
        for k in range(1, 4)
    ]

    def wait_for(part, sem):
        pltpu.make_async_copy(part, part, sem).wait()

    def norm(_):
        keep_seed.wait()
        layer.mask_seed()
        smalls.after_x(0)
        layer.small_arrays()
        layer.norm_in()

    def middle_rows(_):
        layer.middle_rows()
        for pair in (pairs - 2, pairs - 1):
            layer.probs_store(pair, pair % 2).wait()
        for pair in (0, 1):
            layer.probs_load(pair, pair).start()

    def lower(n):
        layer.lower(n)
        if n == width // 256 - 1:
            block_store.start()

    def middle_norm(_):
        block_store.wait()
        layer.middle_norm()
        rel_grad[...] = jnp.zeros_like(rel_grad)

    def input_grad(_):
        layer.input_grad()
        grad_store.start()

    def small_sums(_):
        layer.small_grads()
        for copy in back_copies:
            copy.start()

    def small_sum(_):
        wait_for(small_in, back_sems.at[1])
        total = small_out[shard]
        for k in range(7):
            total = total + small_in[k]
        small_rep[copy_id] = total
        for copy in rep_copies:
            copy.start()

    def small_done(_):
        wait_for(small_rep.at[0:3], back_sems.at[3])
        small_result[...] = (small_rep[0] + small_rep[1]) + (small_rep[2] + small_rep[3])

    work = {
        SEND_Z: gather.send_z,
        SEND_X: gather.send_x,
        GOT_SECOND: gather.after_second,
        GOT_BESIDE: gather.after_beside,
        GOT_ACROSS: gather.after_across,
        GOT_X: gather.after_x,
        GOT_Y: gather.after_y,
        GOT_CORE: gather.after_core,
        DRAIN: gather.drain,
        SMALL_Z: smalls.send_z,
        SMALL_X: smalls.send_x,
        SMALL_SECOND: smalls.after_second,
        SMALL_BESIDE: smalls.after_beside,
        SMALL_ACROSS: smalls.after_across,
        SUM_SEND: scatter.start,
        SUM_CORE: scatter.after_core,
        SUM_Y: scatter.after_y,
        SUM_X: scatter.after_x,
        SUM_Z: scatter.after_z,
        SUM_BACK: scatter.after_back_y,
        SUM_DONE: sum_done,
        NORM: norm,
        PROJECT: layer.project,
        ATTEND: lambda u: loop(2, functools.partial(layer.attend, u)),
        MIDDLE: middle_rows,
        RAISE: layer.raise_unit,
        OUTER_GRAD: lambda k: loop(4, lambda n: layer.outer_grad(4 * k + n)),
        LOWER: lower,
        RAISED_GRAD: lambda k: loop(4, lambda n: layer.raised_grad(4 * k + n)),
        INNER_GRAD: lambda k: loop(2, lambda n: layer.inner_grad(2 * k + n)),
        MIDDLE_GRAD: layer.middle_grad,
        MIDDLE_NORM: middle_norm,
        OUTPUT_GRAD: lambda _: layer.square_grad(attended, lambda c: mid_low[:, c], 7),
        ATTENDED_GRAD: lambda _: layer.attended_grad(),
        ATTEND_BACK: lambda u: loop(2, functools.partial(layer.attend_back, u)),
        SQUARE_GRAD: lambda u: layer.square_grad(normed, lambda c: qkv[u, :, c], 4 + u),
        NORMED_GRAD: layer.normed_grad,
        INPUT_GRAD: input_grad,
        SMALL: small_sums,
        SMALL_SUM: small_sum,
        SMALL_DONE: small_done,
    }
    for name, n in ORDER:
        work[name](n)
    gather.drain(1)
    smalls.drain(0)
    scatter.drain()
    wait_for(small_in, back_sems.at[0])
    wait_for(small_rep.at[0:3], back_sems.at[2])
    wait_for(own_sum, misc_sems.at[2])
    grad_store.wait()


def fused_call(length, x, cot, gain_a, gain_f, table, square, inner, outer):
    rows, width = square[0].shape
    units = 4 + 2 * (inner.shape[1] // width)
    heads = table.shape[1]
    seq = x.shape[0]
    half = rows // 2
    part = half // 3
    hidden = inner.shape[1]
    low, wide = jnp.bfloat16, jnp.float32
    anywhere = pl.BlockSpec(memory_space=pl.ANY)
    within = pl.BlockSpec(memory_space=pltpu.VMEM)
    sems = pltpu.SemaphoreType.DMA
    vm = pltpu.VMEM
    head_rows = -(-heads // 8) * 8
    return pl.pallas_call(
        fused_kernel,
        out_shape=(
            jax.ShapeDtypeStruct((seq, width), low),
            jax.ShapeDtypeStruct((seq, width), wide),
            jax.ShapeDtypeStruct((units, rows, width), low),
            jax.ShapeDtypeStruct((8, 128), wide),
            jax.ShapeDtypeStruct((heads // 2, 2, seq, seq), low),
        ),
        in_specs=[pl.BlockSpec(memory_space=pltpu.SMEM), within, anywhere]
        + [within] * 3
        + [anywhere] * 6,
        out_specs=[anywhere, anywhere, anywhere, within, anywhere],
        scratch_shapes=[
            vm((4, 2, units + 8, rows, width), low),
            vm((units, rows, width), low),
            vm((6, 4, 2, half, width), low),
            vm((units, 4, 2, part, width), low),
            vm((units, 4, 2 * part, width), low),
            vm((units, 4, 2 * part, width), low),
            vm((16, 128), wide),
            vm((8, 16, 128), low),
            vm((8, 8, 128), wide),
            vm((7, 8, 128), wide),
            vm((4, 8, 128), wide),
            vm((2, 2, seq, seq), low),
            vm((seq, width), low),
            vm((3, seq, width), low),
            vm((seq, width), low),
            vm((seq, width), wide),
            vm((seq, width), low),
            vm((seq, hidden), low),
            vm((seq, hidden), low),
            vm((seq, width), low),
            vm((seq, width), wide),
            vm((seq, width), low),
            vm((2, seq, seq), wide),
            vm((head_rows, 512), wide),
            vm((128, 512), wide),
            vm((1, width), wide),
            vm((1, width), wide),
            vm((1, width), wide),
            vm((1, width), wide),
            vm((2, 128, 128 * 7), wide),
            vm((2, seq, seq), low),
            sems((2,)),
            sems((units, Gather.slots)),
            sems((4 + units,)),
            sems((units, Scatter.slots)),
            sems((1,)),
            sems((4,)),
            sems((4,)),
            sems((2,)),
            sems((3,)),
            sems((2,)),
        ],
        compiler_params=pltpu.CompilerParams(
            collective_id=0, has_side_effects=True, vmem_limit_bytes=63 * 2**20
        ),
    )(length, x, cot, gain_a, gain_f, table, *square, inner, outer)


def finish_kernel(
    block_in, grad_in, sums_far, small, block_out, grad_out, query_out, key_out, value_out,
    output_out, gain_a, table, inner_out, outer_out, gain_f, block, grad, query, key, value, output,
    inner, outer, sums, in_sems, out_sems,
):
    units, rows, width = sums.shape
    chunks = inner.shape[1] // width
    third = width // 3
    straight = ((block_in, block, block_out), (grad_in, grad, grad_out))
    loads = [pltpu.make_async_copy(sums_far.at[n], sums.at[n], in_sems.at[n]) for n in range(units)]
    loads += [
        pltpu.make_async_copy(far, near, in_sems.at[units + n])
        for n, (far, near, _) in enumerate(straight)
    ]
    for copy in loads[units:] + loads[:units]:
        copy.start()
    stores = []

    def store(near, far):
        stores.append(pltpu.make_async_copy(near, far, out_sems.at[len(stores)]))
        stores[-1].start()

    for n, (_, near, far) in enumerate(straight):
        loads[units + n].wait()
        store(near, far)
    gain_a[...] = small[0:1, :rows]
    gain_f[...] = small[1:2, :rows]
    table[...] = small[2 : 2 + table.shape[0], : table.shape[1]]
    for i in range(chunks):
        part = pl.ds(i * rows, rows)
        loads[i].wait()
        outer[part, :] = sums[i].astype(jnp.float32)
        store(outer.at[part], outer_out.at[part])
    for i in range(chunks):
        part = pl.ds(i * width, width)
        loads[chunks + i].wait()
        inner[:, part] = sums[chunks + i].astype(jnp.float32)
        store(inner.at[:, part], inner_out.at[:, part])
    loads[2 * chunks].wait()
    output[...] = sums[2 * chunks].astype(jnp.float32)
    store(output, output_out)
    for u in range(3):
        loads[2 * chunks + 1 + u].wait()
        for n, ref in enumerate((query, key, value)):
            ref[:, u * third : (u + 1) * third] = sums[
                2 * chunks + 1 + u, :, n * third : (n + 1) * third
            ].astype(jnp.float32)
    for near, far in ((query, query_out), (key, key_out), (value, value_out)):
        store(near, far)
    for copy in stores:
        copy.wait()


def finish_call(block, grad, sums, small, table_shape, inner_shape, outer_shape):
    units, rows, width = sums.shape
    wide = jnp.float32
    anywhere = pl.BlockSpec(memory_space=pl.ANY)
    within = pl.BlockSpec(memory_space=pltpu.VMEM)
    shapes = [(rows, width)] * 4 + [(1, rows), table_shape, inner_shape, outer_shape, (1, rows)]
    places = [anywhere] * 4 + [within] * 2 + [anywhere] * 2 + [within]
    staged = [shape for shape, place in zip(shapes, places) if place is anywhere]
    return pl.pallas_call(
        finish_kernel,
        out_shape=[
            jax.ShapeDtypeStruct(block.shape, block.dtype),
            jax.ShapeDtypeStruct(grad.shape, grad.dtype),
        ]
        + [jax.ShapeDtypeStruct(shape, wide) for shape in shapes],
        in_specs=[anywhere, anywhere, anywhere, within],
        out_specs=[anywhere, anywhere] + places,
        scratch_shapes=[
            pltpu.VMEM(block.shape, block.dtype),
            pltpu.VMEM(grad.shape, grad.dtype),
            *[pltpu.VMEM(shape, wide) for shape in staged],
            pltpu.VMEM(sums.shape, sums.dtype),
            pltpu.SemaphoreType.DMA((units + 2,)),
            pltpu.SemaphoreType.DMA((units + 2,)),
        ],
        compiler_params=pltpu.CompilerParams(vmem_limit_bytes=63 * 2**20),
    )(block, grad, sums, small)


def local_linked(
    inputs, lengths, cotangent, query_weight, key_weight, value_weight, output_weight,
    attention_gain, bias_table, inner_weight, outer_weight, feedforward_gain,
):
    rows = query_weight.shape[0]
    square = (query_weight, key_weight, value_weight, output_weight)
    block, grad, sums, small, _ = fused_call(
        lengths, inputs[0], cotangent[0], attention_gain.reshape(1, rows),
        feedforward_gain.reshape(1, rows), bias_table, square, inner_weight, outer_weight,
    )
    block, grad, query, key, value, output, gain_a, table, inner, outer, gain_f = finish_call(
        block, grad, sums, small, bias_table.shape, inner_weight.shape, outer_weight.shape
    )
    return (
        block[None], grad[None], query, key, value, output, gain_a.reshape(rows), table, inner,
        outer, gain_f.reshape(rows),
    )


def local(inputs, lengths, cotangent, *shards):
    block_output, input_grad, gradients = compute(inputs, lengths, cotangent, gather_all(*shards))
    return (block_output, input_grad) + sum_all(gradients)


def can_link(mesh):
    return mesh.shape["fsdp"] == 8 and mesh.shape["rep"] == 4


def solution(mesh):
    placed = (
        P(("fsdp", "rep"), None, None),
        P(("fsdp", "rep")),
        P(("fsdp", "rep"), None, None),
        P("fsdp", None),
        P("fsdp", None),
        P("fsdp", None),
        P("fsdp", None),
        P("fsdp"),
        P("fsdp", None),
        P("fsdp", None),
        P("fsdp", None),
        P("fsdp"),
    )
    return jax.shard_map(
        local_linked if can_link(mesh) else local,
        mesh=mesh,
        in_specs=placed,
        out_specs=(
            P(("fsdp", "rep"), None, None),
            P(("fsdp", "rep"), None, None),
            P("fsdp", None),
            P("fsdp", None),
            P("fsdp", None),
            P("fsdp", None),
            P("fsdp"),
            P("fsdp", None),
            P("fsdp", None),
            P("fsdp", None),
            P("fsdp"),
        ),
        check_vma=False,
    )
```

```python
import functools

import jax
import jax.numpy as jnp
from jax import lax
import jax.experimental.pallas as pl
import jax.experimental.pallas.tpu as pltpu
from jax.sharding import PartitionSpec as P

NB = 32


epsilon = 1e-06
highest = lax.Precision.HIGHEST
gelu_coeff = 0.7978845608028654
masked_score = -1e30


def bucket_of(offset):
    half_count = NB // 2
    exact_count = half_count // 2
    distance = jnp.abs(offset)
    beyond = jnp.full(offset.shape, exact_count, jnp.int32)
    for exponent in range(1, half_count - exact_count):
        beyond = beyond + (distance * distance >= exact_count * exact_count * 2**exponent).astype(
            jnp.int32
        )
    nearby = jnp.where(distance < exact_count, distance, beyond)
    return jnp.where(offset > 0, half_count, 0).astype(jnp.int32) + nearby


def rms_norm(values, gain_vector):
    inverse_rms = lax.rsqrt(jnp.mean(values * values, axis=-1, keepdims=True) + epsilon)
    return values * inverse_rms * gain_vector


def gelu(values):
    return (
        0.5 * values * (1.0 + jnp.tanh(gelu_coeff * (values + 0.044715 * values * values * values)))
    )


def dot(a,b): return jnp.dot(a,b,preferred_element_type=jnp.float32)
def dot_t(a,b): return lax.dot_general(a,b,(((1,),(1,)),((),())),preferred_element_type=jnp.float32)
def dot_c(a,b): return lax.dot_general(a,b,(((0,),(0,)),((),())),preferred_element_type=jnp.float32)

def fwd_kernel(T, len_ref, q_ref, k_ref, v_ref, rel_ref, o_ref, p_ref, strip):
    hp=pl.program_id(0)
    seq=q_ref.shape[0]; nb=seq//T
    lane=lax.broadcasted_iota(jnp.int32,(1,128),1)
    kcol=lax.broadcasted_iota(jnp.int32,(1,seq),1)
    mask=jnp.where(kcol<len_ref[0],0.0,-1e30)
    k=k_ref[...]; v=v_ref[...]
    for hh in range(2):
        mine=(lane>=64) if hh else (lane<64)
        rel=rel_ref[pl.ds(hh,1),:]
        W=4*T
        rolled=pltpu.roll(jnp.broadcast_to(rel,(T,W)),0,axis=1,stride=1,stride_axis=0)
        strip[:, 2*T:5*T]=rolled[:, :3*T]
        far_neg=rel[:, 0:1]; far_pos=rel[:, 3*T-1:3*T]
        strip[:, 0:2*T]=jnp.broadcast_to(far_neg,(T,2*T))
        strip[:, 5*T:7*T]=jnp.broadcast_to(far_pos,(T,2*T))
        for I in range(nb):
            q=jnp.where(mine,q_ref[I*T:(I+1)*T,:],jnp.bfloat16(0))
            s=dot_t(q,k)+(strip[:, (3-I)*T:(3-I)*T+seq]+mask)
            m=jnp.max(s,axis=-1,keepdims=True)
            e=jnp.exp(s-m)
            tot=jnp.sum(e,axis=-1,keepdims=True)
            p=(e*(1.0/tot)).astype(jnp.bfloat16)
            p_ref[hh,I*T:(I+1)*T,:]=p
            o=dot(p,v)
            if hh==0:
                o_ref[I*T:(I+1)*T,:]=o.astype(jnp.bfloat16)
            else:
                o_ref[I*T:(I+1)*T,:]=jnp.where(mine,o.astype(jnp.bfloat16),o_ref[I*T:(I+1)*T,:])

def bwd_kernel(T, q_ref, k_ref, v_ref, do_ref, p_ref, dq_ref, dk_ref, dv_ref, db_ref, ds_ref):
    seq=q_ref.shape[0]; nb=seq//T
    lane=lax.broadcasted_iota(jnp.int32,(1,128),1)
    k=k_ref[...]; v=v_ref[...]
    dks=[];dvs=[]
    for hh in range(2):
        mine=(lane>=64) if hh else (lane<64)
        acc=[None]*5
        for I in range(nb):
            sl=slice(I*T,(I+1)*T)
            do=jnp.where(mine,do_ref[sl,:],jnp.bfloat16(0))
            dp=dot_t(do,v)
            p=p_ref[hh,sl,:].astype(jnp.float32)
            t=p*dp
            delta=jnp.sum(t,axis=-1,keepdims=True)
            ds=(t-p*delta).astype(jnp.bfloat16)
            ds_ref[sl,:]=ds
            dsf=ds.astype(jnp.float32)
            for J in range(nb):
                d=min(2,max(-2,J-I))+2
                x=dsf[:,J*T:(J+1)*T]
                acc[d]=x if acc[d] is None else acc[d]+x
            dq=dot(ds,k)
            if hh==0: dq_ref[sl,:]=dq.astype(jnp.bfloat16)
            else: dq_ref[sl,:]=jnp.where(mine,dq.astype(jnp.bfloat16),dq_ref[sl,:])
        near=jnp.concatenate([acc[1],acc[2],acc[3],jnp.zeros((T,T),jnp.float32)],axis=1)
        total=shear_sum(near,4*T)
        far=jnp.concatenate([jnp.zeros((1,2*T),jnp.float32),jnp.sum(acc[4],axis=0,keepdims=True),jnp.sum(acc[0],axis=0,keepdims=True)],axis=1)
        db_ref[hh:hh+1,:]=total+far
        dk=dot_c(q_ref[...],ds_ref[...]).T; dv=dot_c(do_ref[...],p_ref[hh]).T
        dks.append(dk); dvs.append(dv)
    dk_ref[...]=jnp.where(lane<64,dks[0],dks[1]).astype(jnp.bfloat16)
    dv_ref[...]=jnp.where(lane<64,dvs[0],dvs[1]).astype(jnp.bfloat16)

def rel_hits(tile):
    slot = jnp.arange(4 * tile, dtype=jnp.int32)
    offset = jnp.where(slot < 3 * tile, slot - tile, slot - 5 * tile)
    bucket_ids = jnp.arange(NB, dtype=jnp.int32)
    return (bucket_of(offset)[None, :] == bucket_ids[:, None]).astype(jnp.bfloat16)


def rel_vec(table, tile):
    return dot_c(table, rel_hits(tile))


def shear_sum(block, width):
    rows = block.shape[0]
    while rows > 8:
        rows //= 2
        block = block[:rows] + pltpu.roll(block[rows:], width - rows, axis=1)
    total = block[0:1]
    for r in range(1, 8):
        total = total + pltpu.roll(block[r : r + 1], width - r, axis=1)
    return total


def att_fwd(q,k,v,rel,length,T=128):
    seq,D=q.shape; H=rel.shape[0]
    blk=pl.BlockSpec((seq,128),lambda h: (0,h))
    return pl.pallas_call(functools.partial(fwd_kernel,T),grid=(H//2,),
        in_specs=[pl.BlockSpec(memory_space=pltpu.SMEM),blk,blk,blk,pl.BlockSpec((None,2,4*T),lambda h:(h,0,0))],
        out_specs=[blk,pl.BlockSpec((2,seq,seq),lambda h:(h,0,0))],
        out_shape=[jax.ShapeDtypeStruct((seq,D),jnp.bfloat16),jax.ShapeDtypeStruct((H,seq,seq),jnp.bfloat16)],
        scratch_shapes=[pltpu.VMEM((T,7*T),jnp.float32)],
        compiler_params=pltpu.CompilerParams(vmem_limit_bytes=40*2**20))(length,q,k,v,rel.reshape(H//2,2,4*T))
def att_bwd(q,k,v,do,p,T=128):
    seq,D=q.shape; H=p.shape[0]
    blk=pl.BlockSpec((seq,128),lambda h: (0,h))
    o=jax.ShapeDtypeStruct((seq,D),jnp.bfloat16)
    outs=pl.pallas_call(functools.partial(bwd_kernel,T),grid=(H//2,),
        in_specs=[blk,blk,blk,blk,pl.BlockSpec((2,seq,seq),lambda h:(h,0,0))],
        out_specs=[blk,blk,blk,pl.BlockSpec((None,2,4*T),lambda h:(h,0,0))],
        out_shape=[o,o,o,jax.ShapeDtypeStruct((H//2,2,4*T),jnp.float32)],
        scratch_shapes=[pltpu.VMEM((seq,seq),jnp.bfloat16)],
        compiler_params=pltpu.CompilerParams(vmem_limit_bytes=40*2**20))(q,k,v,do,p)
    return *outs[:3],outs[3].reshape(H,4*T)

def contract_rows(left, right):
    return lax.dot_general(
        left, right, (((0,), (0,)), ((), ())), preferred_element_type=jnp.float32
    )


def contract_cols(left, right):
    return lax.dot_general(
        left, right, (((1,), (1,)), ((), ())), preferred_element_type=jnp.float32
    )


MESH = pl.DeviceIdType.MESH


def coords():
    shard = lax.axis_index("fsdp")
    copy = lax.axis_index("rep")
    return shard // 2, shard % 2, copy // 2, copy % 2


def greet(peers, at_end):
    barrier = pltpu.get_barrier_semaphore()
    for peer in peers[:-1]:
        pl.semaphore_signal(barrier, inc=1, device_id=peer, device_id_type=MESH)

    def last():
        pl.semaphore_signal(barrier, inc=1, device_id=peers[-1], device_id_type=MESH)

    pl.when(~at_end)(last)


def all_greeted(peers, at_end):
    barrier = pltpu.get_barrier_semaphore()
    pl.semaphore_wait(barrier, jnp.where(at_end, len(peers) - 1, len(peers)))


class Links:
    def __init__(self, rows, send_sems, recv_sems):
        self.send_sems, self.recv_sems = send_sems, recv_sems
        self.z, self.x, self.y, self.c = coords()
        half = rows // 2
        part = half // 3
        at = lambda start, size: pl.ds(pl.multiple_of(start, part), size)
        first = half * self.c
        other = half * (1 - self.c)
        self.half, self.other_half = at(first, half), at(other, half)
        self.plane = at(first + part * self.y, 2 * part)
        self.shared = at(first + part, part)
        self.own_third = at(first + 2 * part * self.y, part)
        self.other_third = at(first + 2 * part * (1 - self.y), part)
        self.shared_in = at(part * self.y, part)
        self.third_in = at(part * (1 - self.y), part)

    def copy(self, src, dst, g, send, slot, device):
        return pltpu.make_async_remote_copy(
            src_ref=src,
            dst_ref=dst,
            send_sem=self.send_sems.at[send],
            recv_sem=self.recv_sems.at[g, slot],
            device_id=device,
            device_id_type=MESH,
        )

    def to_x(self):
        return (self.z * 2 + 1 - self.x, self.y * 2 + self.c)

    def to_y(self):
        return (self.z * 2 + self.x, (1 - self.y) * 2 + self.c)

    def to_core(self):
        return (self.z * 2 + self.x, self.y * 2 + 1 - self.c)

    def to_z(self, k):
        return (lax.rem(self.z + k, 4) * 2 + self.x, self.y * 2 + self.c)

    def z_before(self, k):
        return lax.rem(self.z + 4 - k, 4)


class Gather(Links):
    slots = 6

    def __init__(self, full, send_sems, recv_sems):
        super().__init__(full.shape[3], send_sems, recv_sems)
        self.full = full
        self.beside = self.z + 1 - 2 * lax.rem(self.z, 2)
        self.second = lax.rem(self.z + 2, 4)
        self.across = 3 - self.z
        self.at_end = (self.z == 0) | (self.z == 3)
        self.early = range(4, 8)

    def peers(self):
        near = [self.to_x(), self.to_y(), self.to_core()]
        return near + [self.at_z(a) for a in (self.second, self.beside, self.across)]

    def block(self, g, a, rows):
        return self.full.at[a, self.x, g, rows]

    def column(self, g, rows):
        return self.full.at[:, 1 - self.x, g, rows]

    def move(self, part, g, slot, device):
        return pltpu.make_async_remote_copy(
            src_ref=part,
            dst_ref=part,
            send_sem=self.send_sems.at[0 if g in self.early else 1],
            recv_sem=self.recv_sems.at[g, slot],
            device_id=device,
            device_id_type=MESH,
        )

    def at_z(self, a):
        return (a * 2 + self.x, self.y * 2 + self.c)

    def z_copy(self, g, to, slot):
        return self.move(self.block(g, self.z, self.plane), g, slot, self.at_z(to))

    def x_copy(self, g, a):
        return self.move(self.block(g, a, self.plane), g, 3, self.to_x())

    def y_copy(self, g, a):
        return self.move(self.block(g, a, self.own_third), g, 4, self.to_y())

    def core_copy(self, g, a):
        return self.move(self.block(g, a, self.half), g, 5, self.to_core())

    def arrived(self, part, g, slot):
        pltpu.make_async_copy(part, part, self.recv_sems.at[g, slot]).wait()

    def others(self):
        return (self.beside, self.second, self.across)

    def send_z(self, g):
        self.z_copy(g, self.second, 0).start()
        self.z_copy(g, self.beside, 1).start()
        pl.when(~self.at_end)(lambda: self.z_copy(g, self.across, 2).start())

    def send_x(self, g):
        self.x_copy(g, self.z).start()

    def spread(self, g, a, slot):
        self.arrived(self.block(g, a, self.plane), g, slot)
        if slot == 0:
            part = self.block(g, a, self.plane)
            pl.when(~self.at_end)(lambda: self.move(part, g, 2, self.at_z(self.beside)).start())
        self.x_copy(g, a).start()
        self.y_copy(g, a).start()

    def after_second(self, g):
        self.spread(g, self.second, 0)

    def after_beside(self, g):
        self.spread(g, self.beside, 1)

    def after_across(self, g):
        self.spread(g, self.across, 2)

    def after_x(self, g):
        self.arrived(self.column(g, self.plane), g, 3)
        self.move(self.column(g, self.own_third), g, 4, self.to_y()).start()

    def after_y(self, g):
        third = self.own_third.size
        self.arrived(self.full.at[0, 0, 0:7, 0:third], g, 4)
        for a in self.others():
            self.core_copy(g, a).start()
        self.move(self.column(g, self.half), g, 5, self.to_core()).start()

    def after_core(self, g):
        self.arrived(self.full.at[0, 0, 0:7, 0 : self.half.size], g, 5)

    def drain(self, n):
        count = len(self.early)
        units = self.full.shape[2] - 8
        rows = self.full.shape[3] * (count if n == 0 else units - count) // units

        def wait(blocks):
            part = self.full.at[:, :, 0:blocks, 0:rows]
            pltpu.make_async_copy(part, part, self.send_sems.at[n]).wait()

        pl.when(self.at_end)(lambda: wait(10))
        pl.when(~self.at_end)(lambda: wait(11))


class SmallGather(Gather):
    def move(self, part, g, slot, device):
        return pltpu.make_async_remote_copy(
            src_ref=part,
            dst_ref=part,
            send_sem=self.send_sems.at[0],
            recv_sem=self.recv_sems.at[slot],
            device_id=device,
            device_id_type=MESH,
        )

    def __init__(self, links, full, send_sems, recv_sems):
        self.__dict__.update(links.__dict__)
        self.full, self.send_sems, self.recv_sems = full, send_sems, recv_sems

    def block(self, g, a, rows):
        return self.full.at[a * 2 + self.x]

    def y_copy(self, g, a):
        return self

    def start(self):
        pass

    def arrived(self, part, g, slot):
        pltpu.make_async_copy(part, part, self.recv_sems.at[slot]).wait()

    def after_x(self, g):
        self.arrived(self.full.at[0:4], g, 3)

    def drain(self, n):
        def wait(blocks):
            part = self.full.at[0:blocks]
            pltpu.make_async_copy(part, part, self.send_sems.at[0]).wait()

        pl.when(self.at_end)(lambda: wait(6))
        pl.when(~self.at_end)(lambda: wait(8))


class Scatter(Links):
    slots = 6

    def __init__(self, slot, full, own, from_core, from_y, from_x, from_z, send_sems, recv_sems):
        super().__init__(own.shape[1], send_sems, recv_sems)
        self.slot, self.full, self.own = slot, full, own
        self.from_core, self.from_y, self.from_x, self.from_z = from_core, from_y, from_x, from_z

    def core_copy(self, g):
        part = self.full.at[:, :, self.slot(g), self.other_half]
        ring = g % self.from_core.shape[0]
        return self.copy(part, self.from_core.at[ring], g, 0, 0, self.to_core())

    def y_copy(self, g):
        part = self.full.at[:, :, self.slot(g), self.other_third]
        return self.copy(part, self.from_y.at[g], g, 1, 1, self.to_y())

    def x_copy(self, g):
        part = self.full.at[:, 1 - self.x, self.slot(g), self.plane]
        return self.copy(part, self.from_x.at[g], g, 1, 2, self.to_x())

    def z_copy(self, g, k):
        part = self.full.at[lax.rem(self.z + k, 4), self.x, self.slot(g), self.plane]
        return self.copy(part, self.from_z.at[g, k - 1], g, 2, 3, self.to_z(k))

    def back_y_copy(self, g):
        part = self.own.at[g, self.plane]
        return self.copy(part, self.from_z.at[g, 3], g, 4 + g, 4, self.to_y())

    def back_core_copy(self, g):
        part = self.own.at[g, self.half]
        return self.copy(part, part, g, 3, 5, self.to_core())

    def start(self, g):
        self.core_copy(g).start()

    def after_core(self, g):
        self.core_copy(g).wait_recv()
        ring = g % self.from_core.shape[0]
        for a in range(4):
            for b in range(2):
                self.full[a, b, self.slot(g), self.half] += self.from_core[ring, a, b]
        self.y_copy(g).start()

    def after_y(self, g):
        self.y_copy(g).wait_recv()
        for a in range(4):
            for b in range(2):
                self.full[a, b, self.slot(g), self.own_third] += self.from_y[g, a, b]
        self.x_copy(g).start()

    def after_x(self, g):
        self.x_copy(g).wait_recv()
        for a in range(4):
            self.full[a, self.x, self.slot(g), self.plane] += self.from_x[g, a]
        for k in (1, 2, 3):
            self.z_copy(g, k).start()

    def after_z(self, g):
        total = self.full[self.z, self.x, self.slot(g), self.plane].astype(jnp.float32)
        part = self.from_z.at[g, 0:3]
        pltpu.make_async_copy(part, part, self.recv_sems.at[g, 3]).wait()
        for k in (1, 2, 3):
            total = total + self.from_z[g, k - 1].astype(jnp.float32)
        self.own[g, self.plane] = total.astype(jnp.bfloat16)
        self.back_y_copy(g).start()

    def after_back_y(self, g):
        self.back_y_copy(g).wait_recv()
        self.back_y_copy(g).wait_send()
        got = self.from_z.at[g, 3]
        self.own[g, self.shared] += got[self.shared_in]
        self.own[g, self.other_third] = got[self.third_in]
        self.back_core_copy(g).start()

    def after_back_core(self, g):
        part = self.own.at[g, self.other_half]
        self.copy(part, part, g, 3, 5, self.to_core()).wait_recv()

    def drain(self):
        units, rows = self.own.shape[:2]
        half = rows // 2
        for n, part in (
            (0, self.full.at[:, :, 0 : units // 2]),
            (1, self.full.at[:, :, 0 : units // 3]),
            (2, self.full.at[:, :, 0 : units // 4, 0:half]),
            (3, self.own.at[0 : units // 2]),
        ):
            pltpu.make_async_copy(part, part, self.send_sems.at[n]).wait()


def compute(inputs, lengths, cotangent, weights):
    (
        full_query, full_key, full_value, full_output, full_gain, full_table, full_inner,
        full_outer, full_ffn_gain,
    ) = weights
    pairs_here, seq_len, model_width = inputs.shape
    row_count = pairs_here * seq_len
    head_count = full_table.shape[1]
    tile = 128
    relative = rel_vec(full_table, tile)
    flat_inputs = inputs.reshape(row_count, model_width).astype(jnp.float32)
    normed = rms_norm(flat_inputs, full_gain.astype(jnp.float32)).astype(jnp.bfloat16)
    joined = jnp.concatenate((full_query, full_key, full_value), axis=1)
    projected = jnp.dot(normed, joined, preferred_element_type=jnp.float32).astype(jnp.bfloat16)
    queries = projected[:, :model_width]
    key_rows = projected[:, model_width : 2 * model_width]
    value_rows = projected[:, 2 * model_width :]
    pair_rows = [slice(n * seq_len, (n + 1) * seq_len) for n in range(pairs_here)]
    forward_parts = [
        att_fwd(queries[r], key_rows[r], value_rows[r], relative, lengths[n : n + 1], tile)
        for n, r in enumerate(pair_rows)
    ]
    attended = jnp.concatenate([part[0] for part in forward_parts], axis=0)
    middle = flat_inputs + jnp.dot(attended, full_output, preferred_element_type=jnp.float32)
    normed_ffn = rms_norm(middle, full_ffn_gain.astype(jnp.float32)).astype(jnp.bfloat16)
    raised = jnp.dot(normed_ffn, full_inner, preferred_element_type=jnp.float32)
    active = gelu(raised).astype(jnp.bfloat16)
    lowered = jnp.dot(active, full_outer, preferred_element_type=jnp.float32)
    block_output = (middle + lowered).astype(jnp.bfloat16).reshape(pairs_here, seq_len, model_width)
    positions = jnp.arange(seq_len, dtype=jnp.int32)
    row_live = (positions[None, :] < lengths[:, None]).astype(jnp.float32)
    seed_rows = (cotangent.astype(jnp.float32) * row_live[:, :, None]).reshape(
        row_count, model_width
    )
    seed_low = seed_rows.astype(jnp.bfloat16)
    grad_active = contract_cols(seed_low, full_outer)
    grad_outer = contract_rows(active, seed_low)
    grad_raised = jax.vjp(gelu, raised)[1](grad_active)[0].astype(jnp.bfloat16)
    grad_inner = contract_rows(normed_ffn, grad_raised)
    grad_normed_ffn = contract_cols(grad_raised, full_inner)
    ffn_pull = jax.vjp(rms_norm, middle, full_ffn_gain.astype(jnp.float32))[1]
    grad_middle_part, grad_ffn_gain = ffn_pull(grad_normed_ffn)
    grad_middle = seed_rows + grad_middle_part
    joined = jnp.concatenate((full_query, full_key, full_value), axis=1)
    middle_low = grad_middle.astype(jnp.bfloat16)
    grad_attended = contract_cols(middle_low, full_output).astype(jnp.bfloat16)
    grad_output = contract_rows(attended, middle_low)
    backward_parts = [
        att_bwd(
            queries[r], key_rows[r], value_rows[r], grad_attended[r], forward_parts[n][1], tile
        )
        for n, r in enumerate(pair_rows)
    ]
    grad_projected = jnp.concatenate(
        [jnp.concatenate(part[:3], axis=1) for part in backward_parts], axis=0
    )
    grad_joined = contract_rows(normed, grad_projected)
    grad_normed = contract_cols(grad_projected, joined)
    attention_pull = jax.vjp(rms_norm, flat_inputs, full_gain.astype(jnp.float32))[1]
    grad_inputs_part, grad_attention_gain = attention_pull(grad_normed)
    input_grad = (grad_middle + grad_inputs_part).reshape(pairs_here, seq_len, model_width)
    grad_relative = sum(part[3] for part in backward_parts)
    grad_table = lax.dot_general(
        rel_hits(tile).astype(jnp.float32),
        grad_relative,
        (((1,), (1,)), ((), ())),
        precision=highest,
    )
    return block_output, input_grad, (
        grad_joined[:, :model_width],
        grad_joined[:, model_width : 2 * model_width],
        grad_joined[:, 2 * model_width :],
        grad_output,
        grad_attention_gain,
        grad_table,
        grad_inner,
        grad_outer,
        grad_ffn_gain,
    )


def gather_all(query_weight, key_weight, value_weight, output_weight, attention_gain, bias_table,
               inner_weight, outer_weight, feedforward_gain):
    return tuple(
        lax.all_gather(part, "fsdp", axis=0, tiled=True)
        for part in (
            query_weight, key_weight, value_weight, output_weight, attention_gain, bias_table,
            inner_weight, outer_weight, feedforward_gain,
        )
    )


def sum_all(gradients):
    def one(part):
        part = lax.psum_scatter(
            part.astype(jnp.bfloat16), "fsdp", scatter_dimension=0, tiled=True
        )
        return lax.psum(part, "rep").astype(jnp.float32)

    return tuple(one(part) for part in gradients)


def gelu_parts(z):
    square = z * z
    t = jnp.tanh(gelu_coeff * z * (1.0 + 0.044715 * square))
    half = 0.5 * (1.0 + t)
    slope = half + (0.5 * gelu_coeff) * z * (1.0 - t * t) * (1.0 + (3 * 0.044715) * square)
    return z * half, slope


def lanes(start, size):
    return pl.ds(start if isinstance(start, int) else pl.multiple_of(start, 128), size)


def rows_at(start, size):
    return pl.ds(pl.multiple_of(start, size), size)


def loop(count, body):
    def step(n, carry):
        body(n)
        return carry

    lax.fori_loop(0, count, step, 0)


def norm_back(grad, gain, values):
    inverse = lax.rsqrt(jnp.mean(values * values, axis=-1, keepdims=True) + epsilon)
    scaled = grad * gain
    centre = jnp.mean(scaled * values, axis=-1, keepdims=True)
    back = inverse * scaled - values * (inverse * inverse * inverse * centre)
    return back, jnp.sum(grad * values * inverse, axis=0, keepdims=True)


class Layer:
    def __init__(self, **refs):
        self.__dict__.update(refs)
        self.seq, self.width = self.x.shape
        self.tile = 128
        self.row_block = 128
        self.shard_rows = self.bank.shape[3]

    def unit(self, u, column=None, size=None):
        if column is None:
            block = self.bank[:, :, u]
        else:
            block = self.bank[:, :, u, :, lanes(column, size)]
        return block.reshape(-1, block.shape[-1])

    def row_chunks(self, body):
        size = self.row_block
        loop(self.seq // size, lambda n: body(rows_at(n * size, size)))

    def small_arrays(self):
        flat = self.all_small[...].reshape(-1, 128)
        tile = self.tile
        slot = lax.broadcasted_iota(jnp.int32, (flat.shape[0], 4 * tile), 1)
        offset = jnp.where(slot < 3 * tile, slot - tile, slot - 5 * tile)
        row = lax.broadcasted_iota(jnp.int32, (flat.shape[0], 4 * tile), 0)
        per = NB // 8
        inside = row % 16 - 2
        wanted = jnp.where((inside >= 0) & (inside < per), (row // 16) * per + inside, -1)
        hits = (bucket_of(offset) == wanted).astype(jnp.bfloat16)
        self.rel[...] = dot_c(flat, hits)[: self.rel.shape[0]]
        for index, ref in ((0, self.gain_a), (1, self.gain_f)):
            total = jnp.zeros((1, self.width), jnp.float32)
            for shard in range(8):
                part = self.all_small[shard].astype(jnp.float32)[index : index + 1]
                wide = jnp.concatenate(
                    [part, jnp.zeros((1, self.width - 128), jnp.float32)], axis=1
                )
                total = total + (
                    pltpu.roll(wide, shard * self.shard_rows, axis=1) if shard else wide
                )
            ref[...] = total

    def norm_in(self):
        gain = self.gain_a[...]

        def body(r):
            self.normed[r] = rms_norm(self.x[r].astype(jnp.float32), gain).astype(jnp.bfloat16)

        self.row_chunks(body)

    def mask_seed(self):
        def body(r):
            index = lax.broadcasted_iota(jnp.int32, (self.row_block, 1), 0) + r.start
            live = index < self.length[0]
            self.seed[r] = jnp.where(live, self.seed[r], jnp.bfloat16(0))

        self.row_chunks(body)

    def project(self, u):
        def body(n):
            self.qkv[u, :, lanes(n * 256, 256)] = dot(
                self.normed[...], self.unit(u, n * 256, 256)
            ).astype(jnp.bfloat16)

        loop(self.width // 256, body)

    def strip_for(self, head, strip):
        tile = self.tile
        rel = self.rel[pl.ds(head, 1), :]
        rolled = pltpu.roll(
            jnp.broadcast_to(rel, (tile, 4 * tile)), 0, axis=1, stride=1, stride_axis=0
        )
        strip[:, 2 * tile : 5 * tile] = rolled[:, : 3 * tile]
        strip[:, : 2 * tile] = jnp.broadcast_to(rel[:, :1], (tile, 2 * tile))
        strip[:, 5 * tile :] = jnp.broadcast_to(rel[:, 3 * tile - 1 : 3 * tile], (tile, 2 * tile))

    def pair_lanes(self, slot):
        third = self.width // 3
        return [lanes(slot * 128 + n * third, 128) for n in range(3)]

    def probs_store(self, pair, slot):
        return pltpu.make_async_copy(
            self.probs.at[slot], self.probs_far.at[pair], self.probs_sems.at[slot]
        )

    def probs_load(self, pair, slot):
        return pltpu.make_async_copy(
            self.probs_far.at[pair], self.probs.at[slot], self.probs_sems.at[slot]
        )

    def attend(self, unit, slot):
        tile, seq = self.tile, self.seq
        pair = 2 * unit + slot
        if unit > 0:
            self.probs_store(pair, slot).wait()
        lane = lax.broadcasted_iota(jnp.int32, (1, 128), 1)
        own = (lane < 64, lane >= 64)
        key_at = lax.broadcasted_iota(jnp.int32, (1, seq), 1)
        mask = jnp.where(key_at < self.length[0], 0.0, masked_score)
        q_at, k_at, v_at = self.pair_lanes(slot)
        q = self.qkv[unit, :, q_at]
        k = self.qkv[unit, :, k_at]
        v = self.qkv[unit, :, v_at]
        for head in range(2):
            self.strip_for(pair * 2 + head, self.strip.at[head])
            self.scores[head] = dot_t(jnp.where(own[head], q, jnp.bfloat16(0)), k)

        def soften(head):
            for block in range(seq // tile):
                r = slice(block * tile, (block + 1) * tile)
                first = (seq // tile - 1 - block) * tile
                bias = self.strip[head, :, first : first + seq]
                scores = self.scores[head, r, :] + (bias + mask)
                peak = jnp.max(scores, axis=-1, keepdims=True)
                raised = jnp.exp(scores - peak)
                total = jnp.sum(raised, axis=-1, keepdims=True)
                self.probs[slot, head, r, :] = (raised * (1.0 / total)).astype(jnp.bfloat16)
            return dot(self.probs[slot, head], v)

        outs = [soften(head) for head in range(2)]
        self.attended[:, lanes(pair * 128, 128)] = jnp.where(own[0], *outs).astype(jnp.bfloat16)
        self.probs_store(pair, slot).start()

    def middle_rows(self):
        def body(n):
            c = lanes(n * 256, 256)
            self.middle[:, c] = self.x[:, c].astype(jnp.float32) + dot(
                self.attended[...], self.unit(3, n * 256, 256)
            )

        loop(self.width // 256, body)
        gain = self.gain_f[...]

        def norm(r):
            self.normed_ffn[r] = rms_norm(self.middle[r], gain).astype(jnp.bfloat16)

        self.row_chunks(norm)

    def raise_unit(self, i):
        def body(n):
            raised = dot(self.normed_ffn[...], self.unit(4 + i, n * 256, 256))
            active, slope = gelu_parts(raised)
            c = lanes(i * self.width + n * 256, 256)
            self.active[:, c] = active.astype(jnp.bfloat16)
            self.slope[:, c] = slope.astype(jnp.bfloat16)

        loop(self.width // 256, body)

    def outer_grad(self, shard):
        size = 4 * self.shard_rows
        block = dot_c(self.active[:, lanes(shard * size, size)], self.seed[...])
        self.bank[shard // 2, shard % 2, 12:16] = block.astype(jnp.bfloat16).reshape(
            4, self.shard_rows, self.width
        )

    def lower(self, n):
        outer = self.bank[:, :, 8:12, :, lanes(n * 256, 256)].reshape(-1, 256)
        c = lanes(n * 256, 256)
        self.mid_low[:, c] = (self.middle[:, c] + dot(self.active[...], outer)).astype(
            jnp.bfloat16
        )

    def raised_grad(self, shard):
        size = 4 * self.shard_rows
        outer = self.bank[shard // 2, shard % 2, 8:12].reshape(size, self.width)
        c = lanes(shard * size, size)
        grad = dot_t(self.seed[...], outer) * self.slope[:, c].astype(jnp.float32)
        self.slope[:, c] = grad.astype(jnp.bfloat16)

    def inner_grad(self, i):
        def body(n):
            c = lanes(i * self.width + n * 256, 256)
            block = dot_c(self.normed_ffn[...], self.slope[:, c]).astype(jnp.bfloat16)
            self.bank[:, :, 16 + i, :, lanes(n * 256, 256)] = block.reshape(
                4, 2, self.shard_rows, 256
            )

        loop(self.width // 256, body)

    def middle_grad(self, part):
        total = None
        for i in range(4):
            inner = self.bank[2 * part : 2 * part + 2, :, 4 + i].reshape(-1, self.width)
            term = dot_t(self.slope[:, i * self.width : (i + 1) * self.width], inner)
            total = term if total is None else total + term
        size = self.width // 2
        self.grad_mid[:, part * size : (part + 1) * size] = total

    def middle_norm(self):
        gain = self.gain_f[...]
        self.gain_f_grad[...] = jnp.zeros_like(self.gain_f_grad)

        def body(r):
            back, terms = norm_back(self.grad_mid[r], gain, self.middle[r])
            total = self.seed[r].astype(jnp.float32) + back
            self.gain_f_grad[...] += terms
            self.grad_mid[r] = total
            self.mid_low[r] = total.astype(jnp.bfloat16)

        self.row_chunks(body)

    def square_grad(self, left, right, slot):
        def body(n):
            block = dot_c(left[...], right(lanes(n * 256, 256))).astype(jnp.bfloat16)
            self.bank[:, :, slot, :, lanes(n * 256, 256)] = block.reshape(
                4, 2, self.shard_rows, 256
            )

        loop(self.width // 256, body)

    def attended_grad(self):
        size = self.width // 2
        for part in range(2):
            weight = self.bank[2 * part : 2 * part + 2, :, 3].reshape(size, self.width)
            self.attended[:, part * size : (part + 1) * size] = dot_t(
                self.mid_low[...], weight
            ).astype(jnp.bfloat16)

    def attend_back(self, unit, slot):
        tile, seq = self.tile, self.seq
        pair = 2 * unit + slot
        self.probs_load(pair, slot).wait()
        lane = lax.broadcasted_iota(jnp.int32, (1, 128), 1)
        own = (lane < 64, lane >= 64)
        q_at, k_at, v_at = self.pair_lanes(slot)
        q = self.qkv[unit, :, q_at]
        k = self.qkv[unit, :, k_at]
        v = self.qkv[unit, :, v_at]
        grad_out = self.attended[:, lanes(pair * 128, 128)]
        blocks = seq // tile
        for head in range(2):
            self.scores[head] = dot_t(jnp.where(own[head], grad_out, jnp.bfloat16(0)), v)

        def back(head):
            sums = [None] * 5
            for block in range(blocks):
                r = slice(block * tile, (block + 1) * tile)
                probs = self.probs[slot, head, r, :].astype(jnp.float32)
                weighted = probs * self.scores[head, r, :]
                centre = jnp.sum(weighted, axis=-1, keepdims=True)
                grad = weighted - probs * centre
                self.grad_scores[head, r, :] = grad.astype(jnp.bfloat16)
                for other in range(blocks):
                    apart = min(2, max(-2, other - block)) + 2
                    part = grad[:, other * tile : (other + 1) * tile]
                    sums[apart] = part if sums[apart] is None else sums[apart] + part
            zero = jnp.zeros((tile, tile), jnp.float32)
            near = shear_sum(jnp.concatenate([sums[1], sums[2], sums[3], zero], axis=1), 4 * tile)
            far = jnp.concatenate(
                [
                    jnp.zeros((1, 2 * tile), jnp.float32),
                    jnp.sum(sums[4], axis=0, keepdims=True),
                    jnp.sum(sums[0], axis=0, keepdims=True),
                ],
                axis=1,
            )
            self.rel_grad[pl.ds(pair * 2 + head, 1), :] = near + far
            return (
                dot(self.grad_scores[head], k),
                dot_c(q, self.grad_scores[head]).T,
                dot_c(grad_out, self.probs[slot, head]).T,
            )

        for at, first, second in zip((q_at, k_at, v_at), back(0), back(1)):
            self.qkv[unit, :, at] = jnp.where(own[0], first, second).astype(jnp.bfloat16)
        if 2 * unit + 2 < self.probs_far.shape[0]:
            self.probs_load(pair + 2, slot).start()

    def normed_grad(self, part):
        size = self.width // 2
        total = None
        for u in range(3):
            weight = self.bank[2 * part : 2 * part + 2, :, u].reshape(size, self.width)
            term = dot_t(self.qkv[u], weight)
            total = term if total is None else total + term
        self.middle[:, part * size : (part + 1) * size] = total

    def input_grad(self):
        gain = self.gain_a[...]
        self.gain_a_grad[...] = jnp.zeros_like(self.gain_a_grad)

        def body(r):
            back, terms = norm_back(self.middle[r], gain, self.x[r].astype(jnp.float32))
            self.gain_a_grad[...] += terms
            self.grad_mid[r] += back

        self.row_chunks(body)

    def small_grads(self):
        tile = self.tile
        shape = (64, 4 * tile)
        slot = lax.broadcasted_iota(jnp.int32, shape, 1)
        offset = jnp.where(slot < 3 * tile, slot - tile, slot - 5 * tile)
        row = lax.broadcasted_iota(jnp.int32, shape, 0)
        per = NB // 8
        inside = row % 8 - 2
        wanted = jnp.where((inside >= 0) & (inside < per), (row // 8) * per + inside, -1)
        hits = (bucket_of(offset) == wanted).astype(jnp.float32)
        table = lax.dot_general(
            hits,
            self.rel_grad[...],
            (((1,), (1,)), ((), ())),
            precision=highest,
            preferred_element_type=jnp.float32,
        )
        rows = lax.broadcasted_iota(jnp.int32, (8, 128), 0)
        lane = lax.broadcasted_iota(jnp.int32, (8, 128), 1)
        for shard in range(8):
            block = table[8 * shard : 8 * shard + 8]
            for index, ref in ((0, self.gain_a_grad), (1, self.gain_f_grad)):
                wide = ref[...]
                if shard:
                    wide = pltpu.roll(wide, self.width - shard * self.shard_rows, axis=1)
                here = (rows == index) & (lane < self.shard_rows)
                block = jnp.where(here, jnp.broadcast_to(wide[:, :128], (8, 128)), block)
            self.small_out[shard] = block


(
    SEND_Z, SEND_X, GOT_SECOND, GOT_BESIDE, GOT_ACROSS, GOT_X, GOT_Y, GOT_CORE, DRAIN, SMALL_Z,
    SMALL_X, SMALL_SECOND, SMALL_BESIDE, SMALL_ACROSS, SUM_SEND, SUM_CORE, SUM_Y, SUM_X, SUM_Z,
    SUM_BACK, SUM_DONE, NORM, PROJECT, ATTEND, MIDDLE, RAISE, OUTER_GRAD, LOWER, RAISED_GRAD,
    INNER_GRAD, MIDDLE_GRAD, MIDDLE_NORM, OUTPUT_GRAD, ATTENDED_GRAD, ATTEND_BACK, SQUARE_GRAD,
    NORMED_GRAD, INPUT_GRAD, SMALL, SMALL_SUM, SMALL_DONE,
) = range(41)

ORDER = (
    (SMALL_Z, 0), (SMALL_X, 0), (SEND_X, 4), (SEND_Z, 1), (SEND_X, 7), (SEND_X, 1), (SEND_X, 2),
    (SEND_X, 0), (SEND_Z, 0), (GOT_SECOND, 1), (GOT_SECOND, 0), (SEND_X, 6), (SEND_Z, 2),
    (GOT_BESIDE, 1), (SMALL_SECOND, 0), (SMALL_BESIDE, 0), (GOT_ACROSS, 1), (SMALL_ACROSS, 0),
    (SEND_Z, 3), (GOT_ACROSS, 0), (GOT_BESIDE, 0), (GOT_BESIDE, 2), (GOT_SECOND, 2), (GOT_X, 1),
    (SEND_Z, 5), (GOT_X, 0), (SEND_X, 3), (GOT_ACROSS, 2), (GOT_SECOND, 3), (SEND_Z, 4),
    (GOT_SECOND, 5), (GOT_ACROSS, 3), (GOT_BESIDE, 5), (NORM, 0), (GOT_Y, 1), (GOT_Y, 0),
    (GOT_X, 2), (GOT_BESIDE, 3), (SEND_Z, 6), (SEND_Z, 11), (SEND_X, 5), (GOT_CORE, 1),
    (PROJECT, 1), (GOT_CORE, 0), (GOT_SECOND, 4), (PROJECT, 0), (SEND_Z, 7), (GOT_ACROSS, 5),
    (GOT_Y, 2), (SEND_X, 11), (GOT_X, 3), (GOT_BESIDE, 4), (ATTEND, 0), (GOT_SECOND, 6),
    (SEND_Z, 9), (GOT_ACROSS, 4), (GOT_X, 5), (GOT_BESIDE, 6), (GOT_CORE, 2), (PROJECT, 2),
    (GOT_BESIDE, 11), (GOT_SECOND, 11), (ATTEND, 1), (GOT_ACROSS, 6), (GOT_X, 4), (GOT_Y, 3),
    (GOT_SECOND, 7), (SEND_Z, 10), (ATTEND, 2), (GOT_Y, 5), (SEND_Z, 8), (GOT_ACROSS, 7),
    (GOT_BESIDE, 7), (GOT_SECOND, 9), (GOT_CORE, 3), (GOT_X, 6), (SEND_X, 9), (GOT_Y, 4),
    (MIDDLE, 0), (GOT_BESIDE, 9), (GOT_ACROSS, 11), (GOT_CORE, 5), (GOT_CORE, 4), (RAISE, 0),
    (GOT_ACROSS, 9), (GOT_X, 7), (GOT_SECOND, 8), (GOT_Y, 6), (RAISE, 1), (GOT_ACROSS, 8),
    (GOT_BESIDE, 8), (GOT_BESIDE, 10), (SEND_X, 8), (GOT_CORE, 6), (RAISE, 2), (GOT_X, 11),
    (GOT_Y, 7), (GOT_SECOND, 10), (OUTER_GRAD, 0), (GOT_X, 9), (GOT_CORE, 7), (GOT_ACROSS, 10),
    (RAISE, 3), (SEND_X, 10), (GOT_X, 8), (GOT_Y, 11), (OUTER_GRAD, 1), (GOT_X, 10),
    (SUM_SEND, 0), (SUM_SEND, 1), (GOT_Y, 9), (SUM_CORE, 0), (GOT_Y, 8), (SUM_CORE, 1),
    (DRAIN, 0), (GOT_Y, 10), (GOT_CORE, 9), (GOT_CORE, 11), (SUM_SEND, 2), (GOT_CORE, 8),
    (SUM_SEND, 3), (GOT_CORE, 10), (RAISED_GRAD, 0), (SUM_Y, 0), (SUM_CORE, 2), (INNER_GRAD, 0),
    (SUM_CORE, 3), (SUM_SEND, 4), (LOWER, 0), (SUM_Y, 1), (RAISED_GRAD, 1), (SUM_SEND, 5),
    (SUM_CORE, 4), (LOWER, 1), (SUM_X, 0), (SUM_Y, 2), (MIDDLE_GRAD, 0), (SUM_X, 1),
    (INNER_GRAD, 1), (SUM_SEND, 6), (SUM_CORE, 5), (SUM_Y, 3), (MIDDLE_GRAD, 1), (SUM_CORE, 6),
    (LOWER, 2), (SUM_X, 2), (SUM_SEND, 7), (MIDDLE_NORM, 0), (SUM_Y, 4), (OUTPUT_GRAD, 0),
    (ATTENDED_GRAD, 0), (SUM_X, 3), (SUM_SEND, 8), (SUM_CORE, 7), (ATTEND_BACK, 0), (SUM_X, 4),
    (SUM_Y, 5), (SUM_CORE, 8), (ATTEND_BACK, 1), (SUM_Y, 7), (SUM_Z, 4), (SUM_X, 5),
    (SQUARE_GRAD, 0), (SUM_SEND, 9), (SQUARE_GRAD, 1), (SUM_Y, 8), (SUM_Z, 0), (SUM_SEND, 10),
    (SUM_Y, 6), (SUM_Z, 1), (SUM_CORE, 9), (SUM_X, 7), (ATTEND_BACK, 2), (SUM_X, 8),
    (SUM_CORE, 10), (SQUARE_GRAD, 2), (SUM_Y, 9), (SUM_SEND, 11), (SUM_X, 6), (SUM_CORE, 11),
    (SUM_Z, 3), (SUM_Z, 2), (SUM_BACK, 4), (NORMED_GRAD, 0), (SUM_Y, 10), (NORMED_GRAD, 1),
    (SUM_X, 9), (INPUT_GRAD, 0), (SUM_BACK, 1), (SUM_Y, 11), (SUM_Z, 5), (SUM_Z, 7), (SUM_Z, 8),
    (SUM_X, 10), (SUM_BACK, 2), (SUM_BACK, 5), (SUM_DONE, 2), (SUM_Z, 6), (SUM_X, 11),
    (SUM_BACK, 6), (SMALL, 0), (SUM_BACK, 7), (SUM_BACK, 3), (SUM_Z, 10), (SUM_Z, 9),
    (SMALL_SUM, 0), (SUM_BACK, 0), (SUM_Z, 11), (SUM_DONE, 5), (SUM_DONE, 3), (SUM_DONE, 1),
    (SUM_BACK, 10), (SUM_BACK, 8), (SUM_DONE, 0), (SMALL_DONE, 0), (SUM_DONE, 8), (SUM_DONE, 6),
    (SUM_BACK, 9), (SUM_BACK, 11), (SUM_DONE, 9), (SUM_DONE, 10), (SUM_DONE, 7), (SUM_DONE, 4),
    (SUM_DONE, 11),
)


def order_slot(n):
    return n + 12 if n < 8 else (7 if n == 8 else n - 5)


def fused_kernel(
    length, x, cot, gain_a_own, gain_f_own, table_own, query_own, key_own, value_own, output_own,
    inner_own, outer_own,
    block_far, grad_far, own_far, small_result, probs_far,
    bank, own_sum, from_core, from_y, from_x, from_z, small_wide, all_small, small_out,
    small_in, small_rep, probs, normed, qkv, attended, middle, normed_ffn, active, slope, seed,
    grad_mid, mid_low, scores, rel, rel_grad, gain_a, gain_f, gain_a_grad,
    gain_f_grad, strip, grad_scores,
    sends, recvs, sum_sends, sum_recvs, small_sends, small_recvs, back_sems, probs_sems,
    misc_sems, keep_sems,
):
    shard = lax.axis_index("fsdp")
    copy_id = lax.axis_index("rep")
    layer = Layer(
        length=length, x=x, bank=bank, all_small=all_small, small_out=small_out,
        probs=probs, probs_far=probs_far, probs_sems=probs_sems, normed=normed, qkv=qkv,
        attended=attended, middle=middle, normed_ffn=normed_ffn, active=active, slope=slope,
        seed=seed, grad_mid=grad_mid, mid_low=mid_low, scores=scores,
        rel=rel, rel_grad=rel_grad, gain_a=gain_a, gain_f=gain_f, gain_a_grad=gain_a_grad,
        gain_f_grad=gain_f_grad, strip=strip, grad_scores=grad_scores,
    )
    rows, width = query_own.shape
    chunks = inner_own.shape[1] // width
    units = 4 + 2 * chunks
    gather = Gather(bank, sends, recvs)
    scatter = Scatter(
        order_slot, bank, own_sum, from_core, from_y, from_x, from_z, sum_sends, sum_recvs
    )
    pairs = probs_far.shape[0]

    def remote(src, dst, send, recv, device):
        return pltpu.make_async_remote_copy(
            src_ref=src, dst_ref=dst, send_sem=send, recv_sem=recv, device_id=device,
            device_id_type=MESH,
        )

    def peer(k):
        return (lax.rem(shard + k, 8), copy_id)

    def rep_peer(k):
        return (shard, lax.rem(copy_id + k, 4))

    parts = [output_own]
    parts += [inner_own.at[:, pl.ds(i * width, width)] for i in range(chunks)]
    parts += [outer_own.at[pl.ds(i * rows, rows)] for i in range(chunks)]
    third = width // 3
    homes = [
        (part.at[:, pl.ds(u * third, third)], bank.at[gather.z, gather.x, u, :, pl.ds(n * third, third)])
        for u in range(3)
        for n, part in enumerate((query_own, key_own, value_own))
    ]
    homes += [(part, bank.at[gather.z, gather.x, 3 + u]) for u, part in enumerate(parts)]
    keeps = [
        pltpu.make_async_copy(part, home, keep_sems.at[0]) for part, home in homes
    ]
    keep_seed = pltpu.make_async_copy(cot, seed, keep_sems.at[1])
    keeps.append(keep_seed)
    peers = gather.peers()
    greet(peers, gather.at_end)
    for copy in keeps:
        copy.start()
    small_wide[...] = jnp.zeros_like(small_wide)
    small_wide[0:1, :rows] = gain_a_own[...].astype(jnp.float32)
    small_wide[1:2, :rows] = gain_f_own[...].astype(jnp.float32)
    per, heads = table_own.shape
    small_wide[2 : 2 + per, :heads] = table_own[...].astype(jnp.float32)
    all_small[shard] = small_wide[...].astype(jnp.bfloat16)
    smalls = SmallGather(gather, all_small, small_sends, small_recvs)
    mine = bank.at[gather.z, gather.x, 0:units]
    pltpu.make_async_copy(mine, mine, keep_sems.at[0]).wait()
    all_greeted(peers, gather.at_end)

    def store(n):
        return pltpu.make_async_copy(own_sum.at[n], own_far.at[n], misc_sems.at[2])

    def sum_done(n):
        scatter.after_back_core(n)
        store(n).start()

    block_store = pltpu.make_async_copy(mid_low, block_far, misc_sems.at[0])
    grad_store = pltpu.make_async_copy(grad_mid, grad_far, misc_sems.at[1])
    back_copies = [
        remote(
            small_out.at[lax.rem(shard + k, 8)], small_in.at[k - 1], back_sems.at[0],
            back_sems.at[1], peer(k),
        )
        for k in range(1, 8)
    ]
    rep_copies = [
        remote(
            small_rep.at[copy_id], small_rep.at[copy_id], back_sems.at[2], back_sems.at[3],
            rep_peer(k),
        )
        for k in range(1, 4)
    ]

    def wait_for(part, sem):
        pltpu.make_async_copy(part, part, sem).wait()

    def norm(_):
        keep_seed.wait()
        layer.mask_seed()
        smalls.after_x(0)
        layer.small_arrays()
        layer.norm_in()

    def middle_rows(_):
        layer.middle_rows()
        for pair in (pairs - 2, pairs - 1):
            layer.probs_store(pair, pair % 2).wait()
        for pair in (0, 1):
            layer.probs_load(pair, pair).start()

    def lower(n):
        layer.lower(n)
        if n == width // 256 - 1:
            block_store.start()

    def middle_norm(_):
        block_store.wait()
        layer.middle_norm()
        rel_grad[...] = jnp.zeros_like(rel_grad)

    def input_grad(_):
        layer.input_grad()
        grad_store.start()

    def small_sums(_):
        layer.small_grads()
        for copy in back_copies:
            copy.start()

    def small_sum(_):
        wait_for(small_in, back_sems.at[1])
        total = small_out[shard]
        for k in range(7):
            total = total + small_in[k]
        small_rep[copy_id] = total
        for copy in rep_copies:
            copy.start()

    def small_done(_):
        wait_for(small_rep.at[0:3], back_sems.at[3])
        small_result[...] = (small_rep[0] + small_rep[1]) + (small_rep[2] + small_rep[3])

    work = {
        SEND_Z: gather.send_z,
        SEND_X: gather.send_x,
        GOT_SECOND: gather.after_second,
        GOT_BESIDE: gather.after_beside,
        GOT_ACROSS: gather.after_across,
        GOT_X: gather.after_x,
        GOT_Y: gather.after_y,
        GOT_CORE: gather.after_core,
        DRAIN: gather.drain,
        SMALL_Z: smalls.send_z,
        SMALL_X: smalls.send_x,
        SMALL_SECOND: smalls.after_second,
        SMALL_BESIDE: smalls.after_beside,
        SMALL_ACROSS: smalls.after_across,
        SUM_SEND: scatter.start,
        SUM_CORE: scatter.after_core,
        SUM_Y: scatter.after_y,
        SUM_X: scatter.after_x,
        SUM_Z: scatter.after_z,
        SUM_BACK: scatter.after_back_y,
        SUM_DONE: sum_done,
        NORM: norm,
        PROJECT: layer.project,
        ATTEND: lambda u: loop(2, functools.partial(layer.attend, u)),
        MIDDLE: middle_rows,
        RAISE: layer.raise_unit,
        OUTER_GRAD: lambda k: loop(4, lambda n: layer.outer_grad(4 * k + n)),
        LOWER: lower,
        RAISED_GRAD: lambda k: loop(4, lambda n: layer.raised_grad(4 * k + n)),
        INNER_GRAD: lambda k: loop(2, lambda n: layer.inner_grad(2 * k + n)),
        MIDDLE_GRAD: layer.middle_grad,
        MIDDLE_NORM: middle_norm,
        OUTPUT_GRAD: lambda _: layer.square_grad(attended, lambda c: mid_low[:, c], 7),
        ATTENDED_GRAD: lambda _: layer.attended_grad(),
        ATTEND_BACK: lambda u: loop(2, functools.partial(layer.attend_back, u)),
        SQUARE_GRAD: lambda u: layer.square_grad(normed, lambda c: qkv[u, :, c], 4 + u),
        NORMED_GRAD: layer.normed_grad,
        INPUT_GRAD: input_grad,
        SMALL: small_sums,
        SMALL_SUM: small_sum,
        SMALL_DONE: small_done,
    }
    for name, n in ORDER:
        work[name](n)
    gather.drain(1)
    smalls.drain(0)
    scatter.drain()
    wait_for(small_in, back_sems.at[0])
    wait_for(small_rep.at[0:3], back_sems.at[2])
    wait_for(own_sum, misc_sems.at[2])
    grad_store.wait()


def fused_call(length, x, cot, gain_a, gain_f, table, square, inner, outer):
    rows, width = square[0].shape
    units = 4 + 2 * (inner.shape[1] // width)
    heads = table.shape[1]
    seq = x.shape[0]
    half = rows // 2
    part = half // 3
    hidden = inner.shape[1]
    low, wide = jnp.bfloat16, jnp.float32
    anywhere = pl.BlockSpec(memory_space=pl.ANY)
    within = pl.BlockSpec(memory_space=pltpu.VMEM)
    sems = pltpu.SemaphoreType.DMA
    vm = pltpu.VMEM
    head_rows = -(-heads // 8) * 8
    return pl.pallas_call(
        fused_kernel,
        out_shape=(
            jax.ShapeDtypeStruct((seq, width), low),
            jax.ShapeDtypeStruct((seq, width), wide),
            jax.ShapeDtypeStruct((units, rows, width), low),
            jax.ShapeDtypeStruct((8, 128), wide),
            jax.ShapeDtypeStruct((heads // 2, 2, seq, seq), low),
        ),
        in_specs=[pl.BlockSpec(memory_space=pltpu.SMEM), within, anywhere]
        + [within] * 3
        + [anywhere] * 6,
        out_specs=[anywhere, anywhere, anywhere, within, anywhere],
        scratch_shapes=[
            vm((4, 2, units + 8, rows, width), low),
            vm((units, rows, width), low),
            vm((6, 4, 2, half, width), low),
            vm((units, 4, 2, part, width), low),
            vm((units, 4, 2 * part, width), low),
            vm((units, 4, 2 * part, width), low),
            vm((16, 128), wide),
            vm((8, 16, 128), low),
            vm((8, 8, 128), wide),
            vm((7, 8, 128), wide),
            vm((4, 8, 128), wide),
            vm((2, 2, seq, seq), low),
            vm((seq, width), low),
            vm((3, seq, width), low),
            vm((seq, width), low),
            vm((seq, width), wide),
            vm((seq, width), low),
            vm((seq, hidden), low),
            vm((seq, hidden), low),
            vm((seq, width), low),
            vm((seq, width), wide),
            vm((seq, width), low),
            vm((2, seq, seq), wide),
            vm((head_rows, 512), wide),
            vm((128, 512), wide),
            vm((1, width), wide),
            vm((1, width), wide),
            vm((1, width), wide),
            vm((1, width), wide),
            vm((2, 128, 128 * 7), wide),
            vm((2, seq, seq), low),
            sems((2,)),
            sems((units, Gather.slots)),
            sems((4 + units,)),
            sems((units, Scatter.slots)),
            sems((1,)),
            sems((4,)),
            sems((4,)),
            sems((2,)),
            sems((3,)),
            sems((2,)),
        ],
        compiler_params=pltpu.CompilerParams(
            collective_id=0, has_side_effects=True, vmem_limit_bytes=63 * 2**20
        ),
    )(length, x, cot, gain_a, gain_f, table, *square, inner, outer)


def finish_kernel(
    block_in, grad_in, sums_far, small, block_out, grad_out, query_out, key_out, value_out,
    output_out, gain_a, table, inner_out, outer_out, gain_f, block, grad, query, key, value, output,
    inner, outer, sums, in_sems, out_sems,
):
    units, rows, width = sums.shape
    chunks = inner.shape[1] // width
    third = width // 3
    straight = ((block_in, block, block_out), (grad_in, grad, grad_out))
    loads = [pltpu.make_async_copy(sums_far.at[n], sums.at[n], in_sems.at[n]) for n in range(units)]
    loads += [
        pltpu.make_async_copy(far, near, in_sems.at[units + n])
        for n, (far, near, _) in enumerate(straight)
    ]
    for copy in loads[units:] + loads[:units]:
        copy.start()
    stores = []

    def store(near, far):
        stores.append(pltpu.make_async_copy(near, far, out_sems.at[len(stores)]))
        stores[-1].start()

    for n, (_, near, far) in enumerate(straight):
        loads[units + n].wait()
        store(near, far)
    gain_a[...] = small[0:1, :rows]
    gain_f[...] = small[1:2, :rows]
    table[...] = small[2 : 2 + table.shape[0], : table.shape[1]]
    for i in range(chunks):
        part = pl.ds(i * rows, rows)
        loads[i].wait()
        outer[part, :] = sums[i].astype(jnp.float32)
        store(outer.at[part], outer_out.at[part])
    for i in range(chunks):
        part = pl.ds(i * width, width)
        loads[chunks + i].wait()
        inner[:, part] = sums[chunks + i].astype(jnp.float32)
        store(inner.at[:, part], inner_out.at[:, part])
    loads[2 * chunks].wait()
    output[...] = sums[2 * chunks].astype(jnp.float32)
    store(output, output_out)
    for u in range(3):
        loads[2 * chunks + 1 + u].wait()
        for n, ref in enumerate((query, key, value)):
            ref[:, u * third : (u + 1) * third] = sums[
                2 * chunks + 1 + u, :, n * third : (n + 1) * third
            ].astype(jnp.float32)
    for near, far in ((query, query_out), (key, key_out), (value, value_out)):
        store(near, far)
    for copy in stores:
        copy.wait()


def finish_call(block, grad, sums, small, table_shape, inner_shape, outer_shape):
    units, rows, width = sums.shape
    wide = jnp.float32
    anywhere = pl.BlockSpec(memory_space=pl.ANY)
    within = pl.BlockSpec(memory_space=pltpu.VMEM)
    shapes = [(rows, width)] * 4 + [(1, rows), table_shape, inner_shape, outer_shape, (1, rows)]
    places = [anywhere] * 4 + [within] * 2 + [anywhere] * 2 + [within]
    staged = [shape for shape, place in zip(shapes, places) if place is anywhere]
    return pl.pallas_call(
        finish_kernel,
        out_shape=[
            jax.ShapeDtypeStruct(block.shape, block.dtype),
            jax.ShapeDtypeStruct(grad.shape, grad.dtype),
        ]
        + [jax.ShapeDtypeStruct(shape, wide) for shape in shapes],
        in_specs=[anywhere, anywhere, anywhere, within],
        out_specs=[anywhere, anywhere] + places,
        scratch_shapes=[
            pltpu.VMEM(block.shape, block.dtype),
            pltpu.VMEM(grad.shape, grad.dtype),
            *[pltpu.VMEM(shape, wide) for shape in staged],
            pltpu.VMEM(sums.shape, sums.dtype),
            pltpu.SemaphoreType.DMA((units + 2,)),
            pltpu.SemaphoreType.DMA((units + 2,)),
        ],
        compiler_params=pltpu.CompilerParams(vmem_limit_bytes=63 * 2**20),
    )(block, grad, sums, small)


def local_linked(
    inputs, lengths, cotangent, query_weight, key_weight, value_weight, output_weight,
    attention_gain, bias_table, inner_weight, outer_weight, feedforward_gain,
):
    rows = query_weight.shape[0]
    square = (query_weight, key_weight, value_weight, output_weight)
    block, grad, sums, small, _ = fused_call(
        lengths, inputs[0], cotangent[0], attention_gain.reshape(1, rows),
        feedforward_gain.reshape(1, rows), bias_table, square, inner_weight, outer_weight,
    )
    block, grad, query, key, value, output, gain_a, table, inner, outer, gain_f = finish_call(
        block, grad, sums, small, bias_table.shape, inner_weight.shape, outer_weight.shape
    )
    return (
        block[None], grad[None], query, key, value, output, gain_a.reshape(rows), table, inner,
        outer, gain_f.reshape(rows),
    )


def local(inputs, lengths, cotangent, *shards):
    block_output, input_grad, gradients = compute(inputs, lengths, cotangent, gather_all(*shards))
    return (block_output, input_grad) + sum_all(gradients)


def can_link(mesh):
    return mesh.shape["fsdp"] == 8 and mesh.shape["rep"] == 4


def solution(mesh):
    placed = (
        P(("fsdp", "rep"), None, None),
        P(("fsdp", "rep")),
        P(("fsdp", "rep"), None, None),
        P("fsdp", None),
        P("fsdp", None),
        P("fsdp", None),
        P("fsdp", None),
        P("fsdp"),
        P("fsdp", None),
        P("fsdp", None),
        P("fsdp", None),
        P("fsdp"),
    )
    return jax.shard_map(
        local_linked if can_link(mesh) else local,
        mesh=mesh,
        in_specs=placed,
        out_specs=(
            P(("fsdp", "rep"), None, None),
            P(("fsdp", "rep"), None, None),
            P("fsdp", None),
            P("fsdp", None),
            P("fsdp", None),
            P("fsdp", None),
            P("fsdp"),
            P("fsdp", None),
            P("fsdp", None),
            P("fsdp", None),
            P("fsdp"),
        ),
        check_vma=False,
    )
```

```python
import functools

import jax
import jax.numpy as jnp
from jax import lax
import jax.experimental.pallas as pl
import jax.experimental.pallas.tpu as pltpu
from jax.sharding import PartitionSpec as P

NB = 32


epsilon = 1e-06
highest = lax.Precision.HIGHEST
gelu_coeff = 0.7978845608028654
masked_score = -1e30


def bucket_of(offset):
    half_count = NB // 2
    exact_count = half_count // 2
    distance = jnp.abs(offset)
    beyond = jnp.full(offset.shape, exact_count, jnp.int32)
    for exponent in range(1, half_count - exact_count):
        beyond = beyond + (distance * distance >= exact_count * exact_count * 2**exponent).astype(
            jnp.int32
        )
    nearby = jnp.where(distance < exact_count, distance, beyond)
    return jnp.where(offset > 0, half_count, 0).astype(jnp.int32) + nearby


def rms_norm(values, gain_vector):
    inverse_rms = lax.rsqrt(jnp.mean(values * values, axis=-1, keepdims=True) + epsilon)
    return values * inverse_rms * gain_vector


def gelu(values):
    return (
        0.5 * values * (1.0 + jnp.tanh(gelu_coeff * (values + 0.044715 * values * values * values)))
    )


def dot(a,b): return jnp.dot(a,b,preferred_element_type=jnp.float32)
def dot_t(a,b): return lax.dot_general(a,b,(((1,),(1,)),((),())),preferred_element_type=jnp.float32)
def dot_c(a,b): return lax.dot_general(a,b,(((0,),(0,)),((),())),preferred_element_type=jnp.float32)

def fwd_kernel(T, len_ref, q_ref, k_ref, v_ref, rel_ref, o_ref, p_ref, strip):
    hp=pl.program_id(0)
    seq=q_ref.shape[0]; nb=seq//T
    lane=lax.broadcasted_iota(jnp.int32,(1,128),1)
    kcol=lax.broadcasted_iota(jnp.int32,(1,seq),1)
    mask=jnp.where(kcol<len_ref[0],0.0,-1e30)
    k=k_ref[...]; v=v_ref[...]
    for hh in range(2):
        mine=(lane>=64) if hh else (lane<64)
        rel=rel_ref[pl.ds(hh,1),:]
        W=4*T
        rolled=pltpu.roll(jnp.broadcast_to(rel,(T,W)),0,axis=1,stride=1,stride_axis=0)
        strip[:, 2*T:5*T]=rolled[:, :3*T]
        far_neg=rel[:, 0:1]; far_pos=rel[:, 3*T-1:3*T]
        strip[:, 0:2*T]=jnp.broadcast_to(far_neg,(T,2*T))
        strip[:, 5*T:7*T]=jnp.broadcast_to(far_pos,(T,2*T))
        for I in range(nb):
            q=jnp.where(mine,q_ref[I*T:(I+1)*T,:],jnp.bfloat16(0))
            s=dot_t(q,k)+(strip[:, (3-I)*T:(3-I)*T+seq]+mask)
            m=jnp.max(s,axis=-1,keepdims=True)
            e=jnp.exp(s-m)
            tot=jnp.sum(e,axis=-1,keepdims=True)
            p=(e*(1.0/tot)).astype(jnp.bfloat16)
            p_ref[hh,I*T:(I+1)*T,:]=p
            o=dot(p,v)
            if hh==0:
                o_ref[I*T:(I+1)*T,:]=o.astype(jnp.bfloat16)
            else:
                o_ref[I*T:(I+1)*T,:]=jnp.where(mine,o.astype(jnp.bfloat16),o_ref[I*T:(I+1)*T,:])

def bwd_kernel(T, q_ref, k_ref, v_ref, do_ref, p_ref, dq_ref, dk_ref, dv_ref, db_ref, ds_ref):
    seq=q_ref.shape[0]; nb=seq//T
    lane=lax.broadcasted_iota(jnp.int32,(1,128),1)
    k=k_ref[...]; v=v_ref[...]
    dks=[];dvs=[]
    for hh in range(2):
        mine=(lane>=64) if hh else (lane<64)
        acc=[None]*5
        for I in range(nb):
            sl=slice(I*T,(I+1)*T)
            do=jnp.where(mine,do_ref[sl,:],jnp.bfloat16(0))
            dp=dot_t(do,v)
            p=p_ref[hh,sl,:].astype(jnp.float32)
            t=p*dp
            delta=jnp.sum(t,axis=-1,keepdims=True)
            ds=(t-p*delta).astype(jnp.bfloat16)
            ds_ref[sl,:]=ds
            dsf=ds.astype(jnp.float32)
            for J in range(nb):
                d=min(2,max(-2,J-I))+2
                x=dsf[:,J*T:(J+1)*T]
                acc[d]=x if acc[d] is None else acc[d]+x
            dq=dot(ds,k)
            if hh==0: dq_ref[sl,:]=dq.astype(jnp.bfloat16)
            else: dq_ref[sl,:]=jnp.where(mine,dq.astype(jnp.bfloat16),dq_ref[sl,:])
        near=jnp.concatenate([acc[1],acc[2],acc[3],jnp.zeros((T,T),jnp.float32)],axis=1)
        total=shear_sum(near,4*T)
        far=jnp.concatenate([jnp.zeros((1,2*T),jnp.float32),jnp.sum(acc[4],axis=0,keepdims=True),jnp.sum(acc[0],axis=0,keepdims=True)],axis=1)
        db_ref[hh:hh+1,:]=total+far
        dk=dot_c(q_ref[...],ds_ref[...]).T; dv=dot_c(do_ref[...],p_ref[hh]).T
        dks.append(dk); dvs.append(dv)
    dk_ref[...]=jnp.where(lane<64,dks[0],dks[1]).astype(jnp.bfloat16)
    dv_ref[...]=jnp.where(lane<64,dvs[0],dvs[1]).astype(jnp.bfloat16)

def rel_hits(tile):
    slot = jnp.arange(4 * tile, dtype=jnp.int32)
    offset = jnp.where(slot < 3 * tile, slot - tile, slot - 5 * tile)
    bucket_ids = jnp.arange(NB, dtype=jnp.int32)
    return (bucket_of(offset)[None, :] == bucket_ids[:, None]).astype(jnp.bfloat16)


def rel_vec(table, tile):
    return dot_c(table, rel_hits(tile))


def shear_sum(block, width):
    rows = block.shape[0]
    while rows > 8:
        rows //= 2
        block = block[:rows] + pltpu.roll(block[rows:], width - rows, axis=1)
    total = block[0:1]
    for r in range(1, 8):
        total = total + pltpu.roll(block[r : r + 1], width - r, axis=1)
    return total


def att_fwd(q,k,v,rel,length,T=128):
    seq,D=q.shape; H=rel.shape[0]
    blk=pl.BlockSpec((seq,128),lambda h: (0,h))
    return pl.pallas_call(functools.partial(fwd_kernel,T),grid=(H//2,),
        in_specs=[pl.BlockSpec(memory_space=pltpu.SMEM),blk,blk,blk,pl.BlockSpec((None,2,4*T),lambda h:(h,0,0))],
        out_specs=[blk,pl.BlockSpec((2,seq,seq),lambda h:(h,0,0))],
        out_shape=[jax.ShapeDtypeStruct((seq,D),jnp.bfloat16),jax.ShapeDtypeStruct((H,seq,seq),jnp.bfloat16)],
        scratch_shapes=[pltpu.VMEM((T,7*T),jnp.float32)],
        compiler_params=pltpu.CompilerParams(vmem_limit_bytes=40*2**20))(length,q,k,v,rel.reshape(H//2,2,4*T))
def att_bwd(q,k,v,do,p,T=128):
    seq,D=q.shape; H=p.shape[0]
    blk=pl.BlockSpec((seq,128),lambda h: (0,h))
    o=jax.ShapeDtypeStruct((seq,D),jnp.bfloat16)
    outs=pl.pallas_call(functools.partial(bwd_kernel,T),grid=(H//2,),
        in_specs=[blk,blk,blk,blk,pl.BlockSpec((2,seq,seq),lambda h:(h,0,0))],
        out_specs=[blk,blk,blk,pl.BlockSpec((None,2,4*T),lambda h:(h,0,0))],
        out_shape=[o,o,o,jax.ShapeDtypeStruct((H//2,2,4*T),jnp.float32)],
        scratch_shapes=[pltpu.VMEM((seq,seq),jnp.bfloat16)],
        compiler_params=pltpu.CompilerParams(vmem_limit_bytes=40*2**20))(q,k,v,do,p)
    return *outs[:3],outs[3].reshape(H,4*T)

def contract_rows(left, right):
    return lax.dot_general(
        left, right, (((0,), (0,)), ((), ())), preferred_element_type=jnp.float32
    )


def contract_cols(left, right):
    return lax.dot_general(
        left, right, (((1,), (1,)), ((), ())), preferred_element_type=jnp.float32
    )


MESH = pl.DeviceIdType.MESH


def coords():
    shard = lax.axis_index("fsdp")
    copy = lax.axis_index("rep")
    return shard // 2, shard % 2, copy // 2, copy % 2


def greet(peers, at_end):
    barrier = pltpu.get_barrier_semaphore()
    for peer in peers[:-1]:
        pl.semaphore_signal(barrier, inc=1, device_id=peer, device_id_type=MESH)

    def last():
        pl.semaphore_signal(barrier, inc=1, device_id=peers[-1], device_id_type=MESH)

    pl.when(~at_end)(last)


def all_greeted(peers, at_end):
    barrier = pltpu.get_barrier_semaphore()
    pl.semaphore_wait(barrier, jnp.where(at_end, len(peers) - 1, len(peers)))


class Links:
    def __init__(self, rows, send_sems, recv_sems):
        self.send_sems, self.recv_sems = send_sems, recv_sems
        self.z, self.x, self.y, self.c = coords()
        half = rows // 2
        part = half // 3
        at = lambda start, size: pl.ds(pl.multiple_of(start, part), size)
        first = half * self.c
        other = half * (1 - self.c)
        self.half, self.other_half = at(first, half), at(other, half)
        self.plane = at(first + part * self.y, 2 * part)
        self.shared = at(first + part, part)
        self.own_third = at(first + 2 * part * self.y, part)
        self.other_third = at(first + 2 * part * (1 - self.y), part)
        self.shared_in = at(part * self.y, part)
        self.third_in = at(part * (1 - self.y), part)

    def copy(self, src, dst, g, send, slot, device):
        return pltpu.make_async_remote_copy(
            src_ref=src,
            dst_ref=dst,
            send_sem=self.send_sems.at[send],
            recv_sem=self.recv_sems.at[g, slot],
            device_id=device,
            device_id_type=MESH,
        )

    def to_x(self):
        return (self.z * 2 + 1 - self.x, self.y * 2 + self.c)

    def to_y(self):
        return (self.z * 2 + self.x, (1 - self.y) * 2 + self.c)

    def to_core(self):
        return (self.z * 2 + self.x, self.y * 2 + 1 - self.c)

    def to_z(self, k):
        return (lax.rem(self.z + k, 4) * 2 + self.x, self.y * 2 + self.c)

    def z_before(self, k):
        return lax.rem(self.z + 4 - k, 4)


class Gather(Links):
    slots = 7

    def __init__(self, full, send_sems, recv_sems):
        super().__init__(full.shape[3], send_sems, recv_sems)
        self.full = full
        self.beside = self.z + 1 - 2 * lax.rem(self.z, 2)
        self.second = lax.rem(self.z + 2, 4)
        self.across = 3 - self.z
        self.at_end = (self.z == 0) | (self.z == 3)
        self.early = range(4, 8)

    def peers(self):
        near = [self.to_x(), self.to_y(), self.to_core()]
        return near + [self.at_z(a) for a in (self.second, self.beside, self.across)]

    def block(self, g, a, rows):
        return self.full.at[a, self.x, g, rows]

    def column(self, g, rows):
        return self.full.at[:, 1 - self.x, g, rows]

    def move(self, part, g, slot, device):
        return pltpu.make_async_remote_copy(
            src_ref=part,
            dst_ref=part,
            send_sem=self.send_sems.at[0 if g in self.early else 1],
            recv_sem=self.recv_sems.at[g, slot],
            device_id=device,
            device_id_type=MESH,
        )

    def at_z(self, a):
        return (a * 2 + self.x, self.y * 2 + self.c)

    def z_copy(self, g, to, slot):
        return self.move(self.block(g, self.z, self.plane), g, slot, self.at_z(to))

    def x_copy(self, g, a):
        return self.move(self.block(g, a, self.plane), g, 3, self.to_x())

    def y_copy(self, g, a):
        return self.move(self.block(g, a, self.own_third), g, 4, self.to_y())

    def core_copy(self, g, a):
        return self.move(self.block(g, a, self.half), g, 5, self.to_core())

    def arrived(self, part, g, slot):
        pltpu.make_async_copy(part, part, self.recv_sems.at[g, slot]).wait()

    def others(self):
        return (self.beside, self.second, self.across)

    def send_z(self, g):
        self.z_copy(g, self.second, 0).start()
        self.z_copy(g, self.beside, 1).start()
        pl.when(~self.at_end)(lambda: self.z_copy(g, self.across, 2).start())

    def send_x(self, g):
        part = self.block(g, self.z, self.plane)
        self.move(part, g, 6 if g % 3 == 2 else 3, self.to_x()).start()

    def pass_beside(self, g):
        part = self.full.at[self.z, 1 - self.x, g, self.plane]
        self.arrived(part, g, 6)
        self.move(part, g, 3, self.at_z(self.beside)).start()

    def spread(self, g, a, slot):
        self.arrived(self.block(g, a, self.plane), g, slot)
        if slot == 0:
            part = self.block(g, a, self.plane)
            pl.when(~self.at_end)(lambda: self.move(part, g, 2, self.at_z(self.beside)).start())
        if slot != 1 or g % 3 != 2:
            self.x_copy(g, a).start()
        self.y_copy(g, a).start()

    def after_second(self, g):
        self.spread(g, self.second, 0)

    def after_beside(self, g):
        self.spread(g, self.beside, 1)

    def after_across(self, g):
        self.spread(g, self.across, 2)

    def after_x(self, g):
        rows = self.plane.size
        part = self.full.at[0, 0, 0:3, 0:rows] if g % 3 == 2 else self.column(g, self.plane)
        self.arrived(part, g, 3)
        self.move(self.column(g, self.own_third), g, 4, self.to_y()).start()

    def after_y(self, g):
        third = self.own_third.size
        self.arrived(self.full.at[0, 0, 0:7, 0:third], g, 4)
        for a in self.others():
            self.core_copy(g, a).start()
        self.move(self.column(g, self.half), g, 5, self.to_core()).start()

    def after_core(self, g):
        self.arrived(self.full.at[0, 0, 0:7, 0 : self.half.size], g, 5)

    def drain(self, n):
        count = len(self.early)
        units = self.full.shape[2] - 8
        rows = self.full.shape[3] * (count if n == 0 else units - count) // units

        def wait(blocks):
            part = self.full.at[:, :, 0:blocks, 0:rows]
            pltpu.make_async_copy(part, part, self.send_sems.at[n]).wait()

        pl.when(self.at_end)(lambda: wait(10))
        pl.when(~self.at_end)(lambda: wait(11))


class SmallGather(Gather):
    def move(self, part, g, slot, device):
        return pltpu.make_async_remote_copy(
            src_ref=part,
            dst_ref=part,
            send_sem=self.send_sems.at[0],
            recv_sem=self.recv_sems.at[slot],
            device_id=device,
            device_id_type=MESH,
        )

    def __init__(self, links, full, send_sems, recv_sems):
        self.__dict__.update(links.__dict__)
        self.full, self.send_sems, self.recv_sems = full, send_sems, recv_sems

    def block(self, g, a, rows):
        return self.full.at[a * 2 + self.x]

    def y_copy(self, g, a):
        return self

    def start(self):
        pass

    def arrived(self, part, g, slot):
        pltpu.make_async_copy(part, part, self.recv_sems.at[slot]).wait()

    def after_x(self, g):
        self.arrived(self.full.at[0:4], g, 3)

    def drain(self, n):
        def wait(blocks):
            part = self.full.at[0:blocks]
            pltpu.make_async_copy(part, part, self.send_sems.at[0]).wait()

        pl.when(self.at_end)(lambda: wait(6))
        pl.when(~self.at_end)(lambda: wait(8))


class Scatter(Links):
    slots = 6
    whole = (0, 2)

    def rows(self, g):
        return self.half if g in self.whole else self.plane

    def count(self, g):
        return self.rows(g).size

    def sender(self, g, n):
        return 3 + n + self.own.shape[0] if g in self.whole else n

    def __init__(self, slot, full, own, from_core, from_y, from_x, from_z, send_sems, recv_sems):
        super().__init__(own.shape[1], send_sems, recv_sems)
        self.slot, self.full, self.own = slot, full, own
        self.from_core, self.from_y, self.from_x, self.from_z = from_core, from_y, from_x, from_z

    def core_copy(self, g):
        part = self.full.at[:, :, self.slot(g), self.other_half]
        ring = g % self.from_core.shape[0]
        return self.copy(part, self.from_core.at[ring], g, 0, 0, self.to_core())

    def y_copy(self, g):
        part = self.full.at[:, :, self.slot(g), self.other_third]
        return self.copy(part, self.from_y.at[g], g, 1, 1, self.to_y())

    def x_copy(self, g):
        part = self.full.at[:, 1 - self.x, self.slot(g), self.rows(g)]
        there = self.from_x.at[g, :, 0 : self.count(g)]
        return self.copy(part, there, g, self.sender(g, 1), 2, self.to_x())

    def z_copy(self, g, k):
        part = self.full.at[lax.rem(self.z + k, 4), self.x, self.slot(g), self.rows(g)]
        there = self.from_z.at[g, k - 1, 0 : self.count(g)]
        return self.copy(part, there, g, self.sender(g, 2), 3, self.to_z(k))

    def back_y_copy(self, g):
        part = self.own.at[g, self.rows(g)]
        return self.copy(part, self.from_z.at[g, 3, 0 : self.count(g)], g, 4 + g, 4, self.to_y())

    def back_core_copy(self, g):
        part = self.own.at[g, self.half]
        return self.copy(part, part, g, 3, 5, self.to_core())

    def start(self, g):
        self.core_copy(g).start()

    def after_core(self, g):
        self.core_copy(g).wait_recv()
        ring = g % self.from_core.shape[0]
        for a in range(4):
            for b in range(2):
                self.full[a, b, self.slot(g), self.half] += self.from_core[ring, a, b]
        (self.x_copy(g) if g in self.whole else self.y_copy(g)).start()

    def after_y(self, g):
        self.y_copy(g).wait_recv()
        for a in range(4):
            for b in range(2):
                self.full[a, b, self.slot(g), self.own_third] += self.from_y[g, a, b]
        self.x_copy(g).start()

    def after_x(self, g):
        self.x_copy(g).wait_recv()
        for a in range(4):
            part = self.from_x[g, a, 0 : self.count(g)]
            self.full[a, self.x, self.slot(g), self.rows(g)] += part
        for k in (1, 2, 3):
            self.z_copy(g, k).start()

    def after_z(self, g):
        total = self.full[self.z, self.x, self.slot(g), self.rows(g)].astype(jnp.float32)
        part = self.from_z.at[g, 0:3, 0 : self.count(g)]
        pltpu.make_async_copy(part, part, self.recv_sems.at[g, 3]).wait()
        for k in (1, 2, 3):
            total = total + self.from_z[g, k - 1, 0 : self.count(g)].astype(jnp.float32)
        self.own[g, self.rows(g)] = total.astype(jnp.bfloat16)
        self.back_y_copy(g).start()

    def after_back_y(self, g):
        self.back_y_copy(g).wait_recv()
        self.back_y_copy(g).wait_send()
        got = self.from_z.at[g, 3]
        if g in self.whole:
            self.own[g, self.half] += got[...]
        else:
            self.own[g, self.shared] += got[self.shared_in]
            self.own[g, self.other_third] = got[self.third_in]
        self.back_core_copy(g).start()

    def after_back_core(self, g):
        part = self.own.at[g, self.other_half]
        self.copy(part, part, g, 3, 5, self.to_core()).wait_recv()

    def drain(self):
        units, rows = self.own.shape[:2]
        few = len(self.whole)
        part = rows // 3
        for n, part in (
            (0, self.full.at[:, :, 0 : units // 2]),
            (1, self.full.at[:, :, 0 : units - few, 0:part]),
            (2, self.from_z.at[0 : units - few, 0:3, 0:part]),
            (3, self.own.at[0 : units // 2]),
            (4 + units, self.from_x.at[0:few]),
            (5 + units, self.from_z.at[0:few, 0:3]),
        ):
            pltpu.make_async_copy(part, part, self.send_sems.at[n]).wait()


def compute(inputs, lengths, cotangent, weights):
    (
        full_query, full_key, full_value, full_output, full_gain, full_table, full_inner,
        full_outer, full_ffn_gain,
    ) = weights
    pairs_here, seq_len, model_width = inputs.shape
    row_count = pairs_here * seq_len
    head_count = full_table.shape[1]
    tile = 128
    relative = rel_vec(full_table, tile)
    flat_inputs = inputs.reshape(row_count, model_width).astype(jnp.float32)
    normed = rms_norm(flat_inputs, full_gain.astype(jnp.float32)).astype(jnp.bfloat16)
    joined = jnp.concatenate((full_query, full_key, full_value), axis=1)
    projected = jnp.dot(normed, joined, preferred_element_type=jnp.float32).astype(jnp.bfloat16)
    queries = projected[:, :model_width]
    key_rows = projected[:, model_width : 2 * model_width]
    value_rows = projected[:, 2 * model_width :]
    pair_rows = [slice(n * seq_len, (n + 1) * seq_len) for n in range(pairs_here)]
    forward_parts = [
        att_fwd(queries[r], key_rows[r], value_rows[r], relative, lengths[n : n + 1], tile)
        for n, r in enumerate(pair_rows)
    ]
    attended = jnp.concatenate([part[0] for part in forward_parts], axis=0)
    middle = flat_inputs + jnp.dot(attended, full_output, preferred_element_type=jnp.float32)
    normed_ffn = rms_norm(middle, full_ffn_gain.astype(jnp.float32)).astype(jnp.bfloat16)
    raised = jnp.dot(normed_ffn, full_inner, preferred_element_type=jnp.float32)
    active = gelu(raised).astype(jnp.bfloat16)
    lowered = jnp.dot(active, full_outer, preferred_element_type=jnp.float32)
    block_output = (middle + lowered).astype(jnp.bfloat16).reshape(pairs_here, seq_len, model_width)
    positions = jnp.arange(seq_len, dtype=jnp.int32)
    row_live = (positions[None, :] < lengths[:, None]).astype(jnp.float32)
    seed_rows = (cotangent.astype(jnp.float32) * row_live[:, :, None]).reshape(
        row_count, model_width
    )
    seed_low = seed_rows.astype(jnp.bfloat16)
    grad_active = contract_cols(seed_low, full_outer)
    grad_outer = contract_rows(active, seed_low)
    grad_raised = jax.vjp(gelu, raised)[1](grad_active)[0].astype(jnp.bfloat16)
    grad_inner = contract_rows(normed_ffn, grad_raised)
    grad_normed_ffn = contract_cols(grad_raised, full_inner)
    ffn_pull = jax.vjp(rms_norm, middle, full_ffn_gain.astype(jnp.float32))[1]
    grad_middle_part, grad_ffn_gain = ffn_pull(grad_normed_ffn)
    grad_middle = seed_rows + grad_middle_part
    joined = jnp.concatenate((full_query, full_key, full_value), axis=1)
    middle_low = grad_middle.astype(jnp.bfloat16)
    grad_attended = contract_cols(middle_low, full_output).astype(jnp.bfloat16)
    grad_output = contract_rows(attended, middle_low)
    backward_parts = [
        att_bwd(
            queries[r], key_rows[r], value_rows[r], grad_attended[r], forward_parts[n][1], tile
        )
        for n, r in enumerate(pair_rows)
    ]
    grad_projected = jnp.concatenate(
        [jnp.concatenate(part[:3], axis=1) for part in backward_parts], axis=0
    )
    grad_joined = contract_rows(normed, grad_projected)
    grad_normed = contract_cols(grad_projected, joined)
    attention_pull = jax.vjp(rms_norm, flat_inputs, full_gain.astype(jnp.float32))[1]
    grad_inputs_part, grad_attention_gain = attention_pull(grad_normed)
    input_grad = (grad_middle + grad_inputs_part).reshape(pairs_here, seq_len, model_width)
    grad_relative = sum(part[3] for part in backward_parts)
    grad_table = lax.dot_general(
        rel_hits(tile).astype(jnp.float32),
        grad_relative,
        (((1,), (1,)), ((), ())),
        precision=highest,
    )
    return block_output, input_grad, (
        grad_joined[:, :model_width],
        grad_joined[:, model_width : 2 * model_width],
        grad_joined[:, 2 * model_width :],
        grad_output,
        grad_attention_gain,
        grad_table,
        grad_inner,
        grad_outer,
        grad_ffn_gain,
    )


def gather_all(query_weight, key_weight, value_weight, output_weight, attention_gain, bias_table,
               inner_weight, outer_weight, feedforward_gain):
    return tuple(
        lax.all_gather(part, "fsdp", axis=0, tiled=True)
        for part in (
            query_weight, key_weight, value_weight, output_weight, attention_gain, bias_table,
            inner_weight, outer_weight, feedforward_gain,
        )
    )


def sum_all(gradients):
    def one(part):
        part = lax.psum_scatter(
            part.astype(jnp.bfloat16), "fsdp", scatter_dimension=0, tiled=True
        )
        return lax.psum(part, "rep").astype(jnp.float32)

    return tuple(one(part) for part in gradients)


def gelu_parts(z):
    square = z * z
    t = jnp.tanh(gelu_coeff * z * (1.0 + 0.044715 * square))
    half = 0.5 * (1.0 + t)
    slope = half + (0.5 * gelu_coeff) * z * (1.0 - t * t) * (1.0 + (3 * 0.044715) * square)
    return z * half, slope


def lanes(start, size):
    return pl.ds(start if isinstance(start, int) else pl.multiple_of(start, 128), size)


def rows_at(start, size):
    return pl.ds(pl.multiple_of(start, size), size)


def loop(count, body):
    def step(n, carry):
        body(n)
        return carry

    lax.fori_loop(0, count, step, 0)


def norm_back(grad, gain, values):
    inverse = lax.rsqrt(jnp.mean(values * values, axis=-1, keepdims=True) + epsilon)
    scaled = grad * gain
    centre = jnp.mean(scaled * values, axis=-1, keepdims=True)
    back = inverse * scaled - values * (inverse * inverse * inverse * centre)
    return back, jnp.sum(grad * values * inverse, axis=0, keepdims=True)


class Layer:
    def __init__(self, **refs):
        self.__dict__.update(refs)
        self.seq, self.width = self.x.shape
        self.tile = 128
        self.row_block = 128
        self.shard_rows = self.bank.shape[3]

    def unit(self, u, column=None, size=None):
        if column is None:
            block = self.bank[:, :, u]
        else:
            block = self.bank[:, :, u, :, lanes(column, size)]
        return block.reshape(-1, block.shape[-1])

    def row_chunks(self, body):
        size = self.row_block
        loop(self.seq // size, lambda n: body(rows_at(n * size, size)))

    def small_arrays(self):
        flat = self.all_small[...].reshape(-1, 128)
        tile = self.tile
        slot = lax.broadcasted_iota(jnp.int32, (flat.shape[0], 4 * tile), 1)
        offset = jnp.where(slot < 3 * tile, slot - tile, slot - 5 * tile)
        row = lax.broadcasted_iota(jnp.int32, (flat.shape[0], 4 * tile), 0)
        per = NB // 8
        inside = row % 16 - 2
        wanted = jnp.where((inside >= 0) & (inside < per), (row // 16) * per + inside, -1)
        hits = (bucket_of(offset) == wanted).astype(jnp.bfloat16)
        self.rel[...] = dot_c(flat, hits)[: self.rel.shape[0]]
        for index, ref in ((0, self.gain_a), (1, self.gain_f)):
            total = jnp.zeros((1, self.width), jnp.float32)
            for shard in range(8):
                part = self.all_small[shard].astype(jnp.float32)[index : index + 1]
                wide = jnp.concatenate(
                    [part, jnp.zeros((1, self.width - 128), jnp.float32)], axis=1
                )
                total = total + (
                    pltpu.roll(wide, shard * self.shard_rows, axis=1) if shard else wide
                )
            ref[...] = total

    def norm_in(self):
        gain = self.gain_a[...]

        def body(r):
            self.normed[r] = rms_norm(self.x[r].astype(jnp.float32), gain).astype(jnp.bfloat16)

        self.row_chunks(body)

    def mask_seed(self):
        def body(r):
            index = lax.broadcasted_iota(jnp.int32, (self.row_block, 1), 0) + r.start
            live = index < self.length[0]
            self.seed[r] = jnp.where(live, self.seed[r], jnp.bfloat16(0))

        self.row_chunks(body)

    def project(self, u):
        def body(n):
            self.qkv[u, :, lanes(n * 256, 256)] = dot(
                self.normed[...], self.unit(u, n * 256, 256)
            ).astype(jnp.bfloat16)

        loop(self.width // 256, body)

    def strip_for(self, head, strip):
        tile = self.tile
        rel = self.rel[pl.ds(head, 1), :]
        rolled = pltpu.roll(
            jnp.broadcast_to(rel, (tile, 4 * tile)), 0, axis=1, stride=1, stride_axis=0
        )
        strip[:, 2 * tile : 5 * tile] = rolled[:, : 3 * tile]
        strip[:, : 2 * tile] = jnp.broadcast_to(rel[:, :1], (tile, 2 * tile))
        strip[:, 5 * tile :] = jnp.broadcast_to(rel[:, 3 * tile - 1 : 3 * tile], (tile, 2 * tile))

    def pair_lanes(self, slot):
        third = self.width // 3
        return [lanes(slot * 128 + n * third, 128) for n in range(3)]

    def probs_store(self, pair, slot):
        return pltpu.make_async_copy(
            self.probs.at[slot], self.probs_far.at[pair], self.probs_sems.at[slot]
        )

    def probs_load(self, pair, slot):
        return pltpu.make_async_copy(
            self.probs_far.at[pair], self.probs.at[slot], self.probs_sems.at[slot]
        )

    def attend(self, unit, slot):
        tile, seq = self.tile, self.seq
        pair = 2 * unit + slot
        if unit > 0:
            self.probs_store(pair, slot).wait()
        lane = lax.broadcasted_iota(jnp.int32, (1, 128), 1)
        own = (lane < 64, lane >= 64)
        key_at = lax.broadcasted_iota(jnp.int32, (1, seq), 1)
        mask = jnp.where(key_at < self.length[0], 0.0, masked_score)
        q_at, k_at, v_at = self.pair_lanes(slot)
        q = self.qkv[unit, :, q_at]
        k = self.qkv[unit, :, k_at]
        v = self.qkv[unit, :, v_at]
        for head in range(2):
            self.strip_for(pair * 2 + head, self.strip.at[head])
            self.scores[head] = dot_t(jnp.where(own[head], q, jnp.bfloat16(0)), k)

        def soften(head):
            for block in range(seq // tile):
                r = slice(block * tile, (block + 1) * tile)
                first = (seq // tile - 1 - block) * tile
                bias = self.strip[head, :, first : first + seq]
                scores = self.scores[head, r, :] + (bias + mask)
                peak = jnp.max(scores, axis=-1, keepdims=True)
                raised = jnp.exp(scores - peak)
                total = jnp.sum(raised, axis=-1, keepdims=True)
                self.probs[slot, head, r, :] = (raised * (1.0 / total)).astype(jnp.bfloat16)
            return dot(self.probs[slot, head], v)

        outs = [soften(head) for head in range(2)]
        self.attended[:, lanes(pair * 128, 128)] = jnp.where(own[0], *outs).astype(jnp.bfloat16)
        self.probs_store(pair, slot).start()

    def middle_rows(self):
        def body(n):
            c = lanes(n * 256, 256)
            self.middle[:, c] = self.x[:, c].astype(jnp.float32) + dot(
                self.attended[...], self.unit(3, n * 256, 256)
            )

        loop(self.width // 256, body)
        gain = self.gain_f[...]

        def norm(r):
            self.normed_ffn[r] = rms_norm(self.middle[r], gain).astype(jnp.bfloat16)

        self.row_chunks(norm)

    def raise_unit(self, i):
        def body(n):
            raised = dot(self.normed_ffn[...], self.unit(4 + i, n * 256, 256))
            active, slope = gelu_parts(raised)
            c = lanes(i * self.width + n * 256, 256)
            self.active[:, c] = active.astype(jnp.bfloat16)
            self.slope[:, c] = slope.astype(jnp.bfloat16)

        loop(self.width // 256, body)

    def outer_grad(self, shard):
        size = 4 * self.shard_rows
        block = dot_c(self.active[:, lanes(shard * size, size)], self.seed[...])
        self.bank[shard // 2, shard % 2, 12:16] = block.astype(jnp.bfloat16).reshape(
            4, self.shard_rows, self.width
        )

    def lower(self, n):
        outer = self.bank[:, :, 8:12, :, lanes(n * 256, 256)].reshape(-1, 256)
        c = lanes(n * 256, 256)
        self.mid_low[:, c] = (self.middle[:, c] + dot(self.active[...], outer)).astype(
            jnp.bfloat16
        )

    def raised_grad(self, shard):
        size = 4 * self.shard_rows
        outer = self.bank[shard // 2, shard % 2, 8:12].reshape(size, self.width)
        c = lanes(shard * size, size)
        grad = dot_t(self.seed[...], outer) * self.slope[:, c].astype(jnp.float32)
        self.slope[:, c] = grad.astype(jnp.bfloat16)

    def inner_grad(self, i):
        def body(n):
            c = lanes(i * self.width + n * 256, 256)
            block = dot_c(self.normed_ffn[...], self.slope[:, c]).astype(jnp.bfloat16)
            self.bank[:, :, 16 + i, :, lanes(n * 256, 256)] = block.reshape(
                4, 2, self.shard_rows, 256
            )

        loop(self.width // 256, body)

    def middle_grad(self, part):
        total = None
        for i in range(4):
            inner = self.bank[2 * part : 2 * part + 2, :, 4 + i].reshape(-1, self.width)
            term = dot_t(self.slope[:, i * self.width : (i + 1) * self.width], inner)
            total = term if total is None else total + term
        size = self.width // 2
        self.grad_mid[:, part * size : (part + 1) * size] = total

    def middle_norm(self):
        gain = self.gain_f[...]
        self.gain_f_grad[...] = jnp.zeros_like(self.gain_f_grad)

        def body(r):
            back, terms = norm_back(self.grad_mid[r], gain, self.middle[r])
            total = self.seed[r].astype(jnp.float32) + back
            self.gain_f_grad[...] += terms
            self.grad_mid[r] = total
            self.mid_low[r] = total.astype(jnp.bfloat16)

        self.row_chunks(body)

    def square_grad(self, left, right, slot):
        def body(n):
            block = dot_c(left[...], right(lanes(n * 256, 256))).astype(jnp.bfloat16)
            self.bank[:, :, slot, :, lanes(n * 256, 256)] = block.reshape(
                4, 2, self.shard_rows, 256
            )

        loop(self.width // 256, body)

    def attended_grad(self):
        size = self.width // 2
        for part in range(2):
            weight = self.bank[2 * part : 2 * part + 2, :, 3].reshape(size, self.width)
            self.attended[:, part * size : (part + 1) * size] = dot_t(
                self.mid_low[...], weight
            ).astype(jnp.bfloat16)

    def attend_back(self, unit, slot):
        tile, seq = self.tile, self.seq
        pair = 2 * unit + slot
        self.probs_load(pair, slot).wait()
        lane = lax.broadcasted_iota(jnp.int32, (1, 128), 1)
        own = (lane < 64, lane >= 64)
        q_at, k_at, v_at = self.pair_lanes(slot)
        q = self.qkv[unit, :, q_at]
        k = self.qkv[unit, :, k_at]
        v = self.qkv[unit, :, v_at]
        grad_out = self.attended[:, lanes(pair * 128, 128)]
        blocks = seq // tile
        for head in range(2):
            self.scores[head] = dot_t(jnp.where(own[head], grad_out, jnp.bfloat16(0)), v)

        def back(head):
            sums = [None] * 5
            for block in range(blocks):
                r = slice(block * tile, (block + 1) * tile)
                probs = self.probs[slot, head, r, :].astype(jnp.float32)
                weighted = probs * self.scores[head, r, :]
                centre = jnp.sum(weighted, axis=-1, keepdims=True)
                grad = weighted - probs * centre
                self.grad_scores[head, r, :] = grad.astype(jnp.bfloat16)
                for other in range(blocks):
                    apart = min(2, max(-2, other - block)) + 2
                    part = grad[:, other * tile : (other + 1) * tile]
                    sums[apart] = part if sums[apart] is None else sums[apart] + part
            zero = jnp.zeros((tile, tile), jnp.float32)
            near = shear_sum(jnp.concatenate([sums[1], sums[2], sums[3], zero], axis=1), 4 * tile)
            far = jnp.concatenate(
                [
                    jnp.zeros((1, 2 * tile), jnp.float32),
                    jnp.sum(sums[4], axis=0, keepdims=True),
                    jnp.sum(sums[0], axis=0, keepdims=True),
                ],
                axis=1,
            )
            self.rel_grad[pl.ds(pair * 2 + head, 1), :] = near + far
            return (
                dot(self.grad_scores[head], k),
                dot_c(q, self.grad_scores[head]).T,
                dot_c(grad_out, self.probs[slot, head]).T,
            )

        for at, first, second in zip((q_at, k_at, v_at), back(0), back(1)):
            self.qkv[unit, :, at] = jnp.where(own[0], first, second).astype(jnp.bfloat16)
        if 2 * unit + 2 < self.probs_far.shape[0]:
            self.probs_load(pair + 2, slot).start()

    def normed_grad(self, part):
        size = self.width // 2
        total = None
        for u in range(3):
            weight = self.bank[2 * part : 2 * part + 2, :, u].reshape(size, self.width)
            term = dot_t(self.qkv[u], weight)
            total = term if total is None else total + term
        self.middle[:, part * size : (part + 1) * size] = total

    def input_grad(self):
        gain = self.gain_a[...]
        self.gain_a_grad[...] = jnp.zeros_like(self.gain_a_grad)

        def body(r):
            back, terms = norm_back(self.middle[r], gain, self.x[r].astype(jnp.float32))
            self.gain_a_grad[...] += terms
            self.grad_mid[r] += back

        self.row_chunks(body)

    def small_grads(self):
        tile = self.tile
        shape = (64, 4 * tile)
        slot = lax.broadcasted_iota(jnp.int32, shape, 1)
        offset = jnp.where(slot < 3 * tile, slot - tile, slot - 5 * tile)
        row = lax.broadcasted_iota(jnp.int32, shape, 0)
        per = NB // 8
        inside = row % 8 - 2
        wanted = jnp.where((inside >= 0) & (inside < per), (row // 8) * per + inside, -1)
        hits = (bucket_of(offset) == wanted).astype(jnp.float32)
        table = lax.dot_general(
            hits,
            self.rel_grad[...],
            (((1,), (1,)), ((), ())),
            precision=highest,
            preferred_element_type=jnp.float32,
        )
        rows = lax.broadcasted_iota(jnp.int32, (8, 128), 0)
        lane = lax.broadcasted_iota(jnp.int32, (8, 128), 1)
        for shard in range(8):
            block = table[8 * shard : 8 * shard + 8]
            for index, ref in ((0, self.gain_a_grad), (1, self.gain_f_grad)):
                wide = ref[...]
                if shard:
                    wide = pltpu.roll(wide, self.width - shard * self.shard_rows, axis=1)
                here = (rows == index) & (lane < self.shard_rows)
                block = jnp.where(here, jnp.broadcast_to(wide[:, :128], (8, 128)), block)
            self.small_out[shard] = block


(
    SEND_Z, SEND_X, GOT_SECOND, GOT_BESIDE, GOT_ACROSS, GOT_X, GOT_Y, GOT_CORE, DRAIN,
    PASS_BESIDE, SMALL_Z, SMALL_X, SMALL_SECOND, SMALL_BESIDE, SMALL_ACROSS, SUM_SEND, SUM_CORE,
    SUM_Y, SUM_X, SUM_Z, SUM_BACK, SUM_DONE, NORM, PROJECT, ATTEND, MIDDLE, RAISE, OUTER_GRAD,
    LOWER, RAISED_GRAD, INNER_GRAD, MIDDLE_GRAD, MIDDLE_NORM, OUTPUT_GRAD, ATTENDED_GRAD,
    ATTEND_BACK, SQUARE_GRAD, NORMED_GRAD, INPUT_GRAD, SMALL, SMALL_SUM, SMALL_DONE,
) = range(42)

ORDER = (
    (SMALL_Z, 0), (SMALL_X, 0), (SEND_X, 7), (SEND_Z, 0), (SEND_X, 3), (SEND_X, 4), (SEND_X, 2),
    (GOT_SECOND, 0), (SEND_X, 0), (SEND_X, 9), (SEND_Z, 1), (GOT_ACROSS, 0), (SEND_Z, 2),
    (SEND_X, 1), (GOT_BESIDE, 0), (SMALL_SECOND, 0), (SMALL_BESIDE, 0), (SMALL_ACROSS, 0),
    (GOT_SECOND, 1), (GOT_BESIDE, 1), (PASS_BESIDE, 2), (GOT_ACROSS, 1), (SEND_Z, 3),
    (GOT_BESIDE, 2), (GOT_SECOND, 2), (GOT_X, 0), (SEND_Z, 4), (NORM, 0), (GOT_ACROSS, 2),
    (GOT_SECOND, 3), (GOT_X, 1), (GOT_BESIDE, 3), (SEND_Z, 7), (GOT_ACROSS, 3), (GOT_BESIDE, 4),
    (GOT_Y, 0), (GOT_SECOND, 4), (GOT_CORE, 0), (SEND_Z, 6), (GOT_X, 2), (SEND_X, 5), (SEND_Z, 5),
    (PROJECT, 0), (GOT_ACROSS, 4), (GOT_Y, 1), (GOT_X, 3), (GOT_SECOND, 7), (ATTEND, 0),
    (GOT_CORE, 1), (GOT_BESIDE, 7), (PROJECT, 1), (SEND_Z, 9), (SEND_X, 6), (GOT_X, 4),
    (GOT_Y, 2), (GOT_ACROSS, 7), (GOT_SECOND, 6), (GOT_BESIDE, 6), (ATTEND, 1), (GOT_ACROSS, 6),
    (GOT_Y, 3), (GOT_CORE, 2), (GOT_SECOND, 5), (GOT_X, 7), (SEND_X, 11), (PASS_BESIDE, 5),
    (GOT_ACROSS, 5), (SEND_Z, 8), (PROJECT, 2), (GOT_SECOND, 9), (GOT_X, 6), (SEND_X, 8),
    (SEND_Z, 11), (GOT_CORE, 3), (GOT_BESIDE, 5), (ATTEND, 2), (SEND_Z, 10), (GOT_Y, 7),
    (GOT_X, 5), (GOT_SECOND, 8), (GOT_Y, 4), (MIDDLE, 0), (GOT_Y, 6), (GOT_BESIDE, 9),
    (GOT_BESIDE, 8), (GOT_ACROSS, 9), (GOT_CORE, 7), (PASS_BESIDE, 11), (RAISE, 3), (GOT_CORE, 4),
    (GOT_BESIDE, 10), (GOT_CORE, 6), (GOT_SECOND, 11), (GOT_Y, 5), (PASS_BESIDE, 8),
    (GOT_ACROSS, 8), (GOT_BESIDE, 11), (RAISE, 2), (GOT_ACROSS, 11), (GOT_SECOND, 10), (GOT_X, 9),
    (GOT_CORE, 5), (DRAIN, 0), (RAISE, 0), (GOT_X, 8), (GOT_ACROSS, 10), (RAISE, 1), (SEND_X, 10),
    (GOT_X, 11), (OUTER_GRAD, 1), (GOT_X, 10), (GOT_Y, 8), (GOT_Y, 9), (OUTER_GRAD, 0),
    (GOT_Y, 11), (SUM_SEND, 0), (GOT_Y, 10), (GOT_CORE, 9), (SUM_SEND, 1), (GOT_CORE, 8),
    (SUM_CORE, 0), (SUM_SEND, 2), (GOT_CORE, 11), (SUM_SEND, 3), (GOT_CORE, 10), (RAISED_GRAD, 0),
    (SUM_CORE, 1), (INNER_GRAD, 0), (SUM_SEND, 4), (SUM_CORE, 2), (LOWER, 0), (SUM_SEND, 5),
    (SUM_CORE, 3), (SUM_X, 0), (RAISED_GRAD, 1), (SUM_CORE, 4), (MIDDLE_GRAD, 0), (SUM_Y, 1),
    (INNER_GRAD, 1), (SUM_SEND, 6), (SUM_X, 2), (LOWER, 1), (SUM_CORE, 5), (SUM_SEND, 7),
    (LOWER, 2), (SUM_Y, 4), (SUM_Y, 3), (MIDDLE_GRAD, 1), (SUM_CORE, 6), (SUM_X, 1),
    (MIDDLE_NORM, 0), (OUTPUT_GRAD, 0), (ATTENDED_GRAD, 0), (SUM_CORE, 7), (SUM_X, 4),
    (ATTEND_BACK, 0), (SUM_SEND, 8), (SUM_Y, 5), (SUM_X, 3), (SUM_Y, 6), (SQUARE_GRAD, 0),
    (SUM_SEND, 9), (SUM_CORE, 8), (ATTEND_BACK, 1), (SUM_CORE, 9), (SUM_X, 5), (SUM_Y, 7),
    (ATTEND_BACK, 2), (SUM_X, 6), (SUM_Z, 1), (SUM_Z, 3), (SUM_Y, 9), (SQUARE_GRAD, 1),
    (SUM_SEND, 10), (SQUARE_GRAD, 2), (SUM_X, 7), (SUM_Y, 8), (SUM_SEND, 11), (SUM_CORE, 10),
    (SUM_CORE, 11), (SUM_X, 9), (NORMED_GRAD, 0), (SUM_Y, 10), (NORMED_GRAD, 1), (SUM_Z, 6),
    (SUM_BACK, 3), (SUM_X, 8), (INPUT_GRAD, 0), (SUM_Y, 11), (SUM_Z, 9), (SMALL, 0), (SUM_Z, 0),
    (SUM_X, 10), (SUM_Z, 8), (SUM_Z, 7), (SUM_BACK, 0), (SUM_Z, 4), (SMALL_SUM, 0), (SUM_Z, 2),
    (SUM_X, 11), (SUM_BACK, 8), (SUM_Z, 10), (SUM_Z, 5), (SUM_Z, 11), (SUM_BACK, 2),
    (SUM_BACK, 7), (SUM_DONE, 0), (SUM_BACK, 4), (SMALL_DONE, 0), (SUM_DONE, 3), (SUM_BACK, 10),
    (SUM_BACK, 5), (SUM_BACK, 1), (SUM_DONE, 7), (SUM_BACK, 6), (SUM_BACK, 9), (SUM_DONE, 5),
    (SUM_BACK, 11), (SUM_DONE, 2), (SUM_DONE, 1), (SUM_DONE, 6), (SUM_DONE, 9), (SUM_DONE, 8),
    (SUM_DONE, 4), (SUM_DONE, 10), (SUM_DONE, 11),
)


def order_slot(n):
    return n + 12 if n < 8 else (7 if n == 8 else n - 5)


def fused_kernel(
    length, x, cot, gain_a_own, gain_f_own, table_own, query_own, key_own, value_own, output_own,
    inner_own, outer_own,
    block_far, grad_far, own_far, small_result, probs_far,
    bank, own_sum, from_core, from_y, from_x, from_z, small_wide, all_small, small_out,
    small_in, small_rep, probs, normed, qkv, attended, middle, normed_ffn, active, slope, seed,
    grad_mid, mid_low, scores, rel, rel_grad, gain_a, gain_f, gain_a_grad,
    gain_f_grad, strip, grad_scores,
    sends, recvs, sum_sends, sum_recvs, small_sends, small_recvs, back_sems, probs_sems,
    misc_sems, keep_sems,
):
    shard = lax.axis_index("fsdp")
    copy_id = lax.axis_index("rep")
    layer = Layer(
        length=length, x=x, bank=bank, all_small=all_small, small_out=small_out,
        probs=probs, probs_far=probs_far, probs_sems=probs_sems, normed=normed, qkv=qkv,
        attended=attended, middle=middle, normed_ffn=normed_ffn, active=active, slope=slope,
        seed=seed, grad_mid=grad_mid, mid_low=mid_low, scores=scores,
        rel=rel, rel_grad=rel_grad, gain_a=gain_a, gain_f=gain_f, gain_a_grad=gain_a_grad,
        gain_f_grad=gain_f_grad, strip=strip, grad_scores=grad_scores,
    )
    rows, width = query_own.shape
    chunks = inner_own.shape[1] // width
    units = 4 + 2 * chunks
    gather = Gather(bank, sends, recvs)
    scatter = Scatter(
        order_slot, bank, own_sum, from_core, from_y, from_x, from_z, sum_sends, sum_recvs
    )
    pairs = probs_far.shape[0]

    def remote(src, dst, send, recv, device):
        return pltpu.make_async_remote_copy(
            src_ref=src, dst_ref=dst, send_sem=send, recv_sem=recv, device_id=device,
            device_id_type=MESH,
        )

    def peer(k):
        return (lax.rem(shard + k, 8), copy_id)

    def rep_peer(k):
        return (shard, lax.rem(copy_id + k, 4))

    parts = [output_own]
    parts += [inner_own.at[:, pl.ds(i * width, width)] for i in range(chunks)]
    parts += [outer_own.at[pl.ds(i * rows, rows)] for i in range(chunks)]
    third = width // 3
    homes = [
        (part.at[:, pl.ds(u * third, third)], bank.at[gather.z, gather.x, u, :, pl.ds(n * third, third)])
        for u in range(3)
        for n, part in enumerate((query_own, key_own, value_own))
    ]
    homes += [(part, bank.at[gather.z, gather.x, 3 + u]) for u, part in enumerate(parts)]
    keeps = [
        pltpu.make_async_copy(part, home, keep_sems.at[0]) for part, home in homes
    ]
    keep_seed = pltpu.make_async_copy(cot, seed, keep_sems.at[1])
    keeps.append(keep_seed)
    peers = gather.peers()
    greet(peers, gather.at_end)
    for copy in keeps:
        copy.start()
    small_wide[...] = jnp.zeros_like(small_wide)
    small_wide[0:1, :rows] = gain_a_own[...].astype(jnp.float32)
    small_wide[1:2, :rows] = gain_f_own[...].astype(jnp.float32)
    per, heads = table_own.shape
    small_wide[2 : 2 + per, :heads] = table_own[...].astype(jnp.float32)
    all_small[shard] = small_wide[...].astype(jnp.bfloat16)
    smalls = SmallGather(gather, all_small, small_sends, small_recvs)
    mine = bank.at[gather.z, gather.x, 0:units]
    pltpu.make_async_copy(mine, mine, keep_sems.at[0]).wait()
    all_greeted(peers, gather.at_end)

    def store(n):
        return pltpu.make_async_copy(own_sum.at[n], own_far.at[n], misc_sems.at[2])

    def sum_done(n):
        scatter.after_back_core(n)
        store(n).start()

    block_store = pltpu.make_async_copy(mid_low, block_far, misc_sems.at[0])
    grad_store = pltpu.make_async_copy(grad_mid, grad_far, misc_sems.at[1])
    back_copies = [
        remote(
            small_out.at[lax.rem(shard + k, 8)], small_in.at[k - 1], back_sems.at[0],
            back_sems.at[1], peer(k),
        )
        for k in range(1, 8)
    ]
    rep_copies = [
        remote(
            small_rep.at[copy_id], small_rep.at[copy_id], back_sems.at[2], back_sems.at[3],
            rep_peer(k),
        )
        for k in range(1, 4)
    ]

    def wait_for(part, sem):
        pltpu.make_async_copy(part, part, sem).wait()

    def norm(_):
        keep_seed.wait()
        layer.mask_seed()
        smalls.after_x(0)
        layer.small_arrays()
        layer.norm_in()

    def middle_rows(_):
        layer.middle_rows()
        for pair in (pairs - 2, pairs - 1):
            layer.probs_store(pair, pair % 2).wait()
        for pair in (0, 1):
            layer.probs_load(pair, pair).start()

    def lower(n):
        layer.lower(n)
        if n == width // 256 - 1:
            block_store.start()

    def middle_norm(_):
        block_store.wait()
        layer.middle_norm()
        rel_grad[...] = jnp.zeros_like(rel_grad)

    def input_grad(_):
        layer.input_grad()
        grad_store.start()

    def small_sums(_):
        layer.small_grads()
        for copy in back_copies:
            copy.start()

    def small_sum(_):
        wait_for(small_in, back_sems.at[1])
        total = small_out[shard]
        for k in range(7):
            total = total + small_in[k]
        small_rep[copy_id] = total
        for copy in rep_copies:
            copy.start()

    def small_done(_):
        wait_for(small_rep.at[0:3], back_sems.at[3])
        small_result[...] = (small_rep[0] + small_rep[1]) + (small_rep[2] + small_rep[3])

    work = {
        SEND_Z: gather.send_z,
        SEND_X: gather.send_x,
        GOT_SECOND: gather.after_second,
        GOT_BESIDE: gather.after_beside,
        GOT_ACROSS: gather.after_across,
        GOT_X: gather.after_x,
        GOT_Y: gather.after_y,
        GOT_CORE: gather.after_core,
        DRAIN: gather.drain,
        PASS_BESIDE: gather.pass_beside,
        SMALL_Z: smalls.send_z,
        SMALL_X: smalls.send_x,
        SMALL_SECOND: smalls.after_second,
        SMALL_BESIDE: smalls.after_beside,
        SMALL_ACROSS: smalls.after_across,
        SUM_SEND: scatter.start,
        SUM_CORE: scatter.after_core,
        SUM_Y: scatter.after_y,
        SUM_X: scatter.after_x,
        SUM_Z: scatter.after_z,
        SUM_BACK: scatter.after_back_y,
        SUM_DONE: sum_done,
        NORM: norm,
        PROJECT: layer.project,
        ATTEND: lambda u: loop(2, functools.partial(layer.attend, u)),
        MIDDLE: middle_rows,
        RAISE: layer.raise_unit,
        OUTER_GRAD: lambda k: loop(4, lambda n: layer.outer_grad(4 * k + n)),
        LOWER: lower,
        RAISED_GRAD: lambda k: loop(4, lambda n: layer.raised_grad(4 * k + n)),
        INNER_GRAD: lambda k: loop(2, lambda n: layer.inner_grad(2 * k + n)),
        MIDDLE_GRAD: layer.middle_grad,
        MIDDLE_NORM: middle_norm,
        OUTPUT_GRAD: lambda _: layer.square_grad(attended, lambda c: mid_low[:, c], 7),
        ATTENDED_GRAD: lambda _: layer.attended_grad(),
        ATTEND_BACK: lambda u: loop(2, functools.partial(layer.attend_back, u)),
        SQUARE_GRAD: lambda u: layer.square_grad(normed, lambda c: qkv[u, :, c], 4 + u),
        NORMED_GRAD: layer.normed_grad,
        INPUT_GRAD: input_grad,
        SMALL: small_sums,
        SMALL_SUM: small_sum,
        SMALL_DONE: small_done,
    }
    for name, n in ORDER:
        work[name](n)
    gather.drain(1)
    smalls.drain(0)
    scatter.drain()
    wait_for(small_in, back_sems.at[0])
    wait_for(small_rep.at[0:3], back_sems.at[2])
    wait_for(own_sum, misc_sems.at[2])
    grad_store.wait()


def fused_call(length, x, cot, gain_a, gain_f, table, square, inner, outer):
    rows, width = square[0].shape
    units = 4 + 2 * (inner.shape[1] // width)
    heads = table.shape[1]
    seq = x.shape[0]
    half = rows // 2
    part = half // 3
    hidden = inner.shape[1]
    low, wide = jnp.bfloat16, jnp.float32
    anywhere = pl.BlockSpec(memory_space=pl.ANY)
    within = pl.BlockSpec(memory_space=pltpu.VMEM)
    sems = pltpu.SemaphoreType.DMA
    vm = pltpu.VMEM
    head_rows = -(-heads // 8) * 8
    return pl.pallas_call(
        fused_kernel,
        out_shape=(
            jax.ShapeDtypeStruct((seq, width), low),
            jax.ShapeDtypeStruct((seq, width), wide),
            jax.ShapeDtypeStruct((units, rows, width), low),
            jax.ShapeDtypeStruct((8, 128), wide),
            jax.ShapeDtypeStruct((heads // 2, 2, seq, seq), low),
        ),
        in_specs=[pl.BlockSpec(memory_space=pltpu.SMEM), within, anywhere]
        + [within] * 3
        + [anywhere] * 6,
        out_specs=[anywhere, anywhere, anywhere, within, anywhere],
        scratch_shapes=[
            vm((4, 2, units + 8, rows, width), low),
            vm((units, rows, width), low),
            vm((6, 4, 2, half, width), low),
            vm((units, 4, 2, part, width), low),
            vm((units, 4, half, width), low),
            vm((units, 4, half, width), low),
            vm((16, 128), wide),
            vm((8, 16, 128), low),
            vm((8, 8, 128), wide),
            vm((7, 8, 128), wide),
            vm((4, 8, 128), wide),
            vm((2, 2, seq, seq), low),
            vm((seq, width), low),
            vm((3, seq, width), low),
            vm((seq, width), low),
            vm((seq, width), wide),
            vm((seq, width), low),
            vm((seq, hidden), low),
            vm((seq, hidden), low),
            vm((seq, width), low),
            vm((seq, width), wide),
            vm((seq, width), low),
            vm((2, seq, seq), wide),
            vm((head_rows, 512), wide),
            vm((128, 512), wide),
            vm((1, width), wide),
            vm((1, width), wide),
            vm((1, width), wide),
            vm((1, width), wide),
            vm((2, 128, 128 * 7), wide),
            vm((2, seq, seq), low),
            sems((2,)),
            sems((units, Gather.slots)),
            sems((6 + units,)),
            sems((units, Scatter.slots)),
            sems((1,)),
            sems((4,)),
            sems((4,)),
            sems((2,)),
            sems((3,)),
            sems((2,)),
        ],
        compiler_params=pltpu.CompilerParams(
            collective_id=0, has_side_effects=True, vmem_limit_bytes=63 * 2**20
        ),
    )(length, x, cot, gain_a, gain_f, table, *square, inner, outer)


def finish_kernel(
    block_in, grad_in, sums_far, small, block_out, grad_out, query_out, key_out, value_out,
    output_out, gain_a, table, inner_out, outer_out, gain_f, block, grad, query, key, value, output,
    inner, outer, sums, in_sems, out_sems,
):
    units, rows, width = sums.shape
    chunks = inner.shape[1] // width
    third = width // 3
    straight = ((block_in, block, block_out), (grad_in, grad, grad_out))
    loads = [pltpu.make_async_copy(sums_far.at[n], sums.at[n], in_sems.at[n]) for n in range(units)]
    loads += [
        pltpu.make_async_copy(far, near, in_sems.at[units + n])
        for n, (far, near, _) in enumerate(straight)
    ]
    for copy in loads[units:] + loads[:units]:
        copy.start()
    stores = []

    def store(near, far):
        stores.append(pltpu.make_async_copy(near, far, out_sems.at[len(stores)]))
        stores[-1].start()

    for n, (_, near, far) in enumerate(straight):
        loads[units + n].wait()
        store(near, far)
    gain_a[...] = small[0:1, :rows]
    gain_f[...] = small[1:2, :rows]
    table[...] = small[2 : 2 + table.shape[0], : table.shape[1]]
    for i in range(chunks):
        part = pl.ds(i * rows, rows)
        loads[i].wait()
        outer[part, :] = sums[i].astype(jnp.float32)
        store(outer.at[part], outer_out.at[part])
    for i in range(chunks):
        part = pl.ds(i * width, width)
        loads[chunks + i].wait()
        inner[:, part] = sums[chunks + i].astype(jnp.float32)
        store(inner.at[:, part], inner_out.at[:, part])
    loads[2 * chunks].wait()
    output[...] = sums[2 * chunks].astype(jnp.float32)
    store(output, output_out)
    for u in range(3):
        loads[2 * chunks + 1 + u].wait()
        for n, ref in enumerate((query, key, value)):
            ref[:, u * third : (u + 1) * third] = sums[
                2 * chunks + 1 + u, :, n * third : (n + 1) * third
            ].astype(jnp.float32)
    for near, far in ((query, query_out), (key, key_out), (value, value_out)):
        store(near, far)
    for copy in stores:
        copy.wait()


def finish_call(block, grad, sums, small, table_shape, inner_shape, outer_shape):
    units, rows, width = sums.shape
    wide = jnp.float32
    anywhere = pl.BlockSpec(memory_space=pl.ANY)
    within = pl.BlockSpec(memory_space=pltpu.VMEM)
    shapes = [(rows, width)] * 4 + [(1, rows), table_shape, inner_shape, outer_shape, (1, rows)]
    places = [anywhere] * 4 + [within] * 2 + [anywhere] * 2 + [within]
    staged = [shape for shape, place in zip(shapes, places) if place is anywhere]
    return pl.pallas_call(
        finish_kernel,
        out_shape=[
            jax.ShapeDtypeStruct(block.shape, block.dtype),
            jax.ShapeDtypeStruct(grad.shape, grad.dtype),
        ]
        + [jax.ShapeDtypeStruct(shape, wide) for shape in shapes],
        in_specs=[anywhere, anywhere, anywhere, within],
        out_specs=[anywhere, anywhere] + places,
        scratch_shapes=[
            pltpu.VMEM(block.shape, block.dtype),
            pltpu.VMEM(grad.shape, grad.dtype),
            *[pltpu.VMEM(shape, wide) for shape in staged],
            pltpu.VMEM(sums.shape, sums.dtype),
            pltpu.SemaphoreType.DMA((units + 2,)),
            pltpu.SemaphoreType.DMA((units + 2,)),
        ],
        compiler_params=pltpu.CompilerParams(vmem_limit_bytes=63 * 2**20),
    )(block, grad, sums, small)


def local_linked(
    inputs, lengths, cotangent, query_weight, key_weight, value_weight, output_weight,
    attention_gain, bias_table, inner_weight, outer_weight, feedforward_gain,
):
    rows = query_weight.shape[0]
    square = (query_weight, key_weight, value_weight, output_weight)
    block, grad, sums, small, _ = fused_call(
        lengths, inputs[0], cotangent[0], attention_gain.reshape(1, rows),
        feedforward_gain.reshape(1, rows), bias_table, square, inner_weight, outer_weight,
    )
    block, grad, query, key, value, output, gain_a, table, inner, outer, gain_f = finish_call(
        block, grad, sums, small, bias_table.shape, inner_weight.shape, outer_weight.shape
    )
    return (
        block[None], grad[None], query, key, value, output, gain_a.reshape(rows), table, inner,
        outer, gain_f.reshape(rows),
    )


def local(inputs, lengths, cotangent, *shards):
    block_output, input_grad, gradients = compute(inputs, lengths, cotangent, gather_all(*shards))
    return (block_output, input_grad) + sum_all(gradients)


def can_link(mesh):
    return mesh.shape["fsdp"] == 8 and mesh.shape["rep"] == 4


def solution(mesh):
    placed = (
        P(("fsdp", "rep"), None, None),
        P(("fsdp", "rep")),
        P(("fsdp", "rep"), None, None),
        P("fsdp", None),
        P("fsdp", None),
        P("fsdp", None),
        P("fsdp", None),
        P("fsdp"),
        P("fsdp", None),
        P("fsdp", None),
        P("fsdp", None),
        P("fsdp"),
    )
    return jax.shard_map(
        local_linked if can_link(mesh) else local,
        mesh=mesh,
        in_specs=placed,
        out_specs=(
            P(("fsdp", "rep"), None, None),
            P(("fsdp", "rep"), None, None),
            P("fsdp", None),
            P("fsdp", None),
            P("fsdp", None),
            P("fsdp", None),
            P("fsdp"),
            P("fsdp", None),
            P("fsdp", None),
            P("fsdp", None),
            P("fsdp"),
        ),
        check_vma=False,
    )
```

```python
import functools

import jax
import jax.numpy as jnp
from jax import lax
import jax.experimental.pallas as pl
import jax.experimental.pallas.tpu as pltpu
from jax.sharding import PartitionSpec as P

NB = 32


epsilon = 1e-06
highest = lax.Precision.HIGHEST
gelu_coeff = 0.7978845608028654
masked_score = -1e30


def bucket_of(offset):
    half_count = NB // 2
    exact_count = half_count // 2
    distance = jnp.abs(offset)
    beyond = jnp.full(offset.shape, exact_count, jnp.int32)
    for exponent in range(1, half_count - exact_count):
        beyond = beyond + (distance * distance >= exact_count * exact_count * 2**exponent).astype(
            jnp.int32
        )
    nearby = jnp.where(distance < exact_count, distance, beyond)
    return jnp.where(offset > 0, half_count, 0).astype(jnp.int32) + nearby


def rms_norm(values, gain_vector):
    inverse_rms = lax.rsqrt(jnp.mean(values * values, axis=-1, keepdims=True) + epsilon)
    return values * inverse_rms * gain_vector


def gelu(values):
    return (
        0.5 * values * (1.0 + jnp.tanh(gelu_coeff * (values + 0.044715 * values * values * values)))
    )


def dot(a,b): return jnp.dot(a,b,preferred_element_type=jnp.float32)
def dot_t(a,b): return lax.dot_general(a,b,(((1,),(1,)),((),())),preferred_element_type=jnp.float32)
def dot_c(a,b): return lax.dot_general(a,b,(((0,),(0,)),((),())),preferred_element_type=jnp.float32)

def fwd_kernel(T, len_ref, q_ref, k_ref, v_ref, rel_ref, o_ref, p_ref, strip):
    hp=pl.program_id(0)
    seq=q_ref.shape[0]; nb=seq//T
    lane=lax.broadcasted_iota(jnp.int32,(1,128),1)
    kcol=lax.broadcasted_iota(jnp.int32,(1,seq),1)
    mask=jnp.where(kcol<len_ref[0],0.0,-1e30)
    k=k_ref[...]; v=v_ref[...]
    for hh in range(2):
        mine=(lane>=64) if hh else (lane<64)
        rel=rel_ref[pl.ds(hh,1),:]
        W=4*T
        rolled=pltpu.roll(jnp.broadcast_to(rel,(T,W)),0,axis=1,stride=1,stride_axis=0)
        strip[:, 2*T:5*T]=rolled[:, :3*T]
        far_neg=rel[:, 0:1]; far_pos=rel[:, 3*T-1:3*T]
        strip[:, 0:2*T]=jnp.broadcast_to(far_neg,(T,2*T))
        strip[:, 5*T:7*T]=jnp.broadcast_to(far_pos,(T,2*T))
        for I in range(nb):
            q=jnp.where(mine,q_ref[I*T:(I+1)*T,:],jnp.bfloat16(0))
            s=dot_t(q,k)+(strip[:, (3-I)*T:(3-I)*T+seq]+mask)
            m=jnp.max(s,axis=-1,keepdims=True)
            e=jnp.exp(s-m)
            tot=jnp.sum(e,axis=-1,keepdims=True)
            p=(e*(1.0/tot)).astype(jnp.bfloat16)
            p_ref[hh,I*T:(I+1)*T,:]=p
            o=dot(p,v)
            if hh==0:
                o_ref[I*T:(I+1)*T,:]=o.astype(jnp.bfloat16)
            else:
                o_ref[I*T:(I+1)*T,:]=jnp.where(mine,o.astype(jnp.bfloat16),o_ref[I*T:(I+1)*T,:])

def bwd_kernel(T, q_ref, k_ref, v_ref, do_ref, p_ref, dq_ref, dk_ref, dv_ref, db_ref, ds_ref):
    seq=q_ref.shape[0]; nb=seq//T
    lane=lax.broadcasted_iota(jnp.int32,(1,128),1)
    k=k_ref[...]; v=v_ref[...]
    dks=[];dvs=[]
    for hh in range(2):
        mine=(lane>=64) if hh else (lane<64)
        acc=[None]*5
        for I in range(nb):
            sl=slice(I*T,(I+1)*T)
            do=jnp.where(mine,do_ref[sl,:],jnp.bfloat16(0))
            dp=dot_t(do,v)
            p=p_ref[hh,sl,:].astype(jnp.float32)
            t=p*dp
            delta=jnp.sum(t,axis=-1,keepdims=True)
            ds=(t-p*delta).astype(jnp.bfloat16)
            ds_ref[sl,:]=ds
            dsf=ds.astype(jnp.float32)
            for J in range(nb):
                d=min(2,max(-2,J-I))+2
                x=dsf[:,J*T:(J+1)*T]
                acc[d]=x if acc[d] is None else acc[d]+x
            dq=dot(ds,k)
            if hh==0: dq_ref[sl,:]=dq.astype(jnp.bfloat16)
            else: dq_ref[sl,:]=jnp.where(mine,dq.astype(jnp.bfloat16),dq_ref[sl,:])
        near=jnp.concatenate([acc[1],acc[2],acc[3],jnp.zeros((T,T),jnp.float32)],axis=1)
        total=shear_sum(near,4*T)
        far=jnp.concatenate([jnp.zeros((1,2*T),jnp.float32),jnp.sum(acc[4],axis=0,keepdims=True),jnp.sum(acc[0],axis=0,keepdims=True)],axis=1)
        db_ref[hh:hh+1,:]=total+far
        dk=dot_c(q_ref[...],ds_ref[...]).T; dv=dot_c(do_ref[...],p_ref[hh]).T
        dks.append(dk); dvs.append(dv)
    dk_ref[...]=jnp.where(lane<64,dks[0],dks[1]).astype(jnp.bfloat16)
    dv_ref[...]=jnp.where(lane<64,dvs[0],dvs[1]).astype(jnp.bfloat16)

def rel_hits(tile):
    slot = jnp.arange(4 * tile, dtype=jnp.int32)
    offset = jnp.where(slot < 3 * tile, slot - tile, slot - 5 * tile)
    bucket_ids = jnp.arange(NB, dtype=jnp.int32)
    return (bucket_of(offset)[None, :] == bucket_ids[:, None]).astype(jnp.bfloat16)


def rel_vec(table, tile):
    return dot_c(table, rel_hits(tile))


def shear_sum(block, width):
    rows = block.shape[0]
    while rows > 8:
        rows //= 2
        block = block[:rows] + pltpu.roll(block[rows:], width - rows, axis=1)
    total = block[0:1]
    for r in range(1, 8):
        total = total + pltpu.roll(block[r : r + 1], width - r, axis=1)
    return total


def att_fwd(q,k,v,rel,length,T=128):
    seq,D=q.shape; H=rel.shape[0]
    blk=pl.BlockSpec((seq,128),lambda h: (0,h))
    return pl.pallas_call(functools.partial(fwd_kernel,T),grid=(H//2,),
        in_specs=[pl.BlockSpec(memory_space=pltpu.SMEM),blk,blk,blk,pl.BlockSpec((None,2,4*T),lambda h:(h,0,0))],
        out_specs=[blk,pl.BlockSpec((2,seq,seq),lambda h:(h,0,0))],
        out_shape=[jax.ShapeDtypeStruct((seq,D),jnp.bfloat16),jax.ShapeDtypeStruct((H,seq,seq),jnp.bfloat16)],
        scratch_shapes=[pltpu.VMEM((T,7*T),jnp.float32)],
        compiler_params=pltpu.CompilerParams(vmem_limit_bytes=40*2**20))(length,q,k,v,rel.reshape(H//2,2,4*T))
def att_bwd(q,k,v,do,p,T=128):
    seq,D=q.shape; H=p.shape[0]
    blk=pl.BlockSpec((seq,128),lambda h: (0,h))
    o=jax.ShapeDtypeStruct((seq,D),jnp.bfloat16)
    outs=pl.pallas_call(functools.partial(bwd_kernel,T),grid=(H//2,),
        in_specs=[blk,blk,blk,blk,pl.BlockSpec((2,seq,seq),lambda h:(h,0,0))],
        out_specs=[blk,blk,blk,pl.BlockSpec((None,2,4*T),lambda h:(h,0,0))],
        out_shape=[o,o,o,jax.ShapeDtypeStruct((H//2,2,4*T),jnp.float32)],
        scratch_shapes=[pltpu.VMEM((seq,seq),jnp.bfloat16)],
        compiler_params=pltpu.CompilerParams(vmem_limit_bytes=40*2**20))(q,k,v,do,p)
    return *outs[:3],outs[3].reshape(H,4*T)

def contract_rows(left, right):
    return lax.dot_general(
        left, right, (((0,), (0,)), ((), ())), preferred_element_type=jnp.float32
    )


def contract_cols(left, right):
    return lax.dot_general(
        left, right, (((1,), (1,)), ((), ())), preferred_element_type=jnp.float32
    )


MESH = pl.DeviceIdType.MESH


def coords():
    shard = lax.axis_index("fsdp")
    copy = lax.axis_index("rep")
    return shard // 2, shard % 2, copy // 2, copy % 2


def greet(peers, at_end):
    barrier = pltpu.get_barrier_semaphore()
    for peer in peers[:-1]:
        pl.semaphore_signal(barrier, inc=1, device_id=peer, device_id_type=MESH)

    def last():
        pl.semaphore_signal(barrier, inc=1, device_id=peers[-1], device_id_type=MESH)

    pl.when(~at_end)(last)


def all_greeted(peers, at_end):
    barrier = pltpu.get_barrier_semaphore()
    pl.semaphore_wait(barrier, jnp.where(at_end, len(peers) - 1, len(peers)))


class Links:
    def __init__(self, rows, send_sems, recv_sems):
        self.send_sems, self.recv_sems = send_sems, recv_sems
        self.z, self.x, self.y, self.c = coords()
        half = rows // 2
        part = half // 3
        at = lambda start, size: pl.ds(pl.multiple_of(start, part), size)
        first = half * self.c
        other = half * (1 - self.c)
        self.half, self.other_half = at(first, half), at(other, half)
        self.plane = at(first + part * self.y, 2 * part)
        self.shared = at(first + part, part)
        self.own_third = at(first + 2 * part * self.y, part)
        self.other_third = at(first + 2 * part * (1 - self.y), part)
        self.shared_in = at(part * self.y, part)
        self.third_in = at(part * (1 - self.y), part)

    def copy(self, src, dst, g, send, slot, device):
        return pltpu.make_async_remote_copy(
            src_ref=src,
            dst_ref=dst,
            send_sem=self.send_sems.at[send],
            recv_sem=self.recv_sems.at[g, slot],
            device_id=device,
            device_id_type=MESH,
        )

    def to_x(self):
        return (self.z * 2 + 1 - self.x, self.y * 2 + self.c)

    def to_y(self):
        return (self.z * 2 + self.x, (1 - self.y) * 2 + self.c)

    def to_core(self):
        return (self.z * 2 + self.x, self.y * 2 + 1 - self.c)

    def to_z(self, k):
        return (lax.rem(self.z + k, 4) * 2 + self.x, self.y * 2 + self.c)

    def z_before(self, k):
        return lax.rem(self.z + 4 - k, 4)


class Gather(Links):
    slots = 7

    def __init__(self, full, send_sems, recv_sems):
        super().__init__(full.shape[3], send_sems, recv_sems)
        self.full = full
        self.beside = self.z + 1 - 2 * lax.rem(self.z, 2)
        self.second = lax.rem(self.z + 2, 4)
        self.across = 3 - self.z
        self.at_end = (self.z == 0) | (self.z == 3)
        self.early = range(4, 8)

    def peers(self):
        near = [self.to_x(), self.to_y(), self.to_core()]
        return near + [self.at_z(a) for a in (self.second, self.beside, self.across)]

    def block(self, g, a, rows):
        return self.full.at[a, self.x, g, rows]

    def column(self, g, rows):
        return self.full.at[:, 1 - self.x, g, rows]

    def move(self, part, g, slot, device):
        return pltpu.make_async_remote_copy(
            src_ref=part,
            dst_ref=part,
            send_sem=self.send_sems.at[0 if g in self.early else 1],
            recv_sem=self.recv_sems.at[g, slot],
            device_id=device,
            device_id_type=MESH,
        )

    def at_z(self, a):
        return (a * 2 + self.x, self.y * 2 + self.c)

    def z_copy(self, g, to, slot):
        return self.move(self.block(g, self.z, self.plane), g, slot, self.at_z(to))

    def x_copy(self, g, a):
        return self.move(self.block(g, a, self.plane), g, 3, self.to_x())

    def y_copy(self, g, a):
        return self.move(self.block(g, a, self.own_third), g, 4, self.to_y())

    def core_copy(self, g, a):
        return self.move(self.block(g, a, self.half), g, 5, self.to_core())

    def arrived(self, part, g, slot):
        pltpu.make_async_copy(part, part, self.recv_sems.at[g, slot]).wait()

    def others(self):
        return (self.beside, self.second, self.across)

    def send_z(self, g):
        self.z_copy(g, self.second, 0).start()
        self.z_copy(g, self.beside, 1).start()
        pl.when(~self.at_end)(lambda: self.z_copy(g, self.across, 2).start())

    def send_x(self, g):
        part = self.block(g, self.z, self.plane)
        self.move(part, g, 6 if g % 3 == 2 else 3, self.to_x()).start()

    def pass_beside(self, g):
        part = self.full.at[self.z, 1 - self.x, g, self.plane]
        self.arrived(part, g, 6)
        self.move(part, g, 3, self.at_z(self.beside)).start()

    def spread(self, g, a, slot):
        self.arrived(self.block(g, a, self.plane), g, slot)
        if slot == 0:
            part = self.block(g, a, self.plane)
            pl.when(~self.at_end)(lambda: self.move(part, g, 2, self.at_z(self.beside)).start())
        if slot != 1 or g % 3 != 2:
            self.x_copy(g, a).start()
        self.y_copy(g, a).start()

    def after_second(self, g):
        self.spread(g, self.second, 0)

    def after_beside(self, g):
        self.spread(g, self.beside, 1)

    def after_across(self, g):
        self.spread(g, self.across, 2)

    def after_x(self, g):
        rows = self.plane.size
        part = self.full.at[0, 0, 0:3, 0:rows] if g % 3 == 2 else self.column(g, self.plane)
        self.arrived(part, g, 3)
        self.move(self.column(g, self.own_third), g, 4, self.to_y()).start()

    def after_y(self, g):
        third = self.own_third.size
        self.arrived(self.full.at[0, 0, 0:7, 0:third], g, 4)
        for a in self.others():
            self.core_copy(g, a).start()
        self.move(self.column(g, self.half), g, 5, self.to_core()).start()

    def after_core(self, g):
        self.arrived(self.full.at[0, 0, 0:7, 0 : self.half.size], g, 5)

    def drain(self, n):
        count = len(self.early)
        units = self.full.shape[2] - 8
        rows = self.full.shape[3] * (count if n == 0 else units - count) // units

        def wait(blocks):
            part = self.full.at[:, :, 0:blocks, 0:rows]
            pltpu.make_async_copy(part, part, self.send_sems.at[n]).wait()

        pl.when(self.at_end)(lambda: wait(10))
        pl.when(~self.at_end)(lambda: wait(11))


class SmallGather(Gather):
    def move(self, part, g, slot, device):
        return pltpu.make_async_remote_copy(
            src_ref=part,
            dst_ref=part,
            send_sem=self.send_sems.at[0],
            recv_sem=self.recv_sems.at[slot],
            device_id=device,
            device_id_type=MESH,
        )

    def __init__(self, links, full, send_sems, recv_sems):
        self.__dict__.update(links.__dict__)
        self.full, self.send_sems, self.recv_sems = full, send_sems, recv_sems

    def block(self, g, a, rows):
        return self.full.at[a * 2 + self.x]

    def y_copy(self, g, a):
        return self

    def start(self):
        pass

    def arrived(self, part, g, slot):
        pltpu.make_async_copy(part, part, self.recv_sems.at[slot]).wait()

    def after_x(self, g):
        self.arrived(self.full.at[0:4], g, 3)

    def drain(self, n):
        def wait(blocks):
            part = self.full.at[0:blocks]
            pltpu.make_async_copy(part, part, self.send_sems.at[0]).wait()

        pl.when(self.at_end)(lambda: wait(6))
        pl.when(~self.at_end)(lambda: wait(8))


class Scatter(Links):
    slots = 6
    whole = (0, 2)

    def rows(self, g):
        return self.half if g in self.whole else self.plane

    def count(self, g):
        return self.rows(g).size

    def sender(self, g, n):
        return 3 + n + self.own.shape[0] if g in self.whole else n

    def __init__(self, slot, full, own, from_core, from_y, from_x, from_z, send_sems, recv_sems):
        super().__init__(own.shape[1], send_sems, recv_sems)
        self.slot, self.full, self.own = slot, full, own
        self.from_core, self.from_y, self.from_x, self.from_z = from_core, from_y, from_x, from_z

    def core_copy(self, g):
        part = self.full.at[:, :, self.slot(g), self.other_half]
        ring = g % self.from_core.shape[0]
        return self.copy(part, self.from_core.at[ring], g, 0, 0, self.to_core())

    def y_copy(self, g):
        part = self.full.at[:, :, self.slot(g), self.other_third]
        return self.copy(part, self.from_y.at[g], g, 1, 1, self.to_y())

    def x_copy(self, g):
        part = self.full.at[:, 1 - self.x, self.slot(g), self.rows(g)]
        there = self.from_x.at[g, :, 0 : self.count(g)]
        return self.copy(part, there, g, self.sender(g, 1), 2, self.to_x())

    def z_copy(self, g, k):
        part = self.full.at[lax.rem(self.z + k, 4), self.x, self.slot(g), self.rows(g)]
        there = self.from_z.at[g, k - 1, 0 : self.count(g)]
        return self.copy(part, there, g, self.sender(g, 2), 3, self.to_z(k))

    def back_y_copy(self, g):
        part = self.own.at[g, self.rows(g)]
        return self.copy(part, self.from_z.at[g, 3, 0 : self.count(g)], g, 4 + g, 4, self.to_y())

    def back_core_copy(self, g):
        part = self.own.at[g, self.half]
        return self.copy(part, part, g, 3, 5, self.to_core())

    def start(self, g):
        self.core_copy(g).start()

    def after_core(self, g):
        self.core_copy(g).wait_recv()
        ring = g % self.from_core.shape[0]
        for a in range(4):
            for b in range(2):
                self.full[a, b, self.slot(g), self.half] += self.from_core[ring, a, b]
        (self.x_copy(g) if g in self.whole else self.y_copy(g)).start()

    def after_y(self, g):
        self.y_copy(g).wait_recv()
        for a in range(4):
            for b in range(2):
                self.full[a, b, self.slot(g), self.own_third] += self.from_y[g, a, b]
        self.x_copy(g).start()

    def after_x(self, g):
        self.x_copy(g).wait_recv()
        for a in range(4):
            part = self.from_x[g, a, 0 : self.count(g)]
            self.full[a, self.x, self.slot(g), self.rows(g)] += part
        for k in (1, 2, 3):
            self.z_copy(g, k).start()

    def after_z(self, g):
        total = self.full[self.z, self.x, self.slot(g), self.rows(g)].astype(jnp.float32)
        part = self.from_z.at[g, 0:3, 0 : self.count(g)]
        pltpu.make_async_copy(part, part, self.recv_sems.at[g, 3]).wait()
        for k in (1, 2, 3):
            total = total + self.from_z[g, k - 1, 0 : self.count(g)].astype(jnp.float32)
        self.own[g, self.rows(g)] = total.astype(jnp.bfloat16)
        self.back_y_copy(g).start()

    def after_back_y(self, g):
        self.back_y_copy(g).wait_recv()
        self.back_y_copy(g).wait_send()
        got = self.from_z.at[g, 3]
        if g in self.whole:
            self.own[g, self.half] += got[...]
        else:
            self.own[g, self.shared] += got[self.shared_in]
            self.own[g, self.other_third] = got[self.third_in]
        self.back_core_copy(g).start()

    def after_back_core(self, g):
        part = self.own.at[g, self.other_half]
        self.copy(part, part, g, 3, 5, self.to_core()).wait_recv()

    def drain(self):
        units, rows = self.own.shape[:2]
        few = len(self.whole)
        part = rows // 3
        for n, part in (
            (0, self.full.at[:, :, 0 : units // 2]),
            (1, self.full.at[:, :, 0 : units - few, 0:part]),
            (2, self.from_z.at[0 : units - few, 0:3, 0:part]),
            (3, self.own.at[0 : units // 2]),
            (4 + units, self.from_x.at[0:few]),
            (5 + units, self.from_z.at[0:few, 0:3]),
        ):
            pltpu.make_async_copy(part, part, self.send_sems.at[n]).wait()


def compute(inputs, lengths, cotangent, weights):
    (
        full_query, full_key, full_value, full_output, full_gain, full_table, full_inner,
        full_outer, full_ffn_gain,
    ) = weights
    pairs_here, seq_len, model_width = inputs.shape
    row_count = pairs_here * seq_len
    head_count = full_table.shape[1]
    tile = 128
    relative = rel_vec(full_table, tile)
    flat_inputs = inputs.reshape(row_count, model_width).astype(jnp.float32)
    normed = rms_norm(flat_inputs, full_gain.astype(jnp.float32)).astype(jnp.bfloat16)
    joined = jnp.concatenate((full_query, full_key, full_value), axis=1)
    projected = jnp.dot(normed, joined, preferred_element_type=jnp.float32).astype(jnp.bfloat16)
    queries = projected[:, :model_width]
    key_rows = projected[:, model_width : 2 * model_width]
    value_rows = projected[:, 2 * model_width :]
    pair_rows = [slice(n * seq_len, (n + 1) * seq_len) for n in range(pairs_here)]
    forward_parts = [
        att_fwd(queries[r], key_rows[r], value_rows[r], relative, lengths[n : n + 1], tile)
        for n, r in enumerate(pair_rows)
    ]
    attended = jnp.concatenate([part[0] for part in forward_parts], axis=0)
    middle = flat_inputs + jnp.dot(attended, full_output, preferred_element_type=jnp.float32)
    normed_ffn = rms_norm(middle, full_ffn_gain.astype(jnp.float32)).astype(jnp.bfloat16)
    raised = jnp.dot(normed_ffn, full_inner, preferred_element_type=jnp.float32)
    active = gelu(raised).astype(jnp.bfloat16)
    lowered = jnp.dot(active, full_outer, preferred_element_type=jnp.float32)
    block_output = (middle + lowered).astype(jnp.bfloat16).reshape(pairs_here, seq_len, model_width)
    positions = jnp.arange(seq_len, dtype=jnp.int32)
    row_live = (positions[None, :] < lengths[:, None]).astype(jnp.float32)
    seed_rows = (cotangent.astype(jnp.float32) * row_live[:, :, None]).reshape(
        row_count, model_width
    )
    seed_low = seed_rows.astype(jnp.bfloat16)
    grad_active = contract_cols(seed_low, full_outer)
    grad_outer = contract_rows(active, seed_low)
    grad_raised = jax.vjp(gelu, raised)[1](grad_active)[0].astype(jnp.bfloat16)
    grad_inner = contract_rows(normed_ffn, grad_raised)
    grad_normed_ffn = contract_cols(grad_raised, full_inner)
    ffn_pull = jax.vjp(rms_norm, middle, full_ffn_gain.astype(jnp.float32))[1]
    grad_middle_part, grad_ffn_gain = ffn_pull(grad_normed_ffn)
    grad_middle = seed_rows + grad_middle_part
    joined = jnp.concatenate((full_query, full_key, full_value), axis=1)
    middle_low = grad_middle.astype(jnp.bfloat16)
    grad_attended = contract_cols(middle_low, full_output).astype(jnp.bfloat16)
    grad_output = contract_rows(attended, middle_low)
    backward_parts = [
        att_bwd(
            queries[r], key_rows[r], value_rows[r], grad_attended[r], forward_parts[n][1], tile
        )
        for n, r in enumerate(pair_rows)
    ]
    grad_projected = jnp.concatenate(
        [jnp.concatenate(part[:3], axis=1) for part in backward_parts], axis=0
    )
    grad_joined = contract_rows(normed, grad_projected)
    grad_normed = contract_cols(grad_projected, joined)
    attention_pull = jax.vjp(rms_norm, flat_inputs, full_gain.astype(jnp.float32))[1]
    grad_inputs_part, grad_attention_gain = attention_pull(grad_normed)
    input_grad = (grad_middle + grad_inputs_part).reshape(pairs_here, seq_len, model_width)
    grad_relative = sum(part[3] for part in backward_parts)
    grad_table = lax.dot_general(
        rel_hits(tile).astype(jnp.float32),
        grad_relative,
        (((1,), (1,)), ((), ())),
        precision=highest,
    )
    return block_output, input_grad, (
        grad_joined[:, :model_width],
        grad_joined[:, model_width : 2 * model_width],
        grad_joined[:, 2 * model_width :],
        grad_output,
        grad_attention_gain,
        grad_table,
        grad_inner,
        grad_outer,
        grad_ffn_gain,
    )


def gather_all(query_weight, key_weight, value_weight, output_weight, attention_gain, bias_table,
               inner_weight, outer_weight, feedforward_gain):
    return tuple(
        lax.all_gather(part, "fsdp", axis=0, tiled=True)
        for part in (
            query_weight, key_weight, value_weight, output_weight, attention_gain, bias_table,
            inner_weight, outer_weight, feedforward_gain,
        )
    )


def sum_all(gradients):
    def one(part):
        part = lax.psum_scatter(
            part.astype(jnp.bfloat16), "fsdp", scatter_dimension=0, tiled=True
        )
        return lax.psum(part, "rep").astype(jnp.float32)

    return tuple(one(part) for part in gradients)


def gelu_parts(z):
    square = z * z
    t = jnp.tanh(gelu_coeff * z * (1.0 + 0.044715 * square))
    half = 0.5 * (1.0 + t)
    slope = half + (0.5 * gelu_coeff) * z * (1.0 - t * t) * (1.0 + (3 * 0.044715) * square)
    return z * half, slope


def lanes(start, size):
    return pl.ds(start if isinstance(start, int) else pl.multiple_of(start, 128), size)


def rows_at(start, size):
    return pl.ds(pl.multiple_of(start, size), size)


def loop(count, body):
    def step(n, carry):
        body(n)
        return carry

    lax.fori_loop(0, count, step, 0)


def norm_back(grad, gain, values):
    inverse = lax.rsqrt(jnp.mean(values * values, axis=-1, keepdims=True) + epsilon)
    scaled = grad * gain
    centre = jnp.mean(scaled * values, axis=-1, keepdims=True)
    back = inverse * scaled - values * (inverse * inverse * inverse * centre)
    return back, jnp.sum(grad * values * inverse, axis=0, keepdims=True)


class Layer:
    def __init__(self, **refs):
        self.__dict__.update(refs)
        self.seq, self.width = self.x.shape
        self.tile = 128
        self.row_block = 128
        self.shard_rows = self.bank.shape[3]

    def unit(self, u, column=None, size=None):
        if column is None:
            block = self.bank[:, :, u]
        else:
            block = self.bank[:, :, u, :, lanes(column, size)]
        return block.reshape(-1, block.shape[-1])

    def row_chunks(self, body):
        size = self.row_block
        loop(self.seq // size, lambda n: body(rows_at(n * size, size)))

    def small_arrays(self):
        flat = self.all_small[...].reshape(-1, 128)
        tile = self.tile
        slot = lax.broadcasted_iota(jnp.int32, (flat.shape[0], 4 * tile), 1)
        offset = jnp.where(slot < 3 * tile, slot - tile, slot - 5 * tile)
        row = lax.broadcasted_iota(jnp.int32, (flat.shape[0], 4 * tile), 0)
        per = NB // 8
        inside = row % 16 - 2
        wanted = jnp.where((inside >= 0) & (inside < per), (row // 16) * per + inside, -1)
        hits = (bucket_of(offset) == wanted).astype(jnp.bfloat16)
        self.rel[...] = dot_c(flat, hits)[: self.rel.shape[0]]
        for index, ref in ((0, self.gain_a), (1, self.gain_f)):
            total = jnp.zeros((1, self.width), jnp.float32)
            for shard in range(8):
                part = self.all_small[shard].astype(jnp.float32)[index : index + 1]
                wide = jnp.concatenate(
                    [part, jnp.zeros((1, self.width - 128), jnp.float32)], axis=1
                )
                total = total + (
                    pltpu.roll(wide, shard * self.shard_rows, axis=1) if shard else wide
                )
            ref[...] = total

    def norm_in(self):
        gain = self.gain_a[...]

        def body(r):
            self.normed[r] = rms_norm(self.x[r].astype(jnp.float32), gain).astype(jnp.bfloat16)

        self.row_chunks(body)

    def mask_seed(self):
        def body(r):
            index = lax.broadcasted_iota(jnp.int32, (self.row_block, 1), 0) + r.start
            live = index < self.length[0]
            self.seed[r] = jnp.where(live, self.seed[r], jnp.bfloat16(0))

        self.row_chunks(body)

    def project(self, u):
        def body(n):
            self.qkv[u, :, lanes(n * 256, 256)] = dot(
                self.normed[...], self.unit(u, n * 256, 256)
            ).astype(jnp.bfloat16)

        loop(self.width // 256, body)

    def strip_for(self, head, strip):
        tile = self.tile
        rel = self.rel[pl.ds(head, 1), :]
        rolled = pltpu.roll(
            jnp.broadcast_to(rel, (tile, 4 * tile)), 0, axis=1, stride=1, stride_axis=0
        )
        strip[:, 2 * tile : 5 * tile] = rolled[:, : 3 * tile]
        strip[:, : 2 * tile] = jnp.broadcast_to(rel[:, :1], (tile, 2 * tile))
        strip[:, 5 * tile :] = jnp.broadcast_to(rel[:, 3 * tile - 1 : 3 * tile], (tile, 2 * tile))

    def pair_lanes(self, slot):
        third = self.width // 3
        return [lanes(slot * 128 + n * third, 128) for n in range(3)]

    def probs_store(self, pair, slot):
        return pltpu.make_async_copy(
            self.probs.at[slot], self.probs_far.at[pair], self.probs_sems.at[slot]
        )

    def probs_load(self, pair, slot):
        return pltpu.make_async_copy(
            self.probs_far.at[pair], self.probs.at[slot], self.probs_sems.at[slot]
        )

    def attend(self, unit, slot):
        tile, seq = self.tile, self.seq
        pair = 2 * unit + slot
        if unit > 0:
            self.probs_store(pair, slot).wait()
        lane = lax.broadcasted_iota(jnp.int32, (1, 128), 1)
        own = (lane < 64, lane >= 64)
        key_at = lax.broadcasted_iota(jnp.int32, (1, seq), 1)
        mask = jnp.where(key_at < self.length[0], 0.0, masked_score)
        q_at, k_at, v_at = self.pair_lanes(slot)
        q = self.qkv[unit, :, q_at]
        k = self.qkv[unit, :, k_at]
        v = self.qkv[unit, :, v_at]
        for head in range(2):
            self.strip_for(pair * 2 + head, self.strip.at[head])
            self.scores[head] = dot_t(jnp.where(own[head], q, jnp.bfloat16(0)), k)

        def soften(head):
            for block in range(seq // tile):
                r = slice(block * tile, (block + 1) * tile)
                first = (seq // tile - 1 - block) * tile
                bias = self.strip[head, :, first : first + seq]
                scores = self.scores[head, r, :] + (bias + mask)
                peak = jnp.max(scores, axis=-1, keepdims=True)
                raised = jnp.exp(scores - peak)
                total = jnp.sum(raised, axis=-1, keepdims=True)
                self.probs[slot, head, r, :] = (raised * (1.0 / total)).astype(jnp.bfloat16)
            return dot(self.probs[slot, head], v)

        outs = [soften(head) for head in range(2)]
        self.attended[:, lanes(pair * 128, 128)] = jnp.where(own[0], *outs).astype(jnp.bfloat16)
        self.probs_store(pair, slot).start()

    def middle_rows(self):
        def body(n):
            c = lanes(n * 256, 256)
            self.middle[:, c] = self.x[:, c].astype(jnp.float32) + dot(
                self.attended[...], self.unit(3, n * 256, 256)
            )

        loop(self.width // 256, body)
        gain = self.gain_f[...]

        def norm(r):
            self.normed_ffn[r] = rms_norm(self.middle[r], gain).astype(jnp.bfloat16)

        self.row_chunks(norm)

    def raise_unit(self, i):
        def body(n):
            raised = dot(self.normed_ffn[...], self.unit(4 + i, n * 256, 256))
            active, slope = gelu_parts(raised)
            c = lanes(i * self.width + n * 256, 256)
            self.active[:, c] = active.astype(jnp.bfloat16)
            self.slope[:, c] = slope.astype(jnp.bfloat16)

        loop(self.width // 256, body)

    def outer_grad(self, shard):
        size = 4 * self.shard_rows
        block = dot_c(self.active[:, lanes(shard * size, size)], self.seed[...])
        self.bank[shard // 2, shard % 2, 12:16] = block.astype(jnp.bfloat16).reshape(
            4, self.shard_rows, self.width
        )

    def lower(self, n):
        outer = self.bank[:, :, 8:12, :, lanes(n * 256, 256)].reshape(-1, 256)
        c = lanes(n * 256, 256)
        self.mid_low[:, c] = (self.middle[:, c] + dot(self.active[...], outer)).astype(
            jnp.bfloat16
        )

    def raised_grad(self, shard):
        size = 4 * self.shard_rows
        outer = self.bank[shard // 2, shard % 2, 8:12].reshape(size, self.width)
        c = lanes(shard * size, size)
        grad = dot_t(self.seed[...], outer) * self.slope[:, c].astype(jnp.float32)
        self.slope[:, c] = grad.astype(jnp.bfloat16)

    def inner_grad(self, i):
        def body(n):
            c = lanes(i * self.width + n * 256, 256)
            block = dot_c(self.normed_ffn[...], self.slope[:, c]).astype(jnp.bfloat16)
            self.bank[:, :, 16 + i, :, lanes(n * 256, 256)] = block.reshape(
                4, 2, self.shard_rows, 256
            )

        loop(self.width // 256, body)

    def middle_grad(self, part):
        total = None
        for i in range(4):
            inner = self.bank[2 * part : 2 * part + 2, :, 4 + i].reshape(-1, self.width)
            term = dot_t(self.slope[:, i * self.width : (i + 1) * self.width], inner)
            total = term if total is None else total + term
        size = self.width // 2
        self.grad_mid[:, part * size : (part + 1) * size] = total

    def middle_norm(self):
        gain = self.gain_f[...]
        self.gain_f_grad[...] = jnp.zeros_like(self.gain_f_grad)

        def body(r):
            back, terms = norm_back(self.grad_mid[r], gain, self.middle[r])
            total = self.seed[r].astype(jnp.float32) + back
            self.gain_f_grad[...] += terms
            self.grad_mid[r] = total
            self.mid_low[r] = total.astype(jnp.bfloat16)

        self.row_chunks(body)

    def square_grad(self, left, right, slot):
        def body(n):
            block = dot_c(left[...], right(lanes(n * 256, 256))).astype(jnp.bfloat16)
            self.bank[:, :, slot, :, lanes(n * 256, 256)] = block.reshape(
                4, 2, self.shard_rows, 256
            )

        loop(self.width // 256, body)

    def attended_grad(self):
        size = self.width // 2
        for part in range(2):
            weight = self.bank[2 * part : 2 * part + 2, :, 3].reshape(size, self.width)
            self.attended[:, part * size : (part + 1) * size] = dot_t(
                self.mid_low[...], weight
            ).astype(jnp.bfloat16)

    def attend_back(self, unit, slot):
        tile, seq = self.tile, self.seq
        pair = 2 * unit + slot
        self.probs_load(pair, slot).wait()
        lane = lax.broadcasted_iota(jnp.int32, (1, 128), 1)
        own = (lane < 64, lane >= 64)
        q_at, k_at, v_at = self.pair_lanes(slot)
        q = self.qkv[unit, :, q_at]
        k = self.qkv[unit, :, k_at]
        v = self.qkv[unit, :, v_at]
        grad_out = self.attended[:, lanes(pair * 128, 128)]
        blocks = seq // tile
        for head in range(2):
            self.scores[head] = dot_t(jnp.where(own[head], grad_out, jnp.bfloat16(0)), v)

        def back(head):
            sums = [None] * 5
            for block in range(blocks):
                r = slice(block * tile, (block + 1) * tile)
                probs = self.probs[slot, head, r, :].astype(jnp.float32)
                weighted = probs * self.scores[head, r, :]
                centre = jnp.sum(weighted, axis=-1, keepdims=True)
                grad = weighted - probs * centre
                self.grad_scores[head, r, :] = grad.astype(jnp.bfloat16)
                for other in range(blocks):
                    apart = min(2, max(-2, other - block)) + 2
                    part = grad[:, other * tile : (other + 1) * tile]
                    sums[apart] = part if sums[apart] is None else sums[apart] + part
            zero = jnp.zeros((tile, tile), jnp.float32)
            near = shear_sum(jnp.concatenate([sums[1], sums[2], sums[3], zero], axis=1), 4 * tile)
            far = jnp.concatenate(
                [
                    jnp.zeros((1, 2 * tile), jnp.float32),
                    jnp.sum(sums[4], axis=0, keepdims=True),
                    jnp.sum(sums[0], axis=0, keepdims=True),
                ],
                axis=1,
            )
            self.rel_grad[pl.ds(pair * 2 + head, 1), :] = near + far
            return (
                dot(self.grad_scores[head], k),
                dot_c(q, self.grad_scores[head]).T,
                dot_c(grad_out, self.probs[slot, head]).T,
            )

        for at, first, second in zip((q_at, k_at, v_at), back(0), back(1)):
            self.qkv[unit, :, at] = jnp.where(own[0], first, second).astype(jnp.bfloat16)
        if 2 * unit + 2 < self.probs_far.shape[0]:
            self.probs_load(pair + 2, slot).start()

    def normed_grad(self, part):
        size = self.width // 2
        total = None
        for u in range(3):
            weight = self.bank[2 * part : 2 * part + 2, :, u].reshape(size, self.width)
            term = dot_t(self.qkv[u], weight)
            total = term if total is None else total + term
        self.middle[:, part * size : (part + 1) * size] = total

    def input_grad(self):
        gain = self.gain_a[...]
        self.gain_a_grad[...] = jnp.zeros_like(self.gain_a_grad)

        def body(r):
            back, terms = norm_back(self.middle[r], gain, self.x[r].astype(jnp.float32))
            self.gain_a_grad[...] += terms
            self.grad_mid[r] += back

        self.row_chunks(body)

    def small_grads(self):
        tile = self.tile
        shape = (64, 4 * tile)
        slot = lax.broadcasted_iota(jnp.int32, shape, 1)
        offset = jnp.where(slot < 3 * tile, slot - tile, slot - 5 * tile)
        row = lax.broadcasted_iota(jnp.int32, shape, 0)
        per = NB // 8
        inside = row % 8 - 2
        wanted = jnp.where((inside >= 0) & (inside < per), (row // 8) * per + inside, -1)
        hits = (bucket_of(offset) == wanted).astype(jnp.float32)
        table = lax.dot_general(
            hits,
            self.rel_grad[...],
            (((1,), (1,)), ((), ())),
            precision=highest,
            preferred_element_type=jnp.float32,
        )
        rows = lax.broadcasted_iota(jnp.int32, (8, 128), 0)
        lane = lax.broadcasted_iota(jnp.int32, (8, 128), 1)
        for shard in range(8):
            block = table[8 * shard : 8 * shard + 8]
            for index, ref in ((0, self.gain_a_grad), (1, self.gain_f_grad)):
                wide = ref[...]
                if shard:
                    wide = pltpu.roll(wide, self.width - shard * self.shard_rows, axis=1)
                here = (rows == index) & (lane < self.shard_rows)
                block = jnp.where(here, jnp.broadcast_to(wide[:, :128], (8, 128)), block)
            self.small_out[shard] = block


(
    SEND_Z, SEND_X, GOT_SECOND, GOT_BESIDE, GOT_ACROSS, GOT_X, GOT_Y, GOT_CORE, DRAIN,
    PASS_BESIDE, SMALL_Z, SMALL_X, SMALL_SECOND, SMALL_BESIDE, SMALL_ACROSS, SUM_SEND, SUM_CORE,
    SUM_Y, SUM_X, SUM_Z, SUM_BACK, SUM_DONE, NORM, PROJECT, ATTEND, MIDDLE, RAISE, OUTER_GRAD,
    LOWER, RAISED_GRAD, INNER_GRAD, MIDDLE_GRAD, MIDDLE_NORM, OUTPUT_GRAD, ATTENDED_GRAD,
    ATTEND_BACK, SQUARE_GRAD, NORMED_GRAD, INPUT_GRAD, SMALL, SMALL_SUM, SMALL_DONE,
) = range(42)

ORDER = (
    (SMALL_Z, 0), (SMALL_X, 0), (SEND_Z, 0), (SEND_X, 5), (SEND_X, 0), (SEND_X, 3), (SEND_X, 7),
    (SEND_X, 1), (GOT_BESIDE, 0), (SMALL_SECOND, 0), (SMALL_BESIDE, 0), (SEND_Z, 1), (SEND_Z, 2),
    (GOT_SECOND, 0), (SEND_X, 2), (GOT_ACROSS, 0), (SMALL_ACROSS, 0), (PASS_BESIDE, 5),
    (GOT_BESIDE, 1), (GOT_SECOND, 1), (SEND_Z, 4), (PASS_BESIDE, 2), (GOT_BESIDE, 2), (GOT_X, 0),
    (GOT_ACROSS, 1), (GOT_SECOND, 2), (SEND_Z, 3), (NORM, 0), (SEND_X, 4), (GOT_BESIDE, 4),
    (GOT_X, 1), (GOT_ACROSS, 2), (SEND_Z, 7), (GOT_SECOND, 3), (GOT_SECOND, 4), (GOT_Y, 0),
    (GOT_X, 2), (GOT_Y, 1), (GOT_BESIDE, 3), (GOT_CORE, 0), (SEND_Z, 6), (GOT_ACROSS, 3),
    (GOT_SECOND, 7), (PROJECT, 0), (GOT_BESIDE, 7), (GOT_ACROSS, 4), (SEND_Z, 5), (SEND_X, 6),
    (GOT_CORE, 1), (GOT_Y, 2), (PROJECT, 1), (GOT_X, 3), (GOT_BESIDE, 6), (GOT_CORE, 2),
    (GOT_SECOND, 6), (SEND_Z, 9), (ATTEND, 0), (GOT_ACROSS, 7), (GOT_Y, 3), (GOT_X, 4),
    (GOT_SECOND, 5), (GOT_BESIDE, 5), (SEND_Z, 8), (GOT_ACROSS, 6), (SEND_X, 8), (SEND_Z, 11),
    (ATTEND, 1), (GOT_X, 7), (GOT_BESIDE, 9), (GOT_ACROSS, 5), (SEND_X, 11), (PROJECT, 2),
    (GOT_X, 6), (ATTEND, 2), (GOT_SECOND, 9), (GOT_SECOND, 8), (GOT_Y, 7), (SEND_Z, 10),
    (PASS_BESIDE, 8), (SEND_X, 9), (GOT_BESIDE, 11), (GOT_CORE, 3), (MIDDLE, 0), (GOT_Y, 6),
    (GOT_CORE, 7), (GOT_X, 5), (GOT_ACROSS, 9), (GOT_Y, 4), (GOT_ACROSS, 8), (RAISE, 3),
    (GOT_CORE, 6), (SEND_X, 10), (GOT_BESIDE, 8), (GOT_SECOND, 11), (RAISE, 2), (GOT_ACROSS, 11),
    (PASS_BESIDE, 11), (GOT_X, 8), (GOT_X, 9), (GOT_Y, 5), (GOT_SECOND, 10), (OUTER_GRAD, 1),
    (GOT_ACROSS, 10), (DRAIN, 0), (GOT_CORE, 5), (GOT_BESIDE, 10), (GOT_CORE, 4), (RAISE, 1),
    (GOT_X, 11), (GOT_Y, 8), (RAISE, 0), (GOT_X, 10), (GOT_Y, 9), (OUTER_GRAD, 0), (SUM_SEND, 0),
    (GOT_Y, 11), (SUM_CORE, 0), (GOT_Y, 10), (SUM_SEND, 1), (SUM_SEND, 2), (GOT_CORE, 8),
    (SUM_SEND, 3), (GOT_CORE, 9), (GOT_CORE, 11), (GOT_CORE, 10), (RAISED_GRAD, 0), (SUM_CORE, 1),
    (SUM_CORE, 2), (INNER_GRAD, 0), (SUM_SEND, 4), (SUM_SEND, 5), (SUM_X, 0), (SUM_CORE, 3),
    (LOWER, 0), (RAISED_GRAD, 1), (SUM_Y, 1), (SUM_CORE, 4), (MIDDLE_GRAD, 0), (SUM_X, 2),
    (LOWER, 1), (MIDDLE_GRAD, 1), (SUM_Y, 3), (SUM_CORE, 5), (INNER_GRAD, 1), (SUM_SEND, 6),
    (SUM_Y, 4), (SUM_SEND, 7), (SUM_X, 1), (LOWER, 2), (MIDDLE_NORM, 0), (SUM_X, 3),
    (SUM_CORE, 6), (OUTPUT_GRAD, 0), (SUM_Y, 5), (ATTENDED_GRAD, 0), (SUM_CORE, 7),
    (ATTEND_BACK, 0), (SUM_SEND, 8), (SUM_X, 4), (SQUARE_GRAD, 0), (SUM_Y, 6), (SUM_CORE, 8),
    (SUM_SEND, 9), (SUM_X, 5), (ATTEND_BACK, 1), (SUM_Y, 7), (SQUARE_GRAD, 1), (SUM_CORE, 9),
    (SUM_X, 6), (SUM_Y, 8), (SUM_SEND, 10), (ATTEND_BACK, 2), (SUM_X, 7), (SUM_CORE, 10),
    (SQUARE_GRAD, 2), (SUM_SEND, 11), (SUM_Y, 9), (SUM_CORE, 11), (SUM_X, 8), (SUM_Z, 6),
    (NORMED_GRAD, 1), (SUM_Y, 10), (SUM_Z, 3), (SUM_X, 9), (SUM_Z, 0), (SUM_Y, 11), (SUM_Z, 2),
    (SUM_Z, 8), (NORMED_GRAD, 0), (SUM_BACK, 6), (SUM_Z, 1), (SUM_X, 10), (SUM_Z, 9), (SUM_Z, 5),
    (INPUT_GRAD, 0), (SUM_BACK, 0), (SUM_X, 11), (SUM_Z, 4), (SUM_Z, 7), (SUM_DONE, 0),
    (SMALL, 0), (SUM_BACK, 2), (SUM_Z, 10), (SMALL_SUM, 0), (SUM_BACK, 8), (SUM_BACK, 9),
    (SUM_BACK, 5), (SUM_Z, 11), (SUM_BACK, 1), (SUM_BACK, 10), (SUM_DONE, 2), (SUM_DONE, 1),
    (SUM_BACK, 7), (SUM_BACK, 3), (SUM_DONE, 6), (SUM_BACK, 4), (SUM_BACK, 11), (SUM_DONE, 5),
    (SUM_DONE, 10), (SUM_DONE, 3), (SUM_DONE, 7), (SUM_DONE, 9), (SMALL_DONE, 0), (SUM_DONE, 4),
    (SUM_DONE, 8), (SUM_DONE, 11),
)


def order_slot(n):
    return n + 12 if n < 8 else (7 if n == 8 else n - 5)


def fused_kernel(
    length, x, cot, gain_a_own, gain_f_own, table_own, query_own, key_own, value_own, output_own,
    inner_own, outer_own,
    block_far, grad_far, own_far, small_result, probs_far,
    bank, own_sum, from_core, from_y, from_x, from_z, small_wide, all_small, small_out,
    small_in, small_rep, probs, normed, qkv, attended, middle, normed_ffn, active, slope, seed,
    grad_mid, mid_low, scores, rel, rel_grad, gain_a, gain_f, gain_a_grad,
    gain_f_grad, strip, grad_scores,
    sends, recvs, sum_sends, sum_recvs, small_sends, small_recvs, back_sems, probs_sems,
    misc_sems, keep_sems,
):
    shard = lax.axis_index("fsdp")
    copy_id = lax.axis_index("rep")
    layer = Layer(
        length=length, x=x, bank=bank, all_small=all_small, small_out=small_out,
        probs=probs, probs_far=probs_far, probs_sems=probs_sems, normed=normed, qkv=qkv,
        attended=attended, middle=middle, normed_ffn=normed_ffn, active=active, slope=slope,
        seed=seed, grad_mid=grad_mid, mid_low=mid_low, scores=scores,
        rel=rel, rel_grad=rel_grad, gain_a=gain_a, gain_f=gain_f, gain_a_grad=gain_a_grad,
        gain_f_grad=gain_f_grad, strip=strip, grad_scores=grad_scores,
    )
    rows, width = query_own.shape
    chunks = inner_own.shape[1] // width
    units = 4 + 2 * chunks
    gather = Gather(bank, sends, recvs)
    scatter = Scatter(
        order_slot, bank, own_sum, from_core, from_y, from_x, from_z, sum_sends, sum_recvs
    )
    pairs = probs_far.shape[0]

    def remote(src, dst, send, recv, device):
        return pltpu.make_async_remote_copy(
            src_ref=src, dst_ref=dst, send_sem=send, recv_sem=recv, device_id=device,
            device_id_type=MESH,
        )

    def peer(k):
        return (lax.rem(shard + k, 8), copy_id)

    def rep_peer(k):
        return (shard, lax.rem(copy_id + k, 4))

    parts = [output_own]
    parts += [inner_own.at[:, pl.ds(i * width, width)] for i in range(chunks)]
    parts += [outer_own.at[pl.ds(i * rows, rows)] for i in range(chunks)]
    third = width // 3
    homes = [
        (part.at[:, pl.ds(u * third, third)], bank.at[gather.z, gather.x, u, :, pl.ds(n * third, third)])
        for u in range(3)
        for n, part in enumerate((query_own, key_own, value_own))
    ]
    homes += [(part, bank.at[gather.z, gather.x, 3 + u]) for u, part in enumerate(parts)]
    keeps = [
        pltpu.make_async_copy(part, home, keep_sems.at[0]) for part, home in homes
    ]
    keep_seed = pltpu.make_async_copy(cot, seed, keep_sems.at[1])
    keeps.append(keep_seed)
    peers = gather.peers()
    greet(peers, gather.at_end)
    for copy in keeps:
        copy.start()
    small_wide[...] = jnp.zeros_like(small_wide)
    small_wide[0:1, :rows] = gain_a_own[...].astype(jnp.float32)
    small_wide[1:2, :rows] = gain_f_own[...].astype(jnp.float32)
    per, heads = table_own.shape
    small_wide[2 : 2 + per, :heads] = table_own[...].astype(jnp.float32)
    all_small[shard] = small_wide[...].astype(jnp.bfloat16)
    smalls = SmallGather(gather, all_small, small_sends, small_recvs)
    mine = bank.at[gather.z, gather.x, 0:units]
    pltpu.make_async_copy(mine, mine, keep_sems.at[0]).wait()
    all_greeted(peers, gather.at_end)

    def store(n):
        return pltpu.make_async_copy(own_sum.at[n], own_far.at[n], misc_sems.at[2])

    def sum_done(n):
        scatter.after_back_core(n)
        store(n).start()

    block_store = pltpu.make_async_copy(mid_low, block_far, misc_sems.at[0])
    grad_store = pltpu.make_async_copy(grad_mid, grad_far, misc_sems.at[1])
    back_copies = [
        remote(
            small_out.at[lax.rem(shard + k, 8)], small_in.at[k - 1], back_sems.at[0],
            back_sems.at[1], peer(k),
        )
        for k in range(1, 8)
    ]
    rep_copies = [
        remote(
            small_rep.at[copy_id], small_rep.at[copy_id], back_sems.at[2], back_sems.at[3],
            rep_peer(k),
        )
        for k in range(1, 4)
    ]

    def wait_for(part, sem):
        pltpu.make_async_copy(part, part, sem).wait()

    def norm(_):
        keep_seed.wait()
        layer.mask_seed()
        smalls.after_x(0)
        layer.small_arrays()
        layer.norm_in()

    def middle_rows(_):
        layer.middle_rows()
        for pair in (pairs - 2, pairs - 1):
            layer.probs_store(pair, pair % 2).wait()
        for pair in (0, 1):
            layer.probs_load(pair, pair).start()

    def lower(n):
        layer.lower(n)
        if n == width // 256 - 1:
            block_store.start()

    def middle_norm(_):
        block_store.wait()
        layer.middle_norm()
        rel_grad[...] = jnp.zeros_like(rel_grad)

    def input_grad(_):
        layer.input_grad()
        grad_store.start()

    def small_sums(_):
        layer.small_grads()
        for copy in back_copies:
            copy.start()

    def small_sum(_):
        wait_for(small_in, back_sems.at[1])
        total = small_out[shard]
        for k in range(7):
            total = total + small_in[k]
        small_rep[copy_id] = total
        for copy in rep_copies:
            copy.start()

    def small_done(_):
        wait_for(small_rep.at[0:3], back_sems.at[3])
        small_result[...] = (small_rep[0] + small_rep[1]) + (small_rep[2] + small_rep[3])

    work = {
        SEND_Z: gather.send_z,
        SEND_X: gather.send_x,
        GOT_SECOND: gather.after_second,
        GOT_BESIDE: gather.after_beside,
        GOT_ACROSS: gather.after_across,
        GOT_X: gather.after_x,
        GOT_Y: gather.after_y,
        GOT_CORE: gather.after_core,
        DRAIN: gather.drain,
        PASS_BESIDE: gather.pass_beside,
        SMALL_Z: smalls.send_z,
        SMALL_X: smalls.send_x,
        SMALL_SECOND: smalls.after_second,
        SMALL_BESIDE: smalls.after_beside,
        SMALL_ACROSS: smalls.after_across,
        SUM_SEND: scatter.start,
        SUM_CORE: scatter.after_core,
        SUM_Y: scatter.after_y,
        SUM_X: scatter.after_x,
        SUM_Z: scatter.after_z,
        SUM_BACK: scatter.after_back_y,
        SUM_DONE: sum_done,
        NORM: norm,
        PROJECT: layer.project,
        ATTEND: lambda u: loop(2, functools.partial(layer.attend, u)),
        MIDDLE: middle_rows,
        RAISE: layer.raise_unit,
        OUTER_GRAD: lambda k: loop(4, lambda n: layer.outer_grad(4 * k + n)),
        LOWER: lower,
        RAISED_GRAD: lambda k: loop(4, lambda n: layer.raised_grad(4 * k + n)),
        INNER_GRAD: lambda k: loop(2, lambda n: layer.inner_grad(2 * k + n)),
        MIDDLE_GRAD: layer.middle_grad,
        MIDDLE_NORM: middle_norm,
        OUTPUT_GRAD: lambda _: layer.square_grad(attended, lambda c: mid_low[:, c], 7),
        ATTENDED_GRAD: lambda _: layer.attended_grad(),
        ATTEND_BACK: lambda u: loop(2, functools.partial(layer.attend_back, u)),
        SQUARE_GRAD: lambda u: layer.square_grad(normed, lambda c: qkv[u, :, c], 4 + u),
        NORMED_GRAD: layer.normed_grad,
        INPUT_GRAD: input_grad,
        SMALL: small_sums,
        SMALL_SUM: small_sum,
        SMALL_DONE: small_done,
    }
    for name, n in ORDER:
        work[name](n)
    gather.drain(1)
    smalls.drain(0)
    scatter.drain()
    wait_for(small_in, back_sems.at[0])
    wait_for(small_rep.at[0:3], back_sems.at[2])
    wait_for(own_sum, misc_sems.at[2])
    grad_store.wait()


def fused_call(length, x, cot, gain_a, gain_f, table, square, inner, outer):
    rows, width = square[0].shape
    units = 4 + 2 * (inner.shape[1] // width)
    heads = table.shape[1]
    seq = x.shape[0]
    half = rows // 2
    part = half // 3
    hidden = inner.shape[1]
    low, wide = jnp.bfloat16, jnp.float32
    anywhere = pl.BlockSpec(memory_space=pl.ANY)
    within = pl.BlockSpec(memory_space=pltpu.VMEM)
    sems = pltpu.SemaphoreType.DMA
    vm = pltpu.VMEM
    head_rows = -(-heads // 8) * 8
    return pl.pallas_call(
        fused_kernel,
        out_shape=(
            jax.ShapeDtypeStruct((seq, width), low),
            jax.ShapeDtypeStruct((seq, width), wide),
            jax.ShapeDtypeStruct((units, rows, width), low),
            jax.ShapeDtypeStruct((8, 128), wide),
            jax.ShapeDtypeStruct((heads // 2, 2, seq, seq), low),
        ),
        in_specs=[pl.BlockSpec(memory_space=pltpu.SMEM), within, anywhere]
        + [within] * 3
        + [anywhere] * 6,
        out_specs=[anywhere, anywhere, anywhere, within, anywhere],
        scratch_shapes=[
            vm((4, 2, units + 8, rows, width), low),
            vm((units, rows, width), low),
            vm((6, 4, 2, half, width), low),
            vm((units, 4, 2, part, width), low),
            vm((units, 4, half, width), low),
            vm((units, 4, half, width), low),
            vm((16, 128), wide),
            vm((8, 16, 128), low),
            vm((8, 8, 128), wide),
            vm((7, 8, 128), wide),
            vm((4, 8, 128), wide),
            vm((2, 2, seq, seq), low),
            vm((seq, width), low),
            vm((3, seq, width), low),
            vm((seq, width), low),
            vm((seq, width), wide),
            vm((seq, width), low),
            vm((seq, hidden), low),
            vm((seq, hidden), low),
            vm((seq, width), low),
            vm((seq, width), wide),
            vm((seq, width), low),
            vm((2, seq, seq), wide),
            vm((head_rows, 512), wide),
            vm((128, 512), wide),
            vm((1, width), wide),
            vm((1, width), wide),
            vm((1, width), wide),
            vm((1, width), wide),
            vm((2, 128, 128 * 7), wide),
            vm((2, seq, seq), low),
            sems((2,)),
            sems((units, Gather.slots)),
            sems((6 + units,)),
            sems((units, Scatter.slots)),
            sems((1,)),
            sems((4,)),
            sems((4,)),
            sems((2,)),
            sems((3,)),
            sems((2,)),
        ],
        compiler_params=pltpu.CompilerParams(
            collective_id=0, has_side_effects=True, vmem_limit_bytes=127 * 2**19
        ),
    )(length, x, cot, gain_a, gain_f, table, *square, inner, outer)


def finish_kernel(
    block_in, grad_in, sums_far, small, block_out, grad_out, query_out, key_out, value_out,
    output_out, gain_a, table, inner_out, outer_out, gain_f, block, grad, query, key, value, output,
    inner, outer, sums, in_sems, out_sems,
):
    units, rows, width = sums.shape
    chunks = inner.shape[1] // width
    third = width // 3
    straight = ((block_in, block, block_out), (grad_in, grad, grad_out))
    loads = [pltpu.make_async_copy(sums_far.at[n], sums.at[n], in_sems.at[n]) for n in range(units)]
    loads += [
        pltpu.make_async_copy(far, near, in_sems.at[units + n])
        for n, (far, near, _) in enumerate(straight)
    ]
    for copy in loads[units:] + loads[:units]:
        copy.start()
    stores = []

    def store(near, far):
        stores.append(pltpu.make_async_copy(near, far, out_sems.at[len(stores)]))
        stores[-1].start()

    for n, (_, near, far) in enumerate(straight):
        loads[units + n].wait()
        store(near, far)
    gain_a[...] = small[0:1, :rows]
    gain_f[...] = small[1:2, :rows]
    table[...] = small[2 : 2 + table.shape[0], : table.shape[1]]
    for i in range(chunks):
        part = pl.ds(i * rows, rows)
        loads[i].wait()
        outer[part, :] = sums[i].astype(jnp.float32)
        store(outer.at[part], outer_out.at[part])
    for i in range(chunks):
        part = pl.ds(i * width, width)
        loads[chunks + i].wait()
        inner[:, part] = sums[chunks + i].astype(jnp.float32)
        store(inner.at[:, part], inner_out.at[:, part])
    loads[2 * chunks].wait()
    output[...] = sums[2 * chunks].astype(jnp.float32)
    store(output, output_out)
    for u in range(3):
        loads[2 * chunks + 1 + u].wait()
        for n, ref in enumerate((query, key, value)):
            ref[:, u * third : (u + 1) * third] = sums[
                2 * chunks + 1 + u, :, n * third : (n + 1) * third
            ].astype(jnp.float32)
    for near, far in ((query, query_out), (key, key_out), (value, value_out)):
        store(near, far)
    for copy in stores:
        copy.wait()


def finish_call(block, grad, sums, small, table_shape, inner_shape, outer_shape):
    units, rows, width = sums.shape
    wide = jnp.float32
    anywhere = pl.BlockSpec(memory_space=pl.ANY)
    within = pl.BlockSpec(memory_space=pltpu.VMEM)
    shapes = [(rows, width)] * 4 + [(1, rows), table_shape, inner_shape, outer_shape, (1, rows)]
    places = [anywhere] * 4 + [within] * 2 + [anywhere] * 2 + [within]
    staged = [shape for shape, place in zip(shapes, places) if place is anywhere]
    return pl.pallas_call(
        finish_kernel,
        out_shape=[
            jax.ShapeDtypeStruct(block.shape, block.dtype),
            jax.ShapeDtypeStruct(grad.shape, grad.dtype),
        ]
        + [jax.ShapeDtypeStruct(shape, wide) for shape in shapes],
        in_specs=[anywhere, anywhere, anywhere, within],
        out_specs=[anywhere, anywhere] + places,
        scratch_shapes=[
            pltpu.VMEM(block.shape, block.dtype),
            pltpu.VMEM(grad.shape, grad.dtype),
            *[pltpu.VMEM(shape, wide) for shape in staged],
            pltpu.VMEM(sums.shape, sums.dtype),
            pltpu.SemaphoreType.DMA((units + 2,)),
            pltpu.SemaphoreType.DMA((units + 2,)),
        ],
        compiler_params=pltpu.CompilerParams(vmem_limit_bytes=63 * 2**20),
    )(block, grad, sums, small)


def local_linked(
    inputs, lengths, cotangent, query_weight, key_weight, value_weight, output_weight,
    attention_gain, bias_table, inner_weight, outer_weight, feedforward_gain,
):
    rows = query_weight.shape[0]
    square = (query_weight, key_weight, value_weight, output_weight)
    block, grad, sums, small, _ = fused_call(
        lengths, inputs[0], cotangent[0], attention_gain.reshape(1, rows),
        feedforward_gain.reshape(1, rows), bias_table, square, inner_weight, outer_weight,
    )
    block, grad, query, key, value, output, gain_a, table, inner, outer, gain_f = finish_call(
        block, grad, sums, small, bias_table.shape, inner_weight.shape, outer_weight.shape
    )
    return (
        block[None], grad[None], query, key, value, output, gain_a.reshape(rows), table, inner,
        outer, gain_f.reshape(rows),
    )


def local(inputs, lengths, cotangent, *shards):
    block_output, input_grad, gradients = compute(inputs, lengths, cotangent, gather_all(*shards))
    return (block_output, input_grad) + sum_all(gradients)


def can_link(mesh):
    return mesh.shape["fsdp"] == 8 and mesh.shape["rep"] == 4


def solution(mesh):
    placed = (
        P(("fsdp", "rep"), None, None),
        P(("fsdp", "rep")),
        P(("fsdp", "rep"), None, None),
        P("fsdp", None),
        P("fsdp", None),
        P("fsdp", None),
        P("fsdp", None),
        P("fsdp"),
        P("fsdp", None),
        P("fsdp", None),
        P("fsdp", None),
        P("fsdp"),
    )
    return jax.shard_map(
        local_linked if can_link(mesh) else local,
        mesh=mesh,
        in_specs=placed,
        out_specs=(
            P(("fsdp", "rep"), None, None),
            P(("fsdp", "rep"), None, None),
            P("fsdp", None),
            P("fsdp", None),
            P("fsdp", None),
            P("fsdp", None),
            P("fsdp"),
            P("fsdp", None),
            P("fsdp", None),
            P("fsdp", None),
            P("fsdp"),
        ),
        check_vma=False,
    )
```
